32 devices in a mesh: dp: 4 (over z), ctx: 8 (over y, x, core).
Axes of the slice: x: 2, y: 2, z: 4, core: 2. Of those that a mesh axis runs over, the one named last changes fastest.
Arguments:
- inputs: bfloat16 [4, 1024, 2048], P('dp', 'ctx'), may hold values from -12 to 12
- cotangent: bfloat16 [4, 1024, 2048], P('dp', 'ctx'), may hold values from -6 to 6
- documents: int32 [4, 1024], P('dp'), may hold values from 0 to 4, as said below
- block_place: int32 [8], replicated, may hold values from 0 to 7, as said below
- params: float32 [2048, 32768], P(('dp', 'ctx'))
- first_moment: float32 [2048, 32768], P(('dp', 'ctx'))
- second_moment: float32 [2048, 32768], P(('dp', 'ctx')), as said below
- gains: float32 [4, 2048], replicated, as said below
- gains_first: float32 [4, 2048], replicated
- gains_second: float32 [4, 2048], replicated, as said below
Outputs:
- output: bfloat16 [4, 1024, 2048], P('dp', 'ctx')
- input_grad: bfloat16 [4, 1024, 2048], P('dp', 'ctx')
- grad_norm: float32 [], replicated
- new_params: float32 [2048, 32768], P(('dp', 'ctx'))
- new_first: float32 [2048, 32768], P(('dp', 'ctx'))
- new_second: float32 [2048, 32768], P(('dp', 'ctx'))
- new_gains: float32 [4, 2048], replicated
- new_gains_first: float32 [4, 2048], replicated
- new_gains_second: float32 [4, 2048], replicated
The draws below stay inside these ranges and needn't reach their ends.
Inputs may be any that keep to these rules, and one draw needn't show every extreme that they name: A permutation: ctx index c holds sequence block block_place[c] of its row. `documents`: along sequence positions the ids never fall; in each row one document has tokens in every block. `second_moment`: positive. `gains`: positive. `gains_second`: positive.
All inputs are finite; a program needn't handle non-finite values.
Results may differ from the reference program's by a relative error of at most 0.015.
Values may be sent and summed in bfloat16 or wider, within the bound.
A program may use at most 1 GiB of HBM per device.

```python
import math
import jax
import jax.numpy as jnp
from jax import lax

D = 2048
FF = 8192
HD = 128
GROUP = 128
SEQ = 1024
ROWS = 4
NPARAM = 67117056
STEP = 10
N_CTX = 8


def layout(key):
    perm_key, cut_key = jax.random.split(key)
    placement = jax.random.permutation(perm_key, N_CTX).astype(jnp.int32)
    key_one, key_two, key_three, key_four = jax.random.split(cut_key, 4)
    start_big = jax.random.randint(key_one, (ROWS, 1), 2, GROUP)
    start_small = jax.random.randint(key_two, (ROWS, 1), 1, start_big)
    end_big = jax.random.randint(key_three, (ROWS, 1), SEQ - GROUP + 1, SEQ - 1)
    end_small = jax.random.randint(key_four, (ROWS, 1), end_big + 1, SEQ)
    indices = jnp.arange(SEQ, dtype=jnp.int32)
    positions = placement[indices // GROUP] * GROUP + indices % GROUP
    spots = positions[None, :]
    doc_ids = (spots >= start_small).astype(jnp.int32) + (spots >= start_big).astype(jnp.int32) + (spots >= end_big).astype(jnp.int32) + (spots >= end_small).astype(jnp.int32)
    return (placement, doc_ids)


def width_ramp(base):
    column_frac = jnp.arange(D, dtype=jnp.float32) / (D - 1)
    mean_square = (base * base - 1.0) / (2.0 * math.log(base))
    return base ** column_frac / math.sqrt(mean_square)


def draw_block_place(key, part):
    return layout(key)[0]


def draw_documents(key, part):
    return layout(key)[1]


def draw_inputs(key, part):
    key = jax.random.fold_in(key, 11)
    device_of = jnp.arange(ROWS, dtype=jnp.float32)[:, None] * N_CTX + (jnp.arange(SEQ) // GROUP).astype(jnp.float32)[None, :]
    row_frac = device_of / (ROWS * N_CTX - 1)
    base = jnp.clip(jax.random.normal(key, (ROWS, SEQ, D), jnp.float32), -4.0, 4.0)
    column_ramp = width_ramp(5.0)
    row_ramp = 1.5 ** row_frac
    return (base * column_ramp[None, None, :] * row_ramp[:, :, None]).astype(jnp.bfloat16)


def draw_params(key, part):
    key = jax.random.fold_in(key, 12)
    columns = jnp.arange(4 * D + 3 * FF)
    spread = jnp.where(columns >= 4 * D + 2 * FF, FF ** (-0.5), D ** (-0.5)).astype(jnp.float32)
    base = jnp.clip(jax.random.normal(key, (D, 4 * D + 3 * FF), jnp.float32), -4.0, 4.0)
    return base * spread[None, :]


def draw_gains(key, part):
    key = jax.random.fold_in(key, 13)
    column_frac = jnp.arange(D, dtype=jnp.float32) / (D - 1)
    key_one, key_two = jax.random.split(key)
    out_ramp = width_ramp(5.0)
    near = jax.random.uniform(key_one, (2, D), jnp.float32, 0.9, 1.1) * (1.7 ** column_frac)[None, :]
    far = jax.random.uniform(key_two, (2, D), jnp.float32, 0.8, 1.25) * out_ramp[None, :]
    return jnp.concatenate([near, far], axis=0)


def draw_first_moment(key, part):
    key = jax.random.fold_in(key, 21)
    ramp = width_ramp(5.0)
    base = jnp.clip(jax.random.normal(key, (D, 4 * D + 3 * FF), jnp.float32), -4.0, 4.0)
    return base * ramp[:, None] * (0.11 / NPARAM ** 0.5)


def draw_second_moment(key, part):
    key = jax.random.fold_in(key, 22)
    ramp = width_ramp(5.0)
    base = jax.random.uniform(key, (D, 4 * D + 3 * FF), jnp.float32, 1.0, 4.0)
    return base * (ramp * ramp)[:, None] * (0.053 / NPARAM)


def draw_gains_first(key, part):
    key = jax.random.fold_in(key, 23)
    return jnp.clip(jax.random.normal(key, (4, D), jnp.float32), -4.0, 4.0) * (0.3 / NPARAM ** 0.5)


def draw_gains_second(key, part):
    key = jax.random.fold_in(key, 24)
    return jax.random.uniform(key, (4, D), jnp.float32, 1.0, 4.0) * (0.05 / NPARAM)


def level_of(key, dims, cuts, smallest, high):
    factor_of = 1.0
    for position, shards_of in cuts:
        steps = jax.random.uniform(jax.random.fold_in(jax.random.fold_in(key, 6), position), (shards_of,), jnp.float32, smallest / len(cuts), high / len(cuts))
        factor_of = factor_of * jnp.repeat(jnp.exp(steps), dims[position] // shards_of).reshape((-1,) + (1,) * (len(dims) - 1 - position))
    return factor_of


def noise(own_key, shape, scale, reach, pieces=(), held_as=jnp.bfloat16):
    result = scale * jax.random.normal(own_key, shape, jnp.float32)
    if pieces:
        result = result * level_of(own_key, shape, pieces, -0.22, 0.18)
    return jnp.clip(result, -reach, reach).astype(held_as)


def setup_inputs(seed: int = 0) -> dict:
    keys = jax.random.split(jax.random.key(seed), 11)
    return {
        "inputs": draw_inputs(jax.random.fold_in(keys[10], 71), 0),
        "cotangent": noise(keys[1], (ROWS, SEQ, D), 1.0, 6.0, ((0, 4), (1, 8))),
        "documents": draw_documents(jax.random.fold_in(keys[10], 71), 0),
        "block_place": draw_block_place(jax.random.fold_in(keys[10], 71), 0),
        "params": draw_params(jax.random.fold_in(keys[10], 71), 0),
        "first_moment": draw_first_moment(jax.random.fold_in(keys[10], 71), 0),
        "second_moment": draw_second_moment(jax.random.fold_in(keys[10], 71), 0),
        "gains": draw_gains(jax.random.fold_in(keys[10], 71), 0),
        "gains_first": draw_gains_first(jax.random.fold_in(keys[10], 71), 0),
        "gains_second": draw_gains_second(jax.random.fold_in(keys[10], 71), 0),
    }


EPS = 1e-06
THETA = 500000.0
CLIP = 1.0
BETA1 = 0.9
BETA2 = 0.95
RATE = 0.03
GAIN_RATE = 0.8
DECAY = 0.1
ADAM_EPS = 1e-08

@jax.custom_vjp
def low(v):
    return lax.optimization_barrier(v.astype(jnp.bfloat16)).astype(jnp.float32)

@jax.custom_vjp
def low_back(v):
    return v

def low_keep(v):
    return (low(v), None)

def low_pass(kept, grad):
    return (grad,)

def back_keep(v):
    return (v, None)

def back_low(kept, grad):
    return (low(grad),)
low.defvjp(low_keep, low_pass)
low_back.defvjp(back_keep, back_low)

def rms_scale(values):
    return lax.rsqrt(lax.optimization_barrier(jnp.mean(values * values, axis=-1, keepdims=True)) + EPS)

def rope_tables(positions, head_size):
    half_size = head_size // 2
    freqs = THETA ** (-jnp.arange(half_size, dtype=jnp.float32) * 2.0 / head_size)
    angles = positions.astype(jnp.float32)[:, None] * freqs[None, :]
    return (jnp.cos(angles), jnp.sin(angles))

def rotate(values, cos_tab, sine_tab):
    half_size = values.shape[-1] // 2
    first_half = values[..., :half_size]
    second_half = values[..., half_size:]
    cos_b = cos_tab[:, None, :]
    sine_b = sine_tab[:, None, :]
    return jnp.concatenate([first_half * cos_b - second_half * sine_b, second_half * cos_b + first_half * sine_b], axis=-1)

def layer(wide_bf, gain_rows, tokens, doc_ids, positions, cos_tab, sine_tab):
    precise = lax.Precision.HIGHEST
    head_count = D // HD
    w_qkv = wide_bf[:, :3 * D]
    wo_t = wide_bf[:, 3 * D:4 * D]
    w_gu = wide_bf[:, 4 * D:4 * D + 2 * FF]
    wd_t = wide_bf[:, 4 * D + 2 * FF:]
    projected = jnp.dot(tokens, w_qkv, precision=precise)
    q_pre = low_back(projected[:, :D])
    k_pre = low_back(projected[:, D:2 * D])
    values = low(low_back(projected[:, 2 * D:]))
    q_norm = q_pre * rms_scale(q_pre) * gain_rows[0]
    k_norm = k_pre * rms_scale(k_pre) * gain_rows[1]
    queries = low(rotate(q_norm.reshape(SEQ, head_count, HD), cos_tab, sine_tab) * HD ** (-0.5))
    keys_all = low(rotate(k_norm.reshape(SEQ, head_count, HD), cos_tab, sine_tab))
    values_h = values.reshape(SEQ, head_count, HD)
    span_len = min(512, SEQ)

    def attend_block(inputs_blk):
        query_blk, pos_blk, doc_blk = inputs_blk
        scores = low_back(jnp.einsum('qhd,khd->hqk', query_blk, keys_all, precision=precise))
        visible = (doc_ids[None, :] == doc_blk[:, None]) & (positions[None, :] <= pos_blk[:, None])
        probs = jax.nn.softmax(jnp.where(visible[None], scores, -jnp.inf), axis=-1)
        return jnp.einsum('hqk,khd->qhd', probs, values_h, precision=precise)
    blocks_n = SEQ // span_len
    attended = lax.map(jax.checkpoint(attend_block), (queries.reshape(blocks_n, span_len, head_count, HD), positions.reshape(blocks_n, span_len), doc_ids.reshape(blocks_n, span_len)))
    attn_out = low(low_back(attended.reshape(SEQ, D)))
    branch = low_back(jnp.dot(attn_out, wo_t.T, precision=precise))
    hidden1 = tokens + branch * rms_scale(branch) * gain_rows[2]
    h1_low = low(hidden1)
    gate_up = jnp.dot(h1_low, w_gu, precision=precise)
    gate_pre = low_back(gate_up[:, :FF])
    up_pre = low_back(gate_up[:, FF:])
    inner_act = low(jax.nn.silu(gate_pre) * up_pre)
    mlp_out = low_back(jnp.dot(inner_act, wd_t.T, precision=precise))
    return hidden1 + mlp_out * rms_scale(mlp_out) * gain_rows[3]

def adam_update(weight, first_in, second_in, clipped, rate, decay):
    new_first = BETA1 * first_in + (1.0 - BETA1) * clipped
    new_second = BETA2 * second_in + (1.0 - BETA2) * clipped * clipped
    first_hat = new_first / (1.0 - BETA1 ** STEP)
    second_hat = new_second / (1.0 - BETA2 ** STEP)
    new_weight = weight - rate * (first_hat / (jnp.sqrt(second_hat) + ADAM_EPS) + decay * weight)
    return (new_weight, new_first, new_second)

def reference(inputs, cotangent, documents, block_place, params, first_moment, second_moment, gains, gains_first, gains_second):
    indices = jnp.arange(SEQ, dtype=jnp.int32)
    positions = (block_place[indices // GROUP] * GROUP + indices % GROUP).astype(jnp.int32)
    cos_tab, sine_tab = rope_tables(positions, HD)

    def forward(tokens_all, masters, gain_rows):
        wide_bf = low(masters)

        def one_row(carried, row_data):
            tokens, doc_ids = row_data
            return (carried, layer(wide_bf, gain_rows, tokens, doc_ids, positions, cos_tab, sine_tab))
        carried, outs = lax.scan(one_row, jnp.zeros((), jnp.float32), (tokens_all, documents))
        return outs
    outs, pullback = jax.vjp(forward, inputs.astype(jnp.float32), params, gains)
    d_inputs, d_params, d_gains = pullback(cotangent.astype(jnp.float32))
    square_sum = jnp.sum(d_params * d_params) + jnp.sum(d_gains * d_gains)
    grad_norm = jnp.sqrt(square_sum)
    factor = CLIP / (grad_norm + 1e-06)
    new_params, new_first, new_second = adam_update(params, first_moment, second_moment, d_params * factor, RATE, DECAY)
    new_gains, new_gains_first, new_gains_second = adam_update(gains, gains_first, gains_second, d_gains * factor, GAIN_RATE, 0.0)
    return (outs.astype(jnp.bfloat16), d_inputs.astype(jnp.bfloat16), grad_norm, new_params, new_first, new_second, new_gains, new_gains_first, new_gains_second)
```

```python
import jax
import jax.numpy as jnp
from jax import lax
from jax.sharding import PartitionSpec as P

HD = 128
STEP = 10
EPS = 1e-06
THETA = 500000.0
CLIP = 1.0
BETA1 = 0.9
BETA2 = 0.95
RATE = 0.03
GAIN_RATE = 0.8
DECAY = 0.1
ADAM_EPS = 1e-08
BF = jnp.bfloat16
F32 = jnp.float32


def rms_scale(values):
    return lax.rsqrt(jnp.mean(values * values, axis=-1, keepdims=True) + EPS)


def norm_back(upstream, source, scale):
    return scale * (
        upstream - source * scale * scale * jnp.mean(upstream * source, axis=-1, keepdims=True)
    )


def rope_tables(positions, head_size):
    half_size = head_size // 2
    freqs = THETA ** (-jnp.arange(half_size, dtype=jnp.float32) * 2.0 / head_size)
    angles = positions.astype(jnp.float32)[:, None] * freqs[None, :]
    return (jnp.cos(angles), jnp.sin(angles))


def rotate(values, cos_tab, sine_tab):
    shape = values.shape
    values = values.reshape(shape[0], shape[1] // HD, HD)
    half_size = HD // 2
    first_half = values[..., :half_size]
    second_half = values[..., half_size:]
    cos_b = cos_tab[:, None, :]
    sine_b = sine_tab[:, None, :]
    return jnp.concatenate(
        [first_half * cos_b - second_half * sine_b, second_half * cos_b + first_half * sine_b],
        axis=-1,
    ).reshape(shape)


def adam_update(weight, first_in, second_in, clipped, rate, decay):
    new_first = BETA1 * first_in + (1.0 - BETA1) * clipped
    new_second = BETA2 * second_in + (1.0 - BETA2) * clipped * clipped
    first_hat = new_first / (1.0 - BETA1**STEP)
    second_hat = new_second / (1.0 - BETA2**STEP)
    new_weight = weight - rate * (first_hat / (jnp.sqrt(second_hat) + ADAM_EPS) + decay * weight)
    return (new_weight, new_first, new_second)


def dot(a, b):
    return jnp.dot(a, b, preferred_element_type=F32)


def dot_t(a, b):
    return lax.dot_general(a, b, (((1,), (1,)), ((), ())), preferred_element_type=F32)


def t_dot(a, b):
    return lax.dot_general(a, b, (((0,), (0,)), ((), ())), preferred_element_type=F32)


def shards(
    inputs,
    cotangent,
    documents,
    block_place,
    params,
    first_moment,
    second_moment,
    gains,
    gains_first,
    gains_second,
):
    tokens = inputs[0]
    upstream = cotangent[0].astype(F32)
    length, width = tokens.shape
    n_ctx = lax.axis_size("ctx")
    n_dp = lax.axis_size("dp")
    me_ctx = lax.axis_index("ctx")
    seq = length * n_ctx
    rows = params.shape[0]
    ff = (params.shape[1] - 4 * width) // 3
    hc = width // n_ctx
    heads = hc // HD
    fs = ff // n_dp

    def mix(values):
        t = values.shape[0]
        return (
            values.reshape(t, n_dp, n_ctx, rows).transpose(0, 2, 1, 3).reshape(t, width)
        )

    def unmix(values):
        t = values.shape[0]
        return (
            values.reshape(t, n_ctx, n_dp, rows).transpose(0, 2, 1, 3).reshape(t, width)
        )

    low = params.astype(BF)
    wa = low[:, : 4 * width].reshape(rows, 4, n_ctx, hc).transpose(2, 0, 1, 3)
    wa = lax.all_to_all(wa.reshape(n_ctx * rows, 4 * hc), "ctx", 0, 0, tiled=True)
    wa = lax.all_gather(wa, "dp", axis=0, tiled=True)
    w_qkv, w_o = wa[:, : 3 * hc], wa[:, 3 * hc :]
    x_all = lax.all_gather(tokens, "ctx", axis=0, tiled=True)
    wf = low[:, 4 * width :].reshape(rows, 3, n_dp, fs).transpose(2, 0, 1, 3)
    wf = lax.all_to_all(wf.reshape(n_dp * rows, 3 * fs), "dp", 0, 0, tiled=True)
    wf = lax.all_gather(wf, "ctx", axis=0, tiled=True)
    w_gu, w_d = wf[:, : 2 * fs], wf[:, 2 * fs :]

    indices = jnp.arange(seq, dtype=jnp.int32)
    owners = indices // length
    placed = jnp.sum(
        jnp.where(
            owners[:, None] == jnp.arange(n_ctx, dtype=jnp.int32)[None, :], block_place[None, :], 0
        ),
        axis=1,
    )
    pos = placed * length + indices % length
    docs = documents[0]
    visible = (docs[None, :] == docs[:, None]) & (pos[None, :] <= pos[:, None])
    cos_tab, sine_tab = rope_tables(pos, HD)

    my_gains = lax.dynamic_slice_in_dim(gains, me_ctx * hc, hc, axis=1)
    projected = dot(x_all, w_qkv)
    qk_pre = projected[:, : 2 * hc].reshape(seq, 2, hc)
    values = projected[:, 2 * hc :].astype(BF)
    squares = lax.psum(jnp.sum(qk_pre * qk_pre, axis=-1), "ctx")
    scales = lax.rsqrt(squares / width + EPS)
    q_pre, k_pre = qk_pre[:, 0], qk_pre[:, 1]
    q_scale, k_scale = scales[:, :1], scales[:, 1:]
    queries = (rotate(q_pre * q_scale * my_gains[0], cos_tab, sine_tab) * HD ** (-0.5)).astype(BF)
    keys = rotate(k_pre * k_scale * my_gains[1], cos_tab, sine_tab).astype(BF)

    def split(v):
        return v.reshape(seq, heads, HD).transpose(1, 0, 2)

    def join(v):
        return v.transpose(1, 0, 2).reshape(seq, hc)

    qh, kh, vh = split(queries), split(keys), split(values)
    scores = jnp.einsum("hqd,hkd->hqk", qh, kh, preferred_element_type=F32)
    scores = jnp.where(visible[None], scores, -jnp.inf)
    top = jnp.max(scores, axis=-1, keepdims=True)
    weights = jnp.exp(scores - top)
    total = jnp.sum(weights, axis=-1, keepdims=True)
    probs = weights / total
    probs_low = probs.astype(BF)
    attn = jnp.einsum("hqk,hkd->hqd", probs_low, vh, preferred_element_type=F32)
    attn_low = join(attn).astype(BF)
    branch = lax.psum_scatter(
        dot_t(attn_low, w_o).astype(BF), "ctx", scatter_dimension=0, tiled=True
    ).astype(F32)
    a_scale = rms_scale(branch)
    hidden1 = tokens.astype(F32) + branch * a_scale * gains[2]

    h1_all = lax.all_gather(mix(hidden1.astype(BF)), "dp", axis=0, tiled=True)
    gate_up = dot(h1_all, w_gu)
    gate_pre, up_pre = gate_up[:, :fs], gate_up[:, fs:]
    gate_sig = jax.nn.sigmoid(gate_pre)
    silu_val = gate_pre * gate_sig
    inner = (silu_val * up_pre).astype(BF)
    mlp_out = unmix(
        lax.psum_scatter(
            dot_t(inner, w_d).astype(BF), "dp", scatter_dimension=0, tiled=True
        ).astype(F32)
    )
    m_scale = rms_scale(mlp_out)
    result = hidden1 + mlp_out * m_scale * gains[3]

    g_ff_part = jnp.sum(upstream * mlp_out * m_scale, axis=0)
    d_mlp = norm_back(upstream * gains[3], mlp_out, m_scale).astype(BF)
    d_mlp_all = lax.all_gather(mix(d_mlp), "dp", axis=0, tiled=True)
    d_inner = dot(d_mlp_all, w_d)
    d_gate = d_inner * up_pre * gate_sig * (1.0 + gate_pre * (1.0 - gate_sig))
    d_upper = d_inner * silu_val
    d_gu = jnp.concatenate([d_gate, d_upper], axis=1).astype(BF)
    d_h1 = upstream + unmix(
        lax.psum_scatter(
            dot_t(d_gu, w_gu).astype(BF), "dp", scatter_dimension=0, tiled=True
        ).astype(F32)
    )
    ff_grad = jnp.concatenate([t_dot(h1_all, d_gu), t_dot(d_mlp_all, inner)], axis=1).astype(BF)

    g_attn_part = jnp.sum(d_h1 * branch * a_scale, axis=0)
    d_branch = norm_back(d_h1 * gains[2], branch, a_scale).astype(BF)
    d_branch_all = lax.all_gather(d_branch, "ctx", axis=0, tiled=True)
    ff_grad = lax.psum_scatter(ff_grad, "ctx", scatter_dimension=0, tiled=True)
    ff_grad = lax.all_to_all(ff_grad, "dp", 0, 0, tiled=True)
    d_attn = dot(d_branch_all, w_o).astype(BF)
    dh = split(d_attn)
    delta = jnp.sum(dh.astype(F32) * attn, axis=-1, keepdims=True)
    d_probs = jnp.einsum("hqd,hkd->hqk", dh, vh, preferred_element_type=F32)
    d_scores = (probs * (d_probs - delta)).astype(BF)
    d_query = join(jnp.einsum("hqk,hkd->hqd", d_scores, kh, preferred_element_type=F32))
    d_key = join(jnp.einsum("hqk,hqd->hkd", d_scores, qh, preferred_element_type=F32))
    d_value = join(jnp.einsum("hqk,hqd->hkd", probs_low, dh, preferred_element_type=F32))
    d_qn = rotate(d_query * HD ** (-0.5), cos_tab, -sine_tab)
    d_kn = rotate(d_key, cos_tab, -sine_tab)
    g_q_part = jnp.sum(d_qn * q_pre * q_scale, axis=0)
    g_k_part = jnp.sum(d_kn * k_pre * k_scale, axis=0)
    e_q, e_k = d_qn * my_gains[0], d_kn * my_gains[1]
    means = (
        lax.psum(jnp.stack([jnp.sum(e_q * q_pre, -1), jnp.sum(e_k * k_pre, -1)], -1), "ctx") / width
    )
    d_q_pre = q_scale * (e_q - q_pre * q_scale * q_scale * means[:, :1])
    d_k_pre = k_scale * (e_k - k_pre * k_scale * k_scale * means[:, 1:])
    d_qkv = jnp.concatenate([d_q_pre, d_k_pre, d_value], axis=1).astype(BF)
    attn_grad = jnp.concatenate([t_dot(x_all, d_qkv), t_dot(d_branch_all, attn_low)], axis=1)
    attn_grad = lax.psum_scatter(attn_grad.astype(BF), "dp", scatter_dimension=0, tiled=True)
    attn_grad = lax.all_to_all(attn_grad, "ctx", 0, 0, tiled=True)
    d_input = d_h1 + lax.psum_scatter(
        dot_t(d_qkv, w_qkv).astype(BF), "ctx", scatter_dimension=0, tiled=True
    ).astype(F32)

    grad = jnp.concatenate(
        [
            attn_grad.reshape(n_ctx, rows, 4, hc).transpose(1, 2, 0, 3).reshape(rows, 4 * width),
            ff_grad.reshape(n_dp, rows, 3, fs).transpose(1, 2, 0, 3).reshape(rows, 3 * ff),
        ],
        axis=1,
    ).astype(F32)
    gain_part = jnp.stack(
        [
            lax.dynamic_update_slice(jnp.zeros(width, F32), g_q_part, (me_ctx * hc,)),
            lax.dynamic_update_slice(jnp.zeros(width, F32), g_k_part, (me_ctx * hc,)),
            g_attn_part,
            g_ff_part,
        ],
        axis=0,
    )
    square_total, gain_total = lax.psum((jnp.sum(grad * grad), gain_part), ("dp", "ctx"))
    grad_norm = jnp.sqrt(square_total + jnp.sum(gain_total * gain_total))
    factor = CLIP / (grad_norm + 1e-06)
    new_params, new_first, new_second = adam_update(
        params, first_moment, second_moment, grad * factor, RATE, DECAY
    )
    new_gains, new_gains_first, new_gains_second = adam_update(
        gains, gains_first, gains_second, gain_total * factor, GAIN_RATE, 0.0
    )
    return (
        result.astype(BF)[None],
        d_input.astype(BF)[None],
        grad_norm,
        new_params,
        new_first,
        new_second,
        new_gains,
        new_gains_first,
        new_gains_second,
    )


def solution(mesh):
    split, whole = P("dp", "ctx", None), P(("dp", "ctx"), None)
    return jax.shard_map(
        shards,
        mesh=mesh,
        in_specs=(split, split, P("dp", None), P(), whole, whole, whole, P(), P(), P()),
        out_specs=(split, split, P(), whole, whole, whole, P(), P(), P()),
        check_vma=False,
    )
```

```python
import functools

import jax
import jax.numpy as jnp
from jax import lax
from jax.experimental import pallas as pl
from jax.experimental.pallas import tpu as pltpu
from jax.sharding import PartitionSpec as P

HD = 128
STEP = 10
EPS = 1e-06
THETA = 500000.0
CLIP = 1.0
BETA1 = 0.9
BETA2 = 0.95
RATE = 0.03
GAIN_RATE = 0.8
DECAY = 0.1
ADAM_EPS = 1e-08
BF = jnp.bfloat16
F32 = jnp.float32
MESH = pl.DeviceIdType.MESH
ANY = pl.BlockSpec(memory_space=pl.ANY)
VMEM = pl.BlockSpec(memory_space=pltpu.VMEM)


def rms_scale(values):
    return lax.rsqrt(jnp.mean(values * values, axis=-1, keepdims=True) + EPS)


def norm_back(upstream, source, scale):
    return scale * (
        upstream - source * scale * scale * jnp.mean(upstream * source, axis=-1, keepdims=True)
    )


def rope_tables(positions, head_size):
    half_size = head_size // 2
    freqs = THETA ** (-jnp.arange(half_size, dtype=jnp.float32) * 2.0 / head_size)
    angles = positions.astype(jnp.float32)[:, None] * freqs[None, :]
    return (jnp.cos(angles), jnp.sin(angles))


def rotate(values, cos_tab, sine_tab):
    shape = values.shape
    values = values.reshape(shape[0], shape[1] // HD, HD)
    half_size = HD // 2
    first_half = values[..., :half_size]
    second_half = values[..., half_size:]
    cos_b = cos_tab[:, None, :]
    sine_b = sine_tab[:, None, :]
    return jnp.concatenate(
        [first_half * cos_b - second_half * sine_b, second_half * cos_b + first_half * sine_b],
        axis=-1,
    ).reshape(shape)


def adam_update(weight, first_in, second_in, clipped, rate, decay):
    new_first = BETA1 * first_in + (1.0 - BETA1) * clipped
    new_second = BETA2 * second_in + (1.0 - BETA2) * clipped * clipped
    first_hat = new_first / (1.0 - BETA1**STEP)
    second_hat = new_second / (1.0 - BETA2**STEP)
    new_weight = weight - rate * (first_hat / (jnp.sqrt(second_hat) + ADAM_EPS) + decay * weight)
    return (new_weight, new_first, new_second)


def dot(a, b):
    return jnp.dot(a, b, preferred_element_type=F32)


def dot_t(a, b):
    return lax.dot_general(a, b, (((1,), (1,)), ((), ())), preferred_element_type=F32)


def t_dot(a, b):
    return lax.dot_general(a, b, (((0,), (0,)), ((), ())), preferred_element_type=F32)


def greet(peers):
    barrier = pltpu.get_barrier_semaphore()
    for peer in peers:
        pl.semaphore_signal(barrier, inc=1, device_id=peer, device_id_type=MESH)
    pl.semaphore_wait(barrier, len(peers))


def remote(src, dst, send, recv, peer):
    return pltpu.make_async_remote_copy(
        src_ref=src, dst_ref=dst, send_sem=send, recv_sem=recv, device_id=peer, device_id_type=MESH
    )


def params_of(number, vmem=48):
    return pltpu.CompilerParams(
        collective_id=number, has_side_effects=True, vmem_limit_bytes=vmem * 1024 * 1024
    )


def line_steps(n, me, make_right, make_left):
    for s in range(n - 1):

        @pl.when((me < n - 1) & (me >= s))
        def _():
            make_right(s).start()

        @pl.when((me > 0) & (me + s < n))
        def _():
            make_left(s).start()

        @pl.when(me - 1 - s >= 0)
        def _():
            make_right(s, me - 1 - s).wait_recv()

        @pl.when(me + 1 + s < n)
        def _():
            make_left(s, me + 1 + s).wait_recv()

    for s in range(n - 1):

        @pl.when((me < n - 1) & (me >= s))
        def _():
            make_right(s).wait_send()

        @pl.when((me > 0) & (me + s < n))
        def _():
            make_left(s).wait_send()


def pairs_of(n, me):
    half = n // 2
    parity, pair = me % 2, me // 2
    partner = me + 1 - 2 * parity
    ahead = [2 * ((pair + k) % half) + parity for k in range(1, half)]
    behind = [2 * ((pair + half - k) % half) + parity for k in range(1, half)]
    return half, parity, pair, partner, ahead, behind


def gather_dp_kernel(n, x_ref, o_ref, local, sr, rr, sl, rl):
    me, ctx = lax.axis_index("dp"), lax.axis_index("ctx")

    def here(d):
        return (d, ctx)

    greet([here((me + 1) % n), here((me + n - 1) % n)])
    own = pltpu.make_async_copy(x_ref, o_ref.at[me], local)
    own.start()

    def right(s, block=None):
        b = me - s if block is None else block
        return remote(x_ref if s == 0 else o_ref.at[b], o_ref.at[b], sr.at[s], rr.at[s], here(me + 1))

    def left(s, block=None):
        b = me + s if block is None else block
        return remote(x_ref if s == 0 else o_ref.at[b], o_ref.at[b], sl.at[s], rl.at[s], here(me - 1))

    line_steps(n, me, right, left)
    own.wait()


def gather_dp(x, number):
    n = lax.axis_size("dp")
    out = pl.pallas_call(
        functools.partial(gather_dp_kernel, n),
        out_shape=jax.ShapeDtypeStruct((n,) + x.shape, x.dtype),
        in_specs=[ANY],
        out_specs=ANY,
        scratch_shapes=[pltpu.SemaphoreType.DMA] + [pltpu.SemaphoreType.DMA((n - 1,))] * 4,
        compiler_params=params_of(number),
        name="gather_dp",
    )(x)
    return out.reshape((n * x.shape[0],) + x.shape[1:])


def gather_ctx_kernel(n, x_ref, o_ref, local, ss, rs, fs, fr):
    dp, me = lax.axis_index("dp"), lax.axis_index("ctx")
    half, parity, pair, partner, ahead, behind = pairs_of(n, me)
    greet([(dp, partner)] + [(dp, a) for a in ahead])
    own = pltpu.make_async_copy(x_ref, o_ref.at[me], local)
    sends = [
        remote(x_ref, o_ref.at[me], ss.at[k], rs.at[k], (dp, a))
        for k, a in enumerate(ahead + [partner])
    ]
    for copy in sends:
        copy.start()
    own.start()
    forwards = []
    for k, b in enumerate(behind):
        remote(x_ref, o_ref.at[b], ss.at[k], rs.at[k], (dp, b)).wait_recv()
        forward = remote(o_ref.at[b], o_ref.at[b], fs.at[k], fr.at[k], (dp, partner))
        forward.start()
        forwards.append(forward)
    sends[-1].wait_recv()
    for forward in forwards:
        forward.wait()
    for copy in sends:
        copy.wait_send()
    own.wait()


def gather_ctx(x, number):
    n = lax.axis_size("ctx")
    half = n // 2
    out = pl.pallas_call(
        functools.partial(gather_ctx_kernel, n),
        out_shape=jax.ShapeDtypeStruct((n,) + x.shape, x.dtype),
        in_specs=[ANY],
        out_specs=ANY,
        scratch_shapes=[pltpu.SemaphoreType.DMA]
        + [pltpu.SemaphoreType.DMA((half,))] * 2
        + [pltpu.SemaphoreType.DMA((half - 1,))] * 2,
        compiler_params=params_of(number),
        name="gather_ctx",
    )(x)
    return out.reshape((n * x.shape[0],) + x.shape[1:])


def reduce_ctx(n, dp, me, a_ref, w_ref, o_ref, sa, ra, sb, rb, s1, r1, s2, r2):
    half, parity, pair, partner, ahead, behind = pairs_of(n, me)
    length, width = o_ref.shape
    tile = width // 4

    def product(block, store):
        rows = pl.ds(pl.multiple_of(block * length, length), length)

        @pl.loop(0, 4)
        def _(j):
            part = pl.ds(pl.multiple_of(j * tile, tile), tile)
            store(part, dot_t(a_ref[rows, :], w_ref[part, :]))

    first, second = [], []
    for k in range(half):

        def store(part, value, k=k):
            sa[k, :, part] = value.astype(BF)

        product(2 * ((pair + k + 1) % half) + 1 - parity, store)
        copy = remote(sa.at[k], ra.at[k], s1.at[k], r1.at[k], (dp, partner))
        copy.start()
        first.append(copy)
    for k in range(half):
        target = 2 * ((pair + k + 1) % half) + parity
        first[k].wait_recv()

        def store(part, value, k=k):
            value = value + ra[k, :, part].astype(F32)
            if k < half - 1:
                sb[k, :, part] = value.astype(BF)
            else:
                o_ref[:, part] = value

        product(target, store)
        if k < half - 1:
            copy = remote(sb.at[k], rb.at[k], s2.at[k], r2.at[k], (dp, target))
            copy.start()
            second.append(copy)
    for k in range(half - 1):
        second[k].wait_recv()
        o_ref[...] += rb[k].astype(F32)
    return first + second


def scatter_ctx_kernel(n, a_ref, w_ref, o_ref, sa, ra, sb, rb, s1, r1, s2, r2):
    dp, me = lax.axis_index("dp"), lax.axis_index("ctx")
    half, parity, pair, partner, ahead, behind = pairs_of(n, me)
    greet([(dp, partner)] + [(dp, a) for a in ahead])
    for copy in reduce_ctx(n, dp, me, a_ref, w_ref, o_ref, sa, ra, sb, rb, s1, r1, s2, r2):
        copy.wait_send()


def scatter_ctx(a, w, number):
    n = lax.axis_size("ctx")
    half, length, width = n // 2, a.shape[0] // n, w.shape[0]
    dma = pltpu.SemaphoreType.DMA
    return pl.pallas_call(
        functools.partial(scatter_ctx_kernel, n),
        out_shape=jax.ShapeDtypeStruct((length, width), F32),
        in_specs=[VMEM, VMEM],
        out_specs=VMEM,
        scratch_shapes=[
            pltpu.VMEM((half, length, width), BF),
            pltpu.VMEM((half, length, width), BF),
            pltpu.VMEM((half - 1, length, width), BF),
            pltpu.VMEM((half - 1, length, width), BF),
            dma((half,)),
            dma((half,)),
            dma((half - 1,)),
            dma((half - 1,)),
        ],
        compiler_params=params_of(number),
        name="scatter_ctx",
    )(a, w)


def scatter_dp_kernel(n, a_ref, w_ref, o_ref, sa, ra, ss, rs):
    me, ctx = lax.axis_index("dp"), lax.axis_index("ctx")
    length, width = o_ref.shape
    tile = width // 4

    def product(block, out):
        rows = pl.ds(pl.multiple_of(block * length, length), length)

        @pl.loop(0, 4)
        def _(j):
            part = pl.ds(pl.multiple_of(j * tile, tile), tile)
            out[:, part] = dot_t(a_ref[rows, :], w_ref[part, :]).astype(out.dtype)

    greet([((me + k) % n, ctx) for k in range(1, n)])
    copies = []
    for k in range(1, n):
        target = (me + k) % n
        product(target, sa.at[k - 1])
        copy = remote(sa.at[k - 1], ra.at[k - 1], ss.at[k - 1], rs.at[k - 1], (target, ctx))
        copy.start()
        copies.append(copy)
    product(me, o_ref)
    for k in range(n - 1):
        copies[k].wait_recv()
        o_ref[...] += ra[k].astype(F32)
    for copy in copies:
        copy.wait_send()


def scatter_dp(a, w, number):
    n = lax.axis_size("dp")
    length, width = a.shape[0] // n, w.shape[0]
    dma = pltpu.SemaphoreType.DMA
    return pl.pallas_call(
        functools.partial(scatter_dp_kernel, n),
        out_shape=jax.ShapeDtypeStruct((length, width), F32),
        in_specs=[VMEM, VMEM],
        out_specs=VMEM,
        scratch_shapes=[
            pltpu.VMEM((n - 1, length, width), BF),
            pltpu.VMEM((n - 1, length, width), BF),
            dma((n - 1,)),
            dma((n - 1,)),
        ],
        compiler_params=params_of(number, 56),
        name="scatter_dp",
    )(a, w)


def swap_dp_kernel(n, x_ref, o_ref, local, ss, rs):
    me, ctx = lax.axis_index("dp"), lax.axis_index("ctx")
    greet([((me + k) % n, ctx) for k in range(1, n)])
    own = pltpu.make_async_copy(x_ref.at[me], o_ref.at[me], local)
    copies = []
    for k in range(1, n):
        to = (me + k) % n
        copy = remote(x_ref.at[to], o_ref.at[me], ss.at[k - 1], rs.at[k - 1], (to, ctx))
        copy.start()
        copies.append(copy)
    own.start()
    for k in range(1, n):
        source = (me + n - k) % n
        remote(x_ref.at[me], o_ref.at[source], ss.at[k - 1], rs.at[k - 1], (source, ctx)).wait_recv()
    for copy in copies:
        copy.wait_send()
    own.wait()


def swap_dp(x, number):
    n = lax.axis_size("dp")
    dma = pltpu.SemaphoreType.DMA
    return pl.pallas_call(
        functools.partial(swap_dp_kernel, n),
        out_shape=jax.ShapeDtypeStruct(x.shape, x.dtype),
        in_specs=[ANY],
        out_specs=ANY,
        scratch_shapes=[dma, dma((n - 1,)), dma((n - 1,))],
        compiler_params=params_of(number),
        name="swap_dp",
    )(x)


def spread_kernel(n_dp, n, w_ref, x_ref, o_ref, y_ref, local, sa, ra, ss, rs, fs, fr, sr, rr, sl, rl):
    dp, me = lax.axis_index("dp"), lax.axis_index("ctx")
    half, parity, pair, partner, ahead, behind = pairs_of(n, me)
    greet(
        [((dp + 1) % n_dp, me), ((dp + n_dp - 1) % n_dp, me)]
        + [(dp, (me + k) % n) for k in range(1, n)]
    )
    own_w = pltpu.make_async_copy(w_ref.at[me], o_ref.at[dp, me], local.at[0])
    own_x = pltpu.make_async_copy(x_ref, y_ref.at[me], local.at[1])
    own_w.start()
    swaps = []
    for k in range(1, n):
        to = (me + k) % n
        copy = remote(w_ref.at[to], o_ref.at[dp, me], sa.at[k - 1], ra.at[k - 1], (dp, to))
        copy.start()
        swaps.append(copy)
    sends = [
        remote(x_ref, y_ref.at[me], ss.at[k], rs.at[k], (dp, a))
        for k, a in enumerate(ahead + [partner])
    ]
    for copy in sends:
        copy.start()
    own_x.start()

    def right(s, k, b):
        c = (me + n - k) % n
        return remote(o_ref.at[b, c], o_ref.at[b, c], sr.at[s, k], rr.at[s, k], (dp + 1, me))

    def left(s, k, b):
        c = (me + n - k) % n
        return remote(o_ref.at[b, c], o_ref.at[b, c], sl.at[s, k], rl.at[s, k], (dp - 1, me))

    for s in range(n_dp):
        for k in range(n):
            if s == 0 and k == 0:
                own_w.wait()
            elif s == 0:
                source = (me + n - k) % n
                remote(
                    w_ref.at[me], o_ref.at[dp, source], sa.at[k - 1], ra.at[k - 1], (dp, source)
                ).wait_recv()
            else:

                @pl.when(dp >= s)
                def _():
                    right(s - 1, k, dp - s).wait_recv()

                @pl.when(dp + s < n_dp)
                def _():
                    left(s - 1, k, dp + s).wait_recv()

            if s < n_dp - 1:

                @pl.when((dp < n_dp - 1) & (dp >= s))
                def _():
                    right(s, k, dp - s).start()

                @pl.when((dp > 0) & (dp + s < n_dp))
                def _():
                    left(s, k, dp + s).start()

        if s == 0:
            forwards = []
            for k, b in enumerate(behind):
                remote(x_ref, y_ref.at[b], ss.at[k], rs.at[k], (dp, b)).wait_recv()
                forward = remote(y_ref.at[b], y_ref.at[b], fs.at[k], fr.at[k], (dp, partner))
                forward.start()
                forwards.append(forward)
    for s in range(n_dp - 1):
        for k in range(n):

            @pl.when((dp < n_dp - 1) & (dp >= s))
            def _():
                right(s, k, dp - s).wait_send()

            @pl.when((dp > 0) & (dp + s < n_dp))
            def _():
                left(s, k, dp + s).wait_send()

    sends[-1].wait_recv()
    for forward in forwards:
        forward.wait()
    for copy in sends + swaps:
        copy.wait_send()
    own_x.wait()


def spread(w, x, number):
    n_dp, n = lax.axis_size("dp"), lax.axis_size("ctx")
    half = n // 2
    dma = pltpu.SemaphoreType.DMA
    out, x_all = pl.pallas_call(
        functools.partial(spread_kernel, n_dp, n),
        out_shape=(
            jax.ShapeDtypeStruct((n_dp,) + w.shape, w.dtype),
            jax.ShapeDtypeStruct((n,) + x.shape, x.dtype),
        ),
        in_specs=[ANY, ANY],
        out_specs=(ANY, ANY),
        scratch_shapes=[dma((2,)), dma((n - 1,)), dma((n - 1,)), dma((half,)), dma((half,))]
        + [dma((half - 1,))] * 2
        + [dma((n_dp - 1, n))] * 4,
        compiler_params=params_of(number),
        name="spread",
    )(w, x)
    return out.reshape(-1, w.shape[-1]), x_all.reshape(-1, x.shape[-1])


def collect_kernel(
    n_dp, n, g_ref, a_ref, w_ref, o_ref, y_ref,
    own, ra, rc, sb, pa, qa, pb, qb,
    local, sa, rs, sc, rd, s1, r1, s2, r2,
):
    dp, me = lax.axis_index("dp"), lax.axis_index("ctx")
    greet(
        [((dp + k) % n_dp, me) for k in range(1, n_dp)] + [(dp, (me + k) % n) for k in range(1, n)]
    )
    mine = pltpu.make_async_copy(g_ref.at[dp], own, local)
    mine.start()
    first = []
    for c in range(n):
        row = []
        for k in range(1, n_dp):
            to = (dp + k) % n_dp
            copy = remote(
                g_ref.at[to, (me + 1 + c) % n],
                ra.at[c, k - 1],
                sa.at[c, k - 1],
                rs.at[c, k - 1],
                (to, me),
            )
            copy.start()
            row.append(copy)
        first.append(row)
    sums = reduce_ctx(n, dp, me, a_ref, w_ref, y_ref, pa, qa, pb, qb, s1, r1, s2, r2)
    mine.wait()
    second = []
    for c in range(n):
        to = (me + 1 + c) % n
        total = own[to].astype(F32)
        for k in range(n_dp - 1):
            first[c][k].wait_recv()
            total = total + ra[c, k].astype(F32)
        if c < n - 1:
            sb[c] = total.astype(BF)
            copy = remote(sb.at[c], rc.at[c], sc.at[c], rd.at[c], (dp, to))
            copy.start()
            second.append(copy)
        else:
            o_ref[me] = total.astype(BF)
    for c in range(n - 1):
        second[c].wait_recv()
        o_ref[(me + n - 1 - c) % n] = rc[c]
    for row in first:
        for copy in row:
            copy.wait_send()
    for copy in second + sums:
        copy.wait_send()


def collect(g, a, w, number):
    n_dp, n = lax.axis_size("dp"), lax.axis_size("ctx")
    rows, width = g.shape[0] // (n_dp * n), g.shape[1]
    half, length, features = n // 2, a.shape[0] // n, w.shape[0]
    dma = pltpu.SemaphoreType.DMA
    return pl.pallas_call(
        functools.partial(collect_kernel, n_dp, n),
        out_shape=(
            jax.ShapeDtypeStruct((n, rows, width), BF),
            jax.ShapeDtypeStruct((length, features), F32),
        ),
        in_specs=[ANY, VMEM, VMEM],
        out_specs=(VMEM, VMEM),
        scratch_shapes=[
            pltpu.VMEM((n, rows, width), BF),
            pltpu.VMEM((n, n_dp - 1, rows, width), BF),
            pltpu.VMEM((n - 1, rows, width), BF),
            pltpu.VMEM((n - 1, rows, width), BF),
            pltpu.VMEM((half, length, features), BF),
            pltpu.VMEM((half, length, features), BF),
            pltpu.VMEM((half - 1, length, features), BF),
            pltpu.VMEM((half - 1, length, features), BF),
            dma,
            dma((n, n_dp - 1)),
            dma((n, n_dp - 1)),
            dma((n - 1,)),
            dma((n - 1,)),
            dma((half,)),
            dma((half,)),
            dma((half - 1,)),
            dma((half - 1,)),
        ],
        compiler_params=params_of(number),
        name="collect",
    )(g.reshape(n_dp, n, rows, width), a, w)


def total_kernel(n_dp, n, ga_ref, gu_ref, gd_ref, gain_ref, o_ref, mine, buf, part, all_parts, ss, rs, st, rt):
    dp, me = lax.axis_index("dp"), lax.axis_index("ctx")
    gain_rows = gain_ref.shape[0]

    def squares(ref):
        acc = jnp.zeros((ref.shape[1], ref.shape[2]), F32)
        for i in range(ref.shape[0]):
            block = ref[i].astype(F32)
            acc += block * block
        return jnp.sum(acc, axis=0, keepdims=True)

    total = (
        jnp.sum(squares(ga_ref), axis=1, keepdims=True)
        + jnp.sum(squares(gu_ref), axis=1, keepdims=True)
        + jnp.sum(squares(gd_ref), axis=1, keepdims=True)
    )
    mine[0:gain_rows, :] = gain_ref[...]
    mine[gain_rows:, :] = jnp.broadcast_to(total, (8, 128))
    greet(
        [((dp + k) % n_dp, me) for k in range(1, n_dp)] + [(dp, (me + k) % n) for k in range(1, n)]
    )
    copies = []
    for k in range(1, n):
        copy = remote(mine, buf.at[me], ss.at[k - 1], rs.at[k - 1], (dp, (me + k) % n))
        copy.start()
        copies.append(copy)
    buf[me] = mine[...]
    for k in range(1, n):
        source = (me + n - k) % n
        remote(mine, buf.at[source], ss.at[k - 1], rs.at[k - 1], (dp, source)).wait_recv()
    acc = buf[0]
    for j in range(1, n):
        acc = acc + buf[j]
    part[...] = acc
    all_parts[dp] = acc
    for k in range(1, n_dp):
        copy = remote(part, all_parts.at[dp], st.at[k - 1], rt.at[k - 1], ((dp + k) % n_dp, me))
        copy.start()
        copies.append(copy)
    for k in range(1, n_dp):
        source = (dp + n_dp - k) % n_dp
        remote(part, all_parts.at[source], st.at[k - 1], rt.at[k - 1], (source, me)).wait_recv()
    acc = all_parts[0]
    for j in range(1, n_dp):
        acc = acc + all_parts[j]
    o_ref[...] = acc
    for copy in copies:
        copy.wait_send()


def total_over(ga, gu, gd, gain_part, number):
    n_dp, n = lax.axis_size("dp"), lax.axis_size("ctx")
    gain_rows = gain_part.size // 128
    shape = (gain_rows + 8, 128)
    dma = pltpu.SemaphoreType.DMA
    out = pl.pallas_call(
        functools.partial(total_kernel, n_dp, n),
        out_shape=jax.ShapeDtypeStruct(shape, F32),
        in_specs=[VMEM] * 4,
        out_specs=VMEM,
        scratch_shapes=[
            pltpu.VMEM(shape, F32),
            pltpu.VMEM((n,) + shape, F32),
            pltpu.VMEM(shape, F32),
            pltpu.VMEM((n_dp,) + shape, F32),
            dma((n - 1,)),
            dma((n - 1,)),
            dma((n_dp - 1,)),
            dma((n_dp - 1,)),
        ],
        compiler_params=params_of(number),
        name="total",
    )(ga, gu, gd, gain_part.reshape(gain_rows, 128))
    return out[gain_rows, 0], out[:gain_rows].reshape(gain_part.shape)


def adam_kernel(factor_ref, p_ref, m_ref, v_ref, ga_ref, gu_ref, gd_ref, po_ref, mo_ref, vo_ref, g_ref):
    part = pl.program_id(0)
    n, _, four = ga_ref.shape
    hc = four // 4
    fs = gd_ref.shape[2]

    @pl.when(part == 0)
    def _():
        for matrix in range(4):
            for c in range(n):
                start = (matrix * n + c) * hc
                g_ref[:, start : start + hc] = ga_ref[c, :, matrix * hc : (matrix + 1) * hc].astype(F32)

    @pl.when((part == 1) | (part == 2))
    def _():
        for d in range(gu_ref.shape[0]):
            g_ref[:, d * fs : (d + 1) * fs] = gu_ref[d].astype(F32)

    @pl.when(part == 3)
    def _():
        for d in range(gd_ref.shape[0]):
            g_ref[:, d * fs : (d + 1) * fs] = gd_ref[d].astype(F32)

    clipped = g_ref[...] * factor_ref[0, 0]
    new_p, new_m, new_v = adam_update(p_ref[...], m_ref[...], v_ref[...], clipped, RATE, DECAY)
    po_ref[...] = new_p
    mo_ref[...] = new_m
    vo_ref[...] = new_v


def adam(factor, params, first, second, ga, gu, gd):
    rows, columns = params.shape
    n, n_dp, fs = ga.shape[0], gd.shape[0], gd.shape[2]
    block = min(rows, 16)
    steps = rows // block
    wide = pl.BlockSpec((block, columns // 4), lambda i, r: (r, i))
    return pl.pallas_call(
        adam_kernel,
        grid=(4, steps),
        out_shape=(jax.ShapeDtypeStruct(params.shape, F32),) * 3,
        in_specs=[
            pl.BlockSpec(memory_space=pltpu.SMEM),
            wide,
            wide,
            wide,
            pl.BlockSpec((n, block, ga.shape[2]), lambda i, r: (0, jnp.where(i == 0, r, steps - 1), 0)),
            pl.BlockSpec(
                (n_dp, block, fs),
                lambda i, r: (
                    0,
                    jnp.where(i == 0, 0, jnp.where(i == 3, steps - 1, r)),
                    jnp.clip(i - 1, 0, 1),
                ),
            ),
            pl.BlockSpec((n_dp, block, fs), lambda i, r: (0, jnp.where(i == 3, r, 0), 0)),
        ],
        out_specs=(wide, wide, wide),
        scratch_shapes=[pltpu.VMEM((block, columns // 4), F32)],
        compiler_params=pltpu.CompilerParams(vmem_limit_bytes=48 * 1024 * 1024),
        name="adam",
    )(factor.reshape(1, 1), params, first, second, ga, gu, gd)


def arrange_kernel(n, n_dp, p_ref, a_ref, g_ref, u_ref, d_ref):
    part = pl.program_id(0)
    hc = a_ref.shape[2] // 4
    fs = g_ref.shape[2]

    @pl.when(part == 0)
    def _():
        for matrix in range(4):
            for c in range(n):
                start = (matrix * n + c) * hc
                a_ref[c, :, matrix * hc : (matrix + 1) * hc] = p_ref[:, start : start + hc].astype(BF)

    for index, ref in ((1, g_ref), (2, u_ref), (3, d_ref)):

        @pl.when(part == index)
        def _():
            for d in range(n_dp):
                ref[d] = p_ref[:, d * fs : (d + 1) * fs].astype(BF)


def arrange(params, width):
    n_dp, n = lax.axis_size("dp"), lax.axis_size("ctx")
    rows, columns = params.shape
    fs, hc = columns // 4 // n_dp, width // n
    whole = lambda shape: pl.BlockSpec(shape, lambda i: (0,) * len(shape))
    shapes = [(n, rows, 4 * hc)] + [(n_dp, rows, fs)] * 3
    return pl.pallas_call(
        functools.partial(arrange_kernel, n, n_dp),
        grid=(4,),
        out_shape=tuple(jax.ShapeDtypeStruct(s, BF) for s in shapes),
        in_specs=[pl.BlockSpec((rows, columns // 4), lambda i: (0, i))],
        out_specs=tuple(whole(s) for s in shapes),
        compiler_params=pltpu.CompilerParams(vmem_limit_bytes=48 * 1024 * 1024),
        name="arrange",
    )(params)


def shards(
    inputs,
    cotangent,
    documents,
    block_place,
    params,
    first_moment,
    second_moment,
    gains,
    gains_first,
    gains_second,
):
    tokens = inputs[0]
    upstream = cotangent[0].astype(F32)
    length, width = tokens.shape
    n_ctx = lax.axis_size("ctx")
    n_dp = lax.axis_size("dp")
    me_ctx = lax.axis_index("ctx")
    seq = length * n_ctx
    rows = params.shape[0]
    ff = (params.shape[1] - 4 * width) // 3
    hc = width // n_ctx
    heads = hc // HD
    fs = ff // n_dp

    def mix(values):
        t = values.shape[0]
        return (
            values.reshape(t, n_dp, n_ctx, rows).transpose(0, 2, 1, 3).reshape(t, width)
        )

    def unmix(values):
        t = values.shape[0]
        return (
            values.reshape(t, n_ctx, n_dp, rows).transpose(0, 2, 1, 3).reshape(t, width)
        )

    wa, wg, wu, wd = arrange(params, width)
    wgu = swap_dp(jnp.concatenate([wg, wu], axis=2), 10)
    w_gu = lax.all_gather(wgu.reshape(n_dp * rows, 2 * fs), "ctx", axis=0, tiled=True)
    wa, wgu = lax.optimization_barrier((wa, wgu))
    wa, x_all = spread(wa, tokens, 1)
    w_qkv, w_o = wa[:, : 3 * hc], wa[:, 3 * hc :]
    wd, x_all = lax.optimization_barrier((wd, x_all))
    w_d = lax.all_to_all(wd.reshape(n_dp * rows, fs), "dp", 0, 0, tiled=True)
    w_d = lax.all_gather(w_d, "ctx", axis=0, tiled=True)

    indices = jnp.arange(seq, dtype=jnp.int32)
    owners = indices // length
    placed = jnp.sum(
        jnp.where(
            owners[:, None] == jnp.arange(n_ctx, dtype=jnp.int32)[None, :], block_place[None, :], 0
        ),
        axis=1,
    )
    pos = placed * length + indices % length
    docs = documents[0]
    visible = (docs[None, :] == docs[:, None]) & (pos[None, :] <= pos[:, None])
    cos_tab, sine_tab = rope_tables(pos, HD)

    my_gains = lax.dynamic_slice_in_dim(gains, me_ctx * hc, hc, axis=1)
    projected = dot(x_all, w_qkv)
    qk_pre = projected[:, : 2 * hc].reshape(seq, 2, hc)
    values = projected[:, 2 * hc :].astype(BF)
    squares = lax.psum(jnp.sum(qk_pre * qk_pre, axis=-1), "ctx")
    scales = lax.rsqrt(squares / width + EPS)
    q_pre, k_pre = qk_pre[:, 0], qk_pre[:, 1]
    q_scale, k_scale = scales[:, :1], scales[:, 1:]
    queries = (rotate(q_pre * q_scale * my_gains[0], cos_tab, sine_tab) * HD ** (-0.5)).astype(BF)
    keys = rotate(k_pre * k_scale * my_gains[1], cos_tab, sine_tab).astype(BF)

    def split(v):
        return v.reshape(seq, heads, HD).transpose(1, 0, 2)

    def join(v):
        return v.transpose(1, 0, 2).reshape(seq, hc)

    qh, kh, vh = split(queries), split(keys), split(values)
    scores = jnp.einsum("hqd,hkd->hqk", qh, kh, preferred_element_type=F32)
    scores = jnp.where(visible[None], scores, -jnp.inf)
    top = jnp.max(scores, axis=-1, keepdims=True)
    weights = jnp.exp(scores - top)
    total = jnp.sum(weights, axis=-1, keepdims=True)
    probs = weights / total
    probs_low = probs.astype(BF)
    attn = jnp.einsum("hqk,hkd->hqd", probs_low, vh, preferred_element_type=F32)
    attn_low = join(attn).astype(BF)
    attn_low, w_gu = lax.optimization_barrier((attn_low, w_gu))
    branch = scatter_ctx(attn_low, w_o, 2)
    a_scale = rms_scale(branch)
    hidden1 = tokens.astype(F32) + branch * a_scale * gains[2]

    h1_all = gather_dp(mix(hidden1.astype(BF)), 3)
    gate_up = dot(h1_all, w_gu)
    gate_pre, up_pre = gate_up[:, :fs], gate_up[:, fs:]
    gate_sig = jax.nn.sigmoid(gate_pre)
    silu_val = gate_pre * gate_sig
    inner = (silu_val * up_pre).astype(BF)
    mlp_out = unmix(scatter_dp(inner, w_d, 4))
    m_scale = rms_scale(mlp_out)
    result = hidden1 + mlp_out * m_scale * gains[3]

    g_ff_part = jnp.sum(upstream * mlp_out * m_scale, axis=0)
    d_mlp = norm_back(upstream * gains[3], mlp_out, m_scale).astype(BF)
    d_mlp_all = gather_dp(mix(d_mlp), 5)
    d_grad = lax.psum_scatter(
        t_dot(d_mlp_all, inner).astype(BF), "ctx", scatter_dimension=0, tiled=True
    )
    d_inner = dot(d_mlp_all, w_d)
    d_gate = d_inner * up_pre * gate_sig * (1.0 + gate_pre * (1.0 - gate_sig))
    d_upper = d_inner * silu_val
    d_gu = jnp.concatenate([d_gate, d_upper], axis=1).astype(BF)
    d_h1 = upstream + unmix(scatter_dp(d_gu, w_gu, 6))
    gu_grad = t_dot(h1_all, d_gu).astype(BF)

    g_attn_part = jnp.sum(d_h1 * branch * a_scale, axis=0)
    d_branch = norm_back(d_h1 * gains[2], branch, a_scale).astype(BF)
    d_branch_all = gather_ctx(d_branch, 7)
    d_attn = dot(d_branch_all, w_o).astype(BF)
    dh = split(d_attn)
    delta = jnp.sum(dh.astype(F32) * attn, axis=-1, keepdims=True)
    d_probs = jnp.einsum("hqd,hkd->hqk", dh, vh, preferred_element_type=F32)
    d_scores = (probs * (d_probs - delta)).astype(BF)
    d_query = join(jnp.einsum("hqk,hkd->hqd", d_scores, kh, preferred_element_type=F32))
    d_key = join(jnp.einsum("hqk,hqd->hkd", d_scores, qh, preferred_element_type=F32))
    d_value = join(jnp.einsum("hqk,hqd->hkd", probs_low, dh, preferred_element_type=F32))
    d_qn = rotate(d_query * HD ** (-0.5), cos_tab, -sine_tab)
    d_kn = rotate(d_key, cos_tab, -sine_tab)
    g_q_part = jnp.sum(d_qn * q_pre * q_scale, axis=0)
    g_k_part = jnp.sum(d_kn * k_pre * k_scale, axis=0)
    e_q, e_k = d_qn * my_gains[0], d_kn * my_gains[1]
    means = (
        lax.psum(jnp.stack([jnp.sum(e_q * q_pre, -1), jnp.sum(e_k * k_pre, -1)], -1), "ctx") / width
    )
    d_q_pre = q_scale * (e_q - q_pre * q_scale * q_scale * means[:, :1])
    d_k_pre = k_scale * (e_k - k_pre * k_scale * k_scale * means[:, 1:])
    d_qkv = jnp.concatenate([d_q_pre, d_k_pre, d_value], axis=1).astype(BF)
    attn_grad = jnp.concatenate([t_dot(x_all, d_qkv), t_dot(d_branch_all, attn_low)], axis=1)
    d_grad = lax.all_to_all(d_grad, "dp", 0, 0, tiled=True).reshape(n_dp, rows, fs)
    gu_grad = lax.psum_scatter(gu_grad, "ctx", scatter_dimension=0, tiled=True)
    gu_grad = lax.all_to_all(gu_grad, "dp", 0, 0, tiled=True).reshape(n_dp, rows, 2 * fs)
    attn_grad, d_x = collect(attn_grad.astype(BF), d_qkv, w_qkv, 9)
    d_input = d_h1 + d_x

    gain_part = jnp.stack(
        [
            lax.dynamic_update_slice(jnp.zeros(width, F32), g_q_part, (me_ctx * hc,)),
            lax.dynamic_update_slice(jnp.zeros(width, F32), g_k_part, (me_ctx * hc,)),
            g_attn_part,
            g_ff_part,
        ],
        axis=0,
    )
    square_total, gain_total = total_over(attn_grad, gu_grad, d_grad, gain_part, 11)
    grad_norm = jnp.sqrt(square_total + jnp.sum(gain_total * gain_total))
    factor = CLIP / (grad_norm + 1e-06)
    new_params, new_first, new_second = adam(
        factor, params, first_moment, second_moment, attn_grad, gu_grad, d_grad
    )
    new_gains, new_gains_first, new_gains_second = adam_update(
        gains, gains_first, gains_second, gain_total * factor, GAIN_RATE, 0.0
    )
    return (
        result.astype(BF)[None],
        d_input.astype(BF)[None],
        grad_norm,
        new_params,
        new_first,
        new_second,
        new_gains,
        new_gains_first,
        new_gains_second,
    )


def solution(mesh):
    split, whole = P("dp", "ctx", None), P(("dp", "ctx"), None)
    return jax.shard_map(
        shards,
        mesh=mesh,
        in_specs=(split, split, P("dp", None), P(), whole, whole, whole, P(), P(), P()),
        out_specs=(split, split, P(), whole, whole, whole, P(), P(), P()),
        check_vma=False,
    )
```

```python
import functools

import jax
import jax.numpy as jnp
from jax import lax
from jax.experimental import pallas as pl
from jax.experimental.pallas import tpu as pltpu
from jax.sharding import PartitionSpec as P

HD = 128
STEP = 10
EPS = 1e-06
THETA = 500000.0
CLIP = 1.0
BETA1 = 0.9
BETA2 = 0.95
RATE = 0.03
GAIN_RATE = 0.8
DECAY = 0.1
ADAM_EPS = 1e-08
BF = jnp.bfloat16
F32 = jnp.float32
MESH = pl.DeviceIdType.MESH
ANY = pl.BlockSpec(memory_space=pl.ANY)
VMEM = pl.BlockSpec(memory_space=pltpu.VMEM)


def rms_scale(values):
    return lax.rsqrt(jnp.mean(values * values, axis=-1, keepdims=True) + EPS)


def norm_back(upstream, source, scale):
    return scale * (
        upstream - source * scale * scale * jnp.mean(upstream * source, axis=-1, keepdims=True)
    )


def rope_tables(positions, head_size):
    half_size = head_size // 2
    freqs = THETA ** (-jnp.arange(half_size, dtype=jnp.float32) * 2.0 / head_size)
    angles = positions.astype(jnp.float32)[:, None] * freqs[None, :]
    return (jnp.cos(angles), jnp.sin(angles))


def adam_update(weight, first_in, second_in, clipped, rate, decay):
    new_first = BETA1 * first_in + (1.0 - BETA1) * clipped
    new_second = BETA2 * second_in + (1.0 - BETA2) * clipped * clipped
    first_hat = new_first / (1.0 - BETA1**STEP)
    second_hat = new_second / (1.0 - BETA2**STEP)
    new_weight = weight - rate * (first_hat / (jnp.sqrt(second_hat) + ADAM_EPS) + decay * weight)
    return (new_weight, new_first, new_second)


def dot(a, b):
    return jnp.dot(a, b, preferred_element_type=F32)


def dot_t(a, b):
    return lax.dot_general(a, b, (((1,), (1,)), ((), ())), preferred_element_type=F32)


def t_dot(a, b):
    return lax.dot_general(a, b, (((0,), (0,)), ((), ())), preferred_element_type=F32)


def greet(peers):
    barrier = pltpu.get_barrier_semaphore()
    for peer in peers:
        pl.semaphore_signal(barrier, inc=1, device_id=peer, device_id_type=MESH)
    pl.semaphore_wait(barrier, len(peers))


def remote(src, dst, send, recv, peer):
    return pltpu.make_async_remote_copy(
        src_ref=src, dst_ref=dst, send_sem=send, recv_sem=recv, device_id=peer, device_id_type=MESH
    )


def params_of(number, vmem=48):
    return pltpu.CompilerParams(
        collective_id=number, has_side_effects=True, vmem_limit_bytes=vmem * 1024 * 1024
    )


def line_steps(n, me, make_right, make_left):
    for s in range(n - 1):

        @pl.when((me < n - 1) & (me >= s))
        def _():
            make_right(s).start()

        @pl.when((me > 0) & (me + s < n))
        def _():
            make_left(s).start()

        @pl.when(me - 1 - s >= 0)
        def _():
            make_right(s, me - 1 - s).wait_recv()

        @pl.when(me + 1 + s < n)
        def _():
            make_left(s, me + 1 + s).wait_recv()

    for s in range(n - 1):

        @pl.when((me < n - 1) & (me >= s))
        def _():
            make_right(s).wait_send()

        @pl.when((me > 0) & (me + s < n))
        def _():
            make_left(s).wait_send()


def pairs_of(n, me):
    half = n // 2
    parity, pair = me % 2, me // 2
    partner = me + 1 - 2 * parity
    ahead = [2 * ((pair + k) % half) + parity for k in range(1, half)]
    behind = [2 * ((pair + half - k) % half) + parity for k in range(1, half)]
    return half, parity, pair, partner, ahead, behind


def gather_dp_kernel(n, x_ref, o_ref, local, sr, rr, sl, rl):
    me, ctx = lax.axis_index("dp"), lax.axis_index("ctx")

    def here(d):
        return (d, ctx)

    greet([here((me + 1) % n), here((me + n - 1) % n)])
    own = pltpu.make_async_copy(x_ref, o_ref.at[me], local)
    own.start()

    def right(s, block=None):
        b = me - s if block is None else block
        return remote(x_ref if s == 0 else o_ref.at[b], o_ref.at[b], sr.at[s], rr.at[s], here(me + 1))

    def left(s, block=None):
        b = me + s if block is None else block
        return remote(x_ref if s == 0 else o_ref.at[b], o_ref.at[b], sl.at[s], rl.at[s], here(me - 1))

    line_steps(n, me, right, left)
    own.wait()


def gather_dp(x, number):
    n = lax.axis_size("dp")
    out = pl.pallas_call(
        functools.partial(gather_dp_kernel, n),
        out_shape=jax.ShapeDtypeStruct((n,) + x.shape, x.dtype),
        in_specs=[ANY],
        out_specs=ANY,
        scratch_shapes=[pltpu.SemaphoreType.DMA] + [pltpu.SemaphoreType.DMA((n - 1,))] * 4,
        compiler_params=params_of(number),
        name="gather_dp",
    )(x)
    return out.reshape((n * x.shape[0],) + x.shape[1:])


def reduce_ctx(n, dp, me, a_ref, w_ref, cols, o_ref, sa, ra, sb, rb, s1, r1, s2, r2):
    half, parity, pair, partner, ahead, behind = pairs_of(n, me)
    length, width = o_ref.shape
    tile = width // 4

    def product(block, store):
        rows = pl.ds(pl.multiple_of(block * length, length), length)

        @pl.loop(0, 4)
        def _(j):
            part = pl.ds(pl.multiple_of(j * tile, tile), tile)
            store(part, dot_t(a_ref[rows, :], w_ref[part, cols]))

    first, second = [], []
    for k in range(half):

        def store(part, value, k=k):
            sa[k, :, part] = value.astype(BF)

        product(2 * ((pair + k + 1) % half) + 1 - parity, store)
        copy = remote(sa.at[k], ra.at[k], s1.at[k], r1.at[k], (dp, partner))
        copy.start()
        first.append(copy)
    for k in range(half):
        target = 2 * ((pair + k + 1) % half) + parity
        first[k].wait_recv()

        def store(part, value, k=k):
            value = value + ra[k, :, part].astype(F32)
            if k < half - 1:
                sb[k, :, part] = value.astype(BF)
            else:
                o_ref[:, part] = value

        product(target, store)
        if k < half - 1:
            copy = remote(sb.at[k], rb.at[k], s2.at[k], r2.at[k], (dp, target))
            copy.start()
            second.append(copy)
    for k in range(half - 1):
        second[k].wait_recv()
        o_ref[...] += rb[k].astype(F32)
    return first + second


def scatter_dp_kernel(n, pairs, *refs):
    operands, (o_ref, sa, ra, ss, rs) = refs[: 2 * pairs], refs[2 * pairs :]
    me, ctx = lax.axis_index("dp"), lax.axis_index("ctx")
    length, width = o_ref.shape
    tile = width // 4

    def product(block, out):
        rows = pl.ds(pl.multiple_of(block * length, length), length)

        @pl.loop(0, 4)
        def _(j):
            part = pl.ds(pl.multiple_of(j * tile, tile), tile)
            value = dot_t(operands[0][rows, :], operands[1][part, :])
            for i in range(1, pairs):
                value += dot_t(operands[2 * i][rows, :], operands[2 * i + 1][part, :])
            out[:, part] = value.astype(out.dtype)

    greet([((me + k) % n, ctx) for k in range(1, n)])
    copies = []
    for k in range(1, n):
        target = (me + k) % n
        product(target, sa.at[k - 1])
        copy = remote(sa.at[k - 1], ra.at[k - 1], ss.at[k - 1], rs.at[k - 1], (target, ctx))
        copy.start()
        copies.append(copy)
    product(me, o_ref)
    for k in range(n - 1):
        copies[k].wait_recv()
        o_ref[...] += ra[k].astype(F32)
    for copy in copies:
        copy.wait_send()


def scatter_dp(operands, number):
    n = lax.axis_size("dp")
    length, width = operands[0].shape[0] // n, operands[1].shape[0]
    dma = pltpu.SemaphoreType.DMA
    return pl.pallas_call(
        functools.partial(scatter_dp_kernel, n, len(operands) // 2),
        out_shape=jax.ShapeDtypeStruct((length, width), F32),
        in_specs=[VMEM] * len(operands),
        out_specs=VMEM,
        scratch_shapes=[
            pltpu.VMEM((n - 1, length, width), BF),
            pltpu.VMEM((n - 1, length, width), BF),
            dma((n - 1,)),
            dma((n - 1,)),
        ],
        compiler_params=params_of(number, 56),
        name="scatter_dp",
    )(*operands)


def start_kernel(
    n_dp, n, g_ref, w_ref, x_ref, h_ref, o_ref, y_ref, local, sg, rg, sa, ra, ss, rs, fs, fr
):
    dp, me = lax.axis_index("dp"), lax.axis_index("ctx")
    half, parity, pair, partner, ahead, behind = pairs_of(n, me)
    greet(
        [((dp + k) % n_dp, me) for k in range(1, n_dp)] + [(dp, (me + k) % n) for k in range(1, n)]
    )
    owns = [
        pltpu.make_async_copy(g_ref.at[dp], h_ref.at[dp], local.at[0]),
        pltpu.make_async_copy(w_ref.at[me], o_ref.at[me], local.at[1]),
        pltpu.make_async_copy(x_ref, y_ref.at[me], local.at[2]),
    ]
    sends = []
    for k in range(1, n_dp):
        to = (dp + k) % n_dp
        sends.append(remote(g_ref.at[to], h_ref.at[dp], sg.at[k - 1], rg.at[k - 1], (to, me)))
    for k in range(1, n):
        to = (me + k) % n
        sends.append(remote(w_ref.at[to], o_ref.at[me], sa.at[k - 1], ra.at[k - 1], (dp, to)))
    for k, a in enumerate(ahead + [partner]):
        sends.append(remote(x_ref, y_ref.at[me], ss.at[k], rs.at[k], (dp, a)))
    for copy in sends + owns:
        copy.start()
    forwards = []
    for k, b in enumerate(behind):
        remote(x_ref, y_ref.at[b], ss.at[k], rs.at[k], (dp, b)).wait_recv()
        forward = remote(y_ref.at[b], y_ref.at[b], fs.at[k], fr.at[k], (dp, partner))
        forward.start()
        forwards.append(forward)
    sends[-1].wait_recv()
    for k in range(1, n):
        source = (me + n - k) % n
        remote(w_ref.at[me], o_ref.at[source], sa.at[k - 1], ra.at[k - 1], (dp, source)).wait_recv()
    for k in range(1, n_dp):
        source = (dp + n_dp - k) % n_dp
        remote(g_ref.at[dp], h_ref.at[source], sg.at[k - 1], rg.at[k - 1], (source, me)).wait_recv()
    for forward in forwards:
        forward.wait()
    for copy in sends:
        copy.wait_send()
    for copy in owns:
        copy.wait()


def start(g, w, x, number):
    n_dp, n = lax.axis_size("dp"), lax.axis_size("ctx")
    half = n // 2
    dma = pltpu.SemaphoreType.DMA
    g_out, w_out, x_all = pl.pallas_call(
        functools.partial(start_kernel, n_dp, n),
        out_shape=(
            jax.ShapeDtypeStruct(g.shape, g.dtype),
            jax.ShapeDtypeStruct(w.shape, w.dtype),
            jax.ShapeDtypeStruct((n,) + x.shape, x.dtype),
        ),
        in_specs=[ANY] * 3,
        out_specs=(ANY,) * 3,
        scratch_shapes=[dma((3,))]
        + [dma((n_dp - 1,))] * 2
        + [dma((n - 1,))] * 2
        + [dma((half,))] * 2
        + [dma((half - 1,))] * 2,
        compiler_params=params_of(number),
        name="start",
    )(g, w, x)
    return g_out, w_out, x_all.reshape(-1, x.shape[-1])


def swap_behind(x):
    n, me = lax.axis_size("dp"), lax.axis_index("dp")
    out = jnp.zeros_like(x)
    for k in range(n):
        piece = lax.dynamic_index_in_dim(x, (me + k) % n, keepdims=True)
        if k:
            piece = lax.ppermute(piece, "dp", [(i, (i + k) % n) for i in range(n)])
        out = lax.dynamic_update_index_in_dim(out, piece, (me + n - k) % n, 0)
    return out


def collect_kernel(
    n_dp, n, g_ref, a_ref, w_ref, o_ref, y_ref,
    own, ra, rc, sb, pa, qa, pb, qb,
    local, sa, rs, sc, rd, s1, r1, s2, r2,
):
    dp, me = lax.axis_index("dp"), lax.axis_index("ctx")
    greet(
        [((dp + k) % n_dp, me) for k in range(1, n_dp)] + [(dp, (me + k) % n) for k in range(1, n)]
    )
    mine = pltpu.make_async_copy(g_ref.at[dp], own, local)
    mine.start()
    first = []
    for c in range(n):
        row = []
        for k in range(1, n_dp):
            to = (dp + k) % n_dp
            copy = remote(
                g_ref.at[to, (me + 1 + c) % n],
                ra.at[c, k - 1],
                sa.at[c, k - 1],
                rs.at[c, k - 1],
                (to, me),
            )
            copy.start()
            row.append(copy)
        first.append(row)
    sums = reduce_ctx(n, dp, me, a_ref, w_ref, slice(0, a_ref.shape[1]), y_ref, pa, qa, pb, qb, s1, r1, s2, r2)
    mine.wait()
    second = []
    for c in range(n):
        to = (me + 1 + c) % n
        total = own[to].astype(F32)
        for k in range(n_dp - 1):
            first[c][k].wait_recv()
            total = total + ra[c, k].astype(F32)
        if c < n - 1:
            sb[c] = total.astype(BF)
            copy = remote(sb.at[c], rc.at[c], sc.at[c], rd.at[c], (dp, to))
            copy.start()
            second.append(copy)
        else:
            o_ref[me] = total.astype(BF)
    for c in range(n - 1):
        second[c].wait_recv()
        o_ref[(me + n - 1 - c) % n] = rc[c]
    for row in first:
        for copy in row:
            copy.wait_send()
    for copy in second + sums:
        copy.wait_send()


def collect(g, a, w, number):
    n_dp, n = lax.axis_size("dp"), lax.axis_size("ctx")
    rows, width = g.shape[0] // (n_dp * n), g.shape[1]
    half, length, features = n // 2, a.shape[0] // n, w.shape[0]
    dma = pltpu.SemaphoreType.DMA
    return pl.pallas_call(
        functools.partial(collect_kernel, n_dp, n),
        out_shape=(
            jax.ShapeDtypeStruct((n, rows, width), BF),
            jax.ShapeDtypeStruct((length, features), F32),
        ),
        in_specs=[ANY, VMEM, VMEM],
        out_specs=(VMEM, VMEM),
        scratch_shapes=[
            pltpu.VMEM((n, rows, width), BF),
            pltpu.VMEM((n, n_dp - 1, rows, width), BF),
            pltpu.VMEM((n - 1, rows, width), BF),
            pltpu.VMEM((n - 1, rows, width), BF),
            pltpu.VMEM((half, length, features), BF),
            pltpu.VMEM((half, length, features), BF),
            pltpu.VMEM((half - 1, length, features), BF),
            pltpu.VMEM((half - 1, length, features), BF),
            dma,
            dma((n, n_dp - 1)),
            dma((n, n_dp - 1)),
            dma((n - 1,)),
            dma((n - 1,)),
            dma((half,)),
            dma((half,)),
            dma((half - 1,)),
            dma((half - 1,)),
        ],
        compiler_params=params_of(number),
        name="collect",
    )(g.reshape(n_dp, n, rows, width), a, w)


def total_kernel(n_dp, n, ga_ref, gu_ref, gd_ref, gain_ref, o_ref, mine, buf, part, all_parts, ss, rs, st, rt):
    dp, me = lax.axis_index("dp"), lax.axis_index("ctx")
    gain_rows = gain_ref.shape[0]

    def squares(ref):
        acc = jnp.zeros((ref.shape[1], ref.shape[2]), F32)
        for i in range(ref.shape[0]):
            block = ref[i].astype(F32)
            acc += block * block
        return jnp.sum(acc, axis=0, keepdims=True)

    total = (
        jnp.sum(squares(ga_ref), axis=1, keepdims=True)
        + jnp.sum(squares(gu_ref), axis=1, keepdims=True)
        + jnp.sum(squares(gd_ref), axis=1, keepdims=True)
    )
    mine[0:gain_rows, :] = gain_ref[...]
    mine[gain_rows:, :] = jnp.broadcast_to(total, (8, 128))
    greet(
        [((dp + k) % n_dp, me) for k in range(1, n_dp)] + [(dp, (me + k) % n) for k in range(1, n)]
    )
    copies = []
    for k in range(1, n):
        copy = remote(mine, buf.at[me], ss.at[k - 1], rs.at[k - 1], (dp, (me + k) % n))
        copy.start()
        copies.append(copy)
    buf[me] = mine[...]
    for k in range(1, n):
        source = (me + n - k) % n
        remote(mine, buf.at[source], ss.at[k - 1], rs.at[k - 1], (dp, source)).wait_recv()
    acc = buf[0]
    for j in range(1, n):
        acc = acc + buf[j]
    part[...] = acc
    all_parts[dp] = acc
    for k in range(1, n_dp):
        copy = remote(part, all_parts.at[dp], st.at[k - 1], rt.at[k - 1], ((dp + k) % n_dp, me))
        copy.start()
        copies.append(copy)
    for k in range(1, n_dp):
        source = (dp + n_dp - k) % n_dp
        remote(part, all_parts.at[source], st.at[k - 1], rt.at[k - 1], (source, me)).wait_recv()
    acc = all_parts[0]
    for j in range(1, n_dp):
        acc = acc + all_parts[j]
    o_ref[...] = acc
    for copy in copies:
        copy.wait_send()


def total_over(ga, gu, gd, gain_part, number):
    n_dp, n = lax.axis_size("dp"), lax.axis_size("ctx")
    gain_rows = gain_part.size // 128
    shape = (gain_rows + 8, 128)
    dma = pltpu.SemaphoreType.DMA
    out = pl.pallas_call(
        functools.partial(total_kernel, n_dp, n),
        out_shape=jax.ShapeDtypeStruct(shape, F32),
        in_specs=[VMEM] * 4,
        out_specs=VMEM,
        scratch_shapes=[
            pltpu.VMEM(shape, F32),
            pltpu.VMEM((n,) + shape, F32),
            pltpu.VMEM(shape, F32),
            pltpu.VMEM((n_dp,) + shape, F32),
            dma((n - 1,)),
            dma((n - 1,)),
            dma((n_dp - 1,)),
            dma((n_dp - 1,)),
        ],
        compiler_params=params_of(number),
        name="total",
    )(ga, gu, gd, gain_part.reshape(gain_rows, 128))
    return out[gain_rows, 0], out[:gain_rows].reshape(gain_part.shape)


def adam_kernel(factor_ref, p_ref, m_ref, v_ref, ga_ref, gu_ref, gd_ref, po_ref, mo_ref, vo_ref, g_ref):
    part = pl.program_id(0)
    n, _, four = ga_ref.shape
    hc = four // 4
    fs = gd_ref.shape[2]

    @pl.when(part == 0)
    def _():
        for matrix in range(4):
            for c in range(n):
                start = (matrix * n + c) * hc
                g_ref[:, start : start + hc] = ga_ref[c, :, matrix * hc : (matrix + 1) * hc].astype(F32)

    @pl.when((part == 1) | (part == 2))
    def _():
        for d in range(gu_ref.shape[0]):
            g_ref[:, d * fs : (d + 1) * fs] = gu_ref[d].astype(F32)

    @pl.when(part == 3)
    def _():
        for d in range(gd_ref.shape[0]):
            g_ref[:, d * fs : (d + 1) * fs] = gd_ref[d].astype(F32)

    clipped = g_ref[...] * factor_ref[0, 0]
    new_p, new_m, new_v = adam_update(p_ref[...], m_ref[...], v_ref[...], clipped, RATE, DECAY)
    po_ref[...] = new_p
    mo_ref[...] = new_m
    vo_ref[...] = new_v


def adam(factor, params, first, second, ga, gu, gd):
    rows, columns = params.shape
    n, n_dp, fs = ga.shape[0], gd.shape[0], gd.shape[2]
    block = min(rows, 16)
    steps = rows // block
    wide = pl.BlockSpec((block, columns // 4), lambda i, r: (r, i))
    return pl.pallas_call(
        adam_kernel,
        grid=(4, steps),
        out_shape=(jax.ShapeDtypeStruct(params.shape, F32),) * 3,
        in_specs=[
            pl.BlockSpec(memory_space=pltpu.SMEM),
            wide,
            wide,
            wide,
            pl.BlockSpec((n, block, ga.shape[2]), lambda i, r: (0, jnp.where(i == 0, r, steps - 1), 0)),
            pl.BlockSpec(
                (n_dp, block, fs),
                lambda i, r: (
                    0,
                    jnp.where(i == 0, 0, jnp.where(i == 3, steps - 1, r)),
                    jnp.clip(i - 1, 0, 1),
                ),
            ),
            pl.BlockSpec((n_dp, block, fs), lambda i, r: (0, jnp.where(i == 3, r, 0), 0)),
        ],
        out_specs=(wide, wide, wide),
        scratch_shapes=[pltpu.VMEM((block, columns // 4), F32)],
        compiler_params=pltpu.CompilerParams(vmem_limit_bytes=48 * 1024 * 1024),
        name="adam",
    )(factor.reshape(1, 1), params, first, second, ga, gu, gd)


def arrange_kernel(n, n_dp, p_ref, a_ref, g_ref, u_ref, d_ref):
    part = pl.program_id(0)
    hc = a_ref.shape[2] // 4
    fs = g_ref.shape[2]

    @pl.when(part == 0)
    def _():
        for matrix in range(4):
            for c in range(n):
                start = (matrix * n + c) * hc
                a_ref[c, :, matrix * hc : (matrix + 1) * hc] = p_ref[:, start : start + hc].astype(BF)

    for index, ref in ((1, g_ref), (2, u_ref), (3, d_ref)):

        @pl.when(part == index)
        def _():
            for d in range(n_dp):
                ref[d] = p_ref[:, d * fs : (d + 1) * fs].astype(BF)


def arrange(params, width):
    n_dp, n = lax.axis_size("dp"), lax.axis_size("ctx")
    rows, columns = params.shape
    fs, hc = columns // 4 // n_dp, width // n
    whole = lambda shape: pl.BlockSpec(shape, lambda i: (0,) * len(shape))
    shapes = [(n, rows, 4 * hc)] + [(n_dp, rows, fs)] * 3
    return pl.pallas_call(
        functools.partial(arrange_kernel, n, n_dp),
        grid=(4,),
        out_shape=tuple(jax.ShapeDtypeStruct(s, BF) for s in shapes),
        in_specs=[pl.BlockSpec((rows, columns // 4), lambda i: (0, i))],
        out_specs=tuple(whole(s) for s in shapes),
        compiler_params=pltpu.CompilerParams(vmem_limit_bytes=48 * 1024 * 1024),
        name="arrange",
    )(params)


def row_sums(value, row):
    pick = lax.broadcasted_iota(jnp.int32, (8, value.shape[1]), 0) == row
    return lax.dot_general(
        pick.astype(F32),
        value,
        (((1,), (1,)), ((), ())),
        preferred_element_type=F32,
        precision=lax.Precision.HIGHEST,
    )


def exchange(n, dp, me, buf, ss, rs):
    copies = []
    for k in range(1, n):
        copy = remote(buf.at[me], buf.at[me], ss.at[k - 1], rs.at[k - 1], (dp, (me + k) % n))
        copy.start()
        copies.append(copy)
    for k in range(1, n):
        source = (me + n - k) % n
        remote(buf.at[me], buf.at[source], ss.at[k - 1], rs.at[k - 1], (dp, source)).wait_recv()
    total = buf[0]
    for j in range(1, n):
        total = total + buf[j]
    for copy in copies:
        copy.wait_send()
    return total


def turn(value, cos, sine):
    return value * cos + pltpu.roll(value, HD // 2, 1) * sine


def mask_of(rows, info_col, info_row):
    pos_i, doc_i = info_col[rows, 0:1], info_col[rows, 1:2]
    return (info_row[1:2, :] == doc_i) & (info_row[0:1, :] <= pos_i)


def attend_kernel(
    n, x_ref, w_ref, gain_ref, cos_ref, sin_ref, col_ref, row_ref,
    y_ref, q_ref, k_ref, v_ref, o_ref, pre_ref, scale_ref, lse_ref,
    buf, pa, qa, pb, qb, ss, rs, s1, r1, s2, r2,
):
    dp, me = lax.axis_index("dp"), lax.axis_index("ctx")
    seq, width = x_ref.shape
    hc = o_ref.shape[1]
    block = min(seq, 256)
    greet([(dp, (me + k) % n) for k in range(1, n)])

    @pl.loop(0, seq // block)
    def _(i):
        rows = pl.ds(pl.multiple_of(i * block, block), block)
        value = dot(x_ref[rows, :], w_ref[:, : 3 * hc])
        pre_ref[rows, :] = value[:, : 2 * hc]
        v_ref[rows, :] = value[:, 2 * hc :].astype(BF)
        squares = value[:, : 2 * hc] * value[:, : 2 * hc]
        buf[me, :, rows] = row_sums(squares[:, :hc], 0) + row_sums(squares[:, hc:], 1)

    scale_ref[...] = jnp.transpose(lax.rsqrt(exchange(n, dp, me, buf, ss, rs) / width + EPS))

    @pl.loop(0, seq // block)
    def _(i):
        rows = pl.ds(pl.multiple_of(i * block, block), block)
        cos, sine = cos_ref[rows, :], sin_ref[rows, :]
        for which, ref, factor in ((0, q_ref, HD ** (-0.5)), (1, k_ref, 1.0)):
            scale = scale_ref[rows, which : which + 1]
            for start in range(0, hc, HD):
                part = slice(start, start + HD)
                value = pre_ref[rows, which * hc + start : which * hc + start + HD] * scale
                ref[rows, part] = (
                    turn(value * gain_ref[which : which + 1, part], cos, sine) * factor
                ).astype(BF)

    @pl.loop(0, seq // block)
    def _(i):
        rows = pl.ds(pl.multiple_of(i * block, block), block)
        visible = mask_of(rows, col_ref, row_ref)
        for head in range(hc // HD):
            part = slice(head * HD, (head + 1) * HD)
            scores = jnp.where(visible, dot_t(q_ref[rows, part], k_ref[:, part]), -jnp.inf)
            top = jnp.max(scores, axis=1, keepdims=True)
            weights = jnp.exp(scores - top)
            total = jnp.sum(weights, axis=1, keepdims=True)
            o_ref[rows, part] = (dot(weights.astype(BF), v_ref[:, part]) / total).astype(BF)
            lse_ref[rows, head : head + 1] = top + jnp.log(total)

    cols = slice(3 * hc, 4 * hc)
    for copy in reduce_ctx(n, dp, me, o_ref, w_ref, cols, y_ref, pa, qa, pb, qb, s1, r1, s2, r2):
        copy.wait_send()


def attend(x_all, w, gain, cos, sine, info_col, info_row, number):
    n = lax.axis_size("ctx")
    seq, width = x_all.shape
    half, length, hc = n // 2, seq // n, w.shape[1] // 4
    dma = pltpu.SemaphoreType.DMA
    low = jax.ShapeDtypeStruct((seq, hc), BF)
    return pl.pallas_call(
        functools.partial(attend_kernel, n),
        out_shape=(
            jax.ShapeDtypeStruct((length, width), F32),
            low,
            low,
            low,
            low,
            jax.ShapeDtypeStruct((seq, 2 * hc), F32),
            jax.ShapeDtypeStruct((seq, 8), F32),
            jax.ShapeDtypeStruct((seq, 8), F32),
        ),
        in_specs=[VMEM] * 7,
        out_specs=(VMEM,) * 8,
        scratch_shapes=[
            pltpu.VMEM((n, 8, seq), F32),
            pltpu.VMEM((half, length, width), BF),
            pltpu.VMEM((half, length, width), BF),
            pltpu.VMEM((half - 1, length, width), BF),
            pltpu.VMEM((half - 1, length, width), BF),
            dma((n - 1,)),
            dma((n - 1,)),
            dma((half,)),
            dma((half,)),
            dma((half - 1,)),
            dma((half - 1,)),
        ],
        compiler_params=params_of(number),
        name="attend",
    )(x_all, w, gain, cos, sine, info_col, info_row)


def attend_back_kernel(
    n, e_ref, w_ref, gain_ref, cos_ref, sin_ref, col_ref, row_ref,
    q_ref, k_ref, v_ref, pre_ref, scale_ref, lse_ref,
    all_ref, d_ref, gain_out,
    do_ref, dq_ref, dk_ref, dv_ref, mean_ref, buf, ss, rs, s1, r1, s2, r2,
):
    dp, me = lax.axis_index("dp"), lax.axis_index("ctx")
    half, parity, pair, partner, ahead, behind = pairs_of(n, me)
    seq, hc = q_ref.shape
    length, width = e_ref.shape
    block = min(seq, 256)
    greet([(dp, (me + k) % n) for k in range(1, n)])
    sends = [
        remote(e_ref, all_ref.at[me], s1.at[k], r1.at[k], (dp, a))
        for k, a in enumerate(ahead + [partner])
    ]
    for copy in sends:
        copy.start()
    all_ref[me] = e_ref[...]
    dk_ref[...] = jnp.zeros_like(dk_ref)
    dv_ref[...] = jnp.zeros_like(dv_ref)

    def project(b):
        rows = pl.ds(pl.multiple_of(b * length, length), length)
        do_ref[rows, :] = dot(all_ref[b], w_ref[:, 3 * hc : 4 * hc]).astype(BF)

    project(me)
    sends[-1].wait_recv()
    project(partner)
    forwards = []
    for k, b in enumerate(behind):
        remote(e_ref, all_ref.at[b], s1.at[k], r1.at[k], (dp, b)).wait_recv()
        forward = remote(all_ref.at[b], all_ref.at[b], s2.at[k], r2.at[k], (dp, partner))
        forward.start()
        forwards.append(forward)
        project(b)
    for k, b in enumerate(behind):
        forwards[k].wait_recv()
        project(b + 1 - 2 * parity)

    @pl.loop(0, seq // block)
    def _(i):
        rows = pl.ds(pl.multiple_of(i * block, block), block)
        visible = mask_of(rows, col_ref, row_ref)
        for head in range(hc // HD):
            part = slice(head * HD, (head + 1) * HD)
            query, key, value, back = q_ref[rows, part], k_ref[:, part], v_ref[:, part], do_ref[rows, part]
            scores = jnp.where(visible, dot_t(query, key), -jnp.inf)
            probs = jnp.exp(scores - lse_ref[rows, head : head + 1])
            d_probs = dot_t(back, value)
            delta = jnp.sum(probs * d_probs, axis=1, keepdims=True)
            d_scores = (probs * (d_probs - delta)).astype(BF)
            dq_ref[rows, part] = dot(d_scores, key)
            dk_ref[:, part] += t_dot(d_scores, query)
            dv_ref[:, part] += t_dot(probs.astype(BF), back)

    gain_out[...] = jnp.zeros_like(gain_out)

    @pl.loop(0, seq // block)
    def _(i):
        rows = pl.ds(pl.multiple_of(i * block, block), block)
        cos, sine = cos_ref[rows, :], sin_ref[rows, :]
        sums = jnp.zeros((8, block), F32)
        for which, ref, factor in ((0, dq_ref, HD ** (-0.5)), (1, dk_ref, 1.0)):
            scale = scale_ref[rows, which : which + 1]
            for start in range(0, hc, HD):
                part = slice(start, start + HD)
                pre = pre_ref[rows, which * hc + start : which * hc + start + HD]
                value = turn(ref[rows, part] * factor, cos, -sine)
                gain_out[which : which + 1, part] += jnp.sum(value * pre * scale, axis=0, keepdims=True)
                value = value * gain_ref[which : which + 1, part]
                ref[rows, part] = value
                sums += row_sums(value * pre, which)
        buf[me, :, rows] = sums

    mean_ref[...] = jnp.transpose(exchange(n, dp, me, buf, ss, rs) / width)

    @pl.loop(0, seq // block)
    def _(i):
        rows = pl.ds(pl.multiple_of(i * block, block), block)
        for which, ref in ((0, dq_ref), (1, dk_ref)):
            scale = scale_ref[rows, which : which + 1]
            mean = mean_ref[rows, which : which + 1]
            cols = slice(which * hc, (which + 1) * hc)
            value = scale * (ref[rows, :] - pre_ref[rows, cols] * (scale * scale * mean))
            d_ref[rows, cols] = value.astype(BF)
        d_ref[rows, 2 * hc :] = dv_ref[rows, :].astype(BF)

    for copy in sends + forwards:
        copy.wait_send()


def attend_back(e, w, gain, cos, sine, info_col, info_row, q, k, v, pre, scale, lse, number):
    n = lax.axis_size("ctx")
    seq, hc = q.shape
    half, (length, width) = n // 2, e.shape
    dma = pltpu.SemaphoreType.DMA
    all_e, d_qkv, d_gain = pl.pallas_call(
        functools.partial(attend_back_kernel, n),
        out_shape=(
            jax.ShapeDtypeStruct((n, length, width), BF),
            jax.ShapeDtypeStruct((seq, 3 * hc), BF),
            jax.ShapeDtypeStruct((2, hc), F32),
        ),
        in_specs=[VMEM] * 13,
        out_specs=(VMEM,) * 3,
        scratch_shapes=[
            pltpu.VMEM((seq, hc), BF),
            pltpu.VMEM((seq, hc), F32),
            pltpu.VMEM((seq, hc), F32),
            pltpu.VMEM((seq, hc), F32),
            pltpu.VMEM((seq, 8), F32),
            pltpu.VMEM((n, 8, seq), F32),
            dma((n - 1,)),
            dma((n - 1,)),
            dma((half,)),
            dma((half,)),
            dma((half - 1,)),
            dma((half - 1,)),
        ],
        compiler_params=params_of(number),
        name="attend_back",
    )(e, w, gain, cos, sine, info_col, info_row, q, k, v, pre, scale, lse)
    return all_e.reshape(seq, width), d_qkv, d_gain


def shards(
    inputs,
    cotangent,
    documents,
    block_place,
    params,
    first_moment,
    second_moment,
    gains,
    gains_first,
    gains_second,
):
    tokens = inputs[0]
    upstream = cotangent[0].astype(F32)
    length, width = tokens.shape
    n_ctx = lax.axis_size("ctx")
    n_dp = lax.axis_size("dp")
    me_ctx = lax.axis_index("ctx")
    seq = length * n_ctx
    rows = params.shape[0]
    ff = (params.shape[1] - 4 * width) // 3
    hc = width // n_ctx
    heads = hc // HD
    fs = ff // n_dp

    def mix(values):
        t = values.shape[0]
        return (
            values.reshape(t, n_dp, n_ctx, rows).transpose(0, 2, 1, 3).reshape(t, width)
        )

    def unmix(values):
        t = values.shape[0]
        return (
            values.reshape(t, n_ctx, n_dp, rows).transpose(0, 2, 1, 3).reshape(t, width)
        )

    wa, wg, wu, wd = arrange(params, width)
    wg, wa, x_all = start(wg, wa, tokens, 1)
    w_g = lax.all_gather(wg.reshape(n_dp * rows, fs), "ctx", axis=0, tiled=True)
    wa = gather_dp(wa.reshape(n_ctx * rows, 4 * hc), 2)
    wu, wd, wa = lax.optimization_barrier((wu, wd, wa))
    w_u, w_d = [
        lax.all_gather(swap_behind(w).reshape(n_dp * rows, fs), "ctx", axis=0, tiled=True)
        for w in (wu, wd)
    ]

    indices = jnp.arange(seq, dtype=jnp.int32)
    owners = indices // length
    placed = jnp.sum(
        jnp.where(
            owners[:, None] == jnp.arange(n_ctx, dtype=jnp.int32)[None, :], block_place[None, :], 0
        ),
        axis=1,
    )
    pos = placed * length + indices % length
    docs = documents[0]
    info_row = jnp.concatenate([pos[None], docs[None], jnp.zeros((6, seq), jnp.int32)])
    info_col = info_row.T
    cos_tab, sine_tab = rope_tables(pos, HD)
    cos_tab = jnp.concatenate([cos_tab, cos_tab], axis=1)
    sine_tab = jnp.concatenate([-sine_tab, sine_tab], axis=1)
    my_gains = lax.dynamic_slice_in_dim(gains[:2], me_ctx * hc, hc, axis=1)
    tables = (my_gains, cos_tab, sine_tab, info_col, info_row)

    branch, queries, keys, values, attn_low, qk_pre, scales, lse = attend(x_all, wa, *tables, 3)
    a_scale = rms_scale(branch)
    hidden1 = tokens.astype(F32) + branch * a_scale * gains[2]

    h1_all = gather_dp(mix(hidden1.astype(BF)), 4)
    gate_pre, up_pre = dot(h1_all, w_g), dot(h1_all, w_u)
    gate_sig = jax.nn.sigmoid(gate_pre)
    silu_val = gate_pre * gate_sig
    inner = (silu_val * up_pre).astype(BF)
    mlp_out = unmix(scatter_dp((inner, w_d), 5))
    m_scale = rms_scale(mlp_out)
    result = hidden1 + mlp_out * m_scale * gains[3]

    g_ff_part = jnp.sum(upstream * mlp_out * m_scale, axis=0)
    d_mlp = norm_back(upstream * gains[3], mlp_out, m_scale).astype(BF)
    d_mlp_all = gather_dp(mix(d_mlp), 6)
    d_grad = lax.psum_scatter(
        t_dot(d_mlp_all, inner).astype(BF), "ctx", scatter_dimension=0, tiled=True
    )
    d_inner = dot(d_mlp_all, w_d)
    d_gate = (d_inner * up_pre * gate_sig * (1.0 + gate_pre * (1.0 - gate_sig))).astype(BF)
    d_upper = (d_inner * silu_val).astype(BF)
    d_h1 = upstream + unmix(scatter_dp((d_gate, w_g, d_upper, w_u), 7))
    gu_grad = t_dot(h1_all, jnp.concatenate([d_gate, d_upper], axis=1)).astype(BF)

    g_attn_part = jnp.sum(d_h1 * branch * a_scale, axis=0)
    d_branch = norm_back(d_h1 * gains[2], branch, a_scale).astype(BF)
    d_branch_all, d_qkv, d_gain = attend_back(
        d_branch, wa, *tables, queries, keys, values, qk_pre, scales, lse, 8
    )
    attn_grad = jnp.concatenate([t_dot(x_all, d_qkv), t_dot(d_branch_all, attn_low)], axis=1)
    d_grad = lax.all_to_all(d_grad, "dp", 0, 0, tiled=True).reshape(n_dp, rows, fs)
    gu_grad = lax.psum_scatter(gu_grad, "ctx", scatter_dimension=0, tiled=True)
    gu_grad = lax.all_to_all(gu_grad, "dp", 0, 0, tiled=True).reshape(n_dp, rows, 2 * fs)
    attn_grad, d_x = collect(attn_grad.astype(BF), d_qkv, wa, 9)
    d_input = d_h1 + d_x

    gain_part = jnp.stack(
        [
            *lax.dynamic_update_slice(jnp.zeros((2, width), F32), d_gain, (0, me_ctx * hc)),
            g_attn_part,
            g_ff_part,
        ],
        axis=0,
    )
    square_total, gain_total = total_over(attn_grad, gu_grad, d_grad, gain_part, 11)
    grad_norm = jnp.sqrt(square_total + jnp.sum(gain_total * gain_total))
    factor = CLIP / (grad_norm + 1e-06)
    new_params, new_first, new_second = adam(
        factor, params, first_moment, second_moment, attn_grad, gu_grad, d_grad
    )
    new_gains, new_gains_first, new_gains_second = adam_update(
        gains, gains_first, gains_second, gain_total * factor, GAIN_RATE, 0.0
    )
    return (
        result.astype(BF)[None],
        d_input.astype(BF)[None],
        grad_norm,
        new_params,
        new_first,
        new_second,
        new_gains,
        new_gains_first,
        new_gains_second,
    )


def solution(mesh):
    split, whole = P("dp", "ctx", None), P(("dp", "ctx"), None)
    return jax.shard_map(
        shards,
        mesh=mesh,
        in_specs=(split, split, P("dp", None), P(), whole, whole, whole, P(), P(), P()),
        out_specs=(split, split, P(), whole, whole, whole, P(), P(), P()),
        check_vma=False,
    )
```

```python
import functools

import jax
import jax.numpy as jnp
from jax import lax
from jax.experimental import pallas as pl
from jax.experimental.pallas import tpu as pltpu
from jax.sharding import PartitionSpec as P

HD = 128
STEP = 10
EPS = 1e-06
THETA = 500000.0
CLIP = 1.0
BETA1 = 0.9
BETA2 = 0.95
RATE = 0.03
GAIN_RATE = 0.8
DECAY = 0.1
ADAM_EPS = 1e-08
BF = jnp.bfloat16
F32 = jnp.float32
MESH = pl.DeviceIdType.MESH
ANY = pl.BlockSpec(memory_space=pl.ANY)
VMEM = pl.BlockSpec(memory_space=pltpu.VMEM)


def rms_scale(values):
    return lax.rsqrt(jnp.mean(values * values, axis=-1, keepdims=True) + EPS)


def norm_back(upstream, source, scale):
    return scale * (
        upstream - source * scale * scale * jnp.mean(upstream * source, axis=-1, keepdims=True)
    )


def rope_tables(positions, head_size):
    half_size = head_size // 2
    freqs = THETA ** (-jnp.arange(half_size, dtype=jnp.float32) * 2.0 / head_size)
    angles = positions.astype(jnp.float32)[:, None] * freqs[None, :]
    return (jnp.cos(angles), jnp.sin(angles))


def adam_update(weight, first_in, second_in, clipped, rate, decay):
    new_first = BETA1 * first_in + (1.0 - BETA1) * clipped
    new_second = BETA2 * second_in + (1.0 - BETA2) * clipped * clipped
    first_hat = new_first / (1.0 - BETA1**STEP)
    second_hat = new_second / (1.0 - BETA2**STEP)
    new_weight = weight - rate * (first_hat / (jnp.sqrt(second_hat) + ADAM_EPS) + decay * weight)
    return (new_weight, new_first, new_second)


def dot(a, b):
    return jnp.dot(a, b, preferred_element_type=F32)


def dot_t(a, b):
    return lax.dot_general(a, b, (((1,), (1,)), ((), ())), preferred_element_type=F32)


def t_dot(a, b):
    return lax.dot_general(a, b, (((0,), (0,)), ((), ())), preferred_element_type=F32)


def greet(peers):
    barrier = pltpu.get_barrier_semaphore()
    for peer in peers:
        pl.semaphore_signal(barrier, inc=1, device_id=peer, device_id_type=MESH)
    pl.semaphore_wait(barrier, len(peers))


def remote(src, dst, send, recv, peer):
    return pltpu.make_async_remote_copy(
        src_ref=src, dst_ref=dst, send_sem=send, recv_sem=recv, device_id=peer, device_id_type=MESH
    )


def params_of(number, vmem=48):
    return pltpu.CompilerParams(
        collective_id=number, has_side_effects=True, vmem_limit_bytes=vmem * 1024 * 1024
    )


def line_steps(n, me, make_right, make_left):
    for s in range(n - 1):

        @pl.when((me < n - 1) & (me >= s))
        def _():
            make_right(s).start()

        @pl.when((me > 0) & (me + s < n))
        def _():
            make_left(s).start()

        @pl.when(me - 1 - s >= 0)
        def _():
            make_right(s, me - 1 - s).wait_recv()

        @pl.when(me + 1 + s < n)
        def _():
            make_left(s, me + 1 + s).wait_recv()

    for s in range(n - 1):

        @pl.when((me < n - 1) & (me >= s))
        def _():
            make_right(s).wait_send()

        @pl.when((me > 0) & (me + s < n))
        def _():
            make_left(s).wait_send()


def pairs_of(n, me):
    half = n // 2
    parity, pair = me % 2, me // 2
    partner = me + 1 - 2 * parity
    ahead = [2 * ((pair + k) % half) + parity for k in range(1, half)]
    behind = [2 * ((pair + half - k) % half) + parity for k in range(1, half)]
    return half, parity, pair, partner, ahead, behind


def gather_dp_kernel(n, x_ref, o_ref, local, sr, rr, sl, rl):
    me, ctx = lax.axis_index("dp"), lax.axis_index("ctx")

    def here(d):
        return (d, ctx)

    greet([here((me + 1) % n), here((me + n - 1) % n)])
    own = pltpu.make_async_copy(x_ref, o_ref.at[me], local)
    own.start()

    def right(s, block=None):
        b = me - s if block is None else block
        return remote(x_ref if s == 0 else o_ref.at[b], o_ref.at[b], sr.at[s], rr.at[s], here(me + 1))

    def left(s, block=None):
        b = me + s if block is None else block
        return remote(x_ref if s == 0 else o_ref.at[b], o_ref.at[b], sl.at[s], rl.at[s], here(me - 1))

    line_steps(n, me, right, left)
    own.wait()


def gather_dp(x, number):
    n = lax.axis_size("dp")
    out = pl.pallas_call(
        functools.partial(gather_dp_kernel, n),
        out_shape=jax.ShapeDtypeStruct((n,) + x.shape, x.dtype),
        in_specs=[ANY],
        out_specs=ANY,
        scratch_shapes=[pltpu.SemaphoreType.DMA] + [pltpu.SemaphoreType.DMA((n - 1,))] * 4,
        compiler_params=params_of(number),
        name="gather_dp",
    )(x)
    return out.reshape((n * x.shape[0],) + x.shape[1:])


def reduce_ctx(n, dp, me, a_ref, w_ref, cols, o_ref, sa, ra, sb, rb, s1, r1, s2, r2):
    half, parity, pair, partner, ahead, behind = pairs_of(n, me)
    length, width = o_ref.shape
    tile = width // 4

    def product(block, store):
        rows = pl.ds(pl.multiple_of(block * length, length), length)

        @pl.loop(0, 4)
        def _(j):
            part = pl.ds(pl.multiple_of(j * tile, tile), tile)
            store(part, dot_t(a_ref[rows, :], w_ref[part, cols]))

    first, second = [], []
    for k in range(half):

        def store(part, value, k=k):
            sa[k, :, part] = value.astype(BF)

        product(2 * ((pair + k + 1) % half) + 1 - parity, store)
        copy = remote(sa.at[k], ra.at[k], s1.at[k], r1.at[k], (dp, partner))
        copy.start()
        first.append(copy)
    for k in range(half):
        target = 2 * ((pair + k + 1) % half) + parity
        first[k].wait_recv()

        def store(part, value, k=k):
            value = value + ra[k, :, part].astype(F32)
            if k < half - 1:
                sb[k, :, part] = value.astype(BF)
            else:
                o_ref[:, part] = value

        product(target, store)
        if k < half - 1:
            copy = remote(sb.at[k], rb.at[k], s2.at[k], r2.at[k], (dp, target))
            copy.start()
            second.append(copy)
    for k in range(half - 1):
        second[k].wait_recv()
        o_ref[...] += rb[k].astype(F32)
    return first + second


def scatter_dp_kernel(n, pairs, *refs):
    operands, (o_ref, sa, ra, ss, rs) = refs[: 2 * pairs], refs[2 * pairs :]
    me, ctx = lax.axis_index("dp"), lax.axis_index("ctx")
    length, width = o_ref.shape
    tile = width // 4

    def product(block, out):
        rows = pl.ds(pl.multiple_of(block * length, length), length)

        @pl.loop(0, 4)
        def _(j):
            part = pl.ds(pl.multiple_of(j * tile, tile), tile)
            value = dot_t(operands[0][rows, :], operands[1][part, :])
            for i in range(1, pairs):
                value += dot_t(operands[2 * i][rows, :], operands[2 * i + 1][part, :])
            out[:, part] = value.astype(out.dtype)

    greet([((me + k) % n, ctx) for k in range(1, n)])
    copies = []
    for k in range(1, n):
        target = (me + k) % n
        product(target, sa.at[k - 1])
        copy = remote(sa.at[k - 1], ra.at[k - 1], ss.at[k - 1], rs.at[k - 1], (target, ctx))
        copy.start()
        copies.append(copy)
    product(me, o_ref)
    for k in range(n - 1):
        copies[k].wait_recv()
        o_ref[...] += ra[k].astype(F32)
    for copy in copies:
        copy.wait_send()


def scatter_dp(operands, number):
    n = lax.axis_size("dp")
    length, width = operands[0].shape[0] // n, operands[1].shape[0]
    dma = pltpu.SemaphoreType.DMA
    return pl.pallas_call(
        functools.partial(scatter_dp_kernel, n, len(operands) // 2),
        out_shape=jax.ShapeDtypeStruct((length, width), F32),
        in_specs=[VMEM] * len(operands),
        out_specs=VMEM,
        scratch_shapes=[
            pltpu.VMEM((n - 1, length, width), BF),
            pltpu.VMEM((n - 1, length, width), BF),
            dma((n - 1,)),
            dma((n - 1,)),
        ],
        compiler_params=params_of(number, 56),
        name="scatter_dp",
    )(*operands)


def start_kernel(
    n_dp, n, g_ref, w_ref, v_ref, x_ref, h_ref, o_ref, p_ref, y_ref,
    local, sg, rg, sa, ra, sv, rv, ss, rs, fs, fr,
):
    dp, me = lax.axis_index("dp"), lax.axis_index("ctx")
    half, parity, pair, partner, ahead, behind = pairs_of(n, me)
    greet(
        [((dp + k) % n_dp, me) for k in range(1, n_dp)] + [(dp, (me + k) % n) for k in range(1, n)]
    )
    owns = [
        pltpu.make_async_copy(g_ref.at[dp], h_ref.at[dp], local.at[0]),
        pltpu.make_async_copy(w_ref.at[me], o_ref.at[me], local.at[1]),
        pltpu.make_async_copy(x_ref, y_ref.at[me], local.at[2]),
        pltpu.make_async_copy(v_ref.at[me], p_ref.at[me], local.at[3]),
    ]
    sends = []
    for k in range(1, n_dp):
        to = (dp + k) % n_dp
        sends.append(remote(g_ref.at[to], h_ref.at[dp], sg.at[k - 1], rg.at[k - 1], (to, me)))
    for k in range(1, n):
        to = (me + k) % n
        sends.append(remote(w_ref.at[to], o_ref.at[me], sa.at[k - 1], ra.at[k - 1], (dp, to)))
        sends.append(remote(v_ref.at[to], p_ref.at[me], sv.at[k - 1], rv.at[k - 1], (dp, to)))
    for k, a in enumerate(ahead + [partner]):
        sends.append(remote(x_ref, y_ref.at[me], ss.at[k], rs.at[k], (dp, a)))
    for copy in sends + owns:
        copy.start()
    forwards = []
    for k, b in enumerate(behind):
        remote(x_ref, y_ref.at[b], ss.at[k], rs.at[k], (dp, b)).wait_recv()
        forward = remote(y_ref.at[b], y_ref.at[b], fs.at[k], fr.at[k], (dp, partner))
        forward.start()
        forwards.append(forward)
    sends[-1].wait_recv()
    for k in range(1, n):
        source = (me + n - k) % n
        peer = (dp, source)
        remote(w_ref.at[me], o_ref.at[source], sa.at[k - 1], ra.at[k - 1], peer).wait_recv()
        remote(v_ref.at[me], p_ref.at[source], sv.at[k - 1], rv.at[k - 1], peer).wait_recv()
    for k in range(1, n_dp):
        source = (dp + n_dp - k) % n_dp
        remote(g_ref.at[dp], h_ref.at[source], sg.at[k - 1], rg.at[k - 1], (source, me)).wait_recv()
    for forward in forwards:
        forward.wait()
    for copy in sends:
        copy.wait_send()
    for copy in owns:
        copy.wait()


def start(g, w, v, x, number):
    n_dp, n = lax.axis_size("dp"), lax.axis_size("ctx")
    half = n // 2
    dma = pltpu.SemaphoreType.DMA
    g_out, w_out, v_out, x_all = pl.pallas_call(
        functools.partial(start_kernel, n_dp, n),
        out_shape=(
            jax.ShapeDtypeStruct(g.shape, g.dtype),
            jax.ShapeDtypeStruct(w.shape, w.dtype),
            jax.ShapeDtypeStruct(v.shape, v.dtype),
            jax.ShapeDtypeStruct((n,) + x.shape, x.dtype),
        ),
        in_specs=[ANY] * 4,
        out_specs=(ANY,) * 4,
        scratch_shapes=[dma((4,))]
        + [dma((n_dp - 1,))] * 2
        + [dma((n - 1,))] * 4
        + [dma((half,))] * 2
        + [dma((half - 1,))] * 2,
        compiler_params=params_of(number),
        name="start",
    )(g, w, v, x)
    return g_out, w_out, v_out, x_all.reshape(-1, x.shape[-1])


def collect_kernel(
    n_dp, n, g_ref, h_ref, a_ref, w_ref, o_ref, h_out, y_ref,
    own, ra, rc, sb, pa, qa, pb, qb,
    local, sa, rs, sc, rd, s1, r1, s2, r2, sh, rh,
):
    dp, me = lax.axis_index("dp"), lax.axis_index("ctx")
    greet(
        [((dp + k) % n_dp, me) for k in range(1, n_dp)] + [(dp, (me + k) % n) for k in range(1, n)]
    )
    mine = pltpu.make_async_copy(g_ref.at[dp], own, local.at[0])
    mine.start()
    stay = pltpu.make_async_copy(h_ref.at[dp], h_out.at[dp], local.at[1])
    stay.start()
    first = []
    for c in range(n):
        row = []
        for k in range(1, n_dp):
            to = (dp + k) % n_dp
            copy = remote(
                g_ref.at[to, (me + 1 + c) % n],
                ra.at[c, k - 1],
                sa.at[c, k - 1],
                rs.at[c, k - 1],
                (to, me),
            )
            copy.start()
            row.append(copy)
        first.append(row)
    swaps = []
    for k in range(1, n_dp):
        to = (dp + k) % n_dp
        copy = remote(h_ref.at[to], h_out.at[dp], sh.at[k - 1], rh.at[k - 1], (to, me))
        copy.start()
        swaps.append(copy)
    sums = reduce_ctx(n, dp, me, a_ref, w_ref, slice(0, a_ref.shape[1]), y_ref, pa, qa, pb, qb, s1, r1, s2, r2)
    mine.wait()
    second = []
    for c in range(n):
        to = (me + 1 + c) % n
        total = own[to].astype(F32)
        for k in range(n_dp - 1):
            first[c][k].wait_recv()
            total = total + ra[c, k].astype(F32)
        if c < n - 1:
            sb[c] = total.astype(BF)
            copy = remote(sb.at[c], rc.at[c], sc.at[c], rd.at[c], (dp, to))
            copy.start()
            second.append(copy)
        else:
            o_ref[me] = total.astype(BF)
    for c in range(n - 1):
        second[c].wait_recv()
        o_ref[(me + n - 1 - c) % n] = rc[c]
    for k in range(1, n_dp):
        source = (dp + n_dp - k) % n_dp
        remote(h_ref.at[dp], h_out.at[source], sh.at[k - 1], rh.at[k - 1], (source, me)).wait_recv()
    stay.wait()
    for row in first:
        for copy in row:
            copy.wait_send()
    for copy in second + sums + swaps:
        copy.wait_send()


def collect(g, h, a, w, number):
    n_dp, n = lax.axis_size("dp"), lax.axis_size("ctx")
    rows, width = g.shape[0] // (n_dp * n), g.shape[1]
    half, length, features = n // 2, a.shape[0] // n, w.shape[0]
    dma = pltpu.SemaphoreType.DMA
    return pl.pallas_call(
        functools.partial(collect_kernel, n_dp, n),
        out_shape=(
            jax.ShapeDtypeStruct((n, rows, width), BF),
            jax.ShapeDtypeStruct(h.shape, BF),
            jax.ShapeDtypeStruct((length, features), F32),
        ),
        in_specs=[ANY, ANY, VMEM, VMEM],
        out_specs=(VMEM, ANY, VMEM),
        scratch_shapes=[
            pltpu.VMEM((n, rows, width), BF),
            pltpu.VMEM((n, n_dp - 1, rows, width), BF),
            pltpu.VMEM((n - 1, rows, width), BF),
            pltpu.VMEM((n - 1, rows, width), BF),
            pltpu.VMEM((half, length, features), BF),
            pltpu.VMEM((half, length, features), BF),
            pltpu.VMEM((half - 1, length, features), BF),
            pltpu.VMEM((half - 1, length, features), BF),
            dma((2,)),
            dma((n, n_dp - 1)),
            dma((n, n_dp - 1)),
            dma((n - 1,)),
            dma((n - 1,)),
            dma((half,)),
            dma((half,)),
            dma((half - 1,)),
            dma((half - 1,)),
            dma((n_dp - 1,)),
            dma((n_dp - 1,)),
        ],
        compiler_params=params_of(number),
        name="collect",
    )(g.reshape(n_dp, n, rows, width), h, a, w)


def total_kernel(n_dp, n, ga_ref, gu_ref, gd_ref, gain_ref, o_ref, mine, buf, part, all_parts, ss, rs, st, rt):
    dp, me = lax.axis_index("dp"), lax.axis_index("ctx")
    gain_rows = gain_ref.shape[0]

    def squares(ref):
        acc = jnp.zeros((ref.shape[1], ref.shape[2]), F32)
        for i in range(ref.shape[0]):
            block = ref[i].astype(F32)
            acc += block * block
        return jnp.sum(acc, axis=0, keepdims=True)

    total = (
        jnp.sum(squares(ga_ref), axis=1, keepdims=True)
        + jnp.sum(squares(gu_ref), axis=1, keepdims=True)
        + jnp.sum(squares(gd_ref), axis=1, keepdims=True)
    )
    mine[0:gain_rows, :] = gain_ref[...]
    mine[gain_rows:, :] = jnp.broadcast_to(total, (8, 128))
    greet(
        [((dp + k) % n_dp, me) for k in range(1, n_dp)] + [(dp, (me + k) % n) for k in range(1, n)]
    )
    copies = []
    for k in range(1, n):
        copy = remote(mine, buf.at[me], ss.at[k - 1], rs.at[k - 1], (dp, (me + k) % n))
        copy.start()
        copies.append(copy)
    buf[me] = mine[...]
    for k in range(1, n):
        source = (me + n - k) % n
        remote(mine, buf.at[source], ss.at[k - 1], rs.at[k - 1], (dp, source)).wait_recv()
    acc = buf[0]
    for j in range(1, n):
        acc = acc + buf[j]
    part[...] = acc
    all_parts[dp] = acc
    for k in range(1, n_dp):
        copy = remote(part, all_parts.at[dp], st.at[k - 1], rt.at[k - 1], ((dp + k) % n_dp, me))
        copy.start()
        copies.append(copy)
    for k in range(1, n_dp):
        source = (dp + n_dp - k) % n_dp
        remote(part, all_parts.at[source], st.at[k - 1], rt.at[k - 1], (source, me)).wait_recv()
    acc = all_parts[0]
    for j in range(1, n_dp):
        acc = acc + all_parts[j]
    o_ref[...] = acc
    for copy in copies:
        copy.wait_send()


def total_over(ga, gu, gd, gain_part, number):
    n_dp, n = lax.axis_size("dp"), lax.axis_size("ctx")
    gain_rows = gain_part.size // 128
    shape = (gain_rows + 8, 128)
    dma = pltpu.SemaphoreType.DMA
    out = pl.pallas_call(
        functools.partial(total_kernel, n_dp, n),
        out_shape=jax.ShapeDtypeStruct(shape, F32),
        in_specs=[VMEM] * 4,
        out_specs=VMEM,
        scratch_shapes=[
            pltpu.VMEM(shape, F32),
            pltpu.VMEM((n,) + shape, F32),
            pltpu.VMEM(shape, F32),
            pltpu.VMEM((n_dp,) + shape, F32),
            dma((n - 1,)),
            dma((n - 1,)),
            dma((n_dp - 1,)),
            dma((n_dp - 1,)),
        ],
        compiler_params=params_of(number),
        name="total",
    )(ga, gu, gd, gain_part.reshape(gain_rows, 128))
    return out[gain_rows, 0], out[:gain_rows].reshape(gain_part.shape)


def adam_kernel(factor_ref, p_ref, m_ref, v_ref, ga_ref, gu_ref, gd_ref, po_ref, mo_ref, vo_ref, g_ref):
    part = pl.program_id(0)
    n, _, four = ga_ref.shape
    hc = four // 4
    fs = gd_ref.shape[2]

    @pl.when(part == 0)
    def _():
        for matrix in range(4):
            for c in range(n):
                start = (matrix * n + c) * hc
                g_ref[:, start : start + hc] = ga_ref[c, :, matrix * hc : (matrix + 1) * hc].astype(F32)

    @pl.when((part == 1) | (part == 2))
    def _():
        for d in range(gu_ref.shape[0]):
            g_ref[:, d * fs : (d + 1) * fs] = gu_ref[d].astype(F32)

    @pl.when(part == 3)
    def _():
        for d in range(gd_ref.shape[0]):
            g_ref[:, d * fs : (d + 1) * fs] = gd_ref[d].astype(F32)

    clipped = g_ref[...] * factor_ref[0, 0]
    new_p, new_m, new_v = adam_update(p_ref[...], m_ref[...], v_ref[...], clipped, RATE, DECAY)
    po_ref[...] = new_p
    mo_ref[...] = new_m
    vo_ref[...] = new_v


def adam(factor, params, first, second, ga, gu, gd):
    rows, columns = params.shape
    n, n_dp, fs = ga.shape[0], gd.shape[0], gd.shape[2]
    block = min(rows, 16)
    steps = rows // block
    wide = pl.BlockSpec((block, columns // 4), lambda i, r: (r, i))
    return pl.pallas_call(
        adam_kernel,
        grid=(4, steps),
        out_shape=(jax.ShapeDtypeStruct(params.shape, F32),) * 3,
        in_specs=[
            pl.BlockSpec(memory_space=pltpu.SMEM),
            wide,
            wide,
            wide,
            pl.BlockSpec((n, block, ga.shape[2]), lambda i, r: (0, jnp.where(i == 0, r, steps - 1), 0)),
            pl.BlockSpec(
                (n_dp, block, fs),
                lambda i, r: (
                    0,
                    jnp.where(i == 0, 0, jnp.where(i == 3, steps - 1, r)),
                    jnp.clip(i - 1, 0, 1),
                ),
            ),
            pl.BlockSpec((n_dp, block, fs), lambda i, r: (0, jnp.where(i == 3, r, 0), 0)),
        ],
        out_specs=(wide, wide, wide),
        scratch_shapes=[pltpu.VMEM((block, columns // 4), F32)],
        compiler_params=pltpu.CompilerParams(vmem_limit_bytes=48 * 1024 * 1024),
        name="adam",
    )(factor.reshape(1, 1), params, first, second, ga, gu, gd)


def arrange_kernel(n, n_dp, p_ref, a_ref, o_ref, g_ref, d_ref):
    part = pl.program_id(0)
    hc = o_ref.shape[2]
    fs = d_ref.shape[2]

    @pl.when(part == 0)
    def _():
        for matrix in range(4):
            for c in range(n):
                start = (matrix * n + c) * hc
                value = p_ref[:, start : start + hc].astype(BF)
                if matrix < 3:
                    a_ref[c, :, matrix * hc : (matrix + 1) * hc] = value
                else:
                    o_ref[c] = value

    for index, ref, first in ((1, g_ref, 0), (2, g_ref, fs), (3, d_ref, 0)):

        @pl.when(part == index)
        def _():
            for d in range(n_dp):
                ref[d, :, first : first + fs] = p_ref[:, d * fs : (d + 1) * fs].astype(BF)


def arrange(params, width):
    n_dp, n = lax.axis_size("dp"), lax.axis_size("ctx")
    rows, columns = params.shape
    fs, hc = columns // 4 // n_dp, width // n
    whole = lambda shape: pl.BlockSpec(shape, lambda i: (0,) * len(shape))
    shapes = [(n, rows, 3 * hc), (n, rows, hc), (n_dp, rows, 2 * fs), (n_dp, rows, fs)]
    return pl.pallas_call(
        functools.partial(arrange_kernel, n, n_dp),
        grid=(4,),
        out_shape=tuple(jax.ShapeDtypeStruct(s, BF) for s in shapes),
        in_specs=[pl.BlockSpec((rows, columns // 4), lambda i: (0, i))],
        out_specs=tuple(whole(s) for s in shapes),
        compiler_params=pltpu.CompilerParams(vmem_limit_bytes=48 * 1024 * 1024),
        name="arrange",
    )(params)


def row_sums(value, row):
    pick = lax.broadcasted_iota(jnp.int32, (8, value.shape[1]), 0) == row
    return lax.dot_general(
        pick.astype(F32),
        value,
        (((1,), (1,)), ((), ())),
        preferred_element_type=F32,
        precision=lax.Precision.HIGHEST,
    )


def exchange(n, dp, me, buf, ss, rs):
    copies = []
    for k in range(1, n):
        copy = remote(buf.at[me], buf.at[me], ss.at[k - 1], rs.at[k - 1], (dp, (me + k) % n))
        copy.start()
        copies.append(copy)
    for k in range(1, n):
        source = (me + n - k) % n
        remote(buf.at[me], buf.at[source], ss.at[k - 1], rs.at[k - 1], (dp, source)).wait_recv()
    total = buf[0]
    for j in range(1, n):
        total = total + buf[j]
    for copy in copies:
        copy.wait_send()
    return total


def turn(value, cos, sine):
    return value * cos + pltpu.roll(value, HD // 2, 1) * sine


def mask_of(rows, info_col, info_row):
    pos_i, doc_i = info_col[rows, 0:1], info_col[rows, 1:2]
    return (info_row[1:2, :] == doc_i) & (info_row[0:1, :] <= pos_i)


def attend_kernel(
    n_dp, n, x_ref, w_ref, wo_ref, d_ref, gain_ref, cos_ref, sin_ref, col_ref, row_ref,
    y_ref, q_ref, k_ref, v_ref, o_ref, pre_ref, scale_ref, lse_ref, wo_all, d_out,
    buf, pa, qa, pb, qb, ss, rs, s1, r1, s2, r2, sw, rw, sd, rd, local,
):
    dp, me = lax.axis_index("dp"), lax.axis_index("ctx")
    seq, width = x_ref.shape
    hc = o_ref.shape[1]
    block = min(seq, 256)
    greet(
        [((dp + k) % n_dp, me) for k in range(1, n_dp)] + [(dp, (me + k) % n) for k in range(1, n)]
    )
    piece = wo_ref.shape[0]

    def part_of(d):
        return wo_all.at[pl.ds(pl.multiple_of(d * piece, piece), piece), :]

    owns = [
        pltpu.make_async_copy(wo_ref, part_of(dp), local.at[0]),
        pltpu.make_async_copy(d_ref.at[dp], d_out.at[dp], local.at[1]),
    ]
    behind_wo, behind_d = [], []
    for k in range(1, n_dp):
        to = (dp + k) % n_dp
        behind_wo.append(remote(wo_ref, part_of(dp), sw.at[k - 1], rw.at[k - 1], (to, me)))
        behind_d.append(remote(d_ref.at[to], d_out.at[dp], sd.at[k - 1], rd.at[k - 1], (to, me)))
    for copy in behind_wo + behind_d + owns:
        copy.start()

    @pl.loop(0, seq // block)
    def _(i):
        rows = pl.ds(pl.multiple_of(i * block, block), block)
        value = dot(x_ref[rows, :], w_ref[...])
        pre_ref[rows, :] = value[:, : 2 * hc]
        v_ref[rows, :] = value[:, 2 * hc :].astype(BF)
        squares = value[:, : 2 * hc] * value[:, : 2 * hc]
        buf[me, :, rows] = row_sums(squares[:, :hc], 0) + row_sums(squares[:, hc:], 1)

    scale_ref[...] = jnp.transpose(lax.rsqrt(exchange(n, dp, me, buf, ss, rs) / width + EPS))

    @pl.loop(0, seq // block)
    def _(i):
        rows = pl.ds(pl.multiple_of(i * block, block), block)
        cos, sine = cos_ref[rows, :], sin_ref[rows, :]
        for which, ref, factor in ((0, q_ref, HD ** (-0.5)), (1, k_ref, 1.0)):
            scale = scale_ref[rows, which : which + 1]
            for start in range(0, hc, HD):
                part = slice(start, start + HD)
                value = pre_ref[rows, which * hc + start : which * hc + start + HD] * scale
                ref[rows, part] = (
                    turn(value * gain_ref[which : which + 1, part], cos, sine) * factor
                ).astype(BF)

    @pl.loop(0, seq // block)
    def _(i):
        rows = pl.ds(pl.multiple_of(i * block, block), block)
        visible = mask_of(rows, col_ref, row_ref)
        for head in range(hc // HD):
            part = slice(head * HD, (head + 1) * HD)
            scores = jnp.where(visible, dot_t(q_ref[rows, part], k_ref[:, part]), -jnp.inf)
            top = jnp.max(scores, axis=1, keepdims=True)
            weights = jnp.exp(scores - top)
            total = jnp.sum(weights, axis=1, keepdims=True)
            o_ref[rows, part] = (dot(weights.astype(BF), v_ref[:, part]) / total).astype(BF)
            lse_ref[rows, head : head + 1] = top + jnp.log(total)

    owns[0].wait()
    for k in range(1, n_dp):
        source = (dp + n_dp - k) % n_dp
        remote(wo_ref, part_of(source), sw.at[k - 1], rw.at[k - 1], (source, me)).wait_recv()
    cols = slice(0, hc)
    sums = reduce_ctx(n, dp, me, o_ref, wo_all, cols, y_ref, pa, qa, pb, qb, s1, r1, s2, r2)
    for k in range(1, n_dp):
        source = (dp + n_dp - k) % n_dp
        remote(d_ref.at[dp], d_out.at[source], sd.at[k - 1], rd.at[k - 1], (source, me)).wait_recv()
    for copy in sums + behind_wo + behind_d:
        copy.wait_send()
    owns[1].wait()


def attend(x_all, w, wo, d, gain, cos, sine, info_col, info_row, number):
    n_dp, n = lax.axis_size("dp"), lax.axis_size("ctx")
    seq, width = x_all.shape
    half, length, hc = n // 2, seq // n, w.shape[1] // 3
    dma = pltpu.SemaphoreType.DMA
    low = jax.ShapeDtypeStruct((seq, hc), BF)
    return pl.pallas_call(
        functools.partial(attend_kernel, n_dp, n),
        out_shape=(
            jax.ShapeDtypeStruct((length, width), F32),
            low,
            low,
            low,
            low,
            jax.ShapeDtypeStruct((seq, 2 * hc), F32),
            jax.ShapeDtypeStruct((seq, 8), F32),
            jax.ShapeDtypeStruct((seq, 8), F32),
            jax.ShapeDtypeStruct((width, hc), BF),
            jax.ShapeDtypeStruct(d.shape, BF),
        ),
        in_specs=[VMEM] * 2 + [ANY] * 2 + [VMEM] * 5,
        out_specs=(VMEM,) * 9 + (ANY,),
        scratch_shapes=[
            pltpu.VMEM((n, 8, seq), F32),
            pltpu.VMEM((half, length, width), BF),
            pltpu.VMEM((half, length, width), BF),
            pltpu.VMEM((half - 1, length, width), BF),
            pltpu.VMEM((half - 1, length, width), BF),
            dma((n - 1,)),
            dma((n - 1,)),
            dma((half,)),
            dma((half,)),
            dma((half - 1,)),
            dma((half - 1,)),
            dma((n_dp - 1,)),
            dma((n_dp - 1,)),
            dma((n_dp - 1,)),
            dma((n_dp - 1,)),
            dma((2,)),
        ],
        compiler_params=params_of(number),
        name="attend",
    )(x_all, w, wo, d, gain, cos, sine, info_col, info_row)


def attend_back_kernel(
    n, e_ref, w_ref, gain_ref, cos_ref, sin_ref, col_ref, row_ref,
    q_ref, k_ref, v_ref, pre_ref, scale_ref, lse_ref,
    all_ref, d_ref, gain_out,
    do_ref, dq_ref, dk_ref, dv_ref, mean_ref, buf, ss, rs, s1, r1, s2, r2,
):
    dp, me = lax.axis_index("dp"), lax.axis_index("ctx")
    half, parity, pair, partner, ahead, behind = pairs_of(n, me)
    seq, hc = q_ref.shape
    length, width = e_ref.shape
    block = min(seq, 256)
    greet([(dp, (me + k) % n) for k in range(1, n)])
    sends = [
        remote(e_ref, all_ref.at[me], s1.at[k], r1.at[k], (dp, a))
        for k, a in enumerate(ahead + [partner])
    ]
    for copy in sends:
        copy.start()
    all_ref[me] = e_ref[...]
    dk_ref[...] = jnp.zeros_like(dk_ref)
    dv_ref[...] = jnp.zeros_like(dv_ref)

    def project(b):
        rows = pl.ds(pl.multiple_of(b * length, length), length)
        do_ref[rows, :] = dot(all_ref[b], w_ref[...]).astype(BF)

    project(me)
    sends[-1].wait_recv()
    project(partner)
    forwards = []
    for k, b in enumerate(behind):
        remote(e_ref, all_ref.at[b], s1.at[k], r1.at[k], (dp, b)).wait_recv()
        forward = remote(all_ref.at[b], all_ref.at[b], s2.at[k], r2.at[k], (dp, partner))
        forward.start()
        forwards.append(forward)
        project(b)
    for k, b in enumerate(behind):
        forwards[k].wait_recv()
        project(b + 1 - 2 * parity)

    @pl.loop(0, seq // block)
    def _(i):
        rows = pl.ds(pl.multiple_of(i * block, block), block)
        visible = mask_of(rows, col_ref, row_ref)
        for head in range(hc // HD):
            part = slice(head * HD, (head + 1) * HD)
            query, key, value, back = q_ref[rows, part], k_ref[:, part], v_ref[:, part], do_ref[rows, part]
            scores = jnp.where(visible, dot_t(query, key), -jnp.inf)
            probs = jnp.exp(scores - lse_ref[rows, head : head + 1])
            d_probs = dot_t(back, value)
            delta = jnp.sum(probs * d_probs, axis=1, keepdims=True)
            d_scores = (probs * (d_probs - delta)).astype(BF)
            dq_ref[rows, part] = dot(d_scores, key)
            dk_ref[:, part] += t_dot(d_scores, query)
            dv_ref[:, part] += t_dot(probs.astype(BF), back)

    gain_out[...] = jnp.zeros_like(gain_out)

    @pl.loop(0, seq // block)
    def _(i):
        rows = pl.ds(pl.multiple_of(i * block, block), block)
        cos, sine = cos_ref[rows, :], sin_ref[rows, :]
        sums = jnp.zeros((8, block), F32)
        for which, ref, factor in ((0, dq_ref, HD ** (-0.5)), (1, dk_ref, 1.0)):
            scale = scale_ref[rows, which : which + 1]
            for start in range(0, hc, HD):
                part = slice(start, start + HD)
                pre = pre_ref[rows, which * hc + start : which * hc + start + HD]
                value = turn(ref[rows, part] * factor, cos, -sine)
                gain_out[which : which + 1, part] += jnp.sum(value * pre * scale, axis=0, keepdims=True)
                value = value * gain_ref[which : which + 1, part]
                ref[rows, part] = value
                sums += row_sums(value * pre, which)
        buf[me, :, rows] = sums

    mean_ref[...] = jnp.transpose(exchange(n, dp, me, buf, ss, rs) / width)

    @pl.loop(0, seq // block)
    def _(i):
        rows = pl.ds(pl.multiple_of(i * block, block), block)
        for which, ref in ((0, dq_ref), (1, dk_ref)):
            scale = scale_ref[rows, which : which + 1]
            mean = mean_ref[rows, which : which + 1]
            cols = slice(which * hc, (which + 1) * hc)
            value = scale * (ref[rows, :] - pre_ref[rows, cols] * (scale * scale * mean))
            d_ref[rows, cols] = value.astype(BF)
        d_ref[rows, 2 * hc :] = dv_ref[rows, :].astype(BF)

    for copy in sends + forwards:
        copy.wait_send()


def attend_back(e, w, gain, cos, sine, info_col, info_row, q, k, v, pre, scale, lse, number):
    n = lax.axis_size("ctx")
    seq, hc = q.shape
    half, (length, width) = n // 2, e.shape
    dma = pltpu.SemaphoreType.DMA
    all_e, d_qkv, d_gain = pl.pallas_call(
        functools.partial(attend_back_kernel, n),
        out_shape=(
            jax.ShapeDtypeStruct((n, length, width), BF),
            jax.ShapeDtypeStruct((seq, 3 * hc), BF),
            jax.ShapeDtypeStruct((2, hc), F32),
        ),
        in_specs=[VMEM] * 13,
        out_specs=(VMEM,) * 3,
        scratch_shapes=[
            pltpu.VMEM((seq, hc), BF),
            pltpu.VMEM((seq, hc), F32),
            pltpu.VMEM((seq, hc), F32),
            pltpu.VMEM((seq, hc), F32),
            pltpu.VMEM((seq, 8), F32),
            pltpu.VMEM((n, 8, seq), F32),
            dma((n - 1,)),
            dma((n - 1,)),
            dma((half,)),
            dma((half,)),
            dma((half - 1,)),
            dma((half - 1,)),
        ],
        compiler_params=params_of(number),
        name="attend_back",
    )(e, w, gain, cos, sine, info_col, info_row, q, k, v, pre, scale, lse)
    return all_e.reshape(seq, width), d_qkv, d_gain


def shards(
    inputs,
    cotangent,
    documents,
    block_place,
    params,
    first_moment,
    second_moment,
    gains,
    gains_first,
    gains_second,
):
    tokens = inputs[0]
    upstream = cotangent[0].astype(F32)
    length, width = tokens.shape
    n_ctx = lax.axis_size("ctx")
    n_dp = lax.axis_size("dp")
    me_ctx = lax.axis_index("ctx")
    seq = length * n_ctx
    rows = params.shape[0]
    ff = (params.shape[1] - 4 * width) // 3
    hc = width // n_ctx
    heads = hc // HD
    fs = ff // n_dp

    def mix(values):
        t = values.shape[0]
        return (
            values.reshape(t, n_dp, n_ctx, rows).transpose(0, 2, 1, 3).reshape(t, width)
        )

    def unmix(values):
        t = values.shape[0]
        return (
            values.reshape(t, n_ctx, n_dp, rows).transpose(0, 2, 1, 3).reshape(t, width)
        )

    w_qkv, w_o, w_gu, w_d = arrange(params, width)
    w_gu, w_qkv, w_o, x_all = start(w_gu, w_qkv, w_o, tokens, 1)
    w_gu = lax.all_gather(w_gu.reshape(n_dp * rows, 2 * fs), "ctx", axis=0, tiled=True)
    w_qkv = gather_dp(w_qkv.reshape(n_ctx * rows, 3 * hc), 2)

    indices = jnp.arange(seq, dtype=jnp.int32)
    owners = indices // length
    placed = jnp.sum(
        jnp.where(
            owners[:, None] == jnp.arange(n_ctx, dtype=jnp.int32)[None, :], block_place[None, :], 0
        ),
        axis=1,
    )
    pos = placed * length + indices % length
    docs = documents[0]
    info_row = jnp.concatenate([pos[None], docs[None], jnp.zeros((6, seq), jnp.int32)])
    info_col = info_row.T
    cos_tab, sine_tab = rope_tables(pos, HD)
    cos_tab = jnp.concatenate([cos_tab, cos_tab], axis=1)
    sine_tab = jnp.concatenate([-sine_tab, sine_tab], axis=1)
    my_gains = lax.dynamic_slice_in_dim(gains[:2], me_ctx * hc, hc, axis=1)
    tables = (my_gains, cos_tab, sine_tab, info_col, info_row)

    branch, queries, keys, values, attn_low, qk_pre, scales, lse, w_o, w_d = attend(
        x_all, w_qkv, w_o.reshape(n_ctx * rows, hc), w_d, *tables, 3
    )
    w_d = lax.all_gather(w_d.reshape(n_dp * rows, fs), "ctx", axis=0, tiled=True)
    a_scale = rms_scale(branch)
    hidden1 = tokens.astype(F32) + branch * a_scale * gains[2]

    h1_all = gather_dp(mix(hidden1.astype(BF)), 4)
    gate_up = dot(h1_all, w_gu)
    gate_pre, up_pre = gate_up[:, :fs], gate_up[:, fs:]
    gate_sig = jax.nn.sigmoid(gate_pre)
    silu_val = gate_pre * gate_sig
    inner = (silu_val * up_pre).astype(BF)
    mlp_out = unmix(scatter_dp((inner, w_d), 5))
    m_scale = rms_scale(mlp_out)
    result = hidden1 + mlp_out * m_scale * gains[3]

    g_ff_part = jnp.sum(upstream * mlp_out * m_scale, axis=0)
    d_mlp = norm_back(upstream * gains[3], mlp_out, m_scale).astype(BF)
    d_mlp_all = gather_dp(mix(d_mlp), 6)
    d_grad = lax.psum_scatter(
        t_dot(d_mlp_all, inner).astype(BF), "ctx", scatter_dimension=0, tiled=True
    )
    d_inner = dot(d_mlp_all, w_d)
    d_gate = (d_inner * up_pre * gate_sig * (1.0 + gate_pre * (1.0 - gate_sig))).astype(BF)
    d_upper = (d_inner * silu_val).astype(BF)
    d_gu = jnp.concatenate([d_gate, d_upper], axis=1)
    gu_grad = lax.psum_scatter(
        t_dot(h1_all, d_gu).astype(BF), "ctx", scatter_dimension=0, tiled=True
    ).reshape(n_dp, rows, 2 * fs)
    d_h1 = upstream + unmix(scatter_dp((d_gu, w_gu), 7))

    g_attn_part = jnp.sum(d_h1 * branch * a_scale, axis=0)
    d_branch = norm_back(d_h1 * gains[2], branch, a_scale).astype(BF)
    d_grad, d_branch = lax.optimization_barrier((d_grad, d_branch))
    d_branch_all, d_qkv, d_gain = attend_back(
        d_branch, w_o, *tables, queries, keys, values, qk_pre, scales, lse, 8
    )
    attn_grad = jnp.concatenate([t_dot(x_all, d_qkv), t_dot(d_branch_all, attn_low)], axis=1)
    d_grad = lax.all_to_all(d_grad, "dp", 0, 0, tiled=True).reshape(n_dp, rows, fs)
    attn_grad, gu_grad, d_x = collect(attn_grad.astype(BF), gu_grad, d_qkv, w_qkv, 9)
    d_input = d_h1 + d_x

    gain_part = jnp.stack(
        [
            *lax.dynamic_update_slice(jnp.zeros((2, width), F32), d_gain, (0, me_ctx * hc)),
            g_attn_part,
            g_ff_part,
        ],
        axis=0,
    )
    square_total, gain_total = total_over(attn_grad, gu_grad, d_grad, gain_part, 11)
    grad_norm = jnp.sqrt(square_total + jnp.sum(gain_total * gain_total))
    factor = CLIP / (grad_norm + 1e-06)
    new_params, new_first, new_second = adam(
        factor, params, first_moment, second_moment, attn_grad, gu_grad, d_grad
    )
    new_gains, new_gains_first, new_gains_second = adam_update(
        gains, gains_first, gains_second, gain_total * factor, GAIN_RATE, 0.0
    )
    return (
        result.astype(BF)[None],
        d_input.astype(BF)[None],
        grad_norm,
        new_params,
        new_first,
        new_second,
        new_gains,
        new_gains_first,
        new_gains_second,
    )


def solution(mesh):
    split, whole = P("dp", "ctx", None), P(("dp", "ctx"), None)
    return jax.shard_map(
        shards,
        mesh=mesh,
        in_specs=(split, split, P("dp", None), P(), whole, whole, whole, P(), P(), P()),
        out_specs=(split, split, P(), whole, whole, whole, P(), P(), P()),
        check_vma=False,
    )
```

```python
import functools

import jax
import jax.numpy as jnp
from jax import lax
from jax.experimental import pallas as pl
from jax.experimental.pallas import tpu as pltpu
from jax.sharding import PartitionSpec as P

HD = 128
STEP = 10
EPS = 1e-06
THETA = 500000.0
CLIP = 1.0
BETA1 = 0.9
BETA2 = 0.95
RATE = 0.03
GAIN_RATE = 0.8
DECAY = 0.1
ADAM_EPS = 1e-08
BF = jnp.bfloat16
F32 = jnp.float32
MESH = pl.DeviceIdType.MESH
ANY = pl.BlockSpec(memory_space=pl.ANY)
VMEM = pl.BlockSpec(memory_space=pltpu.VMEM)


def rms_scale(values):
    return lax.rsqrt(jnp.mean(values * values, axis=-1, keepdims=True) + EPS)


def norm_back(upstream, source, scale):
    return scale * (
        upstream - source * scale * scale * jnp.mean(upstream * source, axis=-1, keepdims=True)
    )


def rope_tables(positions, head_size):
    half_size = head_size // 2
    freqs = THETA ** (-jnp.arange(half_size, dtype=jnp.float32) * 2.0 / head_size)
    angles = positions.astype(jnp.float32)[:, None] * freqs[None, :]
    return (jnp.cos(angles), jnp.sin(angles))


def adam_update(weight, first_in, second_in, clipped, rate, decay):
    new_first = BETA1 * first_in + (1.0 - BETA1) * clipped
    new_second = BETA2 * second_in + (1.0 - BETA2) * clipped * clipped
    first_hat = new_first / (1.0 - BETA1**STEP)
    second_hat = new_second / (1.0 - BETA2**STEP)
    new_weight = weight - rate * (first_hat / (jnp.sqrt(second_hat) + ADAM_EPS) + decay * weight)
    return (new_weight, new_first, new_second)


def dot(a, b):
    return jnp.dot(a, b, preferred_element_type=F32)


def dot_t(a, b):
    return lax.dot_general(a, b, (((1,), (1,)), ((), ())), preferred_element_type=F32)


def t_dot(a, b):
    return lax.dot_general(a, b, (((0,), (0,)), ((), ())), preferred_element_type=F32)


def greet(peers):
    barrier = pltpu.get_barrier_semaphore()
    for peer in peers:
        pl.semaphore_signal(barrier, inc=1, device_id=peer, device_id_type=MESH)
    pl.semaphore_wait(barrier, len(peers))


def remote(src, dst, send, recv, peer):
    return pltpu.make_async_remote_copy(
        src_ref=src, dst_ref=dst, send_sem=send, recv_sem=recv, device_id=peer, device_id_type=MESH
    )


def params_of(number, vmem=48):
    return pltpu.CompilerParams(
        collective_id=number, has_side_effects=True, vmem_limit_bytes=vmem * 1024 * 1024
    )


def line_steps(n, me, make_right, make_left):
    for s in range(n - 1):

        @pl.when((me < n - 1) & (me >= s))
        def _():
            make_right(s).start()

        @pl.when((me > 0) & (me + s < n))
        def _():
            make_left(s).start()

        @pl.when(me - 1 - s >= 0)
        def _():
            make_right(s, me - 1 - s).wait_recv()

        @pl.when(me + 1 + s < n)
        def _():
            make_left(s, me + 1 + s).wait_recv()

    for s in range(n - 1):

        @pl.when((me < n - 1) & (me >= s))
        def _():
            make_right(s).wait_send()

        @pl.when((me > 0) & (me + s < n))
        def _():
            make_left(s).wait_send()


def pairs_of(n, me):
    half = n // 2
    parity, pair = me % 2, me // 2
    partner = me + 1 - 2 * parity
    ahead = [2 * ((pair + k) % half) + parity for k in range(1, half)]
    behind = [2 * ((pair + half - k) % half) + parity for k in range(1, half)]
    return half, parity, pair, partner, ahead, behind


def gather_dp_kernel(n, x_ref, o_ref, local, sr, rr, sl, rl):
    me, ctx = lax.axis_index("dp"), lax.axis_index("ctx")

    def here(d):
        return (d, ctx)

    greet([here((me + 1) % n), here((me + n - 1) % n)])
    own = pltpu.make_async_copy(x_ref, o_ref.at[me], local)
    own.start()

    def right(s, block=None):
        b = me - s if block is None else block
        return remote(x_ref if s == 0 else o_ref.at[b], o_ref.at[b], sr.at[s], rr.at[s], here(me + 1))

    def left(s, block=None):
        b = me + s if block is None else block
        return remote(x_ref if s == 0 else o_ref.at[b], o_ref.at[b], sl.at[s], rl.at[s], here(me - 1))

    line_steps(n, me, right, left)
    own.wait()


def gather_dp(x, number):
    n = lax.axis_size("dp")
    out = pl.pallas_call(
        functools.partial(gather_dp_kernel, n),
        out_shape=jax.ShapeDtypeStruct((n,) + x.shape, x.dtype),
        in_specs=[ANY],
        out_specs=ANY,
        scratch_shapes=[pltpu.SemaphoreType.DMA] + [pltpu.SemaphoreType.DMA((n - 1,))] * 4,
        compiler_params=params_of(number),
        name="gather_dp",
    )(x)
    return out.reshape((n * x.shape[0],) + x.shape[1:])


def group_of(n_dp, n, dp, me):
    pair, parity = me // 2, me % 2
    return 2 * n_dp, 2 * dp + parity, lambda j: (j // 2, 2 * pair + j % 2)


def greet_all(n_dp, n, dp, me):
    partner = me + 1 - 2 * (me % 2)
    others = [(dp + k) % n_dp for k in range(1, n_dp)]
    greet([(dp, (me + k) % n) for k in range(1, n)] + [(d, c) for d in others for c in (me, partner)])


def swap(src, dst, send, recv, count, mine, place):
    sends, receives = [], []
    for k in range(1, count):
        to, source = (mine + k) % count, (mine + count - k) % count
        sends.append(remote(src.at[to], dst.at[mine], send.at[k - 1], recv.at[k - 1], place(to)))
        receives.append(
            remote(src.at[mine], dst.at[source], send.at[k - 1], recv.at[k - 1], place(source))
        )
    for copy in sends:
        copy.start()
    return sends, receives


def tiles(total, tile, body):
    tile = min(total, tile)

    @pl.loop(0, total // tile)
    def _(j):
        body(pl.ds(pl.multiple_of(j * tile, tile), tile))


def reduce_ctx(n, dp, me, a_ref, w_ref, cols, o_ref, sa, ra, sb, rb, s1, r1, s2, r2):
    half, parity, pair, partner, ahead, behind = pairs_of(n, me)
    length, width = o_ref.shape

    def rows(block):
        return pl.ds(pl.multiple_of(block * length, length), length)

    first, second = [], []
    for k in range(half):
        target = (pair + k + 1) % half

        def give(part):
            value = dot_t(a_ref[rows(2 * target + 1 - parity), :], w_ref[part, cols])
            sa[k, :, part] = value.astype(BF)

        tiles(width, 512, give)
        copy = remote(sa.at[k], ra.at[k], s1.at[k], r1.at[k], (dp, partner))
        copy.start()
        first.append(copy)
        copy.wait_recv()

        def keep(part):
            value = dot_t(a_ref[rows(2 * target + parity), :], w_ref[part, cols])
            value = value + ra[k, :, part].astype(F32)
            if k < half - 1:
                sb[k, :, part] = value.astype(BF)
            else:
                o_ref[:, part] = value

        tiles(width, 512, keep)
        if k < half - 1:
            copy = remote(sb.at[k], rb.at[k], s2.at[k], r2.at[k], (dp, 2 * target + parity))
            copy.start()
            second.append(copy)
    for k in range(half - 1):
        second[k].wait_recv()
        o_ref[...] += rb[k].astype(F32)
    return first + second


def load_rows(hbm, vmem, sems):
    half, n_dp, rows, _ = hbm.shape
    copies = []
    for d in range(n_dp):
        for p in range(half):
            part = pl.ds((d * half + p) * rows, rows)
            copies.append(pltpu.make_async_copy(hbm.at[p, d], vmem.at[part, :], sems.at[d * half + p]))
    for copy in copies:
        copy.start()
    return copies


def gather_group(n, dp, me, all_ref, length, sr, rr, sl, rl, sf, rf, process):
    parity = me % 2
    partner = me + 1 - 2 * parity

    def block(b, side):
        start = (2 * b + side) * length
        return all_ref.at[pl.ds(pl.multiple_of(start, length), length), :]

    def right(s, b):
        return remote(block(b, parity), block(b, parity), sr.at[s], rr.at[s], (dp + 1, me))

    def left(s, b):
        return remote(block(b, parity), block(b, parity), sl.at[s], rl.at[s], (dp - 1, me))

    def aside(b):
        return remote(block(b, parity), block(b, parity), sf.at[b], rf.at[b], (dp, partner))

    def from_aside(b):
        return remote(block(b, 1 - parity), block(b, 1 - parity), sf.at[b], rf.at[b], (dp, partner))

    for s in range(n):
        if s == 0:
            aside(dp).start()
        else:

            @pl.when(dp >= s)
            def _():
                right(s - 1, dp - s).wait_recv()

            @pl.when(dp + s < n)
            def _():
                left(s - 1, dp + s).wait_recv()

        @pl.when((dp < n - 1) & (dp >= s))
        def _():
            right(s, dp - s).start()

        @pl.when((dp > 0) & (dp + s < n))
        def _():
            left(s, dp + s).start()

        if s == 0:
            from_aside(dp).wait_recv()
            process(dp, True)
        else:

            @pl.when(dp >= s)
            def _():
                aside(dp - s).start()

            @pl.when(dp + s < n)
            def _():
                aside(dp + s).start()

            below = jnp.where(dp >= s, 1, 0)
            above = jnp.where(dp + s < n, 1, 0)

            @pl.loop(0, below + above)
            def _(j):
                b = jnp.where(j < below, dp - s, dp + s)
                from_aside(b).wait_recv()
                process(b, False)

    for s in range(n):

        @pl.when((dp < n - 1) & (dp >= s))
        def _():
            right(s, dp - s).wait_send()

        @pl.when((dp > 0) & (dp + s < n))
        def _():
            left(s, dp + s).wait_send()

        aside(s).wait_send()


def gather_sems(n_dp):
    return [pltpu.SemaphoreType.DMA((n_dp,))] * 6


def give_block(dp, me, b, own, a_ref, w_ref, o_ref, sa, ra, sb, rb, s1, r1, s2, r2):
    length, width = o_ref.shape
    parity = me % 2
    partner = me + 1 - 2 * parity

    def rows(side):
        return pl.ds(pl.multiple_of((2 * b + side) * length, length), length)

    def give(part):
        sa[b, :, part] = dot_t(a_ref[rows(1 - parity), :], w_ref[part, :]).astype(BF)

    tiles(width, 512, give)
    copy = remote(sa.at[b], ra.at[b], s1.at[b], r1.at[b], (dp, partner))
    copy.start()
    copy.wait_recv()

    def keep(part):
        value = dot_t(a_ref[rows(parity), :], w_ref[part, :]) + ra[b, :, part].astype(F32)
        if own:
            o_ref[:, part] = value
        else:
            sb[b, :, part] = value.astype(BF)

    tiles(width, 512, keep)
    if not own:
        remote(sb.at[b], rb.at[dp], s2.at[b], r2.at[dp], (b, me)).start()


def give_end(n, dp, me, o_ref, sa, ra, sb, rb, s1, r1, s2, r2):
    partner = me + 1 - 2 * (me % 2)
    for k in range(1, n):
        b = (dp + k) % n
        remote(sb.at[b], rb.at[b], s2.at[b], r2.at[b], (b, me)).wait_recv()
        o_ref[...] += rb[b].astype(F32)
    for k in range(1, n):
        b = (dp + k) % n
        remote(sb.at[b], rb.at[b], s2.at[b], r2.at[b], (b, me)).wait_send()
    for b in range(n):
        remote(sa.at[b], ra.at[b], s1.at[b], r1.at[b], (dp, partner)).wait_send()


def give_scratch(n_dp, length, width):
    return [pltpu.VMEM((n_dp, length, width), BF)] * 4 + [pltpu.SemaphoreType.DMA((n_dp,))] * 4


def greet_group(n_dp, dp, me):
    partner = me + 1 - 2 * (me % 2)
    greet([(dp, partner)] + [((dp + k) % n_dp, me) for k in range(1, n_dp)])


def ff_forward_kernel(
    n_dp, h_ref, up_ref, gain_ref, gu_hbm, d_hbm,
    res_ref, dm_ref, gp_ref, all_ref, pre_ref, hid_ref,
    gu_ref, d_ref, acc, sem_gu, sem_d, *rest,
):
    gather, give = rest[:6], rest[6:]
    dp, me = lax.axis_index("dp"), lax.axis_index("ctx")
    length, width = h_ref.shape
    fh = hid_ref.shape[1]
    loads_gu, loads_d = load_rows(gu_hbm, gu_ref, sem_gu), load_rows(d_hbm, d_ref, sem_d)
    mine = pl.ds(pl.multiple_of((2 * dp + me % 2) * length, length), length)
    all_ref[mine, :] = h_ref[...].astype(BF)
    greet_group(n_dp, dp, me)

    def process(b, own):
        rows = pl.ds(pl.multiple_of(2 * b * length, 2 * length), 2 * length)
        if own:
            for copy in loads_gu:
                copy.wait()

        def hidden(part):
            second = pl.ds(pl.multiple_of(fh + part.start, part.size), part.size)
            gate = dot(all_ref[rows, :], gu_ref[:, part])
            upper = dot(all_ref[rows, :], gu_ref[:, second])
            pre_ref[rows, part] = gate
            pre_ref[rows, second] = upper
            hid_ref[rows, part] = (gate * jax.nn.sigmoid(gate) * upper).astype(BF)

        tiles(fh, 256, hidden)
        if own:
            for copy in loads_d:
                copy.wait()
        give_block(dp, me, b, own, hid_ref, d_ref, acc, *give)

    gather_group(n_dp, dp, me, all_ref, length, *gather, process)
    give_end(n_dp, dp, me, acc, *give)
    gp_ref[...] = jnp.zeros_like(gp_ref)

    def finish(rows):
        out, up, gain = acc[rows, :], up_ref[rows, :].astype(F32), gain_ref[...]
        scale = rms_scale(out)
        res_ref[rows, :] = (h_ref[rows, :] + out * scale * gain).astype(BF)
        gp_ref[...] += jnp.sum(up * out * scale, axis=0, keepdims=True)
        dm_ref[rows, :] = norm_back(up * gain, out, scale).astype(BF)

    tiles(length, 16, finish)


def ff_forward(h1, up, gain, w_gu, w_d, number):
    n_dp = lax.axis_size("dp")
    (length, width), fh = h1.shape, w_d.shape[3]
    tokens = 2 * n_dp * length
    blocks = w_d.shape[0] * n_dp
    low = jax.ShapeDtypeStruct((length, width), BF)
    return pl.pallas_call(
        functools.partial(ff_forward_kernel, n_dp),
        out_shape=(
            low,
            low,
            jax.ShapeDtypeStruct((1, width), F32),
            jax.ShapeDtypeStruct((tokens, width), BF),
            jax.ShapeDtypeStruct((tokens, 2 * fh), F32),
            jax.ShapeDtypeStruct((tokens, fh), BF),
        ),
        in_specs=[VMEM] * 3 + [ANY] * 2,
        out_specs=(VMEM,) * 6,
        scratch_shapes=[
            pltpu.VMEM((width, 2 * fh), BF),
            pltpu.VMEM((width, fh), BF),
            pltpu.VMEM((length, width), F32),
            pltpu.SemaphoreType.DMA((blocks,)),
            pltpu.SemaphoreType.DMA((blocks,)),
        ]
        + gather_sems(n_dp)
        + give_scratch(n_dp, length, width),
        compiler_params=params_of(number, 58),
        name="ff_forward",
    )(h1, up, gain, w_gu, w_d)


def ff_back_kernel(n_dp, dm_ref, d_hbm, pre_hbm, all_ref, dgu_ref, d_ref, pre_ref, sem_d, sem_p, *gather):
    dp, me = lax.axis_index("dp"), lax.axis_index("ctx")
    length, width = dm_ref.shape
    fh = d_ref.shape[1]
    loads = load_rows(d_hbm, d_ref, sem_d)

    def rows_of(b):
        return pl.ds(pl.multiple_of(2 * b * length, 2 * length), 2 * length)

    def load_pre(b):
        return pltpu.make_async_copy(pre_hbm.at[rows_of(b), :], pre_ref.at[rows_of(b), :], sem_p.at[b])

    for k in range(n_dp):
        load_pre((dp + k) % n_dp).start()
    mine = pl.ds(pl.multiple_of((2 * dp + me % 2) * length, length), length)
    all_ref[mine, :] = dm_ref[...]
    greet_group(n_dp, dp, me)

    def process(b, own):
        rows = rows_of(b)
        if own:
            for copy in loads:
                copy.wait()
        load_pre(b).wait()

        def hidden(part):
            second = pl.ds(pl.multiple_of(fh + part.start, part.size), part.size)
            back = dot(all_ref[rows, :], d_ref[:, part])
            gate, upper = pre_ref[rows, part], pre_ref[rows, second]
            sig = jax.nn.sigmoid(gate)
            dgu_ref[rows, part] = (back * upper * sig * (1.0 + gate * (1.0 - sig))).astype(BF)
            dgu_ref[rows, second] = (back * gate * sig).astype(BF)

        tiles(fh, 256, hidden)

    gather_group(n_dp, dp, me, all_ref, length, *gather, process)


def ff_back(dm, w_d, pre, number):
    n_dp = lax.axis_size("dp")
    (length, width), fh = dm.shape, w_d.shape[3]
    tokens = 2 * n_dp * length
    return pl.pallas_call(
        functools.partial(ff_back_kernel, n_dp),
        out_shape=(
            jax.ShapeDtypeStruct((tokens, width), BF),
            jax.ShapeDtypeStruct((tokens, 2 * fh), BF),
        ),
        in_specs=[VMEM, ANY, ANY],
        out_specs=(VMEM,) * 2,
        scratch_shapes=[
            pltpu.VMEM((width, fh), BF),
            pltpu.VMEM((tokens, 2 * fh), F32),
            pltpu.SemaphoreType.DMA((w_d.shape[0] * n_dp,)),
            pltpu.SemaphoreType.DMA((n_dp,)),
        ]
        + gather_sems(n_dp),
        compiler_params=params_of(number, 58),
        name="ff_back",
    )(dm, w_d, pre)


def ff_scatter_kernel(
    n_dp, dgu_ref, gu_hbm, up_ref, branch_ref, gain_ref, dh_ref, db_ref, gp_ref, gu_ref, sem_gu, *give
):
    dp, me = lax.axis_index("dp"), lax.axis_index("ctx")
    length, width = dh_ref.shape
    loads = load_rows(gu_hbm, gu_ref, sem_gu)
    greet_group(n_dp, dp, me)
    for copy in loads:
        copy.wait()

    @pl.loop(1, n_dp)
    def _(k):
        give_block(dp, me, (dp + k) % n_dp, False, dgu_ref, gu_ref, dh_ref, *give)

    give_block(dp, me, dp, True, dgu_ref, gu_ref, dh_ref, *give)
    give_end(n_dp, dp, me, dh_ref, *give)
    gp_ref[...] = jnp.zeros_like(gp_ref)

    def finish(rows):
        grad, branch = dh_ref[rows, :] + up_ref[rows, :].astype(F32), branch_ref[rows, :]
        scale = rms_scale(branch)
        dh_ref[rows, :] = grad
        gp_ref[...] += jnp.sum(grad * branch * scale, axis=0, keepdims=True)
        db_ref[rows, :] = norm_back(grad * gain_ref[...], branch, scale).astype(BF)

    tiles(length, 16, finish)


def ff_scatter(dgu, w_gu, up, branch, gain, number):
    n_dp = lax.axis_size("dp")
    length, width = up.shape
    return pl.pallas_call(
        functools.partial(ff_scatter_kernel, n_dp),
        out_shape=(
            jax.ShapeDtypeStruct((length, width), F32),
            jax.ShapeDtypeStruct((length, width), BF),
            jax.ShapeDtypeStruct((1, width), F32),
        ),
        in_specs=[VMEM, ANY] + [VMEM] * 3,
        out_specs=(VMEM,) * 3,
        scratch_shapes=[
            pltpu.VMEM((width, w_gu.shape[3]), BF),
            pltpu.SemaphoreType.DMA((w_gu.shape[0] * n_dp,)),
        ]
        + give_scratch(n_dp, length, width),
        compiler_params=params_of(number, 56),
        name="ff_scatter",
    )(dgu, w_gu, up, branch, gain)


def ff_grad_kernel(x_ref, d_ref, o_ref):
    value = t_dot(x_ref[...], d_ref[...]).astype(BF)
    rows = o_ref.shape[2]
    for s in range(o_ref.shape[0]):
        o_ref[s, 0] = value[s * rows : (s + 1) * rows]


def ff_grad(x, d, rows):
    n_dp, half = lax.axis_size("dp"), lax.axis_size("ctx") // 2
    (tokens, width), columns = x.shape, d.shape[1]
    block = 256
    many = block // (2 * rows)
    return pl.pallas_call(
        ff_grad_kernel,
        grid=(width // block,),
        out_shape=jax.ShapeDtypeStruct((half, n_dp, 2 * rows, columns), BF),
        in_specs=[
            pl.BlockSpec((tokens, block), lambda i: (0, i)),
            pl.BlockSpec((tokens, columns), lambda i: (0, 0)),
        ],
        out_specs=pl.BlockSpec(
            (many, 1, 2 * rows, columns), lambda i: (i % (half // many), i // (half // many), 0, 0)
        ),
        compiler_params=pltpu.CompilerParams(vmem_limit_bytes=48 * 1024 * 1024),
        cost_estimate=pl.CostEstimate(
            flops=2 * tokens * width * columns,
            bytes_accessed=2 * (tokens * width + tokens * columns + width * columns),
            transcendentals=0,
        ),
        name="ff_grad",
    )(x, d)


def start_kernel(
    n_dp, n, g_ref, w_ref, v_ref, x_ref, h_ref, o_ref, p_ref, y_ref,
    local, sg, rg, sa, ra, sv, rv, ss, rs, fs, fr,
):
    dp, me = lax.axis_index("dp"), lax.axis_index("ctx")
    half, parity, pair, partner, ahead, behind = pairs_of(n, me)
    count, mine, place = group_of(n_dp, n, dp, me)
    greet_all(n_dp, n, dp, me)
    owns = [
        pltpu.make_async_copy(g_ref.at[mine], h_ref.at[mine], local.at[0]),
        pltpu.make_async_copy(w_ref.at[me], o_ref.at[me], local.at[1]),
        pltpu.make_async_copy(x_ref, y_ref.at[me], local.at[2]),
        pltpu.make_async_copy(v_ref.at[me], p_ref.at[me], local.at[3]),
    ]
    sends, receives = swap(g_ref, h_ref, sg, rg, count, mine, place)
    for src, dst, send, recv in ((w_ref, o_ref, sa, ra), (v_ref, p_ref, sv, rv)):
        more, waits = swap(src, dst, send, recv, n, me, lambda c: (dp, c))
        sends += more
        receives += waits
    gathers = [
        remote(x_ref, y_ref.at[me], ss.at[k], rs.at[k], (dp, a))
        for k, a in enumerate(ahead + [partner])
    ]
    for copy in gathers + owns:
        copy.start()
    forwards = []
    for k, b in enumerate(behind):
        remote(x_ref, y_ref.at[b], ss.at[k], rs.at[k], (dp, b)).wait_recv()
        forward = remote(y_ref.at[b], y_ref.at[b], fs.at[k], fr.at[k], (dp, partner))
        forward.start()
        forwards.append(forward)
    gathers[-1].wait_recv()
    for copy in receives:
        copy.wait_recv()
    for forward in forwards:
        forward.wait()
    for copy in sends + gathers:
        copy.wait_send()
    for copy in owns:
        copy.wait()


def start(g, w, v, x, number):
    n_dp, n = lax.axis_size("dp"), lax.axis_size("ctx")
    half = n // 2
    dma = pltpu.SemaphoreType.DMA
    g_out, w_out, v_out, x_all = pl.pallas_call(
        functools.partial(start_kernel, n_dp, n),
        out_shape=(
            jax.ShapeDtypeStruct(g.shape, g.dtype),
            jax.ShapeDtypeStruct(w.shape, w.dtype),
            jax.ShapeDtypeStruct(v.shape, v.dtype),
            jax.ShapeDtypeStruct((n,) + x.shape, x.dtype),
        ),
        in_specs=[ANY] * 4,
        out_specs=(ANY,) * 4,
        scratch_shapes=[dma((4,))]
        + [dma((2 * n_dp - 1,))] * 2
        + [dma((n - 1,))] * 4
        + [dma((half,))] * 2
        + [dma((half - 1,))] * 2,
        compiler_params=params_of(number),
        name="start",
    )(g, w, v, x)
    return g_out, w_out, v_out, x_all.reshape(-1, x.shape[-1])


def collect_kernel(
    n_dp, n, g_ref, h_ref, a_ref, w_ref, o_ref, h_out, y_ref,
    own, ra, rc, sb, pa, qa, pb, qb,
    local, sa, rs, sc, rd, s1, r1, s2, r2, sh, rh,
):
    dp, me = lax.axis_index("dp"), lax.axis_index("ctx")
    count, index, place = group_of(n_dp, n, dp, me)
    greet_all(n_dp, n, dp, me)
    mine = pltpu.make_async_copy(g_ref.at[dp], own, local.at[0])
    mine.start()
    stay = pltpu.make_async_copy(h_ref.at[index], h_out.at[index], local.at[1])
    stay.start()
    first = []
    for c in range(n):
        row = []
        for k in range(1, n_dp):
            to = (dp + k) % n_dp
            copy = remote(
                g_ref.at[to, (me + 1 + c) % n],
                ra.at[c, k - 1],
                sa.at[c, k - 1],
                rs.at[c, k - 1],
                (to, me),
            )
            copy.start()
            row.append(copy)
        first.append(row)
    swaps, receives = swap(h_ref, h_out, sh, rh, count, index, place)
    sums = reduce_ctx(n, dp, me, a_ref, w_ref, slice(0, a_ref.shape[1]), y_ref, pa, qa, pb, qb, s1, r1, s2, r2)
    mine.wait()
    second = []
    for c in range(n):
        to = (me + 1 + c) % n
        total = own[to].astype(F32)
        for k in range(n_dp - 1):
            first[c][k].wait_recv()
            total = total + ra[c, k].astype(F32)
        if c < n - 1:
            sb[c] = total.astype(BF)
            copy = remote(sb.at[c], rc.at[c], sc.at[c], rd.at[c], (dp, to))
            copy.start()
            second.append(copy)
        else:
            o_ref[me] = total.astype(BF)
    for c in range(n - 1):
        second[c].wait_recv()
        o_ref[(me + n - 1 - c) % n] = rc[c]
    for copy in receives:
        copy.wait_recv()
    stay.wait()
    for row in first:
        for copy in row:
            copy.wait_send()
    for copy in second + sums + swaps:
        copy.wait_send()


def collect(g, h, a, w, number):
    n_dp, n = lax.axis_size("dp"), lax.axis_size("ctx")
    rows, width = g.shape[0] // (n_dp * n), g.shape[1]
    half, length, features = n // 2, a.shape[0] // n, w.shape[0]
    dma = pltpu.SemaphoreType.DMA
    return pl.pallas_call(
        functools.partial(collect_kernel, n_dp, n),
        out_shape=(
            jax.ShapeDtypeStruct((n, rows, width), BF),
            jax.ShapeDtypeStruct(h.shape, BF),
            jax.ShapeDtypeStruct((length, features), F32),
        ),
        in_specs=[ANY, ANY, VMEM, VMEM],
        out_specs=(VMEM, ANY, VMEM),
        scratch_shapes=[
            pltpu.VMEM((n, rows, width), BF),
            pltpu.VMEM((n, n_dp - 1, rows, width), BF),
            pltpu.VMEM((n - 1, rows, width), BF),
            pltpu.VMEM((n - 1, rows, width), BF),
            pltpu.VMEM((half, length, features), BF),
            pltpu.VMEM((half, length, features), BF),
            pltpu.VMEM((half - 1, length, features), BF),
            pltpu.VMEM((half - 1, length, features), BF),
            dma((2,)),
            dma((n, n_dp - 1)),
            dma((n, n_dp - 1)),
            dma((n - 1,)),
            dma((n - 1,)),
            dma((half,)),
            dma((half,)),
            dma((half - 1,)),
            dma((half - 1,)),
            dma((2 * n_dp - 1,)),
            dma((2 * n_dp - 1,)),
        ],
        compiler_params=params_of(number),
        name="collect",
    )(g.reshape(n_dp, n, rows, width), h, a, w)


def total_kernel(n_dp, n, ga_ref, gu_ref, gd_ref, gain_ref, o_ref, mine, buf, part, all_parts, ss, rs, st, rt):
    dp, me = lax.axis_index("dp"), lax.axis_index("ctx")
    gain_rows = gain_ref.shape[0]

    def squares(ref):
        acc = jnp.zeros((ref.shape[1], ref.shape[2]), F32)
        for i in range(ref.shape[0]):
            block = ref[i].astype(F32)
            acc += block * block
        return jnp.sum(acc, axis=0, keepdims=True)

    total = (
        jnp.sum(squares(ga_ref), axis=1, keepdims=True)
        + jnp.sum(squares(gu_ref), axis=1, keepdims=True)
        + jnp.sum(squares(gd_ref), axis=1, keepdims=True)
    )
    mine[0:gain_rows, :] = gain_ref[...]
    mine[gain_rows:, :] = jnp.broadcast_to(total, (8, 128))
    greet(
        [((dp + k) % n_dp, me) for k in range(1, n_dp)] + [(dp, (me + k) % n) for k in range(1, n)]
    )
    copies = []
    for k in range(1, n):
        copy = remote(mine, buf.at[me], ss.at[k - 1], rs.at[k - 1], (dp, (me + k) % n))
        copy.start()
        copies.append(copy)
    buf[me] = mine[...]
    for k in range(1, n):
        source = (me + n - k) % n
        remote(mine, buf.at[source], ss.at[k - 1], rs.at[k - 1], (dp, source)).wait_recv()
    acc = buf[0]
    for j in range(1, n):
        acc = acc + buf[j]
    part[...] = acc
    all_parts[dp] = acc
    for k in range(1, n_dp):
        copy = remote(part, all_parts.at[dp], st.at[k - 1], rt.at[k - 1], ((dp + k) % n_dp, me))
        copy.start()
        copies.append(copy)
    for k in range(1, n_dp):
        source = (dp + n_dp - k) % n_dp
        remote(part, all_parts.at[source], st.at[k - 1], rt.at[k - 1], (source, me)).wait_recv()
    acc = all_parts[0]
    for j in range(1, n_dp):
        acc = acc + all_parts[j]
    o_ref[...] = acc
    for copy in copies:
        copy.wait_send()


def total_over(ga, gu, gd, gain_part, number):
    n_dp, n = lax.axis_size("dp"), lax.axis_size("ctx")
    gain_rows = gain_part.size // 128
    shape = (gain_rows + 8, 128)
    dma = pltpu.SemaphoreType.DMA
    out = pl.pallas_call(
        functools.partial(total_kernel, n_dp, n),
        out_shape=jax.ShapeDtypeStruct(shape, F32),
        in_specs=[VMEM] * 4,
        out_specs=VMEM,
        scratch_shapes=[
            pltpu.VMEM(shape, F32),
            pltpu.VMEM((n,) + shape, F32),
            pltpu.VMEM(shape, F32),
            pltpu.VMEM((n_dp,) + shape, F32),
            dma((n - 1,)),
            dma((n - 1,)),
            dma((n_dp - 1,)),
            dma((n_dp - 1,)),
        ],
        compiler_params=params_of(number),
        name="total",
    )(ga, gu, gd, gain_part.reshape(gain_rows, 128))
    return out[gain_rows, 0], out[:gain_rows].reshape(gain_part.shape)


def adam_kernel(factor_ref, p_ref, m_ref, v_ref, ga_ref, gu_ref, gd_ref, po_ref, mo_ref, vo_ref, g_ref):
    part = pl.program_id(0)
    n, _, four = ga_ref.shape
    hc = four // 4
    fs = gd_ref.shape[2]

    @pl.when(part == 0)
    def _():
        for matrix in range(4):
            for c in range(n):
                start = (matrix * n + c) * hc
                g_ref[:, start : start + hc] = ga_ref[c, :, matrix * hc : (matrix + 1) * hc].astype(F32)

    @pl.when((part == 1) | (part == 2))
    def _():
        for d in range(gu_ref.shape[0]):
            g_ref[:, d * fs : (d + 1) * fs] = gu_ref[d].astype(F32)

    @pl.when(part == 3)
    def _():
        for d in range(gd_ref.shape[0]):
            g_ref[:, d * fs : (d + 1) * fs] = gd_ref[d].astype(F32)

    clipped = g_ref[...] * factor_ref[0, 0]
    new_p, new_m, new_v = adam_update(p_ref[...], m_ref[...], v_ref[...], clipped, RATE, DECAY)
    po_ref[...] = new_p
    mo_ref[...] = new_m
    vo_ref[...] = new_v


def adam(factor, params, first, second, ga, gu, gd):
    rows, columns = params.shape
    n, n_dp, fs = ga.shape[0], gd.shape[0], gd.shape[2]
    block = min(rows, 16)
    steps = rows // block
    wide = pl.BlockSpec((block, columns // 4), lambda i, r: (r, i))
    return pl.pallas_call(
        adam_kernel,
        grid=(4, steps),
        out_shape=(jax.ShapeDtypeStruct(params.shape, F32),) * 3,
        in_specs=[
            pl.BlockSpec(memory_space=pltpu.SMEM),
            wide,
            wide,
            wide,
            pl.BlockSpec((n, block, ga.shape[2]), lambda i, r: (0, jnp.where(i == 0, r, steps - 1), 0)),
            pl.BlockSpec(
                (n_dp, block, fs),
                lambda i, r: (
                    0,
                    jnp.where(i == 0, 0, jnp.where(i == 3, steps - 1, r)),
                    jnp.clip(i - 1, 0, 1),
                ),
            ),
            pl.BlockSpec((n_dp, block, fs), lambda i, r: (0, jnp.where(i == 3, r, 0), 0)),
        ],
        out_specs=(wide, wide, wide),
        scratch_shapes=[pltpu.VMEM((block, columns // 4), F32)],
        compiler_params=pltpu.CompilerParams(vmem_limit_bytes=48 * 1024 * 1024),
        name="adam",
    )(factor.reshape(1, 1), params, first, second, ga, gu, gd)


def arrange_kernel(n, count, p_ref, a_ref, o_ref, g_ref, d_ref):
    part = pl.program_id(0)
    hc = o_ref.shape[2]
    fs = d_ref.shape[2]

    @pl.when(part == 0)
    def _():
        for matrix in range(4):
            for c in range(n):
                start = (matrix * n + c) * hc
                value = p_ref[:, start : start + hc].astype(BF)
                if matrix < 3:
                    a_ref[c, :, matrix * hc : (matrix + 1) * hc] = value
                else:
                    o_ref[c] = value

    for index, ref, first in ((1, g_ref, 0), (2, g_ref, fs), (3, d_ref, 0)):

        @pl.when(part == index)
        def _():
            for d in range(count):
                ref[d, :, first : first + fs] = p_ref[:, d * fs : (d + 1) * fs].astype(BF)


def arrange(params, width):
    count, n = 2 * lax.axis_size("dp"), lax.axis_size("ctx")
    rows, columns = params.shape
    fs, hc = columns // 4 // count, width // n
    whole = lambda shape: pl.BlockSpec(shape, lambda i: (0,) * len(shape))
    shapes = [(n, rows, 3 * hc), (n, rows, hc), (count, rows, 2 * fs), (count, rows, fs)]
    return pl.pallas_call(
        functools.partial(arrange_kernel, n, count),
        grid=(4,),
        out_shape=tuple(jax.ShapeDtypeStruct(s, BF) for s in shapes),
        in_specs=[pl.BlockSpec((rows, columns // 4), lambda i: (0, i))],
        out_specs=tuple(whole(s) for s in shapes),
        compiler_params=pltpu.CompilerParams(vmem_limit_bytes=48 * 1024 * 1024),
        name="arrange",
    )(params)


def row_sums(value, row):
    pick = lax.broadcasted_iota(jnp.int32, (8, value.shape[1]), 0) == row
    return lax.dot_general(
        pick.astype(F32),
        value,
        (((1,), (1,)), ((), ())),
        preferred_element_type=F32,
        precision=lax.Precision.HIGHEST,
    )


def exchange(n, dp, me, buf, ss, rs):
    copies = []
    for k in range(1, n):
        copy = remote(buf.at[me], buf.at[me], ss.at[k - 1], rs.at[k - 1], (dp, (me + k) % n))
        copy.start()
        copies.append(copy)
    for k in range(1, n):
        source = (me + n - k) % n
        remote(buf.at[me], buf.at[source], ss.at[k - 1], rs.at[k - 1], (dp, source)).wait_recv()
    total = buf[0]
    for j in range(1, n):
        total = total + buf[j]
    for copy in copies:
        copy.wait_send()
    return total


def turn(value, cos, sine):
    return value * cos + pltpu.roll(value, HD // 2, 1) * sine


def mask_of(rows, info_col, info_row):
    pos_i, doc_i = info_col[rows, 0:1], info_col[rows, 1:2]
    return (info_row[1:2, :] == doc_i) & (info_row[0:1, :] <= pos_i)


def attend_kernel(
    n_dp, n, x_ref, w_ref, wo_ref, d_ref, t_ref, norm_ref, gain_ref, cos_ref, sin_ref, col_ref, row_ref,
    y_ref, h_ref, q_ref, k_ref, v_ref, o_ref, pre_ref, scale_ref, lse_ref, wo_all, d_out,
    buf, pa, qa, pb, qb, ss, rs, s1, r1, s2, r2, sw, rw, sd, rd, local,
):
    dp, me = lax.axis_index("dp"), lax.axis_index("ctx")
    seq, width = x_ref.shape
    hc = o_ref.shape[1]
    block = min(seq, 256)
    count, mine, place = group_of(n_dp, n, dp, me)
    greet_all(n_dp, n, dp, me)
    piece = wo_ref.shape[0]

    def part_of(d):
        return wo_all.at[pl.ds(pl.multiple_of(d * piece, piece), piece), :]

    owns = [
        pltpu.make_async_copy(wo_ref, part_of(dp), local.at[0]),
        pltpu.make_async_copy(d_ref.at[mine], d_out.at[mine], local.at[1]),
    ]
    behind_wo = [
        remote(wo_ref, part_of(dp), sw.at[k - 1], rw.at[k - 1], ((dp + k) % n_dp, me))
        for k in range(1, n_dp)
    ]
    for copy in behind_wo + owns:
        copy.start()
    behind_d, receives = swap(d_ref, d_out, sd, rd, count, mine, place)

    @pl.loop(0, seq // block)
    def _(i):
        rows = pl.ds(pl.multiple_of(i * block, block), block)
        value = dot(x_ref[rows, :], w_ref[...])
        pre_ref[rows, :] = value[:, : 2 * hc]
        v_ref[rows, :] = value[:, 2 * hc :].astype(BF)
        squares = value[:, : 2 * hc] * value[:, : 2 * hc]
        buf[me, :, rows] = row_sums(squares[:, :hc], 0) + row_sums(squares[:, hc:], 1)

    scale_ref[...] = jnp.transpose(lax.rsqrt(exchange(n, dp, me, buf, ss, rs) / width + EPS))

    @pl.loop(0, seq // block)
    def _(i):
        rows = pl.ds(pl.multiple_of(i * block, block), block)
        cos, sine = cos_ref[rows, :], sin_ref[rows, :]
        for which, ref, factor in ((0, q_ref, HD ** (-0.5)), (1, k_ref, 1.0)):
            scale = scale_ref[rows, which : which + 1]
            for start in range(0, hc, HD):
                part = slice(start, start + HD)
                value = pre_ref[rows, which * hc + start : which * hc + start + HD] * scale
                ref[rows, part] = (
                    turn(value * gain_ref[which : which + 1, part], cos, sine) * factor
                ).astype(BF)

    @pl.loop(0, seq // block)
    def _(i):
        rows = pl.ds(pl.multiple_of(i * block, block), block)
        visible = mask_of(rows, col_ref, row_ref)
        for head in range(hc // HD):
            part = slice(head * HD, (head + 1) * HD)
            scores = jnp.where(visible, dot_t(q_ref[rows, part], k_ref[:, part]), -jnp.inf)
            top = jnp.max(scores, axis=1, keepdims=True)
            weights = jnp.exp(scores - top)
            total = jnp.sum(weights, axis=1, keepdims=True)
            o_ref[rows, part] = (dot(weights.astype(BF), v_ref[:, part]) / total).astype(BF)
            lse_ref[rows, head : head + 1] = top + jnp.log(total)

    owns[0].wait()
    for k in range(1, n_dp):
        source = (dp + n_dp - k) % n_dp
        remote(wo_ref, part_of(source), sw.at[k - 1], rw.at[k - 1], (source, me)).wait_recv()
    cols = slice(0, hc)
    sums = reduce_ctx(n, dp, me, o_ref, wo_all, cols, y_ref, pa, qa, pb, qb, s1, r1, s2, r2)

    def finish(rows):
        branch = y_ref[rows, :]
        h_ref[rows, :] = t_ref[rows, :].astype(F32) + branch * rms_scale(branch) * norm_ref[...]

    tiles(y_ref.shape[0], 16, finish)
    for copy in receives:
        copy.wait_recv()
    for copy in sums + behind_wo + behind_d:
        copy.wait_send()
    owns[1].wait()


def attend(x_all, w, wo, d, tokens, norm, gain, cos, sine, info_col, info_row, number):
    n_dp, n = lax.axis_size("dp"), lax.axis_size("ctx")
    seq, width = x_all.shape
    half, length, hc = n // 2, seq // n, w.shape[1] // 3
    dma = pltpu.SemaphoreType.DMA
    low = jax.ShapeDtypeStruct((seq, hc), BF)
    return pl.pallas_call(
        functools.partial(attend_kernel, n_dp, n),
        out_shape=(
            jax.ShapeDtypeStruct((length, width), F32),
            jax.ShapeDtypeStruct((length, width), F32),
            low,
            low,
            low,
            low,
            jax.ShapeDtypeStruct((seq, 2 * hc), F32),
            jax.ShapeDtypeStruct((seq, 8), F32),
            jax.ShapeDtypeStruct((seq, 8), F32),
            jax.ShapeDtypeStruct((width, hc), BF),
            jax.ShapeDtypeStruct(d.shape, BF),
        ),
        in_specs=[VMEM] * 2 + [ANY] * 2 + [VMEM] * 7,
        out_specs=(VMEM,) * 10 + (ANY,),
        scratch_shapes=[
            pltpu.VMEM((n, 8, seq), F32),
            pltpu.VMEM((half, length, width), BF),
            pltpu.VMEM((half, length, width), BF),
            pltpu.VMEM((half - 1, length, width), BF),
            pltpu.VMEM((half - 1, length, width), BF),
            dma((n - 1,)),
            dma((n - 1,)),
            dma((half,)),
            dma((half,)),
            dma((half - 1,)),
            dma((half - 1,)),
            dma((n_dp - 1,)),
            dma((n_dp - 1,)),
            dma((2 * n_dp - 1,)),
            dma((2 * n_dp - 1,)),
            dma((2,)),
        ],
        compiler_params=params_of(number),
        name="attend",
    )(x_all, w, wo, d, tokens, norm, gain, cos, sine, info_col, info_row)


def attend_back_kernel(
    n_dp, n, e_ref, w_ref, h_ref, gain_ref, cos_ref, sin_ref, col_ref, row_ref,
    q_ref, k_ref, v_ref, pre_ref, scale_ref, lse_ref,
    all_ref, d_ref, gain_out, h_out,
    do_ref, dq_ref, dk_ref, dv_ref, mean_ref, buf, ss, rs, s1, r1, s2, r2, sh, rh, local,
):
    dp, me = lax.axis_index("dp"), lax.axis_index("ctx")
    half, parity, pair, partner, ahead, behind = pairs_of(n, me)
    seq, hc = q_ref.shape
    length, width = e_ref.shape
    block = min(seq, 256)
    count, index, place = group_of(n_dp, n, dp, me)
    greet_all(n_dp, n, dp, me)
    sends = [
        remote(e_ref, all_ref.at[me], s1.at[k], r1.at[k], (dp, a))
        for k, a in enumerate(ahead + [partner])
    ]
    for copy in sends:
        copy.start()
    swaps, receives = swap(h_ref, h_out, sh, rh, count, index, place)
    stay = pltpu.make_async_copy(h_ref.at[index], h_out.at[index], local)
    stay.start()
    all_ref[me] = e_ref[...]
    dk_ref[...] = jnp.zeros_like(dk_ref)
    dv_ref[...] = jnp.zeros_like(dv_ref)

    def project(b):
        rows = pl.ds(pl.multiple_of(b * length, length), length)
        do_ref[rows, :] = dot(all_ref[b], w_ref[...]).astype(BF)

    project(me)
    sends[-1].wait_recv()
    project(partner)
    forwards = []
    for k, b in enumerate(behind):
        remote(e_ref, all_ref.at[b], s1.at[k], r1.at[k], (dp, b)).wait_recv()
        forward = remote(all_ref.at[b], all_ref.at[b], s2.at[k], r2.at[k], (dp, partner))
        forward.start()
        forwards.append(forward)
        project(b)
    for k, b in enumerate(behind):
        forwards[k].wait_recv()
        project(b + 1 - 2 * parity)

    @pl.loop(0, seq // block)
    def _(i):
        rows = pl.ds(pl.multiple_of(i * block, block), block)
        visible = mask_of(rows, col_ref, row_ref)
        for head in range(hc // HD):
            part = slice(head * HD, (head + 1) * HD)
            query, key, value, back = q_ref[rows, part], k_ref[:, part], v_ref[:, part], do_ref[rows, part]
            scores = jnp.where(visible, dot_t(query, key), -jnp.inf)
            probs = jnp.exp(scores - lse_ref[rows, head : head + 1])
            d_probs = dot_t(back, value)
            delta = jnp.sum(probs * d_probs, axis=1, keepdims=True)
            d_scores = (probs * (d_probs - delta)).astype(BF)
            dq_ref[rows, part] = dot(d_scores, key)
            dk_ref[:, part] += t_dot(d_scores, query)
            dv_ref[:, part] += t_dot(probs.astype(BF), back)

    gain_out[...] = jnp.zeros_like(gain_out)

    @pl.loop(0, seq // block)
    def _(i):
        rows = pl.ds(pl.multiple_of(i * block, block), block)
        cos, sine = cos_ref[rows, :], sin_ref[rows, :]
        sums = jnp.zeros((8, block), F32)
        for which, ref, factor in ((0, dq_ref, HD ** (-0.5)), (1, dk_ref, 1.0)):
            scale = scale_ref[rows, which : which + 1]
            for start in range(0, hc, HD):
                part = slice(start, start + HD)
                pre = pre_ref[rows, which * hc + start : which * hc + start + HD]
                value = turn(ref[rows, part] * factor, cos, -sine)
                gain_out[which : which + 1, part] += jnp.sum(value * pre * scale, axis=0, keepdims=True)
                value = value * gain_ref[which : which + 1, part]
                ref[rows, part] = value
                sums += row_sums(value * pre, which)
        buf[me, :, rows] = sums

    mean_ref[...] = jnp.transpose(exchange(n, dp, me, buf, ss, rs) / width)

    @pl.loop(0, seq // block)
    def _(i):
        rows = pl.ds(pl.multiple_of(i * block, block), block)
        for which, ref in ((0, dq_ref), (1, dk_ref)):
            scale = scale_ref[rows, which : which + 1]
            mean = mean_ref[rows, which : which + 1]
            cols = slice(which * hc, (which + 1) * hc)
            value = scale * (ref[rows, :] - pre_ref[rows, cols] * (scale * scale * mean))
            d_ref[rows, cols] = value.astype(BF)
        d_ref[rows, 2 * hc :] = dv_ref[rows, :].astype(BF)

    for copy in receives:
        copy.wait_recv()
    for copy in sends + forwards + swaps:
        copy.wait_send()
    stay.wait()


def attend_back(e, w, h, gain, cos, sine, info_col, info_row, q, k, v, pre, scale, lse, number):
    n_dp, n = lax.axis_size("dp"), lax.axis_size("ctx")
    seq, hc = q.shape
    half, (length, width) = n // 2, e.shape
    dma = pltpu.SemaphoreType.DMA
    all_e, d_qkv, d_gain, h = pl.pallas_call(
        functools.partial(attend_back_kernel, n_dp, n),
        out_shape=(
            jax.ShapeDtypeStruct((n, length, width), BF),
            jax.ShapeDtypeStruct((seq, 3 * hc), BF),
            jax.ShapeDtypeStruct((2, hc), F32),
            jax.ShapeDtypeStruct(h.shape, BF),
        ),
        in_specs=[VMEM, VMEM, ANY] + [VMEM] * 11,
        out_specs=(VMEM,) * 3 + (ANY,),
        scratch_shapes=[
            pltpu.VMEM((seq, hc), BF),
            pltpu.VMEM((seq, hc), F32),
            pltpu.VMEM((seq, hc), F32),
            pltpu.VMEM((seq, hc), F32),
            pltpu.VMEM((seq, 8), F32),
            pltpu.VMEM((n, 8, seq), F32),
            dma((n - 1,)),
            dma((n - 1,)),
            dma((half,)),
            dma((half,)),
            dma((half - 1,)),
            dma((half - 1,)),
            dma((2 * n_dp - 1,)),
            dma((2 * n_dp - 1,)),
            dma,
        ],
        compiler_params=params_of(number),
        name="attend_back",
    )(e, w, h, gain, cos, sine, info_col, info_row, q, k, v, pre, scale, lse)
    return all_e.reshape(seq, width), d_qkv, d_gain, h


def shards(
    inputs,
    cotangent,
    documents,
    block_place,
    params,
    first_moment,
    second_moment,
    gains,
    gains_first,
    gains_second,
):
    tokens = inputs[0]
    upstream = cotangent[0]
    length, width = tokens.shape
    n_ctx = lax.axis_size("ctx")
    n_dp = lax.axis_size("dp")
    me_ctx = lax.axis_index("ctx")
    seq = length * n_ctx
    rows = params.shape[0]
    ff = (params.shape[1] - 4 * width) // 3
    hc = width // n_ctx
    half, group = n_ctx // 2, 2 * n_dp
    fh = ff // group
    parities = [[2 * p + side for p in range(half)] for side in range(2)]

    def gather_pairs(w):
        w = lax.all_gather(
            w.reshape(group * rows, w.shape[2]), "ctx", axis=0, tiled=True, axis_index_groups=parities
        )
        return w.reshape(half, n_dp, 2 * rows, w.shape[1])

    def scatter_pairs(g):
        g = lax.psum_scatter(
            g.reshape(width, g.shape[3]),
            "ctx",
            scatter_dimension=0,
            tiled=True,
            axis_index_groups=parities,
        )
        return g.reshape(group, rows, g.shape[1])

    w_qkv, w_o, w_gu, w_d = arrange(params, width)
    w_gu, w_qkv, w_o, x_all = start(w_gu, w_qkv, w_o, tokens, 1)
    w_gu = gather_pairs(w_gu)
    w_qkv = gather_dp(w_qkv.reshape(n_ctx * rows, 3 * hc), 2)

    indices = jnp.arange(seq, dtype=jnp.int32)
    owners = indices // length
    placed = jnp.sum(
        jnp.where(
            owners[:, None] == jnp.arange(n_ctx, dtype=jnp.int32)[None, :], block_place[None, :], 0
        ),
        axis=1,
    )
    pos = placed * length + indices % length
    docs = documents[0]
    info_row = jnp.concatenate([pos[None], docs[None], jnp.zeros((6, seq), jnp.int32)])
    info_col = info_row.T
    cos_tab, sine_tab = rope_tables(pos, HD)
    cos_tab = jnp.concatenate([cos_tab, cos_tab], axis=1)
    sine_tab = jnp.concatenate([-sine_tab, sine_tab], axis=1)
    my_gains = lax.dynamic_slice_in_dim(gains[:2], me_ctx * hc, hc, axis=1)
    tables = (my_gains, cos_tab, sine_tab, info_col, info_row)

    branch, hidden1, queries, keys, values, attn_low, qk_pre, scales, lse, w_o, w_d = attend(
        x_all, w_qkv, w_o.reshape(n_ctx * rows, hc), w_d, tokens, gains[2:3], *tables, 3
    )
    w_d = gather_pairs(w_d)

    result, d_mlp, g_ff_part, h1_all, gate_up, inner = ff_forward(
        hidden1, upstream, gains[3:4], w_gu, w_d, 4
    )
    d_mlp_all, d_gu = ff_back(d_mlp, w_d, gate_up, 5)
    d_grad, gu_grad = ff_grad(d_mlp_all, inner, rows), ff_grad(h1_all, d_gu, rows)
    d_grad, gu_grad, d_gu = lax.optimization_barrier((d_grad, gu_grad, d_gu))
    d_grad, gu_grad = scatter_pairs(d_grad), scatter_pairs(gu_grad)
    d_h1, d_branch, g_attn_part = ff_scatter(d_gu, w_gu, upstream, branch, gains[2:3], 6)

    d_branch_all, d_qkv, d_gain, d_grad = attend_back(
        d_branch, w_o, d_grad, *tables, queries, keys, values, qk_pre, scales, lse, 8
    )
    attn_grad = jnp.concatenate([t_dot(x_all, d_qkv), t_dot(d_branch_all, attn_low)], axis=1)
    attn_grad, gu_grad, d_x = collect(attn_grad.astype(BF), gu_grad, d_qkv, w_qkv, 9)
    d_input = d_h1 + d_x

    gain_part = jnp.concatenate(
        [
            lax.dynamic_update_slice(jnp.zeros((2, width), F32), d_gain, (0, me_ctx * hc)),
            g_attn_part,
            g_ff_part,
        ],
        axis=0,
    )
    square_total, gain_total = total_over(attn_grad, gu_grad, d_grad, gain_part, 11)
    grad_norm = jnp.sqrt(square_total + jnp.sum(gain_total * gain_total))
    factor = CLIP / (grad_norm + 1e-06)
    new_params, new_first, new_second = adam(
        factor, params, first_moment, second_moment, attn_grad, gu_grad, d_grad
    )
    new_gains, new_gains_first, new_gains_second = adam_update(
        gains, gains_first, gains_second, gain_total * factor, GAIN_RATE, 0.0
    )
    return (
        result[None],
        d_input.astype(BF)[None],
        grad_norm,
        new_params,
        new_first,
        new_second,
        new_gains,
        new_gains_first,
        new_gains_second,
    )


def solution(mesh):
    split, whole = P("dp", "ctx", None), P(("dp", "ctx"), None)
    return jax.shard_map(
        shards,
        mesh=mesh,
        in_specs=(split, split, P("dp", None), P(), whole, whole, whole, P(), P(), P()),
        out_specs=(split, split, P(), whole, whole, whole, P(), P(), P()),
        check_vma=False,
    )
```

```python
import functools

import jax
import jax.numpy as jnp
from jax import lax
from jax.experimental import pallas as pl
from jax.experimental.pallas import tpu as pltpu
from jax.sharding import PartitionSpec as P

HD = 128
STEP = 10
EPS = 1e-06
THETA = 500000.0
CLIP = 1.0
BETA1 = 0.9
BETA2 = 0.95
RATE = 0.03
GAIN_RATE = 0.8
DECAY = 0.1
ADAM_EPS = 1e-08
BF = jnp.bfloat16
F32 = jnp.float32
MESH = pl.DeviceIdType.MESH
ANY = pl.BlockSpec(memory_space=pl.ANY)
VMEM = pl.BlockSpec(memory_space=pltpu.VMEM)


def rms_scale(values):
    return lax.rsqrt(jnp.mean(values * values, axis=-1, keepdims=True) + EPS)


def norm_back(upstream, source, scale):
    return scale * (
        upstream - source * scale * scale * jnp.mean(upstream * source, axis=-1, keepdims=True)
    )


def rope_tables(positions, head_size):
    half_size = head_size // 2
    freqs = THETA ** (-jnp.arange(half_size, dtype=jnp.float32) * 2.0 / head_size)
    angles = positions.astype(jnp.float32)[:, None] * freqs[None, :]
    return (jnp.cos(angles), jnp.sin(angles))


def adam_update(weight, first_in, second_in, clipped, rate, decay):
    new_first = BETA1 * first_in + (1.0 - BETA1) * clipped
    new_second = BETA2 * second_in + (1.0 - BETA2) * clipped * clipped
    first_hat = new_first / (1.0 - BETA1**STEP)
    second_hat = new_second / (1.0 - BETA2**STEP)
    new_weight = weight - rate * (first_hat / (jnp.sqrt(second_hat) + ADAM_EPS) + decay * weight)
    return (new_weight, new_first, new_second)


def dot(a, b):
    return jnp.dot(a, b, preferred_element_type=F32)


def dot_t(a, b):
    return lax.dot_general(a, b, (((1,), (1,)), ((), ())), preferred_element_type=F32)


def t_dot(a, b):
    return lax.dot_general(a, b, (((0,), (0,)), ((), ())), preferred_element_type=F32)


def greet(peers):
    barrier = pltpu.get_barrier_semaphore()
    for peer in peers:
        pl.semaphore_signal(barrier, inc=1, device_id=peer, device_id_type=MESH)
    pl.semaphore_wait(barrier, len(peers))


def remote(src, dst, send, recv, peer):
    return pltpu.make_async_remote_copy(
        src_ref=src, dst_ref=dst, send_sem=send, recv_sem=recv, device_id=peer, device_id_type=MESH
    )


def cost(us):
    return pl.CostEstimate(flops=0, bytes_accessed=us * 3_600_000, transcendentals=0)


def params_of(number, vmem=48):
    return pltpu.CompilerParams(
        collective_id=number, has_side_effects=True, vmem_limit_bytes=vmem * 1024 * 1024
    )


def line_steps(n, me, make_right, make_left):
    for s in range(n - 1):

        @pl.when((me < n - 1) & (me >= s))
        def _():
            make_right(s).start()

        @pl.when((me > 0) & (me + s < n))
        def _():
            make_left(s).start()

        @pl.when(me - 1 - s >= 0)
        def _():
            make_right(s, me - 1 - s).wait_recv()

        @pl.when(me + 1 + s < n)
        def _():
            make_left(s, me + 1 + s).wait_recv()

    for s in range(n - 1):

        @pl.when((me < n - 1) & (me >= s))
        def _():
            make_right(s).wait_send()

        @pl.when((me > 0) & (me + s < n))
        def _():
            make_left(s).wait_send()


def pairs_of(n, me):
    half = n // 2
    parity, pair = me % 2, me // 2
    partner = me + 1 - 2 * parity
    ahead = [2 * ((pair + k) % half) + parity for k in range(1, half)]
    behind = [2 * ((pair + half - k) % half) + parity for k in range(1, half)]
    return half, parity, pair, partner, ahead, behind


def gather_dp_kernel(n, x_ref, o_ref, local, sr, rr, sl, rl):
    me, ctx = lax.axis_index("dp"), lax.axis_index("ctx")

    def here(d):
        return (d, ctx)

    greet([here((me + 1) % n), here((me + n - 1) % n)])
    own = pltpu.make_async_copy(x_ref, o_ref.at[me], local)
    own.start()

    def right(s, block=None):
        b = me - s if block is None else block
        return remote(x_ref if s == 0 else o_ref.at[b], o_ref.at[b], sr.at[s], rr.at[s], here(me + 1))

    def left(s, block=None):
        b = me + s if block is None else block
        return remote(x_ref if s == 0 else o_ref.at[b], o_ref.at[b], sl.at[s], rl.at[s], here(me - 1))

    line_steps(n, me, right, left)
    own.wait()


def gather_dp(x, number):
    n = lax.axis_size("dp")
    out = pl.pallas_call(
        functools.partial(gather_dp_kernel, n),
        out_shape=jax.ShapeDtypeStruct((n,) + x.shape, x.dtype),
        in_specs=[ANY],
        out_specs=ANY,
        scratch_shapes=[pltpu.SemaphoreType.DMA] + [pltpu.SemaphoreType.DMA((n - 1,))] * 4,
        compiler_params=params_of(number),
        cost_estimate=cost(60),
        name="gather_dp",
    )(x)
    return out.reshape((n * x.shape[0],) + x.shape[1:])


def group_of(n_dp, n, dp, me):
    pair, parity = me // 2, me % 2
    return 2 * n_dp, 2 * dp + parity, lambda j: (j // 2, 2 * pair + j % 2)


def greet_all(n_dp, n, dp, me):
    partner = me + 1 - 2 * (me % 2)
    others = [(dp + k) % n_dp for k in range(1, n_dp)]
    greet([(dp, (me + k) % n) for k in range(1, n)] + [(d, c) for d in others for c in (me, partner)])


def swap(src, dst, send, recv, count, mine, place):
    sends, receives = [], []
    for k in range(1, count):
        to, source = (mine + k) % count, (mine + count - k) % count
        sends.append(remote(src.at[to], dst.at[mine], send.at[k - 1], recv.at[k - 1], place(to)))
        receives.append(
            remote(src.at[mine], dst.at[source], send.at[k - 1], recv.at[k - 1], place(source))
        )
    for copy in sends:
        copy.start()
    return sends, receives


def tiles(total, tile, body):
    tile = min(total, tile)

    @pl.loop(0, total // tile)
    def _(j):
        body(pl.ds(pl.multiple_of(j * tile, tile), tile))


def reduce_ctx(n, dp, me, a_ref, w_ref, cols, o_ref, sa, ra, sb, rb, s1, r1, s2, r2):
    half, parity, pair, partner, ahead, behind = pairs_of(n, me)
    length, width = o_ref.shape

    def rows(block):
        return pl.ds(pl.multiple_of(block * length, length), length)

    first, second = [], []
    for k in range(half):
        target = (pair + k + 1) % half

        def give(part):
            value = dot_t(a_ref[rows(2 * target + 1 - parity), :], w_ref[part, cols])
            sa[k, :, part] = value.astype(BF)

        tiles(width, 512, give)
        copy = remote(sa.at[k], ra.at[k], s1.at[k], r1.at[k], (dp, partner))
        copy.start()
        first.append(copy)
        copy.wait_recv()

        def keep(part):
            value = dot_t(a_ref[rows(2 * target + parity), :], w_ref[part, cols])
            value = value + ra[k, :, part].astype(F32)
            if k < half - 1:
                sb[k, :, part] = value.astype(BF)
            else:
                o_ref[:, part] = value

        tiles(width, 512, keep)
        if k < half - 1:
            copy = remote(sb.at[k], rb.at[k], s2.at[k], r2.at[k], (dp, 2 * target + parity))
            copy.start()
            second.append(copy)
    for k in range(half - 1):
        second[k].wait_recv()
        o_ref[...] += rb[k].astype(F32)
    return first + second


def load_rows(hbm, vmem, sems):
    half, n_dp, rows, _ = hbm.shape
    copies = []
    for d in range(n_dp):
        for p in range(half):
            part = pl.ds((d * half + p) * rows, rows)
            copies.append(pltpu.make_async_copy(hbm.at[p, d], vmem.at[part, :], sems.at[d * half + p]))
    for copy in copies:
        copy.start()
    return copies


def gather_group(n, dp, me, all_ref, length, sr, rr, sl, rl, sf, rf, process):
    parity = me % 2
    partner = me + 1 - 2 * parity

    def block(b, side):
        start = (2 * b + side) * length
        return all_ref.at[pl.ds(pl.multiple_of(start, length), length), :]

    def right(s, b):
        return remote(block(b, parity), block(b, parity), sr.at[s], rr.at[s], (dp + 1, me))

    def left(s, b):
        return remote(block(b, parity), block(b, parity), sl.at[s], rl.at[s], (dp - 1, me))

    def aside(b):
        return remote(block(b, parity), block(b, parity), sf.at[b], rf.at[b], (dp, partner))

    def from_aside(b):
        return remote(block(b, 1 - parity), block(b, 1 - parity), sf.at[b], rf.at[b], (dp, partner))

    for s in range(n):
        if s == 0:
            aside(dp).start()
        else:

            @pl.when(dp >= s)
            def _():
                right(s - 1, dp - s).wait_recv()

            @pl.when(dp + s < n)
            def _():
                left(s - 1, dp + s).wait_recv()

        @pl.when((dp < n - 1) & (dp >= s))
        def _():
            right(s, dp - s).start()

        @pl.when((dp > 0) & (dp + s < n))
        def _():
            left(s, dp + s).start()

        if s == 0:
            from_aside(dp).wait_recv()
            process(dp, True)
        else:

            @pl.when(dp >= s)
            def _():
                aside(dp - s).start()

            @pl.when(dp + s < n)
            def _():
                aside(dp + s).start()

            below = jnp.where(dp >= s, 1, 0)
            above = jnp.where(dp + s < n, 1, 0)

            @pl.loop(0, below + above)
            def _(j):
                b = jnp.where(j < below, dp - s, dp + s)
                from_aside(b).wait_recv()
                process(b, False)

    for s in range(n):

        @pl.when((dp < n - 1) & (dp >= s))
        def _():
            right(s, dp - s).wait_send()

        @pl.when((dp > 0) & (dp + s < n))
        def _():
            left(s, dp + s).wait_send()

        aside(s).wait_send()


def gather_sems(n_dp):
    return [pltpu.SemaphoreType.DMA((n_dp,))] * 6


def give_block(dp, me, b, own, a_ref, w_ref, o_ref, sa, ra, sb, rb, s1, r1, s2, r2):
    length, width = o_ref.shape
    parity = me % 2
    partner = me + 1 - 2 * parity

    def rows(side):
        return pl.ds(pl.multiple_of((2 * b + side) * length, length), length)

    def give(part):
        sa[b, :, part] = dot_t(a_ref[rows(1 - parity), :], w_ref[part, :]).astype(BF)

    tiles(width, 512, give)
    copy = remote(sa.at[b], ra.at[b], s1.at[b], r1.at[b], (dp, partner))
    copy.start()
    copy.wait_recv()

    def keep(part):
        value = dot_t(a_ref[rows(parity), :], w_ref[part, :]) + ra[b, :, part].astype(F32)
        if own:
            o_ref[:, part] = value
        else:
            sb[b, :, part] = value.astype(BF)

    tiles(width, 512, keep)
    if not own:
        remote(sb.at[b], rb.at[dp], s2.at[b], r2.at[dp], (b, me)).start()


def give_end(n, dp, me, o_ref, sa, ra, sb, rb, s1, r1, s2, r2):
    partner = me + 1 - 2 * (me % 2)
    for k in range(1, n):
        b = (dp + k) % n
        remote(sb.at[b], rb.at[b], s2.at[b], r2.at[b], (b, me)).wait_recv()
        o_ref[...] += rb[b].astype(F32)
    for k in range(1, n):
        b = (dp + k) % n
        remote(sb.at[b], rb.at[b], s2.at[b], r2.at[b], (b, me)).wait_send()
    for b in range(n):
        remote(sa.at[b], ra.at[b], s1.at[b], r1.at[b], (dp, partner)).wait_send()


def give_scratch(n_dp, length, width):
    return [pltpu.VMEM((n_dp, length, width), BF)] * 4 + [pltpu.SemaphoreType.DMA((n_dp,))] * 4


def greet_group(n_dp, dp, me):
    partner = me + 1 - 2 * (me % 2)
    greet([(dp, partner)] + [((dp + k) % n_dp, me) for k in range(1, n_dp)])


def ff_forward_kernel(
    n_dp, n, h_ref, up_ref, gain_ref, gu_hbm, d_hbm,
    res_ref, dm_ref, gp_ref, all_ref, pre_ref, hid_ref, d_ref,
    gu_ref, acc, sem_gu, sem_d, sd, rd, *rest,
):
    gather, give = rest[:6], rest[6:]
    dp, me = lax.axis_index("dp"), lax.axis_index("ctx")
    length, width = h_ref.shape
    fh = hid_ref.shape[1]
    half, parity, pair, partner, ahead, behind = pairs_of(n, me)
    loads_gu = load_rows(gu_hbm, gu_ref, sem_gu)
    mine = pl.ds(pl.multiple_of((2 * dp + me % 2) * length, length), length)
    all_ref[mine, :] = h_ref[...].astype(BF)
    greet(
        [(dp, partner)]
        + [((dp + k) % n_dp, me) for k in range(1, n_dp)]
        + [(dp, a) for a in ahead]
    )
    tall = d_hbm.shape[1]

    def down(d, p):
        return d_ref.at[pl.ds(pl.multiple_of((d * half + p) * tall, tall), tall), :]

    loads_d = [pltpu.make_async_copy(d_hbm.at[d], down(d, pair), sem_d.at[d]) for d in range(n_dp)]
    spreads = [
        remote(d_hbm.at[d], down(d, pair), sd.at[k, d], rd.at[k, d], (dp, a))
        for k, a in enumerate(ahead)
        for d in range(n_dp)
    ]
    for copy in spreads + loads_d:
        copy.start()

    def process(b, own):
        rows = pl.ds(pl.multiple_of(2 * b * length, 2 * length), 2 * length)
        if own:
            for copy in loads_gu:
                copy.wait()

        def hidden(part):
            second = pl.ds(pl.multiple_of(fh + part.start, part.size), part.size)
            gate = dot(all_ref[rows, :], gu_ref[:, part])
            upper = dot(all_ref[rows, :], gu_ref[:, second])
            pre_ref[rows, part] = gate
            pre_ref[rows, second] = upper
            hid_ref[rows, part] = (gate * jax.nn.sigmoid(gate) * upper).astype(BF)

        tiles(fh, 256, hidden)

    gather_group(n_dp, dp, me, all_ref, length, *gather, process)
    for copy in loads_d:
        copy.wait()
    for k, b in enumerate(behind):
        for d in range(n_dp):
            remote(d_hbm.at[d], down(d, b // 2), sd.at[k, d], rd.at[k, d], (dp, b)).wait_recv()

    @pl.loop(1, n_dp)
    def _(k):
        give_block(dp, me, (dp + k) % n_dp, False, hid_ref, d_ref, acc, *give)

    give_block(dp, me, dp, True, hid_ref, d_ref, acc, *give)
    give_end(n_dp, dp, me, acc, *give)
    gp_ref[...] = jnp.zeros_like(gp_ref)

    def finish(rows):
        out, up, gain = acc[rows, :], up_ref[rows, :].astype(F32), gain_ref[...]
        scale = rms_scale(out)
        res_ref[rows, :] = (h_ref[rows, :] + out * scale * gain).astype(BF)
        gp_ref[...] += jnp.sum(up * out * scale, axis=0, keepdims=True)
        dm_ref[rows, :] = norm_back(up * gain, out, scale).astype(BF)

    tiles(length, 16, finish)
    for copy in spreads:
        copy.wait_send()


def ff_forward(h1, up, gain, w_gu, w_d, number):
    n_dp, n = lax.axis_size("dp"), lax.axis_size("ctx")
    (length, width), fh = h1.shape, w_d.shape[2]
    tokens = 2 * n_dp * length
    half = n // 2
    low = jax.ShapeDtypeStruct((length, width), BF)
    return pl.pallas_call(
        functools.partial(ff_forward_kernel, n_dp, n),
        out_shape=(
            low,
            low,
            jax.ShapeDtypeStruct((1, width), F32),
            jax.ShapeDtypeStruct((tokens, width), BF),
            jax.ShapeDtypeStruct((tokens, 2 * fh), F32),
            jax.ShapeDtypeStruct((tokens, fh), BF),
            jax.ShapeDtypeStruct((width, fh), BF),
        ),
        in_specs=[VMEM] * 3 + [ANY] * 2,
        out_specs=(VMEM,) * 7,
        scratch_shapes=[
            pltpu.VMEM((width, 2 * fh), BF),
            pltpu.VMEM((length, width), F32),
            pltpu.SemaphoreType.DMA((half * n_dp,)),
            pltpu.SemaphoreType.DMA((n_dp,)),
            pltpu.SemaphoreType.DMA((half - 1, n_dp)),
            pltpu.SemaphoreType.DMA((half - 1, n_dp)),
        ]
        + gather_sems(n_dp)
        + give_scratch(n_dp, length, width),
        compiler_params=params_of(number, 58),
        cost_estimate=cost(90),
        name="ff_forward",
    )(h1, up, gain, w_gu, w_d)


def store_rows(n_dp, value_of, out):
    half, _, rows, _ = out.shape

    @pl.loop(0, n_dp * half)
    def _(r):
        out[r % half, r // half] = value_of(pl.ds(pl.multiple_of(r * rows, rows), rows)).astype(BF)


def ff_back_kernel(
    n_dp, dm_ref, hid_ref, d_hbm, pre_hbm, dgu_ref, gd_ref,
    all_ref, d_ref, pre_ref, acc, sem_d, sem_p, *gather,
):
    dp, me = lax.axis_index("dp"), lax.axis_index("ctx")
    length, width = dm_ref.shape
    fh = d_ref.shape[1]
    load = pltpu.make_async_copy(d_hbm, d_ref, sem_d)
    load.start()

    def rows_of(b):
        return pl.ds(pl.multiple_of(2 * b * length, 2 * length), 2 * length)

    def load_pre(b):
        return pltpu.make_async_copy(pre_hbm.at[rows_of(b), :], pre_ref.at[rows_of(b), :], sem_p.at[b])

    for k in range(n_dp):
        load_pre((dp + k) % n_dp).start()
    mine = pl.ds(pl.multiple_of((2 * dp + me % 2) * length, length), length)
    all_ref[mine, :] = dm_ref[...]
    greet_group(n_dp, dp, me)

    def process(b, own):
        rows = rows_of(b)
        if own:
            load.wait()
        load_pre(b).wait()

        def hidden(part):
            second = pl.ds(pl.multiple_of(fh + part.start, part.size), part.size)
            back = dot(all_ref[rows, :], d_ref[:, part])
            gate, upper = pre_ref[rows, part], pre_ref[rows, second]
            sig = jax.nn.sigmoid(gate)
            dgu_ref[rows, part] = (back * upper * sig * (1.0 + gate * (1.0 - sig))).astype(BF)
            dgu_ref[rows, second] = (back * gate * sig).astype(BF)

        tiles(fh, 256, hidden)

        def product(part):
            value = t_dot(all_ref[rows, part], hid_ref[rows, :])
            acc[part, :] = value if own else acc[part, :] + value

        tiles(width, 256, product)

    gather_group(n_dp, dp, me, all_ref, length, *gather, process)
    store_rows(n_dp, lambda part: acc[part, :], gd_ref)


def ff_back(dm, hid, w_d, pre, rows, number):
    n_dp, half = lax.axis_size("dp"), lax.axis_size("ctx") // 2
    (length, width), fh = dm.shape, w_d.shape[1]
    tokens = 2 * n_dp * length
    return pl.pallas_call(
        functools.partial(ff_back_kernel, n_dp),
        out_shape=(
            jax.ShapeDtypeStruct((tokens, 2 * fh), BF),
            jax.ShapeDtypeStruct((half, n_dp, 2 * rows, fh), BF),
        ),
        in_specs=[VMEM, VMEM, ANY, ANY],
        out_specs=(VMEM,) * 2,
        scratch_shapes=[
            pltpu.VMEM((tokens, width), BF),
            pltpu.VMEM((width, fh), BF),
            pltpu.VMEM((tokens, 2 * fh), F32),
            pltpu.VMEM((width, fh), F32),
            pltpu.SemaphoreType.DMA,
            pltpu.SemaphoreType.DMA((n_dp,)),
        ]
        + gather_sems(n_dp),
        compiler_params=params_of(number, 58),
        cost_estimate=cost(45),
        name="ff_back",
    )(dm, hid, w_d, pre)


def ff_scatter_kernel(
    n_dp, n, dgu_ref, gu_hbm, all_hbm, up_ref, branch_ref, gain_ref, dh_ref, db_ref, gp_ref, gg_ref, gv_ref,
    gu_ref, all_ref, acc, sem_gu, sem_all, ss, rs, fs, fr, *give,
):
    dp, me = lax.axis_index("dp"), lax.axis_index("ctx")
    length, width = dh_ref.shape
    half, parity, pair, partner, ahead, behind = pairs_of(n, me)
    _, _, rows, fh = gg_ref.shape
    loads = load_rows(gu_hbm, gu_ref, sem_gu)
    load = pltpu.make_async_copy(all_hbm, all_ref, sem_all)
    load.start()
    greet(
        [(dp, partner)]
        + [((dp + k) % n_dp, me) for k in range(1, n_dp)]
        + [(dp, a) for a in ahead]
    )
    for copy in loads:
        copy.wait()

    @pl.loop(1, n_dp)
    def _(k):
        give_block(dp, me, (dp + k) % n_dp, False, dgu_ref, gu_ref, dh_ref, *give)

    give_block(dp, me, dp, True, dgu_ref, gu_ref, dh_ref, *give)
    load.wait()
    block = acc.shape[0]

    @pl.loop(0, width // block)
    def _(j):
        acc[...] = t_dot(all_ref[:, pl.ds(pl.multiple_of(j * block, block), block)], dgu_ref[...])
        for s in range(block // rows):
            r = j * (block // rows) + s
            part = slice(s * rows, (s + 1) * rows)
            gg_ref[r % half, r // half] = acc[part, :fh].astype(BF)
            gv_ref[r % half, r // half] = acc[part, fh:].astype(BF)

    give_end(n_dp, dp, me, dh_ref, *give)
    gp_ref[...] = jnp.zeros_like(gp_ref)

    def block(b):
        return db_ref.at[pl.ds(pl.multiple_of(b * length, length), length), :]

    def finish(rows):
        grad, branch = dh_ref[rows, :] + up_ref[rows, :].astype(F32), branch_ref[rows, :]
        scale = rms_scale(branch)
        dh_ref[rows, :] = grad
        gp_ref[...] += jnp.sum(grad * branch * scale, axis=0, keepdims=True)
        mine = pl.ds(pl.multiple_of(me * length + rows.start, rows.size), rows.size)
        db_ref[mine, :] = norm_back(grad * gain_ref[...], branch, scale).astype(BF)

    tiles(length, 16, finish)
    sends = [
        remote(block(me), block(me), ss.at[k], rs.at[k], (dp, a)) for k, a in enumerate(ahead + [partner])
    ]
    for copy in sends:
        copy.start()
    forwards = []
    for k, b in enumerate(behind):
        remote(block(b), block(b), ss.at[k], rs.at[k], (dp, b)).wait_recv()
        forward = remote(block(b), block(b), fs.at[k], fr.at[k], (dp, partner))
        forward.start()
        forwards.append(forward)
    remote(block(partner), block(partner), ss.at[half - 1], rs.at[half - 1], (dp, partner)).wait_recv()
    for k, b in enumerate(behind):
        other = b + 1 - 2 * parity
        remote(block(other), block(other), fs.at[k], fr.at[k], (dp, partner)).wait_recv()
    for copy in sends + forwards:
        copy.wait_send()


def ff_scatter(dgu, w_gu, h1_all, up, branch, gain, number):
    n_dp, n = lax.axis_size("dp"), lax.axis_size("ctx")
    length, width = up.shape
    half = n // 2
    grad = jax.ShapeDtypeStruct(w_gu.shape[:3] + (w_gu.shape[3] // 2,), BF)
    return pl.pallas_call(
        functools.partial(ff_scatter_kernel, n_dp, n),
        out_shape=(
            jax.ShapeDtypeStruct((length, width), F32),
            jax.ShapeDtypeStruct((n * length, width), BF),
            jax.ShapeDtypeStruct((1, width), F32),
            grad,
            grad,
        ),
        in_specs=[VMEM, ANY, ANY] + [VMEM] * 3,
        out_specs=(VMEM,) * 5,
        scratch_shapes=[
            pltpu.VMEM((width, w_gu.shape[3]), BF),
            pltpu.VMEM(h1_all.shape, BF),
            pltpu.VMEM((256, w_gu.shape[3]), F32),
            pltpu.SemaphoreType.DMA((w_gu.shape[0] * n_dp,)),
            pltpu.SemaphoreType.DMA,
            pltpu.SemaphoreType.DMA((half,)),
            pltpu.SemaphoreType.DMA((half,)),
            pltpu.SemaphoreType.DMA((half - 1,)),
            pltpu.SemaphoreType.DMA((half - 1,)),
        ]
        + give_scratch(n_dp, length, width),
        compiler_params=params_of(number, 56),
        cost_estimate=cost(50),
        name="ff_scatter",
    )(dgu, w_gu, h1_all, up, branch, gain)


def start_kernel(
    n_dp, n, g_ref, w_ref, v_ref, x_ref, h_ref, o_ref, p_ref, y_ref,
    local, sg, rg, sa, ra, sv, rv, ss, rs, fs, fr,
):
    dp, me = lax.axis_index("dp"), lax.axis_index("ctx")
    half, parity, pair, partner, ahead, behind = pairs_of(n, me)
    count, mine, place = group_of(n_dp, n, dp, me)
    greet_all(n_dp, n, dp, me)
    owns = [
        pltpu.make_async_copy(g_ref.at[mine], h_ref.at[mine], local.at[0]),
        pltpu.make_async_copy(w_ref.at[me], o_ref.at[me], local.at[1]),
        pltpu.make_async_copy(x_ref, y_ref.at[me], local.at[2]),
        pltpu.make_async_copy(v_ref.at[me], p_ref.at[me], local.at[3]),
    ]
    sends, receives = swap(g_ref, h_ref, sg, rg, count, mine, place)
    for src, dst, send, recv in ((w_ref, o_ref, sa, ra), (v_ref, p_ref, sv, rv)):
        more, waits = swap(src, dst, send, recv, n, me, lambda c: (dp, c))
        sends += more
        receives += waits
    gathers = [
        remote(x_ref, y_ref.at[me], ss.at[k], rs.at[k], (dp, a))
        for k, a in enumerate(ahead + [partner])
    ]
    for copy in gathers + owns:
        copy.start()
    forwards = []
    for k, b in enumerate(behind):
        remote(x_ref, y_ref.at[b], ss.at[k], rs.at[k], (dp, b)).wait_recv()
        forward = remote(y_ref.at[b], y_ref.at[b], fs.at[k], fr.at[k], (dp, partner))
        forward.start()
        forwards.append(forward)
    gathers[-1].wait_recv()
    for copy in receives:
        copy.wait_recv()
    for forward in forwards:
        forward.wait()
    for copy in sends + gathers:
        copy.wait_send()
    for copy in owns:
        copy.wait()


def start(g, w, v, x, number):
    n_dp, n = lax.axis_size("dp"), lax.axis_size("ctx")
    half = n // 2
    dma = pltpu.SemaphoreType.DMA
    g_out, w_out, v_out, x_all = pl.pallas_call(
        functools.partial(start_kernel, n_dp, n),
        out_shape=(
            jax.ShapeDtypeStruct(g.shape, g.dtype),
            jax.ShapeDtypeStruct(w.shape, w.dtype),
            jax.ShapeDtypeStruct(v.shape, v.dtype),
            jax.ShapeDtypeStruct((n,) + x.shape, x.dtype),
        ),
        in_specs=[ANY] * 4,
        out_specs=(ANY,) * 4,
        scratch_shapes=[dma((4,))]
        + [dma((2 * n_dp - 1,))] * 2
        + [dma((n - 1,))] * 4
        + [dma((half,))] * 2
        + [dma((half - 1,))] * 2,
        compiler_params=params_of(number),
        cost_estimate=cost(45),
        name="start",
    )(g, w, v, x)
    return g_out, w_out, v_out, x_all.reshape(-1, x.shape[-1])


def collect_kernel(
    n_dp, n, g_ref, h_ref, a_ref, w_ref, o_ref, h_out, y_ref,
    own, co_ref, pa, qa, pb, qb, local, sw, rw, s1, r1, s2, r2, sh, rh,
):
    dp, me = lax.axis_index("dp"), lax.axis_index("ctx")
    tall = own.shape[0]
    count, index, place = group_of(n_dp, n, dp, me)
    greet_all(n_dp, n, dp, me)
    gives = slab_give(n_dp, dp, me, g_ref, co_ref, sw, rw)
    swaps, receives = swap(h_ref, h_out, sh, rh, count, index, place)
    mine = g_ref.at[pl.ds(pl.multiple_of(dp * tall, tall), tall), :]
    stays = [
        pltpu.make_async_copy(mine, own, local.at[0]),
        pltpu.make_async_copy(h_ref.at[index], h_out.at[index], local.at[1]),
    ]
    for copy in stays:
        copy.start()
    cols = slice(0, a_ref.shape[1])
    sums = reduce_ctx(n, dp, me, a_ref, w_ref, cols, y_ref, pa, qa, pb, qb, s1, r1, s2, r2)
    for copy in stays:
        copy.wait()
    for copy in gives:
        copy.wait_recv()

    def add(part):
        total = own[part, :].astype(F32)
        for k in range(n_dp - 1):
            total = total + co_ref[k, part, :].astype(F32)
        o_ref[part, :] = total.astype(BF)

    tiles(tall, 64, add)
    for copy in receives:
        copy.wait_recv()
    for copy in gives + swaps + sums:
        copy.wait_send()


def collect(g, h, a, w, number):
    n_dp, n = lax.axis_size("dp"), lax.axis_size("ctx")
    tall, width = g.shape[0] // n_dp, g.shape[1]
    half, length, features = n // 2, a.shape[0] // n, w.shape[0]
    dma = pltpu.SemaphoreType.DMA
    return pl.pallas_call(
        functools.partial(collect_kernel, n_dp, n),
        out_shape=(
            jax.ShapeDtypeStruct((tall, width), BF),
            jax.ShapeDtypeStruct(h.shape, BF),
            jax.ShapeDtypeStruct((length, features), F32),
        ),
        in_specs=[ANY, ANY, VMEM, VMEM],
        out_specs=(VMEM, ANY, VMEM),
        scratch_shapes=[
            pltpu.VMEM((tall, width), BF),
            pltpu.VMEM((n_dp - 1, tall, width), BF),
            pltpu.VMEM((half, length, features), BF),
            pltpu.VMEM((half, length, features), BF),
            pltpu.VMEM((half - 1, length, features), BF),
            pltpu.VMEM((half - 1, length, features), BF),
            dma((2,)),
            dma((n_dp - 1,)),
            dma((n_dp - 1,)),
            dma((half,)),
            dma((half,)),
            dma((half - 1,)),
            dma((half - 1,)),
            dma((2 * n_dp - 1,)),
            dma((2 * n_dp - 1,)),
        ],
        compiler_params=params_of(number),
        cost_estimate=cost(70),
        name="collect",
    )(g, h, a, w)


def total_kernel(
    n_dp, n, qk_ref, wv_ref, wo_ref, u_ref, gg_ref, gd_ref, gain_ref, ga_ref, gu_ref, o_ref,
    sb, mine, buf, part, all_parts, local, sx, rx, sh, rh, ss, rs, st, rt,
):
    dp, me = lax.axis_index("dp"), lax.axis_index("ctx")
    gain_rows = gain_ref.shape[0]
    hc = wv_ref.shape[2]
    count, index, place = group_of(n_dp, n, dp, me)
    greet_all(n_dp, n, dp, me)
    swaps, receives = swap(u_ref, gu_ref, sh, rh, count, index, place)
    stay = pltpu.make_async_copy(u_ref.at[index], gu_ref.at[index], local)
    stay.start()
    sb[:, :, : 2 * hc] = qk_ref[...]
    sb[:, :, 2 * hc : 3 * hc] = wv_ref[...]
    sb[:, :, 3 * hc :] = wo_ref[...]
    more, waits = swap(sb, ga_ref, sx, rx, n, me, lambda c: (dp, c))
    ga_ref[me] = sb[me]

    def squares(ref):
        acc = jnp.zeros((ref.shape[1], ref.shape[2]), F32)
        for i in range(ref.shape[0]):
            block = ref[i].astype(F32)
            acc += block * block
        return jnp.sum(jnp.sum(acc, axis=0, keepdims=True), axis=1, keepdims=True)

    total = squares(gg_ref) + squares(gd_ref)
    for copy in waits:
        copy.wait_recv()
    total += squares(ga_ref)
    for copy in receives:
        copy.wait_recv()
    stay.wait()
    total += squares(gu_ref)
    mine[0:gain_rows, :] = gain_ref[...]
    mine[gain_rows:, :] = jnp.broadcast_to(total, (8, 128))
    copies = swaps + more
    for k in range(1, n):
        copy = remote(mine, buf.at[me], ss.at[k - 1], rs.at[k - 1], (dp, (me + k) % n))
        copy.start()
        copies.append(copy)
    buf[me] = mine[...]
    for k in range(1, n):
        source = (me + n - k) % n
        remote(mine, buf.at[source], ss.at[k - 1], rs.at[k - 1], (dp, source)).wait_recv()
    acc = buf[0]
    for j in range(1, n):
        acc = acc + buf[j]
    part[...] = acc
    all_parts[dp] = acc
    for k in range(1, n_dp):
        copy = remote(part, all_parts.at[dp], st.at[k - 1], rt.at[k - 1], ((dp + k) % n_dp, me))
        copy.start()
        copies.append(copy)
    for k in range(1, n_dp):
        source = (dp + n_dp - k) % n_dp
        remote(part, all_parts.at[source], st.at[k - 1], rt.at[k - 1], (source, me)).wait_recv()
    acc = all_parts[0]
    for j in range(1, n_dp):
        acc = acc + all_parts[j]
    o_ref[...] = acc
    for copy in copies:
        copy.wait_send()


def total_over(qk, wv, wo, u, gg, gd, gain_part, number):
    n_dp, n = lax.axis_size("dp"), lax.axis_size("ctx")
    rows, hc = qk.shape[0] // n, wv.shape[1]
    gain_rows = gain_part.size // 128
    shape = (gain_rows + 8, 128)
    dma = pltpu.SemaphoreType.DMA
    ga, gu, out = pl.pallas_call(
        functools.partial(total_kernel, n_dp, n),
        out_shape=(
            jax.ShapeDtypeStruct((n, rows, 4 * hc), BF),
            jax.ShapeDtypeStruct(u.shape, BF),
            jax.ShapeDtypeStruct(shape, F32),
        ),
        in_specs=[VMEM] * 3 + [ANY] + [VMEM] * 3,
        out_specs=(VMEM,) * 3,
        scratch_shapes=[
            pltpu.VMEM((n, rows, 4 * hc), BF),
            pltpu.VMEM(shape, F32),
            pltpu.VMEM((n,) + shape, F32),
            pltpu.VMEM(shape, F32),
            pltpu.VMEM((n_dp,) + shape, F32),
            dma,
            dma((n - 1,)),
            dma((n - 1,)),
            dma((2 * n_dp - 1,)),
            dma((2 * n_dp - 1,)),
            dma((n - 1,)),
            dma((n - 1,)),
            dma((n_dp - 1,)),
            dma((n_dp - 1,)),
        ],
        compiler_params=params_of(number),
        cost_estimate=cost(35),
        name="total",
    )(
        qk.reshape(n, rows, 2 * hc),
        wv.reshape(n, rows, hc),
        wo.reshape(n, rows, hc),
        u,
        gg,
        gd,
        gain_part.reshape(gain_rows, 128),
    )
    return ga, gu, out[gain_rows, 0], out[:gain_rows].reshape(gain_part.shape)


def adam_kernel(factor_ref, p_ref, m_ref, v_ref, ga_ref, gg_ref, gu_ref, gd_ref, po_ref, mo_ref, vo_ref, g_ref):
    part = pl.program_id(0)
    n, _, four = ga_ref.shape
    hc = four // 4
    fs = gd_ref.shape[2]

    @pl.when(part == 0)
    def _():
        for matrix in range(4):
            for c in range(n):
                start = (matrix * n + c) * hc
                g_ref[:, start : start + hc] = ga_ref[c, :, matrix * hc : (matrix + 1) * hc].astype(F32)

    for index, ref in ((1, gg_ref), (2, gu_ref), (3, gd_ref)):

        @pl.when(part == index)
        def _():
            for d in range(ref.shape[0]):
                g_ref[:, d * fs : (d + 1) * fs] = ref[d].astype(F32)

    clipped = g_ref[...] * factor_ref[0, 0]
    new_m = BETA1 * m_ref[...] + (1.0 - BETA1) * clipped
    new_v = BETA2 * v_ref[...] + (1.0 - BETA2) * (clipped * clipped)
    root = jnp.sqrt(new_v * (1.0 / (1.0 - BETA2**STEP))) + ADAM_EPS
    po_ref[...] = p_ref[...] * (1.0 - RATE * DECAY) - (new_m * (RATE / (1.0 - BETA1**STEP))) / root
    mo_ref[...] = new_m
    vo_ref[...] = new_v


def adam(factor, params, first, second, ga, gg, gu, gd):
    rows, columns = params.shape
    n, n_dp, fs = ga.shape[0], gd.shape[0], gd.shape[2]
    block = min(rows, 16)
    steps = rows // block
    wide = pl.BlockSpec((block, columns // 4), lambda i, r: (r, i))
    return pl.pallas_call(
        adam_kernel,
        grid=(4, steps),
        out_shape=(jax.ShapeDtypeStruct(params.shape, F32),) * 3,
        in_specs=[
            pl.BlockSpec(memory_space=pltpu.SMEM),
            wide,
            wide,
            wide,
            pl.BlockSpec((n, block, ga.shape[2]), lambda i, r: (0, jnp.where(i == 0, r, steps - 1), 0)),
            *[
                pl.BlockSpec(
                    (n_dp, block, fs),
                    lambda i, r, part=part: (
                        0,
                        jnp.where(i < part, 0, jnp.where(i == part, r, steps - 1)),
                        0,
                    ),
                )
                for part in (1, 2, 3)
            ],
        ],
        out_specs=(wide, wide, wide),
        scratch_shapes=[pltpu.VMEM((block, columns // 4), F32)],
        compiler_params=pltpu.CompilerParams(vmem_limit_bytes=48 * 1024 * 1024),
        name="adam",
    )(factor.reshape(1, 1), params, first, second, ga, gg, gu, gd)


def arrange_kernel(n, count, p_ref, a_ref, o_ref, g_ref, d_ref):
    part = pl.program_id(0)
    hc = o_ref.shape[2]
    fs = d_ref.shape[2]

    @pl.when(part == 0)
    def _():
        for matrix in range(4):
            for c in range(n):
                start = (matrix * n + c) * hc
                value = p_ref[:, start : start + hc].astype(BF)
                if matrix < 3:
                    a_ref[c, :, matrix * hc : (matrix + 1) * hc] = value
                else:
                    o_ref[c] = value

    for index, ref, first in ((1, g_ref, 0), (2, g_ref, fs), (3, d_ref, 0)):

        @pl.when(part == index)
        def _():
            for d in range(count):
                ref[d, :, first : first + fs] = p_ref[:, d * fs : (d + 1) * fs].astype(BF)


def arrange(params, width):
    count, n = 2 * lax.axis_size("dp"), lax.axis_size("ctx")
    rows, columns = params.shape
    fs, hc = columns // 4 // count, width // n
    whole = lambda shape: pl.BlockSpec(shape, lambda i: (0,) * len(shape))
    shapes = [(n, rows, 3 * hc), (n, rows, hc), (count, rows, 2 * fs), (count, rows, fs)]
    return pl.pallas_call(
        functools.partial(arrange_kernel, n, count),
        grid=(4,),
        out_shape=tuple(jax.ShapeDtypeStruct(s, BF) for s in shapes),
        in_specs=[pl.BlockSpec((rows, columns // 4), lambda i: (0, i))],
        out_specs=tuple(whole(s) for s in shapes),
        compiler_params=pltpu.CompilerParams(vmem_limit_bytes=48 * 1024 * 1024),
        name="arrange",
    )(params)


def row_sums(value, row):
    pick = lax.broadcasted_iota(jnp.int32, (8, value.shape[1]), 0) == row
    return lax.dot_general(
        pick.astype(F32),
        value,
        (((1,), (1,)), ((), ())),
        preferred_element_type=F32,
        precision=lax.Precision.HIGHEST,
    )


def exchange(n, dp, me, buf, ss, rs):
    copies = []
    for k in range(1, n):
        copy = remote(buf.at[me], buf.at[me], ss.at[k - 1], rs.at[k - 1], (dp, (me + k) % n))
        copy.start()
        copies.append(copy)
    for k in range(1, n):
        source = (me + n - k) % n
        remote(buf.at[me], buf.at[source], ss.at[k - 1], rs.at[k - 1], (dp, source)).wait_recv()
    total = buf[0]
    for j in range(1, n):
        total = total + buf[j]
    for copy in copies:
        copy.wait_send()
    return total


def turn(value, cos, sine):
    return value * cos + pltpu.roll(value, HD // 2, 1) * sine


def mask_of(rows, info_col, info_row):
    pos_i, doc_i = info_col[rows, 0:1], info_col[rows, 1:2]
    return (info_row[1:2, :] == doc_i) & (info_row[0:1, :] <= pos_i)


def attend_kernel(
    n_dp, n, x_ref, w_ref, wo_ref, d_ref, t_ref, norm_ref, gain_ref, cos_ref, sin_ref, col_ref, row_ref,
    y_ref, h_ref, q_ref, k_ref, v_ref, o_ref, pre_ref, scale_ref, lse_ref, wo_all, d_out,
    buf, pa, qa, pb, qb, ss, rs, s1, r1, s2, r2, sw, rw, sd, rd, local,
):
    dp, me = lax.axis_index("dp"), lax.axis_index("ctx")
    seq, width = x_ref.shape
    hc = o_ref.shape[1]
    block = min(seq, 256)
    count, mine, place = group_of(n_dp, n, dp, me)
    greet_all(n_dp, n, dp, me)
    piece = wo_ref.shape[0]

    def part_of(d):
        return wo_all.at[pl.ds(pl.multiple_of(d * piece, piece), piece), :]

    owns = [
        pltpu.make_async_copy(wo_ref, part_of(dp), local.at[0]),
        pltpu.make_async_copy(d_ref.at[mine], d_out.at[mine], local.at[1]),
    ]
    behind_wo = [
        remote(wo_ref, part_of(dp), sw.at[k - 1], rw.at[k - 1], ((dp + k) % n_dp, me))
        for k in range(1, n_dp)
    ]
    for copy in behind_wo + owns:
        copy.start()
    behind_d, receives = swap(d_ref, d_out, sd, rd, count, mine, place)

    @pl.loop(0, seq // block)
    def _(i):
        rows = pl.ds(pl.multiple_of(i * block, block), block)
        value = dot(x_ref[rows, :], w_ref[...])
        pre_ref[rows, :] = value[:, : 2 * hc]
        v_ref[rows, :] = value[:, 2 * hc :].astype(BF)
        squares = value[:, : 2 * hc] * value[:, : 2 * hc]
        buf[me, :, rows] = row_sums(squares[:, :hc], 0) + row_sums(squares[:, hc:], 1)

    scale_ref[...] = jnp.transpose(lax.rsqrt(exchange(n, dp, me, buf, ss, rs) / width + EPS))

    @pl.loop(0, seq // block)
    def _(i):
        rows = pl.ds(pl.multiple_of(i * block, block), block)
        cos, sine = cos_ref[rows, :], sin_ref[rows, :]
        for which, ref, factor in ((0, q_ref, HD ** (-0.5)), (1, k_ref, 1.0)):
            scale = scale_ref[rows, which : which + 1]
            for start in range(0, hc, HD):
                part = slice(start, start + HD)
                value = pre_ref[rows, which * hc + start : which * hc + start + HD] * scale
                ref[rows, part] = (
                    turn(value * gain_ref[which : which + 1, part], cos, sine) * factor
                ).astype(BF)

    @pl.loop(0, seq // block)
    def _(i):
        rows = pl.ds(pl.multiple_of(i * block, block), block)
        visible = mask_of(rows, col_ref, row_ref)
        for head in range(hc // HD):
            part = slice(head * HD, (head + 1) * HD)
            scores = jnp.where(visible, dot_t(q_ref[rows, part], k_ref[:, part]), -jnp.inf)
            top = jnp.max(scores, axis=1, keepdims=True)
            weights = jnp.exp(scores - top)
            total = jnp.sum(weights, axis=1, keepdims=True)
            o_ref[rows, part] = (dot(weights.astype(BF), v_ref[:, part]) / total).astype(BF)
            lse_ref[rows, head : head + 1] = top + jnp.log(total)

    owns[0].wait()
    for k in range(1, n_dp):
        source = (dp + n_dp - k) % n_dp
        remote(wo_ref, part_of(source), sw.at[k - 1], rw.at[k - 1], (source, me)).wait_recv()
    cols = slice(0, hc)
    sums = reduce_ctx(n, dp, me, o_ref, wo_all, cols, y_ref, pa, qa, pb, qb, s1, r1, s2, r2)

    def finish(rows):
        branch = y_ref[rows, :]
        h_ref[rows, :] = t_ref[rows, :].astype(F32) + branch * rms_scale(branch) * norm_ref[...]

    tiles(y_ref.shape[0], 16, finish)
    for copy in receives:
        copy.wait_recv()
    for copy in sums + behind_wo + behind_d:
        copy.wait_send()
    owns[1].wait()


def attend(x_all, w, wo, d, tokens, norm, gain, cos, sine, info_col, info_row, number):
    n_dp, n = lax.axis_size("dp"), lax.axis_size("ctx")
    seq, width = x_all.shape
    half, length, hc = n // 2, seq // n, w.shape[1] // 3
    dma = pltpu.SemaphoreType.DMA
    low = jax.ShapeDtypeStruct((seq, hc), BF)
    return pl.pallas_call(
        functools.partial(attend_kernel, n_dp, n),
        out_shape=(
            jax.ShapeDtypeStruct((length, width), F32),
            jax.ShapeDtypeStruct((length, width), F32),
            low,
            low,
            low,
            low,
            jax.ShapeDtypeStruct((seq, 2 * hc), F32),
            jax.ShapeDtypeStruct((seq, 8), F32),
            jax.ShapeDtypeStruct((seq, 8), F32),
            jax.ShapeDtypeStruct((width, hc), BF),
            jax.ShapeDtypeStruct(d.shape, BF),
        ),
        in_specs=[VMEM] * 2 + [ANY] * 2 + [VMEM] * 7,
        out_specs=(VMEM,) * 10 + (ANY,),
        scratch_shapes=[
            pltpu.VMEM((n, 8, seq), F32),
            pltpu.VMEM((half, length, width), BF),
            pltpu.VMEM((half, length, width), BF),
            pltpu.VMEM((half - 1, length, width), BF),
            pltpu.VMEM((half - 1, length, width), BF),
            dma((n - 1,)),
            dma((n - 1,)),
            dma((half,)),
            dma((half,)),
            dma((half - 1,)),
            dma((half - 1,)),
            dma((n_dp - 1,)),
            dma((n_dp - 1,)),
            dma((2 * n_dp - 1,)),
            dma((2 * n_dp - 1,)),
            dma((2,)),
        ],
        compiler_params=params_of(number),
        cost_estimate=cost(60),
        name="attend",
    )(x_all, w, wo, d, tokens, norm, gain, cos, sine, info_col, info_row)


def slab_give(n_dp, dp, me, g_ref, co_ref, sw, rw):
    tall = co_ref.shape[1]
    gives = []
    for k in range(1, n_dp):
        to = (dp + k) % n_dp
        part = pl.ds(pl.multiple_of(to * tall, tall), tall)
        copy = remote(g_ref.at[part, :], co_ref.at[k - 1], sw.at[k - 1], rw.at[k - 1], (to, me))
        copy.start()
        gives.append(copy)
    return gives


def slab_sum(dp, gives, g_ref, co_ref, out_ref):
    tall = co_ref.shape[1]
    total = g_ref[pl.ds(pl.multiple_of(dp * tall, tall), tall), :].astype(F32)
    for k, copy in enumerate(gives):
        copy.wait_recv()
        total = total + co_ref[k].astype(F32)
    out_ref[...] = total.astype(BF)


def greet_wide_group(n_dp, dp, me):
    partner = me + 1 - 2 * (me % 2)
    others = [(dp + k) % n_dp for k in range(1, n_dp)]
    greet([(dp, partner)] + [(d, c) for d in others for c in (me, partner)])


def attend_back_kernel(
    n_dp, n, e_ref, w_ref, h_ref, o_ref, col_ref, row_ref, q_ref, k_ref, v_ref, lse_ref,
    dq_ref, dk_ref, dv_ref, h_out, wo_ref,
    go_ref, co_ref, do_ref, sh, rh, local, sw, rw,
):
    dp, me = lax.axis_index("dp"), lax.axis_index("ctx")
    seq, hc = q_ref.shape
    width = e_ref.shape[1]
    block = min(seq, 256)
    count, index, place = group_of(n_dp, n, dp, me)
    greet_wide_group(n_dp, dp, me)
    swaps, receives = swap(h_ref, h_out, sh, rh, count, index, place)
    stay = pltpu.make_async_copy(h_ref.at[index], h_out.at[index], local)
    stay.start()

    def product(part):
        go_ref[part, :] = t_dot(e_ref[:, part], o_ref[...]).astype(BF)

    tiles(width, 256, product)
    gives = slab_give(n_dp, dp, me, go_ref, co_ref, sw, rw)

    def project(rows):
        do_ref[rows, :] = dot(e_ref[rows, :], w_ref[...]).astype(BF)

    tiles(seq, block, project)
    dk_ref[...] = jnp.zeros_like(dk_ref)
    dv_ref[...] = jnp.zeros_like(dv_ref)

    @pl.loop(0, seq // block)
    def _(i):
        rows = pl.ds(pl.multiple_of(i * block, block), block)
        visible = mask_of(rows, col_ref, row_ref)
        for head in range(hc // HD):
            part = slice(head * HD, (head + 1) * HD)
            query, key, value, back = q_ref[rows, part], k_ref[:, part], v_ref[:, part], do_ref[rows, part]
            scores = jnp.where(visible, dot_t(query, key), -jnp.inf)
            probs = jnp.exp(scores - lse_ref[rows, head : head + 1])
            d_probs = dot_t(back, value)
            delta = jnp.sum(probs * d_probs, axis=1, keepdims=True)
            d_scores = (probs * (d_probs - delta)).astype(BF)
            dq_ref[rows, part] = dot(d_scores, key)
            dk_ref[:, part] += t_dot(d_scores, query)
            dv_ref[:, part] += t_dot(probs.astype(BF), back)

    slab_sum(dp, gives, go_ref, co_ref, wo_ref)
    for copy in receives:
        copy.wait_recv()
    for copy in swaps + gives:
        copy.wait_send()
    stay.wait()


def attend_back(e, w, h, o, info_col, info_row, q, k, v, lse, number):
    n_dp, n = lax.axis_size("dp"), lax.axis_size("ctx")
    (seq, hc), width = q.shape, e.shape[1]
    dma = pltpu.SemaphoreType.DMA
    return pl.pallas_call(
        functools.partial(attend_back_kernel, n_dp, n),
        out_shape=(
            *[jax.ShapeDtypeStruct((seq, hc), F32)] * 3,
            jax.ShapeDtypeStruct(h.shape, BF),
            jax.ShapeDtypeStruct((width // n_dp, hc), BF),
        ),
        in_specs=[VMEM, VMEM, ANY] + [VMEM] * 7,
        out_specs=(VMEM, VMEM, VMEM, ANY, VMEM),
        scratch_shapes=[
            pltpu.VMEM((width, hc), BF),
            pltpu.VMEM((n_dp - 1, width // n_dp, hc), BF),
            pltpu.VMEM((seq, hc), BF),
            dma((2 * n_dp - 1,)),
            dma((2 * n_dp - 1,)),
            dma,
            dma((n_dp - 1,)),
            dma((n_dp - 1,)),
        ],
        compiler_params=params_of(number),
        cost_estimate=cost(45),
        name="attend_back",
    )(e, w, h, o, info_col, info_row, q, k, v, lse)


def project_back_kernel(
    n_dp, n, dq_in, dk_in, dv_ref, x_ref, gain_ref, cos_ref, sin_ref, pre_ref, scale_ref,
    d_ref, gain_out, g_ref, wv_ref,
    dq_ref, dk_ref, mean_ref, buf, go_ref, co_ref, ss, rs, sw, rw,
):
    dp, me = lax.axis_index("dp"), lax.axis_index("ctx")
    seq, hc = dv_ref.shape
    width = x_ref.shape[1]
    block = min(seq, 256)
    greet(
        [(dp, (me + k) % n) for k in range(1, n)] + [((dp + k) % n_dp, me) for k in range(1, n_dp)]
    )
    d_ref[:, 2 * hc :] = dv_ref[...].astype(BF)

    def values(part):
        go_ref[part, :] = t_dot(x_ref[:, part], d_ref[:, 2 * hc :]).astype(BF)

    tiles(width, 256, values)
    gives = slab_give(n_dp, dp, me, go_ref, co_ref, sw, rw)
    gain_out[...] = jnp.zeros_like(gain_out)

    @pl.loop(0, seq // block)
    def _(i):
        rows = pl.ds(pl.multiple_of(i * block, block), block)
        cos, sine = cos_ref[rows, :], sin_ref[rows, :]
        sums = jnp.zeros((8, block), F32)
        for which, source, ref, factor in (
            (0, dq_in, dq_ref, HD ** (-0.5)),
            (1, dk_in, dk_ref, 1.0),
        ):
            scale = scale_ref[rows, which : which + 1]
            for start in range(0, hc, HD):
                part = slice(start, start + HD)
                pre = pre_ref[rows, which * hc + start : which * hc + start + HD]
                value = turn(source[rows, part] * factor, cos, -sine)
                gain_out[which : which + 1, part] += jnp.sum(value * pre * scale, axis=0, keepdims=True)
                value = value * gain_ref[which : which + 1, part]
                ref[rows, part] = value
                sums += row_sums(value * pre, which)
        buf[me, :, rows] = sums

    mean_ref[...] = jnp.transpose(exchange(n, dp, me, buf, ss, rs) / width)

    @pl.loop(0, seq // block)
    def _(i):
        rows = pl.ds(pl.multiple_of(i * block, block), block)
        for which, ref in ((0, dq_ref), (1, dk_ref)):
            scale = scale_ref[rows, which : which + 1]
            mean = mean_ref[rows, which : which + 1]
            cols = slice(which * hc, (which + 1) * hc)
            value = scale * (ref[rows, :] - pre_ref[rows, cols] * (scale * scale * mean))
            d_ref[rows, cols] = value.astype(BF)

    def product(part):
        g_ref[part, :] = t_dot(x_ref[:, part], d_ref[:, : 2 * hc]).astype(BF)

    tiles(width, 256, product)
    slab_sum(dp, gives, go_ref, co_ref, wv_ref)
    for copy in gives:
        copy.wait_send()


def project_back(dq, dk, dv, x, gain, cos, sine, pre, scale, number):
    n_dp, n = lax.axis_size("dp"), lax.axis_size("ctx")
    (seq, hc), width = dq.shape, x.shape[1]
    dma = pltpu.SemaphoreType.DMA
    return pl.pallas_call(
        functools.partial(project_back_kernel, n_dp, n),
        out_shape=(
            jax.ShapeDtypeStruct((seq, 3 * hc), BF),
            jax.ShapeDtypeStruct((2, hc), F32),
            jax.ShapeDtypeStruct((width, 2 * hc), BF),
            jax.ShapeDtypeStruct((width // n_dp, hc), BF),
        ),
        in_specs=[VMEM] * 9,
        out_specs=(VMEM,) * 4,
        scratch_shapes=[
            pltpu.VMEM((seq, hc), F32),
            pltpu.VMEM((seq, hc), F32),
            pltpu.VMEM((seq, 8), F32),
            pltpu.VMEM((n, 8, seq), F32),
            pltpu.VMEM((width, hc), BF),
            pltpu.VMEM((n_dp - 1, width // n_dp, hc), BF),
            dma((n - 1,)),
            dma((n - 1,)),
            dma((n_dp - 1,)),
            dma((n_dp - 1,)),
        ],
        compiler_params=params_of(number),
        cost_estimate=cost(30),
        name="project_back",
    )(dq, dk, dv, x, gain, cos, sine, pre, scale)


def shards(
    inputs,
    cotangent,
    documents,
    block_place,
    params,
    first_moment,
    second_moment,
    gains,
    gains_first,
    gains_second,
):
    tokens = inputs[0]
    upstream = cotangent[0]
    length, width = tokens.shape
    n_ctx = lax.axis_size("ctx")
    n_dp = lax.axis_size("dp")
    me_ctx = lax.axis_index("ctx")
    seq = length * n_ctx
    rows = params.shape[0]
    ff = (params.shape[1] - 4 * width) // 3
    hc = width // n_ctx
    half, group = n_ctx // 2, 2 * n_dp
    fh = ff // group
    parities = [[2 * p + side for p in range(half)] for side in range(2)]

    def gather_pairs(w):
        w = lax.all_gather(
            w.reshape(group * rows, w.shape[2]), "ctx", axis=0, tiled=True, axis_index_groups=parities
        )
        return w.reshape(half, n_dp, 2 * rows, w.shape[1])

    def scatter_pairs(g):
        g = lax.psum_scatter(
            g.reshape(width, g.shape[3]),
            "ctx",
            scatter_dimension=0,
            tiled=True,
            axis_index_groups=parities,
        )
        return g.reshape(group, rows, g.shape[1])

    w_qkv, w_o, w_gu, w_d = arrange(params, width)
    w_gu, w_qkv, w_o, x_all = start(w_gu, w_qkv, w_o, tokens, 1)
    w_gu = gather_pairs(w_gu)
    w_qkv = gather_dp(w_qkv.reshape(n_ctx * rows, 3 * hc), 2)

    indices = jnp.arange(seq, dtype=jnp.int32)
    owners = indices // length
    placed = jnp.sum(
        jnp.where(
            owners[:, None] == jnp.arange(n_ctx, dtype=jnp.int32)[None, :], block_place[None, :], 0
        ),
        axis=1,
    )
    pos = placed * length + indices % length
    docs = documents[0]
    info_row = jnp.concatenate([pos[None], docs[None], jnp.zeros((6, seq), jnp.int32)])
    info_col = info_row.T
    cos_tab, sine_tab = rope_tables(pos, HD)
    cos_tab = jnp.concatenate([cos_tab, cos_tab], axis=1)
    sine_tab = jnp.concatenate([-sine_tab, sine_tab], axis=1)
    my_gains = lax.dynamic_slice_in_dim(gains[:2], me_ctx * hc, hc, axis=1)
    tables = (my_gains, cos_tab, sine_tab, info_col, info_row)

    branch, hidden1, queries, keys, values, attn_low, qk_pre, scales, lse, w_o, w_d = attend(
        x_all, w_qkv, w_o.reshape(n_ctx * rows, hc), w_d, tokens, gains[2:3], *tables, 3
    )

    result, d_mlp, g_ff_part, h1_all, gate_up, inner, w_d = ff_forward(
        hidden1, upstream, gains[3:4], w_gu, w_d.reshape(n_dp, 2 * rows, fh), 4
    )
    d_gu, d_grad = ff_back(d_mlp, inner, w_d, gate_up, rows, 5)
    d_grad = scatter_pairs(d_grad)
    d_h1, d_branch_all, g_attn_part, g_grad, u_grad = ff_scatter(
        d_gu, w_gu, h1_all, upstream, branch, gains[2:3], 6
    )
    g_grad, u_grad = scatter_pairs(g_grad), scatter_pairs(u_grad)

    d_query, d_key, d_value, d_grad, wo_grad = attend_back(
        d_branch_all, w_o, d_grad, attn_low, info_col, info_row, queries, keys, values, lse, 8
    )
    d_qkv, d_gain, qk_grad, wv_grad = project_back(
        d_query, d_key, d_value, x_all, my_gains, cos_tab, sine_tab, qk_pre, scales, 10
    )
    qk_grad, g_grad, d_x = collect(qk_grad, g_grad, d_qkv, w_qkv, 9)
    d_input = d_h1 + d_x

    gain_part = jnp.concatenate(
        [
            lax.dynamic_update_slice(jnp.zeros((2, width), F32), d_gain, (0, me_ctx * hc)),
            g_attn_part,
            g_ff_part,
        ],
        axis=0,
    )
    attn_grad, u_grad, square_total, gain_total = total_over(
        qk_grad, wv_grad, wo_grad, u_grad, g_grad, d_grad, gain_part, 11
    )
    grad_norm = jnp.sqrt(square_total + jnp.sum(gain_total * gain_total))
    factor = CLIP / (grad_norm + 1e-06)
    new_params, new_first, new_second = adam(
        factor, params, first_moment, second_moment, attn_grad, g_grad, u_grad, d_grad
    )
    new_gains, new_gains_first, new_gains_second = adam_update(
        gains, gains_first, gains_second, gain_total * factor, GAIN_RATE, 0.0
    )
    return (
        result[None],
        d_input.astype(BF)[None],
        grad_norm,
        new_params,
        new_first,
        new_second,
        new_gains,
        new_gains_first,
        new_gains_second,
    )


def solution(mesh):
    split, whole = P("dp", "ctx", None), P(("dp", "ctx"), None)
    return jax.shard_map(
        shards,
        mesh=mesh,
        in_specs=(split, split, P("dp", None), P(), whole, whole, whole, P(), P(), P()),
        out_specs=(split, split, P(), whole, whole, whole, P(), P(), P()),
        check_vma=False,
    )
```

```python
import functools

import jax
import jax.numpy as jnp
from jax import lax
from jax.experimental import pallas as pl
from jax.experimental.pallas import tpu as pltpu
from jax.sharding import PartitionSpec as P

HD = 128
STEP = 10
EPS = 1e-06
THETA = 500000.0
CLIP = 1.0
BETA1 = 0.9
BETA2 = 0.95
RATE = 0.03
GAIN_RATE = 0.8
DECAY = 0.1
ADAM_EPS = 1e-08
BF = jnp.bfloat16
F32 = jnp.float32
MESH = pl.DeviceIdType.MESH
ANY = pl.BlockSpec(memory_space=pl.ANY)
VMEM = pl.BlockSpec(memory_space=pltpu.VMEM)


def rms_scale(values):
    return lax.rsqrt(jnp.mean(values * values, axis=-1, keepdims=True) + EPS)


def norm_back(upstream, source, scale):
    return scale * (
        upstream - source * scale * scale * jnp.mean(upstream * source, axis=-1, keepdims=True)
    )


def rope_tables(positions, head_size):
    half_size = head_size // 2
    freqs = THETA ** (-jnp.arange(half_size, dtype=jnp.float32) * 2.0 / head_size)
    angles = positions.astype(jnp.float32)[:, None] * freqs[None, :]
    return (jnp.cos(angles), jnp.sin(angles))


def adam_update(weight, first_in, second_in, clipped, rate, decay):
    new_first = BETA1 * first_in + (1.0 - BETA1) * clipped
    new_second = BETA2 * second_in + (1.0 - BETA2) * clipped * clipped
    first_hat = new_first / (1.0 - BETA1**STEP)
    second_hat = new_second / (1.0 - BETA2**STEP)
    new_weight = weight - rate * (first_hat / (jnp.sqrt(second_hat) + ADAM_EPS) + decay * weight)
    return (new_weight, new_first, new_second)


def dot(a, b):
    return jnp.dot(a, b, preferred_element_type=F32)


def dot_t(a, b):
    return lax.dot_general(a, b, (((1,), (1,)), ((), ())), preferred_element_type=F32)


def t_dot(a, b):
    return lax.dot_general(a, b, (((0,), (0,)), ((), ())), preferred_element_type=F32)


def greet(peers):
    barrier = pltpu.get_barrier_semaphore()
    for peer in peers:
        pl.semaphore_signal(barrier, inc=1, device_id=peer, device_id_type=MESH)
    pl.semaphore_wait(barrier, len(peers))


def remote(src, dst, send, recv, peer):
    return pltpu.make_async_remote_copy(
        src_ref=src, dst_ref=dst, send_sem=send, recv_sem=recv, device_id=peer, device_id_type=MESH
    )


def cost(us):
    return pl.CostEstimate(flops=0, bytes_accessed=us * 3_600_000, transcendentals=0)


def params_of(number, vmem=48):
    return pltpu.CompilerParams(
        collective_id=number, has_side_effects=True, vmem_limit_bytes=vmem * 1024 * 1024
    )


def line_steps(n, me, make_right, make_left):
    for s in range(n - 1):

        @pl.when((me < n - 1) & (me >= s))
        def _():
            make_right(s).start()

        @pl.when((me > 0) & (me + s < n))
        def _():
            make_left(s).start()

        @pl.when(me - 1 - s >= 0)
        def _():
            make_right(s, me - 1 - s).wait_recv()

        @pl.when(me + 1 + s < n)
        def _():
            make_left(s, me + 1 + s).wait_recv()

    for s in range(n - 1):

        @pl.when((me < n - 1) & (me >= s))
        def _():
            make_right(s).wait_send()

        @pl.when((me > 0) & (me + s < n))
        def _():
            make_left(s).wait_send()


def pairs_of(n, me):
    half = n // 2
    parity, pair = me % 2, me // 2
    partner = me + 1 - 2 * parity
    ahead = [2 * ((pair + k) % half) + parity for k in range(1, half)]
    behind = [2 * ((pair + half - k) % half) + parity for k in range(1, half)]
    return half, parity, pair, partner, ahead, behind


def gather_dp_kernel(n, x_ref, o_ref, local, sr, rr, sl, rl):
    me, ctx = lax.axis_index("dp"), lax.axis_index("ctx")

    def here(d):
        return (d, ctx)

    greet([here((me + 1) % n), here((me + n - 1) % n)])
    own = pltpu.make_async_copy(x_ref, o_ref.at[me], local)
    own.start()

    def right(s, block=None):
        b = me - s if block is None else block
        return remote(x_ref if s == 0 else o_ref.at[b], o_ref.at[b], sr.at[s], rr.at[s], here(me + 1))

    def left(s, block=None):
        b = me + s if block is None else block
        return remote(x_ref if s == 0 else o_ref.at[b], o_ref.at[b], sl.at[s], rl.at[s], here(me - 1))

    line_steps(n, me, right, left)
    own.wait()


def gather_dp(x, number):
    n = lax.axis_size("dp")
    out = pl.pallas_call(
        functools.partial(gather_dp_kernel, n),
        out_shape=jax.ShapeDtypeStruct((n,) + x.shape, x.dtype),
        in_specs=[ANY],
        out_specs=ANY,
        scratch_shapes=[pltpu.SemaphoreType.DMA] + [pltpu.SemaphoreType.DMA((n - 1,))] * 4,
        compiler_params=params_of(number),
        cost_estimate=cost(60),
        name="gather_dp",
    )(x)
    return out.reshape((n * x.shape[0],) + x.shape[1:])


def group_of(n_dp, n, dp, me):
    pair, parity = me // 2, me % 2
    return 2 * n_dp, 2 * dp + parity, lambda j: (j // 2, 2 * pair + j % 2)


def greet_all(n_dp, n, dp, me):
    partner = me + 1 - 2 * (me % 2)
    others = [(dp + k) % n_dp for k in range(1, n_dp)]
    greet([(dp, (me + k) % n) for k in range(1, n)] + [(d, c) for d in others for c in (me, partner)])


def swap(src, dst, send, recv, count, mine, place):
    sends, receives = [], []
    for k in range(1, count):
        to, source = (mine + k) % count, (mine + count - k) % count
        sends.append(remote(src.at[to], dst.at[mine], send.at[k - 1], recv.at[k - 1], place(to)))
        receives.append(
            remote(src.at[mine], dst.at[source], send.at[k - 1], recv.at[k - 1], place(source))
        )
    for copy in sends:
        copy.start()
    return sends, receives


def tiles(total, tile, body):
    tile = min(total, tile)

    @pl.loop(0, total // tile)
    def _(j):
        body(pl.ds(pl.multiple_of(j * tile, tile), tile))


def reduce_ctx(n, dp, me, a_ref, w_ref, cols, o_ref, sa, ra, sb, rb, s1, r1, s2, r2):
    half, parity, pair, partner, ahead, behind = pairs_of(n, me)
    length, width = o_ref.shape

    def rows(block):
        return pl.ds(pl.multiple_of(block * length, length), length)

    first, second = [], []
    for k in range(half):
        target = (pair + k + 1) % half

        def give(part):
            value = dot_t(a_ref[rows(2 * target + 1 - parity), :], w_ref[part, cols])
            sa[k, :, part] = value.astype(BF)

        tiles(width, 512, give)
        copy = remote(sa.at[k], ra.at[k], s1.at[k], r1.at[k], (dp, partner))
        copy.start()
        first.append(copy)
        copy.wait_recv()

        def keep(part):
            value = dot_t(a_ref[rows(2 * target + parity), :], w_ref[part, cols])
            value = value + ra[k, :, part].astype(F32)
            if k < half - 1:
                sb[k, :, part] = value.astype(BF)
            else:
                o_ref[:, part] = value

        tiles(width, 512, keep)
        if k < half - 1:
            copy = remote(sb.at[k], rb.at[k], s2.at[k], r2.at[k], (dp, 2 * target + parity))
            copy.start()
            second.append(copy)
    for k in range(half - 1):
        second[k].wait_recv()
        o_ref[...] += rb[k].astype(F32)
    return first + second


def load_rows(hbm, vmem, sems):
    half, n_dp, rows, _ = hbm.shape
    copies = []
    for d in range(n_dp):
        for p in range(half):
            part = pl.ds((d * half + p) * rows, rows)
            copies.append(pltpu.make_async_copy(hbm.at[p, d], vmem.at[part, :], sems.at[d * half + p]))
    for copy in copies:
        copy.start()
    return copies


def gather_group(n, dp, me, all_ref, length, sr, rr, sl, rl, sf, rf, process):
    parity = me % 2
    partner = me + 1 - 2 * parity

    def block(b, side):
        start = (2 * b + side) * length
        return all_ref.at[pl.ds(pl.multiple_of(start, length), length), :]

    def right(s, b):
        return remote(block(b, parity), block(b, parity), sr.at[s], rr.at[s], (dp + 1, me))

    def left(s, b):
        return remote(block(b, parity), block(b, parity), sl.at[s], rl.at[s], (dp - 1, me))

    def aside(b):
        return remote(block(b, parity), block(b, parity), sf.at[b], rf.at[b], (dp, partner))

    def from_aside(b):
        return remote(block(b, 1 - parity), block(b, 1 - parity), sf.at[b], rf.at[b], (dp, partner))

    for s in range(n):
        if s == 0:
            aside(dp).start()
        else:

            @pl.when(dp >= s)
            def _():
                right(s - 1, dp - s).wait_recv()

            @pl.when(dp + s < n)
            def _():
                left(s - 1, dp + s).wait_recv()

        @pl.when((dp < n - 1) & (dp >= s))
        def _():
            right(s, dp - s).start()

        @pl.when((dp > 0) & (dp + s < n))
        def _():
            left(s, dp + s).start()

        if s == 0:
            from_aside(dp).wait_recv()
            process(dp, True)
        else:

            @pl.when(dp >= s)
            def _():
                aside(dp - s).start()

            @pl.when(dp + s < n)
            def _():
                aside(dp + s).start()

            below = jnp.where(dp >= s, 1, 0)
            above = jnp.where(dp + s < n, 1, 0)

            @pl.loop(0, below + above)
            def _(j):
                b = jnp.where(j < below, dp - s, dp + s)
                from_aside(b).wait_recv()
                process(b, False)

    for s in range(n):

        @pl.when((dp < n - 1) & (dp >= s))
        def _():
            right(s, dp - s).wait_send()

        @pl.when((dp > 0) & (dp + s < n))
        def _():
            left(s, dp + s).wait_send()

        aside(s).wait_send()


def gather_sems(n_dp):
    return [pltpu.SemaphoreType.DMA((n_dp,))] * 6


def line_sum(n, dp, me, make, val, o_ref, buf, send, recv, sync, between=None):
    rows_of = lambda ref, body: tiles(ref.shape[0], 32, body)

    def move(way, d):
        to = jnp.where(way == 1, dp + 1, dp - 1)
        return remote(buf.at[way, d], buf.at[way, d], send.at[way, d], recv.at[way, d], (to, me))

    for j in range(1, n):

        @pl.loop(0, 2)
        def _(phase):
            way = jnp.where(2 * dp < n, 1 - phase, phase)
            d = jnp.where(way == 1, n - j, j - 1)
            first = jnp.where(way == 1, 0, n - 1)
            ahead = jnp.where(way == 1, d - dp, dp - d)

            @pl.when(ahead > 0)
            def _():
                make(d, val)

                @pl.when(dp == first)
                def _():
                    def begin(part):
                        buf[way, d, part, :] = val[part, :].astype(BF)

                    rows_of(val, begin)

                @pl.when(dp != first)
                def _():
                    move(way, d).wait_recv()

                    def add(part):
                        buf[way, d, part, :] = (val[part, :] + buf[way, d, part, :].astype(F32)).astype(BF)

                    rows_of(val, add)

                move(way, d).start()

        if between is not None:
            between(j - 1)

    make(dp, o_ref)
    for way, first in ((1, 0), (0, n - 1)):

        @pl.when(dp != first)
        def _():
            move(way, dp).wait_recv()

            def add(part):
                o_ref[part, :] += buf[way, dp, part, :].astype(F32)

            rows_of(val, add)

    sync()
    for j in range(1, n):
        for way, d in ((1, n - j), (0, j - 1)):

            @pl.when((d - dp if way == 1 else dp - d) > 0)
            def _():
                move(way, d).wait_send()


def line_scratch(n_dp, length, width):
    return [
        pltpu.VMEM((length, width), F32),
        pltpu.VMEM((2, n_dp, length, width), BF),
        pltpu.SemaphoreType.DMA((2, n_dp)),
        pltpu.SemaphoreType.DMA((2, n_dp)),
    ]


def part_of_pair(dp, me, a_ref, w_ref, length, sa, ra, s1, r1):
    parity = me % 2
    partner = me + 1 - 2 * parity

    def make(d, out):
        def rows(side):
            return pl.ds(pl.multiple_of((2 * d + side) * length, length), length)

        def give(part):
            sa[d, :, part] = dot_t(a_ref[rows(1 - parity), :], w_ref[part, :]).astype(BF)

        tiles(out.shape[1], 512, give)
        copy = remote(sa.at[d], ra.at[d], s1.at[d], r1.at[d], (dp, partner))
        copy.start()

        def keep(part):
            out[:, part] = dot_t(a_ref[rows(parity), :], w_ref[part, :])

        tiles(out.shape[1], 512, keep)
        copy.wait_recv()

        def add(part):
            out[part, :] += ra[d, part, :].astype(F32)

        tiles(length, 32, add)

    def done(n):
        for d in range(n):
            remote(sa.at[d], ra.at[d], s1.at[d], r1.at[d], (dp, partner)).wait_send()

    return make, done


def pair_scratch(n_dp, length, width):
    return [pltpu.VMEM((n_dp, length, width), BF)] * 2 + [pltpu.SemaphoreType.DMA((n_dp,))] * 2


def greet_group(n_dp, dp, me):
    partner = me + 1 - 2 * (me % 2)
    greet([(dp, partner)] + [((dp + k) % n_dp, me) for k in range(1, n_dp)])


def ff_forward_kernel(
    n_dp, n, h_ref, up_ref, gain_ref, gu_hbm, d_hbm, wo_hbm,
    res_ref, dm_ref, gp_ref, all_out, pre_out, hid_out, d_out, wo_out,
    all_ref, pre_ref, hid_ref, d_ref, gu_ref, acc, sem_gu, sem_d, sem_out, sd, rd, so, ro, fo, go, *rest,
):
    gather, pair_refs, line_refs = rest[:6], rest[6:10], rest[10:]
    dp, me = lax.axis_index("dp"), lax.axis_index("ctx")
    length, width = h_ref.shape
    fh = hid_ref.shape[1]
    half, parity, pair, partner, ahead, behind = pairs_of(n, me)
    loads_gu = load_rows(gu_hbm, gu_ref, sem_gu)
    mine = pl.ds(pl.multiple_of((2 * dp + me % 2) * length, length), length)
    all_ref[mine, :] = h_ref[...].astype(BF)
    greet(
        [(dp, partner)]
        + [((dp + k) % n_dp, me) for k in range(1, n_dp)]
        + [(dp, a) for a in ahead]
    )
    tall = d_hbm.shape[1]

    def down(d, p):
        return d_ref.at[pl.ds(pl.multiple_of((d * half + p) * tall, tall), tall), :]

    loads_d = [pltpu.make_async_copy(d_hbm.at[d], down(d, pair), sem_d.at[d]) for d in range(n_dp)]
    spreads = [
        remote(d_hbm.at[d], down(d, pair), sd.at[k, d], rd.at[k, d], (dp, a))
        for k, a in enumerate(ahead)
        for d in range(n_dp)
    ]
    for copy in spreads + loads_d:
        copy.start()

    def process(b, own):
        rows = pl.ds(pl.multiple_of(2 * b * length, 2 * length), 2 * length)
        if own:
            for copy in loads_gu:
                copy.wait()

        def hidden(part):
            second = pl.ds(pl.multiple_of(fh + part.start, part.size), part.size)
            gate = dot(all_ref[rows, :], gu_ref[:, part])
            upper = dot(all_ref[rows, :], gu_ref[:, second])
            pre_ref[rows, part] = gate
            pre_ref[rows, second] = upper
            hid_ref[rows, part] = (gate * jax.nn.sigmoid(gate) * upper).astype(BF)

        tiles(fh, 256, hidden)

    gather_group(n_dp, dp, me, all_ref, length, *gather, process)
    for copy in loads_d:
        copy.wait()
    for k, b in enumerate(behind):
        for d in range(n_dp):
            remote(d_hbm.at[d], down(d, b // 2), sd.at[k, d], rd.at[k, d], (dp, b)).wait_recv()

    outs = [
        pltpu.make_async_copy(ref, out, sem_out.at[i])
        for i, (ref, out) in enumerate(
            ((all_ref, all_out), (pre_ref, pre_out), (hid_ref, hid_out), (d_ref, d_out))
        )
    ]
    outs.append(pltpu.make_async_copy(wo_hbm, wo_out.at[me], sem_out.at[4]))
    spreads_wo = [
        remote(wo_hbm, wo_out.at[me], so.at[k], ro.at[k], (dp, a)) for k, a in enumerate(ahead + [partner])
    ]
    for copy in outs + spreads_wo:
        copy.start()
    make, done = part_of_pair(dp, me, hid_ref, d_ref, length, *pair_refs)

    gp_ref[...] = jnp.zeros_like(gp_ref)

    def finish(rows):
        out, up, gain = acc[rows, :], up_ref[rows, :].astype(F32), gain_ref[...]
        scale = rms_scale(out)
        res_ref[rows, :] = (h_ref[rows, :] + out * scale * gain).astype(BF)
        gp_ref[...] += jnp.sum(up * out * scale, axis=0, keepdims=True)
        dm_ref[rows, :] = norm_back(up * gain, out, scale).astype(BF)

    forwards = []

    def last():
        for k, b in enumerate(behind):
            remote(wo_hbm, wo_out.at[b], so.at[k], ro.at[k], (dp, b)).wait_recv()
            forward = remote(wo_out.at[b], wo_out.at[b], fo.at[k], go.at[k], (dp, partner))
            forward.start()
            forwards.append(forward)
        tiles(length, 16, finish)

    line_sum(n_dp, dp, me, make, line_refs[0], acc, *line_refs[1:], last)
    done(n_dp)
    spreads_wo[-1].wait_recv()
    for copy in forwards:
        copy.wait_recv()
    for copy in spreads + spreads_wo + forwards:
        copy.wait_send()
    for copy in outs:
        copy.wait()


def ff_forward(h1, up, gain, w_gu, w_d, w_o, number):
    n_dp, n = lax.axis_size("dp"), lax.axis_size("ctx")
    (length, width), fh = h1.shape, w_d.shape[2]
    tokens = 2 * n_dp * length
    half = n // 2
    low = jax.ShapeDtypeStruct((length, width), BF)
    return pl.pallas_call(
        functools.partial(ff_forward_kernel, n_dp, n),
        out_shape=(
            low,
            low,
            jax.ShapeDtypeStruct((1, width), F32),
            jax.ShapeDtypeStruct((tokens, width), BF),
            jax.ShapeDtypeStruct((tokens, 2 * fh), F32),
            jax.ShapeDtypeStruct((tokens, fh), BF),
            jax.ShapeDtypeStruct((width, fh), BF),
            jax.ShapeDtypeStruct((n,) + w_o.shape, BF),
        ),
        in_specs=[VMEM] * 3 + [ANY] * 3,
        out_specs=(VMEM,) * 3 + (ANY,) * 5,
        scratch_shapes=[
            pltpu.VMEM((tokens, width), BF),
            pltpu.VMEM((tokens, 2 * fh), F32),
            pltpu.VMEM((tokens, fh), BF),
            pltpu.VMEM((width, fh), BF),
            pltpu.VMEM((width, 2 * fh), BF),
            pltpu.VMEM((length, width), F32),
            pltpu.SemaphoreType.DMA((half * n_dp,)),
            pltpu.SemaphoreType.DMA((n_dp,)),
            pltpu.SemaphoreType.DMA((5,)),
            pltpu.SemaphoreType.DMA((half - 1, n_dp)),
            pltpu.SemaphoreType.DMA((half - 1, n_dp)),
            pltpu.SemaphoreType.DMA((half,)),
            pltpu.SemaphoreType.DMA((half,)),
            pltpu.SemaphoreType.DMA((half - 1,)),
            pltpu.SemaphoreType.DMA((half - 1,)),
        ]
        + gather_sems(n_dp)
        + pair_scratch(n_dp, length, width)
        + line_scratch(n_dp, length, width),
        compiler_params=params_of(number, 58),
        cost_estimate=cost(90),
        name="ff_forward",
    )(h1, up, gain, w_gu, w_d, w_o)


def store_rows(n_dp, value_of, out):
    half, _, rows, _ = out.shape

    @pl.loop(0, n_dp * half)
    def _(r):
        out[r % half, r // half] = value_of(pl.ds(pl.multiple_of(r * rows, rows), rows)).astype(BF)


def ff_back_kernel(
    n_dp, dm_ref, hid_ref, d_hbm, pre_hbm, dgu_ref, gd_ref,
    all_ref, d_ref, pre_ref, acc, sem_d, sem_p, *gather,
):
    dp, me = lax.axis_index("dp"), lax.axis_index("ctx")
    length, width = dm_ref.shape
    fh = d_ref.shape[1]
    load = pltpu.make_async_copy(d_hbm, d_ref, sem_d)
    load.start()

    def rows_of(b):
        return pl.ds(pl.multiple_of(2 * b * length, 2 * length), 2 * length)

    def load_pre(b):
        return pltpu.make_async_copy(pre_hbm.at[rows_of(b), :], pre_ref.at[rows_of(b), :], sem_p.at[b])

    for k in range(n_dp):
        load_pre((dp + k) % n_dp).start()
    mine = pl.ds(pl.multiple_of((2 * dp + me % 2) * length, length), length)
    all_ref[mine, :] = dm_ref[...]
    greet_group(n_dp, dp, me)

    def process(b, own):
        rows = rows_of(b)
        if own:
            load.wait()
        load_pre(b).wait()

        def hidden(part):
            second = pl.ds(pl.multiple_of(fh + part.start, part.size), part.size)
            back = dot(all_ref[rows, :], d_ref[:, part])
            gate, upper = pre_ref[rows, part], pre_ref[rows, second]
            sig = jax.nn.sigmoid(gate)
            dgu_ref[rows, part] = (back * upper * sig * (1.0 + gate * (1.0 - sig))).astype(BF)
            dgu_ref[rows, second] = (back * gate * sig).astype(BF)

        tiles(fh, 256, hidden)

        def product(part):
            value = t_dot(all_ref[rows, part], hid_ref[rows, :])
            acc[part, :] = value if own else acc[part, :] + value

        tiles(width, 256, product)

    gather_group(n_dp, dp, me, all_ref, length, *gather, process)
    store_rows(n_dp, lambda part: acc[part, :], gd_ref)


def ff_back(dm, hid, w_d, pre, rows, number):
    n_dp, half = lax.axis_size("dp"), lax.axis_size("ctx") // 2
    (length, width), fh = dm.shape, w_d.shape[1]
    tokens = 2 * n_dp * length
    return pl.pallas_call(
        functools.partial(ff_back_kernel, n_dp),
        out_shape=(
            jax.ShapeDtypeStruct((tokens, 2 * fh), BF),
            jax.ShapeDtypeStruct((half, n_dp, 2 * rows, fh), BF),
        ),
        in_specs=[VMEM, VMEM, ANY, ANY],
        out_specs=(VMEM,) * 2,
        scratch_shapes=[
            pltpu.VMEM((tokens, width), BF),
            pltpu.VMEM((width, fh), BF),
            pltpu.VMEM((tokens, 2 * fh), F32),
            pltpu.VMEM((width, fh), F32),
            pltpu.SemaphoreType.DMA,
            pltpu.SemaphoreType.DMA((n_dp,)),
        ]
        + gather_sems(n_dp),
        compiler_params=params_of(number, 58),
        cost_estimate=cost(45),
        name="ff_back",
    )(dm, hid, w_d, pre)


def ff_scatter_kernel(
    n_dp, n, dgu_ref, gu_hbm, all_hbm, wo_hbm, up_ref, branch_ref, gain_ref, dh_ref, dc_ref, do_ref, gp_ref, gg_out, gv_out,
    gg_ref, gv_ref, gu_ref, all_ref, wo_ref, give_ref, db_ref, mix_ref, acc, sem_gu, sem_all, sem_out, ss, rs, sc, rc, *rest,
):
    dp, me = lax.axis_index("dp"), lax.axis_index("ctx")
    length, width = dh_ref.shape
    pair_refs, line_refs = rest[:4], rest[4:]
    half, parity, pair, partner, ahead, behind = pairs_of(n, me)
    _, _, rows, fh = gg_ref.shape
    loads = load_rows(gu_hbm, gu_ref, sem_gu)
    load = pltpu.make_async_copy(all_hbm, all_ref, sem_all)
    load.start()
    load_wo = pltpu.make_async_copy(wo_hbm, wo_ref, sem_out.at[2])
    load_wo.start()
    greet(
        [(dp, (me + k) % n) for k in range(1, n)] + [((dp + k) % n_dp, me) for k in range(1, n_dp)]
    )
    for copy in loads:
        copy.wait()

    make, done = part_of_pair(dp, me, dgu_ref, gu_ref, length, *pair_refs)
    gp_ref[...] = jnp.zeros_like(gp_ref)

    def finish(rows):
        grad, branch = dh_ref[rows, :] + up_ref[rows, :].astype(F32), branch_ref[rows, :]
        scale = rms_scale(branch)
        dh_ref[rows, :] = grad
        gp_ref[...] += jnp.sum(grad * branch * scale, axis=0, keepdims=True)
        db_ref[rows, :] = norm_back(grad * gain_ref[...], branch, scale).astype(BF)

    load.wait()
    tall = acc.shape[0]
    blocks = width // tall
    each = -(-blocks // (n_dp - 1))

    def grads(step):
        @pl.loop(min(step * each, blocks), min((step + 1) * each, blocks))
        def _(j):
            acc[...] = t_dot(all_ref[:, pl.ds(pl.multiple_of(j * tall, tall), tall)], dgu_ref[...])
            for s in range(tall // rows):
                r = j * (tall // rows) + s
                part = slice(s * rows, (s + 1) * rows)
                gg_ref[r % half, r // half] = acc[part, :fh].astype(BF)
                gv_ref[r % half, r // half] = acc[part, fh:].astype(BF)

    val, *line = line_refs
    line_sum(n_dp, dp, me, make, val, dh_ref, *line, lambda: tiles(length, 16, finish), grads)
    done(n_dp)
    outs = [
        pltpu.make_async_copy(ref, out, sem_out.at[i])
        for i, (ref, out) in enumerate(((gg_ref, gg_out), (gv_ref, gv_out)))
    ]
    for copy in outs:
        copy.start()
    load_wo.wait()

    def mine(c):
        return pl.ds(pl.multiple_of(c * length, length), length)

    def send(k):
        to = (me + k) % n
        return remote(give_ref.at[to], do_ref.at[mine(me), :], ss.at[k - 1], rs.at[k - 1], (dp, to))

    def receive(k):
        source = (me + n - k) % n
        return remote(give_ref.at[me], do_ref.at[mine(source), :], ss.at[k - 1], rs.at[k - 1], (dp, source))

    own = rows // 2
    share = n_dp * own
    for c in range(n):
        for d in range(n_dp):
            start, source = c * share + d * own, (d * n + c) * own
            mix_ref[:, start : start + own] = db_ref[:, source : source + own]

    def share_of(c):
        return mix_ref.at[:, pl.ds(pl.multiple_of(c * share, share), share)]

    def send_share(k):
        to = (me + k) % n
        return remote(share_of(to), dc_ref.at[mine(me), :], sc.at[k - 1], rc.at[k - 1], (dp, to))

    def receive_share(k):
        source = (me + n - k) % n
        return remote(share_of(me), dc_ref.at[mine(source), :], sc.at[k - 1], rc.at[k - 1], (dp, source))

    stay = pltpu.make_async_copy(share_of(me), dc_ref.at[mine(me), :], sem_out.at[3])
    stay.start()

    @pl.loop(1, n)
    def _(k):
        to = (me + k) % n
        send_share(k).start()
        give_ref[to] = dot(db_ref[...], wo_ref[to]).astype(BF)
        send(k).start()

    do_ref[mine(me), :] = dot(db_ref[...], wo_ref[me]).astype(BF)
    for k in range(1, n):
        receive(k).wait_recv()
        receive_share(k).wait_recv()
    for k in range(1, n):
        send(k).wait_send()
        send_share(k).wait_send()
    stay.wait()
    for copy in outs:
        copy.wait()


def ff_scatter(dgu, w_gu, h1_all, wo_all, up, branch, gain, number):
    n_dp, n = lax.axis_size("dp"), lax.axis_size("ctx")
    length, width = up.shape
    hc = wo_all.shape[2]
    grad = jax.ShapeDtypeStruct(w_gu.shape[:3] + (w_gu.shape[3] // 2,), BF)
    return pl.pallas_call(
        functools.partial(ff_scatter_kernel, n_dp, n),
        out_shape=(
            jax.ShapeDtypeStruct((length, width), F32),
            jax.ShapeDtypeStruct((n * length, width // n), BF),
            jax.ShapeDtypeStruct((n * length, hc), BF),
            jax.ShapeDtypeStruct((1, width), F32),
            grad,
            grad,
        ),
        in_specs=[VMEM, ANY, ANY, ANY] + [VMEM] * 3,
        out_specs=(VMEM,) * 4 + (ANY,) * 2,
        scratch_shapes=[
            pltpu.VMEM(grad.shape, BF),
            pltpu.VMEM(grad.shape, BF),
            pltpu.VMEM((width, w_gu.shape[3]), BF),
            pltpu.VMEM(h1_all.shape, BF),
            pltpu.VMEM(wo_all.shape, BF),
            pltpu.VMEM((n, length, hc), BF),
            pltpu.VMEM((length, width), BF),
            pltpu.VMEM((length, width), BF),
            pltpu.VMEM((256, w_gu.shape[3]), F32),
            pltpu.SemaphoreType.DMA((w_gu.shape[0] * n_dp,)),
            pltpu.SemaphoreType.DMA,
            pltpu.SemaphoreType.DMA((4,)),
            pltpu.SemaphoreType.DMA((n - 1,)),
            pltpu.SemaphoreType.DMA((n - 1,)),
            pltpu.SemaphoreType.DMA((n - 1,)),
            pltpu.SemaphoreType.DMA((n - 1,)),
        ]
        + pair_scratch(n_dp, length, width)
        + line_scratch(n_dp, length, width),
        compiler_params=params_of(number, 60),
        cost_estimate=cost(50),
        name="ff_scatter",
    )(dgu, w_gu, h1_all, wo_all, up, branch, gain)


def start_kernel(
    n_dp, n, g_ref, w_ref, v_ref, x_ref, h_ref, o_ref, p_ref, y_ref,
    local, sg, rg, sa, ra, sv, rv, ss, rs, fs, fr,
):
    dp, me = lax.axis_index("dp"), lax.axis_index("ctx")
    half, parity, pair, partner, ahead, behind = pairs_of(n, me)
    count, mine, place = group_of(n_dp, n, dp, me)
    greet_all(n_dp, n, dp, me)
    owns = [
        pltpu.make_async_copy(g_ref.at[mine], h_ref.at[mine], local.at[0]),
        pltpu.make_async_copy(w_ref.at[me], o_ref.at[me], local.at[1]),
        pltpu.make_async_copy(x_ref, y_ref.at[me], local.at[2]),
        pltpu.make_async_copy(v_ref.at[me], p_ref.at[me], local.at[3]),
    ]
    sends, receives = swap(g_ref, h_ref, sg, rg, count, mine, place)
    for src, dst, send, recv in ((w_ref, o_ref, sa, ra), (v_ref, p_ref, sv, rv)):
        more, waits = swap(src, dst, send, recv, n, me, lambda c: (dp, c))
        sends += more
        receives += waits
    gathers = [
        remote(x_ref, y_ref.at[me], ss.at[k], rs.at[k], (dp, a))
        for k, a in enumerate(ahead + [partner])
    ]
    for copy in gathers + owns:
        copy.start()
    forwards = []
    for k, b in enumerate(behind):
        remote(x_ref, y_ref.at[b], ss.at[k], rs.at[k], (dp, b)).wait_recv()
        forward = remote(y_ref.at[b], y_ref.at[b], fs.at[k], fr.at[k], (dp, partner))
        forward.start()
        forwards.append(forward)
    gathers[-1].wait_recv()
    for copy in receives:
        copy.wait_recv()
    for forward in forwards:
        forward.wait()
    for copy in sends + gathers:
        copy.wait_send()
    for copy in owns:
        copy.wait()


def start(g, w, v, x, number):
    n_dp, n = lax.axis_size("dp"), lax.axis_size("ctx")
    half = n // 2
    dma = pltpu.SemaphoreType.DMA
    g_out, w_out, v_out, x_all = pl.pallas_call(
        functools.partial(start_kernel, n_dp, n),
        out_shape=(
            jax.ShapeDtypeStruct(g.shape, g.dtype),
            jax.ShapeDtypeStruct(w.shape, w.dtype),
            jax.ShapeDtypeStruct(v.shape, v.dtype),
            jax.ShapeDtypeStruct((n,) + x.shape, x.dtype),
        ),
        in_specs=[ANY] * 4,
        out_specs=(ANY,) * 4,
        scratch_shapes=[dma((4,))]
        + [dma((2 * n_dp - 1,))] * 2
        + [dma((n - 1,))] * 4
        + [dma((half,))] * 2
        + [dma((half - 1,))] * 2,
        compiler_params=params_of(number),
        cost_estimate=cost(45),
        name="start",
    )(g, w, v, x)
    return g_out, w_out, v_out, x_all.reshape(-1, x.shape[-1])


def collect_kernel(
    n_dp, n, g_ref, h_ref, a_ref, w_ref, o_ref, h_out, y_ref,
    own, co_ref, pa, qa, pb, qb, local, sw, rw, s1, r1, s2, r2, sh, rh,
):
    dp, me = lax.axis_index("dp"), lax.axis_index("ctx")
    tall = own.shape[0]
    count, index, place = group_of(n_dp, n, dp, me)
    greet_all(n_dp, n, dp, me)
    gives = slab_give(n_dp, dp, me, g_ref, co_ref, sw, rw)
    swaps, receives = swap(h_ref, h_out, sh, rh, count, index, place)
    mine = g_ref.at[pl.ds(pl.multiple_of(dp * tall, tall), tall), :]
    stays = [
        pltpu.make_async_copy(mine, own, local.at[0]),
        pltpu.make_async_copy(h_ref.at[index], h_out.at[index], local.at[1]),
    ]
    for copy in stays:
        copy.start()
    cols = slice(0, a_ref.shape[1])
    sums = reduce_ctx(n, dp, me, a_ref, w_ref, cols, y_ref, pa, qa, pb, qb, s1, r1, s2, r2)
    for copy in stays:
        copy.wait()
    for copy in gives:
        copy.wait_recv()

    def add(part):
        total = own[part, :].astype(F32)
        for k in range(n_dp - 1):
            total = total + co_ref[k, part, :].astype(F32)
        o_ref[part, :] = total.astype(BF)

    tiles(tall, 64, add)
    for copy in receives:
        copy.wait_recv()
    for copy in gives + swaps + sums:
        copy.wait_send()


def collect(g, h, a, w, number):
    n_dp, n = lax.axis_size("dp"), lax.axis_size("ctx")
    tall, width = g.shape[0] // n_dp, g.shape[1]
    half, length, features = n // 2, a.shape[0] // n, w.shape[0]
    dma = pltpu.SemaphoreType.DMA
    return pl.pallas_call(
        functools.partial(collect_kernel, n_dp, n),
        out_shape=(
            jax.ShapeDtypeStruct((tall, width), BF),
            jax.ShapeDtypeStruct(h.shape, BF),
            jax.ShapeDtypeStruct((length, features), F32),
        ),
        in_specs=[ANY, ANY, VMEM, VMEM],
        out_specs=(VMEM, ANY, VMEM),
        scratch_shapes=[
            pltpu.VMEM((tall, width), BF),
            pltpu.VMEM((n_dp - 1, tall, width), BF),
            pltpu.VMEM((half, length, features), BF),
            pltpu.VMEM((half, length, features), BF),
            pltpu.VMEM((half - 1, length, features), BF),
            pltpu.VMEM((half - 1, length, features), BF),
            dma((2,)),
            dma((n_dp - 1,)),
            dma((n_dp - 1,)),
            dma((half,)),
            dma((half,)),
            dma((half - 1,)),
            dma((half - 1,)),
            dma((2 * n_dp - 1,)),
            dma((2 * n_dp - 1,)),
        ],
        compiler_params=params_of(number),
        cost_estimate=cost(70),
        name="collect",
    )(g, h, a, w)


def total_kernel(
    n_dp, n, qk_ref, wv_ref, wo_ref, u_ref, gg_ref, gd_ref, gain_ref, ga_ref, gu_ref, o_ref,
    sb, mine, buf, part, all_parts, local, sx, rx, sh, rh, ss, rs, st, rt,
):
    dp, me = lax.axis_index("dp"), lax.axis_index("ctx")
    gain_rows = gain_ref.shape[0]
    hc = wv_ref.shape[2]
    count, index, place = group_of(n_dp, n, dp, me)
    greet_all(n_dp, n, dp, me)
    swaps, receives = swap(u_ref, gu_ref, sh, rh, count, index, place)
    stay = pltpu.make_async_copy(u_ref.at[index], gu_ref.at[index], local)
    stay.start()
    sb[:, :, : 2 * hc] = qk_ref[...]
    sb[:, :, 2 * hc : 3 * hc] = wv_ref[...]
    more, waits = swap(sb, ga_ref, sx, rx, n, me, lambda c: (dp, c))
    ga_ref[me] = sb[me]

    def squares(ref):
        acc = jnp.zeros((ref.shape[1], ref.shape[2]), F32)
        for i in range(ref.shape[0]):
            block = ref[i].astype(F32)
            acc += block * block
        return jnp.sum(jnp.sum(acc, axis=0, keepdims=True), axis=1, keepdims=True)

    total = squares(gg_ref) + squares(gd_ref) + squares(wo_ref)
    for copy in waits:
        copy.wait_recv()
    total += squares(ga_ref)
    for copy in receives:
        copy.wait_recv()
    stay.wait()
    total += squares(gu_ref)
    mine[0:gain_rows, :] = gain_ref[...]
    mine[gain_rows:, :] = jnp.broadcast_to(total, (8, 128))
    copies = swaps + more
    for k in range(1, n):
        copy = remote(mine, buf.at[me], ss.at[k - 1], rs.at[k - 1], (dp, (me + k) % n))
        copy.start()
        copies.append(copy)
    buf[me] = mine[...]
    for k in range(1, n):
        source = (me + n - k) % n
        remote(mine, buf.at[source], ss.at[k - 1], rs.at[k - 1], (dp, source)).wait_recv()
    acc = buf[0]
    for j in range(1, n):
        acc = acc + buf[j]
    part[...] = acc
    all_parts[dp] = acc
    for k in range(1, n_dp):
        copy = remote(part, all_parts.at[dp], st.at[k - 1], rt.at[k - 1], ((dp + k) % n_dp, me))
        copy.start()
        copies.append(copy)
    for k in range(1, n_dp):
        source = (dp + n_dp - k) % n_dp
        remote(part, all_parts.at[source], st.at[k - 1], rt.at[k - 1], (source, me)).wait_recv()
    acc = all_parts[0]
    for j in range(1, n_dp):
        acc = acc + all_parts[j]
    o_ref[...] = acc
    for copy in copies:
        copy.wait_send()


def total_over(qk, wv, wo, u, gg, gd, gain_part, number):
    n_dp, n = lax.axis_size("dp"), lax.axis_size("ctx")
    rows, hc = qk.shape[0] // n, wv.shape[1]
    gain_rows = gain_part.size // 128
    shape = (gain_rows + 8, 128)
    dma = pltpu.SemaphoreType.DMA
    ga, gu, out = pl.pallas_call(
        functools.partial(total_kernel, n_dp, n),
        out_shape=(
            jax.ShapeDtypeStruct((n, rows, 3 * hc), BF),
            jax.ShapeDtypeStruct(u.shape, BF),
            jax.ShapeDtypeStruct(shape, F32),
        ),
        in_specs=[VMEM] * 3 + [ANY] + [VMEM] * 3,
        out_specs=(VMEM,) * 3,
        scratch_shapes=[
            pltpu.VMEM((n, rows, 3 * hc), BF),
            pltpu.VMEM(shape, F32),
            pltpu.VMEM((n,) + shape, F32),
            pltpu.VMEM(shape, F32),
            pltpu.VMEM((n_dp,) + shape, F32),
            dma,
            dma((n - 1,)),
            dma((n - 1,)),
            dma((2 * n_dp - 1,)),
            dma((2 * n_dp - 1,)),
            dma((n - 1,)),
            dma((n - 1,)),
            dma((n_dp - 1,)),
            dma((n_dp - 1,)),
        ],
        compiler_params=params_of(number),
        cost_estimate=cost(35),
        name="total",
    )(
        qk.reshape(n, rows, 2 * hc),
        wv.reshape(n, rows, hc),
        wo[None],
        u,
        gg,
        gd,
        gain_part.reshape(gain_rows, 128),
    )
    return ga, gu, out[gain_rows, 0], out[:gain_rows].reshape(gain_part.shape)


def adam_kernel(factor_ref, p_ref, m_ref, v_ref, ga_ref, go_ref, gg_ref, gu_ref, gd_ref, po_ref, mo_ref, vo_ref, g_ref):
    part = pl.program_id(0)
    n, _, three = ga_ref.shape
    hc = three // 3
    fs = gd_ref.shape[2]

    @pl.when(part == 0)
    def _():
        g_ref[:, 3 * n * hc :] = go_ref[...].astype(F32)
        for matrix in range(3):
            for c in range(n):
                start = (matrix * n + c) * hc
                g_ref[:, start : start + hc] = ga_ref[c, :, matrix * hc : (matrix + 1) * hc].astype(F32)

    for index, ref in ((1, gg_ref), (2, gu_ref), (3, gd_ref)):

        @pl.when(part == index)
        def _():
            for d in range(ref.shape[0]):
                g_ref[:, d * fs : (d + 1) * fs] = ref[d].astype(F32)

    clipped = g_ref[...] * factor_ref[0, 0]
    new_m = BETA1 * m_ref[...] + (1.0 - BETA1) * clipped
    new_v = BETA2 * v_ref[...] + (1.0 - BETA2) * (clipped * clipped)
    root = jnp.sqrt(new_v * (1.0 / (1.0 - BETA2**STEP))) + ADAM_EPS
    po_ref[...] = p_ref[...] * (1.0 - RATE * DECAY) - (new_m * (RATE / (1.0 - BETA1**STEP))) / root
    mo_ref[...] = new_m
    vo_ref[...] = new_v


def adam(factor, params, first, second, ga, go, gg, gu, gd):
    rows, columns = params.shape
    n, n_dp, fs = ga.shape[0], gd.shape[0], gd.shape[2]
    block = min(rows, 16)
    steps = rows // block
    wide = pl.BlockSpec((block, columns // 4), lambda i, r: (r, i))
    return pl.pallas_call(
        adam_kernel,
        grid=(4, steps),
        out_shape=(jax.ShapeDtypeStruct(params.shape, F32),) * 3,
        in_specs=[
            pl.BlockSpec(memory_space=pltpu.SMEM),
            wide,
            wide,
            wide,
            pl.BlockSpec((n, block, ga.shape[2]), lambda i, r: (0, jnp.where(i == 0, r, steps - 1), 0)),
            pl.BlockSpec((block, go.shape[1]), lambda i, r: (jnp.where(i == 0, r, steps - 1), 0)),
            *[
                pl.BlockSpec(
                    (n_dp, block, fs),
                    lambda i, r, part=part: (
                        0,
                        jnp.where(i < part, 0, jnp.where(i == part, r, steps - 1)),
                        0,
                    ),
                )
                for part in (1, 2, 3)
            ],
        ],
        out_specs=(wide, wide, wide),
        scratch_shapes=[pltpu.VMEM((block, columns // 4), F32)],
        compiler_params=pltpu.CompilerParams(vmem_limit_bytes=48 * 1024 * 1024),
        name="adam",
    )(factor.reshape(1, 1), params, first, second, ga, go, gg, gu, gd)


def arrange_kernel(n, count, p_ref, a_ref, o_ref, g_ref, d_ref):
    part = pl.program_id(0)
    hc = o_ref.shape[2]
    fs = d_ref.shape[2]

    @pl.when(part == 0)
    def _():
        for matrix in range(4):
            for c in range(n):
                start = (matrix * n + c) * hc
                value = p_ref[:, start : start + hc].astype(BF)
                if matrix < 3:
                    a_ref[c, :, matrix * hc : (matrix + 1) * hc] = value
                else:
                    o_ref[c] = value

    for index, ref, first in ((1, g_ref, 0), (2, g_ref, fs), (3, d_ref, 0)):

        @pl.when(part == index)
        def _():
            for d in range(count):
                ref[d, :, first : first + fs] = p_ref[:, d * fs : (d + 1) * fs].astype(BF)


def arrange(params, width):
    count, n = 2 * lax.axis_size("dp"), lax.axis_size("ctx")
    rows, columns = params.shape
    fs, hc = columns // 4 // count, width // n
    whole = lambda shape: pl.BlockSpec(shape, lambda i: (0,) * len(shape))
    shapes = [(n, rows, 3 * hc), (n, rows, hc), (count, rows, 2 * fs), (count, rows, fs)]
    return pl.pallas_call(
        functools.partial(arrange_kernel, n, count),
        grid=(4,),
        out_shape=tuple(jax.ShapeDtypeStruct(s, BF) for s in shapes),
        in_specs=[pl.BlockSpec((rows, columns // 4), lambda i: (0, i))],
        out_specs=tuple(whole(s) for s in shapes),
        compiler_params=pltpu.CompilerParams(vmem_limit_bytes=48 * 1024 * 1024),
        name="arrange",
    )(params)


def row_sums(value, row):
    pick = lax.broadcasted_iota(jnp.int32, (8, value.shape[1]), 0) == row
    return lax.dot_general(
        pick.astype(F32),
        value,
        (((1,), (1,)), ((), ())),
        preferred_element_type=F32,
        precision=lax.Precision.HIGHEST,
    )


def exchange(n, dp, me, buf, ss, rs):
    copies = []
    for k in range(1, n):
        copy = remote(buf.at[me], buf.at[me], ss.at[k - 1], rs.at[k - 1], (dp, (me + k) % n))
        copy.start()
        copies.append(copy)
    for k in range(1, n):
        source = (me + n - k) % n
        remote(buf.at[me], buf.at[source], ss.at[k - 1], rs.at[k - 1], (dp, source)).wait_recv()
    total = buf[0]
    for j in range(1, n):
        total = total + buf[j]
    for copy in copies:
        copy.wait_send()
    return total


def turn(value, cos, sine):
    return value * cos + pltpu.roll(value, HD // 2, 1) * sine


def mask_of(rows, info_col, info_row):
    pos_i, doc_i = info_col[rows, 0:1], info_col[rows, 1:2]
    return (info_row[1:2, :] == doc_i) & (info_row[0:1, :] <= pos_i)


def attend_kernel(
    n_dp, n, x_ref, w_ref, wo_ref, d_ref, t_ref, norm_ref, gain_ref, cos_ref, sin_ref, col_ref, row_ref,
    y_ref, h_ref, q_ref, k_ref, v_ref, o_ref, pre_ref, scale_ref, lse_ref, wo_all, d_out,
    buf, pa, qa, pb, qb, ss, rs, s1, r1, s2, r2, sw, rw, sd, rd, local,
):
    dp, me = lax.axis_index("dp"), lax.axis_index("ctx")
    seq, width = x_ref.shape
    hc = o_ref.shape[1]
    block = min(seq, 256)
    count, mine, place = group_of(n_dp, n, dp, me)
    greet_all(n_dp, n, dp, me)
    piece = wo_ref.shape[0]

    def part_of(d):
        return wo_all.at[pl.ds(pl.multiple_of(d * piece, piece), piece), :]

    owns = [
        pltpu.make_async_copy(wo_ref, part_of(dp), local.at[0]),
        pltpu.make_async_copy(d_ref.at[mine], d_out.at[mine], local.at[1]),
    ]
    behind_wo = [
        remote(wo_ref, part_of(dp), sw.at[k - 1], rw.at[k - 1], ((dp + k) % n_dp, me))
        for k in range(1, n_dp)
    ]
    for copy in behind_wo + owns:
        copy.start()
    behind_d, receives = swap(d_ref, d_out, sd, rd, count, mine, place)

    @pl.loop(0, seq // block)
    def _(i):
        rows = pl.ds(pl.multiple_of(i * block, block), block)
        value = dot(x_ref[rows, :], w_ref[...])
        pre_ref[rows, :] = value[:, : 2 * hc]
        v_ref[rows, :] = value[:, 2 * hc :].astype(BF)
        squares = value[:, : 2 * hc] * value[:, : 2 * hc]
        buf[me, :, rows] = row_sums(squares[:, :hc], 0) + row_sums(squares[:, hc:], 1)

    scale_ref[...] = jnp.transpose(lax.rsqrt(exchange(n, dp, me, buf, ss, rs) / width + EPS))

    @pl.loop(0, seq // block)
    def _(i):
        rows = pl.ds(pl.multiple_of(i * block, block), block)
        cos, sine = cos_ref[rows, :], sin_ref[rows, :]
        for which, ref, factor in ((0, q_ref, HD ** (-0.5)), (1, k_ref, 1.0)):
            scale = scale_ref[rows, which : which + 1]
            for start in range(0, hc, HD):
                part = slice(start, start + HD)
                value = pre_ref[rows, which * hc + start : which * hc + start + HD] * scale
                ref[rows, part] = (
                    turn(value * gain_ref[which : which + 1, part], cos, sine) * factor
                ).astype(BF)

    @pl.loop(0, seq // block)
    def _(i):
        rows = pl.ds(pl.multiple_of(i * block, block), block)
        visible = mask_of(rows, col_ref, row_ref)
        for head in range(hc // HD):
            part = slice(head * HD, (head + 1) * HD)
            scores = jnp.where(visible, dot_t(q_ref[rows, part], k_ref[:, part]), -jnp.inf)
            top = jnp.max(scores, axis=1, keepdims=True)
            weights = jnp.exp(scores - top)
            total = jnp.sum(weights, axis=1, keepdims=True)
            o_ref[rows, part] = (dot(weights.astype(BF), v_ref[:, part]) / total).astype(BF)
            lse_ref[rows, head : head + 1] = top + jnp.log(total)

    owns[0].wait()
    for k in range(1, n_dp):
        source = (dp + n_dp - k) % n_dp
        remote(wo_ref, part_of(source), sw.at[k - 1], rw.at[k - 1], (source, me)).wait_recv()
    cols = slice(0, hc)
    sums = reduce_ctx(n, dp, me, o_ref, wo_all, cols, y_ref, pa, qa, pb, qb, s1, r1, s2, r2)

    def finish(rows):
        branch = y_ref[rows, :]
        h_ref[rows, :] = t_ref[rows, :].astype(F32) + branch * rms_scale(branch) * norm_ref[...]

    tiles(y_ref.shape[0], 16, finish)
    for copy in receives:
        copy.wait_recv()
    for copy in sums + behind_wo + behind_d:
        copy.wait_send()
    owns[1].wait()


def attend(x_all, w, wo, d, tokens, norm, gain, cos, sine, info_col, info_row, number):
    n_dp, n = lax.axis_size("dp"), lax.axis_size("ctx")
    seq, width = x_all.shape
    half, length, hc = n // 2, seq // n, w.shape[1] // 3
    dma = pltpu.SemaphoreType.DMA
    low = jax.ShapeDtypeStruct((seq, hc), BF)
    return pl.pallas_call(
        functools.partial(attend_kernel, n_dp, n),
        out_shape=(
            jax.ShapeDtypeStruct((length, width), F32),
            jax.ShapeDtypeStruct((length, width), F32),
            low,
            low,
            low,
            low,
            jax.ShapeDtypeStruct((seq, 2 * hc), F32),
            jax.ShapeDtypeStruct((seq, 8), F32),
            jax.ShapeDtypeStruct((seq, 8), F32),
            jax.ShapeDtypeStruct((width, hc), BF),
            jax.ShapeDtypeStruct(d.shape, BF),
        ),
        in_specs=[VMEM] * 2 + [ANY] * 2 + [VMEM] * 7,
        out_specs=(VMEM,) * 10 + (ANY,),
        scratch_shapes=[
            pltpu.VMEM((n, 8, seq), F32),
            pltpu.VMEM((half, length, width), BF),
            pltpu.VMEM((half, length, width), BF),
            pltpu.VMEM((half - 1, length, width), BF),
            pltpu.VMEM((half - 1, length, width), BF),
            dma((n - 1,)),
            dma((n - 1,)),
            dma((half,)),
            dma((half,)),
            dma((half - 1,)),
            dma((half - 1,)),
            dma((n_dp - 1,)),
            dma((n_dp - 1,)),
            dma((2 * n_dp - 1,)),
            dma((2 * n_dp - 1,)),
            dma((2,)),
        ],
        compiler_params=params_of(number),
        cost_estimate=cost(60),
        name="attend",
    )(x_all, w, wo, d, tokens, norm, gain, cos, sine, info_col, info_row)


def slab_give(n_dp, dp, me, g_ref, co_ref, sw, rw):
    tall = co_ref.shape[1]
    gives = []
    for k in range(1, n_dp):
        to = (dp + k) % n_dp
        part = pl.ds(pl.multiple_of(to * tall, tall), tall)
        copy = remote(g_ref.at[part, :], co_ref.at[k - 1], sw.at[k - 1], rw.at[k - 1], (to, me))
        copy.start()
        gives.append(copy)
    return gives


def slab_sum(dp, gives, g_ref, co_ref, out_ref):
    tall = co_ref.shape[1]
    total = g_ref[pl.ds(pl.multiple_of(dp * tall, tall), tall), :].astype(F32)
    for k, copy in enumerate(gives):
        copy.wait_recv()
        total = total + co_ref[k].astype(F32)
    out_ref[...] = total.astype(BF)


def greet_wide_group(n_dp, dp, me):
    partner = me + 1 - 2 * (me % 2)
    others = [(dp + k) % n_dp for k in range(1, n_dp)]
    greet([(dp, partner)] + [(d, c) for d in others for c in (me, partner)])


def attend_back_kernel(
    n_dp, n, e_ref, do_ref, h_ref, o_hbm, col_ref, row_ref, q_ref, k_ref, v_ref, lse_ref,
    dq_ref, dk_ref, dv_ref, h_out, wo_ref,
    o_ref, go_ref, co_ref, sh, rh, local, sw, rw,
):
    dp, me = lax.axis_index("dp"), lax.axis_index("ctx")
    seq, hc = q_ref.shape
    load = pltpu.make_async_copy(o_hbm, o_ref, local.at[1])
    load.start()
    block = min(seq, 256)
    count, index, place = group_of(n_dp, n, dp, me)
    greet_wide_group(n_dp, dp, me)
    swaps, receives = swap(h_ref, h_out, sh, rh, count, index, place)
    stay = pltpu.make_async_copy(h_ref.at[index], h_out.at[index], local.at[0])
    stay.start()

    load.wait()

    @pl.loop(0, n)
    def _(c):
        go_ref[:, pl.ds(pl.multiple_of(c * hc, hc), hc)] = t_dot(e_ref[...], o_ref[c]).astype(BF)

    gives = slab_give(n_dp, dp, me, go_ref, co_ref, sw, rw)
    dk_ref[...] = jnp.zeros_like(dk_ref)
    dv_ref[...] = jnp.zeros_like(dv_ref)

    def attention(i):
        rows = pl.ds(pl.multiple_of(i * block, block), block)
        visible = mask_of(rows, col_ref, row_ref)
        for head in range(hc // HD):
            part = slice(head * HD, (head + 1) * HD)
            query, key, value, back = q_ref[rows, part], k_ref[:, part], v_ref[:, part], do_ref[rows, part]
            scores = jnp.where(visible, dot_t(query, key), -jnp.inf)
            probs = jnp.exp(scores - lse_ref[rows, head : head + 1])
            d_probs = dot_t(back, value)
            delta = jnp.sum(probs * d_probs, axis=1, keepdims=True)
            d_scores = (probs * (d_probs - delta)).astype(BF)
            dq_ref[rows, part] = dot(d_scores, key)
            dk_ref[:, part] += t_dot(d_scores, query)
            dv_ref[:, part] += t_dot(probs.astype(BF), back)

    pl.loop(0, seq // block)(attention)
    slab_sum(dp, gives, go_ref, co_ref, wo_ref)
    for copy in receives:
        copy.wait_recv()
    for copy in swaps + gives:
        copy.wait_send()
    stay.wait()


def attend_back(e, do, h, o_all, info_col, info_row, q, k, v, lse, number):
    n_dp, n = lax.axis_size("dp"), lax.axis_size("ctx")
    (seq, hc), share = q.shape, e.shape[1]
    dma = pltpu.SemaphoreType.DMA
    return pl.pallas_call(
        functools.partial(attend_back_kernel, n_dp, n),
        out_shape=(
            *[jax.ShapeDtypeStruct((seq, hc), F32)] * 3,
            jax.ShapeDtypeStruct(h.shape, BF),
            jax.ShapeDtypeStruct((share // n_dp, n * hc), BF),
        ),
        in_specs=[VMEM, VMEM, ANY, ANY] + [VMEM] * 6,
        out_specs=(VMEM, VMEM, VMEM, ANY, VMEM),
        scratch_shapes=[
            pltpu.VMEM(o_all.shape, BF),
            pltpu.VMEM((share, n * hc), BF),
            pltpu.VMEM((n_dp - 1, share // n_dp, n * hc), BF),
            dma((2 * n_dp - 1,)),
            dma((2 * n_dp - 1,)),
            dma((2,)),
            dma((n_dp - 1,)),
            dma((n_dp - 1,)),
        ],
        compiler_params=params_of(number),
        cost_estimate=cost(45),
        name="attend_back",
    )(e, do, h, o_all, info_col, info_row, q, k, v, lse)


def project_back_kernel(
    n_dp, n, dq_in, dk_in, dv_ref, x_ref, gain_ref, cos_ref, sin_ref, pre_ref, scale_ref,
    d_ref, gain_out, g_ref, wv_ref,
    dq_ref, dk_ref, mean_ref, buf, go_ref, co_ref, ss, rs, sw, rw,
):
    dp, me = lax.axis_index("dp"), lax.axis_index("ctx")
    seq, hc = dv_ref.shape
    width = x_ref.shape[1]
    block = min(seq, 256)
    greet(
        [(dp, (me + k) % n) for k in range(1, n)] + [((dp + k) % n_dp, me) for k in range(1, n_dp)]
    )
    d_ref[:, 2 * hc :] = dv_ref[...].astype(BF)

    def values(part):
        go_ref[part, :] = t_dot(x_ref[:, part], d_ref[:, 2 * hc :]).astype(BF)

    tiles(width, 256, values)
    gives = slab_give(n_dp, dp, me, go_ref, co_ref, sw, rw)
    gain_out[...] = jnp.zeros_like(gain_out)

    @pl.loop(0, seq // block)
    def _(i):
        rows = pl.ds(pl.multiple_of(i * block, block), block)
        cos, sine = cos_ref[rows, :], sin_ref[rows, :]
        sums = jnp.zeros((8, block), F32)
        for which, source, ref, factor in (
            (0, dq_in, dq_ref, HD ** (-0.5)),
            (1, dk_in, dk_ref, 1.0),
        ):
            scale = scale_ref[rows, which : which + 1]
            for start in range(0, hc, HD):
                part = slice(start, start + HD)
                pre = pre_ref[rows, which * hc + start : which * hc + start + HD]
                value = turn(source[rows, part] * factor, cos, -sine)
                gain_out[which : which + 1, part] += jnp.sum(value * pre * scale, axis=0, keepdims=True)
                value = value * gain_ref[which : which + 1, part]
                ref[rows, part] = value
                sums += row_sums(value * pre, which)
        buf[me, :, rows] = sums

    mean_ref[...] = jnp.transpose(exchange(n, dp, me, buf, ss, rs) / width)

    @pl.loop(0, seq // block)
    def _(i):
        rows = pl.ds(pl.multiple_of(i * block, block), block)
        for which, ref in ((0, dq_ref), (1, dk_ref)):
            scale = scale_ref[rows, which : which + 1]
            mean = mean_ref[rows, which : which + 1]
            cols = slice(which * hc, (which + 1) * hc)
            value = scale * (ref[rows, :] - pre_ref[rows, cols] * (scale * scale * mean))
            d_ref[rows, cols] = value.astype(BF)

    def product(part):
        g_ref[part, :] = t_dot(x_ref[:, part], d_ref[:, : 2 * hc]).astype(BF)

    tiles(width, 256, product)
    slab_sum(dp, gives, go_ref, co_ref, wv_ref)
    for copy in gives:
        copy.wait_send()


def project_back(dq, dk, dv, x, gain, cos, sine, pre, scale, number):
    n_dp, n = lax.axis_size("dp"), lax.axis_size("ctx")
    (seq, hc), width = dq.shape, x.shape[1]
    dma = pltpu.SemaphoreType.DMA
    return pl.pallas_call(
        functools.partial(project_back_kernel, n_dp, n),
        out_shape=(
            jax.ShapeDtypeStruct((seq, 3 * hc), BF),
            jax.ShapeDtypeStruct((2, hc), F32),
            jax.ShapeDtypeStruct((width, 2 * hc), BF),
            jax.ShapeDtypeStruct((width // n_dp, hc), BF),
        ),
        in_specs=[VMEM] * 9,
        out_specs=(VMEM,) * 4,
        scratch_shapes=[
            pltpu.VMEM((seq, hc), F32),
            pltpu.VMEM((seq, hc), F32),
            pltpu.VMEM((seq, 8), F32),
            pltpu.VMEM((n, 8, seq), F32),
            pltpu.VMEM((width, hc), BF),
            pltpu.VMEM((n_dp - 1, width // n_dp, hc), BF),
            dma((n - 1,)),
            dma((n - 1,)),
            dma((n_dp - 1,)),
            dma((n_dp - 1,)),
        ],
        compiler_params=params_of(number),
        cost_estimate=cost(30),
        name="project_back",
    )(dq, dk, dv, x, gain, cos, sine, pre, scale)


def shards(
    inputs,
    cotangent,
    documents,
    block_place,
    params,
    first_moment,
    second_moment,
    gains,
    gains_first,
    gains_second,
):
    tokens = inputs[0]
    upstream = cotangent[0]
    length, width = tokens.shape
    n_ctx = lax.axis_size("ctx")
    n_dp = lax.axis_size("dp")
    me_ctx = lax.axis_index("ctx")
    seq = length * n_ctx
    rows = params.shape[0]
    ff = (params.shape[1] - 4 * width) // 3
    hc = width // n_ctx
    half, group = n_ctx // 2, 2 * n_dp
    fh = ff // group
    parities = [[2 * p + side for p in range(half)] for side in range(2)]

    def gather_pairs(w):
        w = lax.all_gather(
            w.reshape(group * rows, w.shape[2]), "ctx", axis=0, tiled=True, axis_index_groups=parities
        )
        return w.reshape(half, n_dp, 2 * rows, w.shape[1])

    def scatter_pairs(g):
        g = lax.psum_scatter(
            g.reshape(width, g.shape[3]),
            "ctx",
            scatter_dimension=0,
            tiled=True,
            axis_index_groups=parities,
        )
        return g.reshape(group, rows, g.shape[1])

    w_qkv, w_o, w_gu, w_d = arrange(params, width)
    w_gu, w_qkv, w_o, x_all = start(w_gu, w_qkv, w_o, tokens, 1)
    w_gu = gather_pairs(w_gu)
    w_qkv = gather_dp(w_qkv.reshape(n_ctx * rows, 3 * hc), 2)

    indices = jnp.arange(seq, dtype=jnp.int32)
    owners = indices // length
    placed = jnp.sum(
        jnp.where(
            owners[:, None] == jnp.arange(n_ctx, dtype=jnp.int32)[None, :], block_place[None, :], 0
        ),
        axis=1,
    )
    pos = placed * length + indices % length
    docs = documents[0]
    info_row = jnp.concatenate([pos[None], docs[None], jnp.zeros((6, seq), jnp.int32)])
    info_col = info_row.T
    cos_tab, sine_tab = rope_tables(pos, HD)
    cos_tab = jnp.concatenate([cos_tab, cos_tab], axis=1)
    sine_tab = jnp.concatenate([-sine_tab, sine_tab], axis=1)
    my_gains = lax.dynamic_slice_in_dim(gains[:2], me_ctx * hc, hc, axis=1)
    tables = (my_gains, cos_tab, sine_tab, info_col, info_row)

    branch, hidden1, queries, keys, values, attn_low, qk_pre, scales, lse, w_o, w_d = attend(
        x_all, w_qkv, w_o.reshape(n_ctx * rows, hc), w_d, tokens, gains[2:3], *tables, 3
    )

    result, d_mlp, g_ff_part, h1_all, gate_up, inner, w_d, w_o = ff_forward(
        hidden1, upstream, gains[3:4], w_gu, w_d.reshape(n_dp, 2 * rows, fh), w_o, 4
    )
    attn_low, d_mlp = lax.optimization_barrier((attn_low, d_mlp))
    attn_all = lax.all_gather(attn_low, "ctx", axis=0)
    d_gu, d_grad = ff_back(d_mlp, inner, w_d, gate_up, rows, 5)
    d_grad = scatter_pairs(d_grad)
    d_h1, d_branch, d_attn, g_attn_part, g_grad, u_grad = ff_scatter(
        d_gu, w_gu, h1_all, w_o, upstream, branch, gains[2:3], 6
    )
    g_grad, u_grad = scatter_pairs(g_grad), scatter_pairs(u_grad)

    d_query, d_key, d_value, d_grad, wo_grad = attend_back(
        d_branch, d_attn, d_grad, attn_all, info_col, info_row, queries, keys, values, lse, 8
    )
    d_qkv, d_gain, qk_grad, wv_grad = project_back(
        d_query, d_key, d_value, x_all, my_gains, cos_tab, sine_tab, qk_pre, scales, 10
    )
    qk_grad, g_grad, d_x = collect(qk_grad, g_grad, d_qkv, w_qkv, 9)
    d_input = d_h1 + d_x

    gain_part = jnp.concatenate(
        [
            lax.dynamic_update_slice(jnp.zeros((2, width), F32), d_gain, (0, me_ctx * hc)),
            g_attn_part,
            g_ff_part,
        ],
        axis=0,
    )
    attn_grad, u_grad, square_total, gain_total = total_over(
        qk_grad, wv_grad, wo_grad, u_grad, g_grad, d_grad, gain_part, 11
    )
    grad_norm = jnp.sqrt(square_total + jnp.sum(gain_total * gain_total))
    factor = CLIP / (grad_norm + 1e-06)
    new_params, new_first, new_second = adam(
        factor, params, first_moment, second_moment, attn_grad, wo_grad, g_grad, u_grad, d_grad
    )
    new_gains, new_gains_first, new_gains_second = adam_update(
        gains, gains_first, gains_second, gain_total * factor, GAIN_RATE, 0.0
    )
    return (
        result[None],
        d_input.astype(BF)[None],
        grad_norm,
        new_params,
        new_first,
        new_second,
        new_gains,
        new_gains_first,
        new_gains_second,
    )


def solution(mesh):
    split, whole = P("dp", "ctx", None), P(("dp", "ctx"), None)
    return jax.shard_map(
        shards,
        mesh=mesh,
        in_specs=(split, split, P("dp", None), P(), whole, whole, whole, P(), P(), P()),
        out_specs=(split, split, P(), whole, whole, whole, P(), P(), P()),
        check_vma=False,
    )
```

```python
import functools

import jax
import jax.numpy as jnp
from jax import lax
from jax.experimental import pallas as pl
from jax.experimental.pallas import tpu as pltpu
from jax.sharding import PartitionSpec as P

HD = 128
STEP = 10
EPS = 1e-06
THETA = 500000.0
CLIP = 1.0
BETA1 = 0.9
BETA2 = 0.95
RATE = 0.03
GAIN_RATE = 0.8
DECAY = 0.1
ADAM_EPS = 1e-08
BF = jnp.bfloat16
F32 = jnp.float32
MESH = pl.DeviceIdType.MESH
ANY = pl.BlockSpec(memory_space=pl.ANY)
VMEM = pl.BlockSpec(memory_space=pltpu.VMEM)


def rms_scale(values):
    return lax.rsqrt(jnp.mean(values * values, axis=-1, keepdims=True) + EPS)


def norm_back(upstream, source, scale):
    return scale * (
        upstream - source * scale * scale * jnp.mean(upstream * source, axis=-1, keepdims=True)
    )


def rope_tables(positions, head_size):
    half_size = head_size // 2
    freqs = THETA ** (-jnp.arange(half_size, dtype=jnp.float32) * 2.0 / head_size)
    angles = positions.astype(jnp.float32)[:, None] * freqs[None, :]
    return (jnp.cos(angles), jnp.sin(angles))


def adam_update(weight, first_in, second_in, clipped, rate, decay):
    new_first = BETA1 * first_in + (1.0 - BETA1) * clipped
    new_second = BETA2 * second_in + (1.0 - BETA2) * clipped * clipped
    first_hat = new_first / (1.0 - BETA1**STEP)
    second_hat = new_second / (1.0 - BETA2**STEP)
    new_weight = weight - rate * (first_hat / (jnp.sqrt(second_hat) + ADAM_EPS) + decay * weight)
    return (new_weight, new_first, new_second)


def dot(a, b):
    return jnp.dot(a, b, preferred_element_type=F32)


def dot_t(a, b):
    return lax.dot_general(a, b, (((1,), (1,)), ((), ())), preferred_element_type=F32)


def t_dot(a, b):
    return lax.dot_general(a, b, (((0,), (0,)), ((), ())), preferred_element_type=F32)


def greet(peers):
    barrier = pltpu.get_barrier_semaphore()
    for peer in peers:
        pl.semaphore_signal(barrier, inc=1, device_id=peer, device_id_type=MESH)
    pl.semaphore_wait(barrier, len(peers))


def remote(src, dst, send, recv, peer):
    return pltpu.make_async_remote_copy(
        src_ref=src, dst_ref=dst, send_sem=send, recv_sem=recv, device_id=peer, device_id_type=MESH
    )


def cost(us):
    return pl.CostEstimate(flops=0, bytes_accessed=us * 3_600_000, transcendentals=0)


def params_of(number, vmem=48):
    return pltpu.CompilerParams(
        collective_id=number, has_side_effects=True, vmem_limit_bytes=vmem * 1024 * 1024
    )


def line_steps(n, me, make_right, make_left):
    for s in range(n - 1):

        @pl.when((me < n - 1) & (me >= s))
        def _():
            make_right(s).start()

        @pl.when((me > 0) & (me + s < n))
        def _():
            make_left(s).start()

        @pl.when(me - 1 - s >= 0)
        def _():
            make_right(s, me - 1 - s).wait_recv()

        @pl.when(me + 1 + s < n)
        def _():
            make_left(s, me + 1 + s).wait_recv()

    for s in range(n - 1):

        @pl.when((me < n - 1) & (me >= s))
        def _():
            make_right(s).wait_send()

        @pl.when((me > 0) & (me + s < n))
        def _():
            make_left(s).wait_send()


def pairs_of(n, me):
    half = n // 2
    parity, pair = me % 2, me // 2
    partner = me + 1 - 2 * parity
    ahead = [2 * ((pair + k) % half) + parity for k in range(1, half)]
    behind = [2 * ((pair + half - k) % half) + parity for k in range(1, half)]
    return half, parity, pair, partner, ahead, behind


def gather_dp_kernel(n, x_ref, o_ref, local, sr, rr, sl, rl):
    me, ctx = lax.axis_index("dp"), lax.axis_index("ctx")

    def here(d):
        return (d, ctx)

    greet([here((me + 1) % n), here((me + n - 1) % n)])
    own = pltpu.make_async_copy(x_ref, o_ref.at[me], local)
    own.start()

    def right(s, block=None):
        b = me - s if block is None else block
        return remote(x_ref if s == 0 else o_ref.at[b], o_ref.at[b], sr.at[s], rr.at[s], here(me + 1))

    def left(s, block=None):
        b = me + s if block is None else block
        return remote(x_ref if s == 0 else o_ref.at[b], o_ref.at[b], sl.at[s], rl.at[s], here(me - 1))

    line_steps(n, me, right, left)
    own.wait()


def gather_dp(x, number):
    n = lax.axis_size("dp")
    out = pl.pallas_call(
        functools.partial(gather_dp_kernel, n),
        out_shape=jax.ShapeDtypeStruct((n,) + x.shape, x.dtype),
        in_specs=[ANY],
        out_specs=ANY,
        scratch_shapes=[pltpu.SemaphoreType.DMA] + [pltpu.SemaphoreType.DMA((n - 1,))] * 4,
        compiler_params=params_of(number),
        cost_estimate=cost(60),
        name="gather_dp",
    )(x)
    return out.reshape((n * x.shape[0],) + x.shape[1:])


def group_of(n_dp, n, dp, me):
    pair, parity = me // 2, me % 2
    return 2 * n_dp, 2 * dp + parity, lambda j: (j // 2, 2 * pair + j % 2)


def greet_all(n_dp, n, dp, me):
    partner = me + 1 - 2 * (me % 2)
    others = [(dp + k) % n_dp for k in range(1, n_dp)]
    greet([(dp, (me + k) % n) for k in range(1, n)] + [(d, c) for d in others for c in (me, partner)])


def across(mine, k, count):
    if count & (count - 1):
        return (mine + k) % count, (mine + count - k) % count
    bit, other = 1, mine
    while bit < count:
        if k & bit:
            other = other + bit - 2 * bit * ((other // bit) % 2)
        bit *= 2
    return other, other


def swap(src, dst, send, recv, count, mine, place):
    sends, receives = [], []
    for k in range(1, count):
        to, source = across(mine, k, count)
        sends.append(remote(src.at[to], dst.at[mine], send.at[k - 1], recv.at[k - 1], place(to)))
        receives.append(
            remote(src.at[mine], dst.at[source], send.at[k - 1], recv.at[k - 1], place(source))
        )
    for copy in sends:
        copy.start()
    return sends, receives


def tiles(total, tile, body):
    tile = min(total, tile)

    @pl.loop(0, total // tile)
    def _(j):
        body(pl.ds(pl.multiple_of(j * tile, tile), tile))


def reduce_ctx(n, dp, me, a_ref, w_ref, cols, o_ref, sa, ra, sb, rb, s1, r1, s2, r2, before=None):
    half, parity, pair, partner, ahead, behind = pairs_of(n, me)
    length, width = o_ref.shape

    def rows(block):
        return pl.ds(pl.multiple_of(block * length, length), length)

    first, second = [], []
    for k in range(half):
        target = (pair + k + 1) % half
        if before is not None:
            before(target, k == 0)

        def give(part):
            value = dot_t(a_ref[rows(2 * target + 1 - parity), :], w_ref[part, cols])
            sa[k, :, part] = value.astype(BF)

        tiles(width, 512, give)
        copy = remote(sa.at[k], ra.at[k], s1.at[k], r1.at[k], (dp, partner))
        copy.start()
        first.append(copy)
        copy.wait_recv()

        def keep(part):
            value = dot_t(a_ref[rows(2 * target + parity), :], w_ref[part, cols])
            value = value + ra[k, :, part].astype(F32)
            if k < half - 1:
                sb[k, :, part] = value.astype(BF)
            else:
                o_ref[:, part] = value

        tiles(width, 512, keep)
        if k < half - 1:
            copy = remote(sb.at[k], rb.at[k], s2.at[k], r2.at[k], (dp, 2 * target + parity))
            copy.start()
            second.append(copy)
    for k in range(half - 1):
        second[k].wait_recv()
        o_ref[...] += rb[k].astype(F32)
    return first + second


def load_rows(hbm, vmem, sems):
    half, n_dp, rows, _ = hbm.shape
    copies = []
    for d in range(n_dp):
        for p in range(half):
            part = pl.ds((d * half + p) * rows, rows)
            copies.append(pltpu.make_async_copy(hbm.at[p, d], vmem.at[part, :], sems.at[d * half + p]))
    for copy in copies:
        copy.start()
    return copies


def gather_group(n, dp, me, all_ref, length, sr, rr, sl, rl, sf, rf, process):
    parity = me % 2
    partner = me + 1 - 2 * parity

    def block(b, side):
        start = (2 * b + side) * length
        return all_ref.at[pl.ds(pl.multiple_of(start, length), length), :]

    def right(s, b):
        return remote(block(b, parity), block(b, parity), sr.at[s], rr.at[s], (dp + 1, me))

    def left(s, b):
        return remote(block(b, parity), block(b, parity), sl.at[s], rl.at[s], (dp - 1, me))

    def aside(b):
        return remote(block(b, parity), block(b, parity), sf.at[b], rf.at[b], (dp, partner))

    def from_aside(b):
        return remote(block(b, 1 - parity), block(b, 1 - parity), sf.at[b], rf.at[b], (dp, partner))

    for s in range(n):
        if s == 0:
            aside(dp).start()
        else:

            @pl.when(dp >= s)
            def _():
                right(s - 1, dp - s).wait_recv()

            @pl.when(dp + s < n)
            def _():
                left(s - 1, dp + s).wait_recv()

        @pl.when((dp < n - 1) & (dp >= s))
        def _():
            right(s, dp - s).start()

        @pl.when((dp > 0) & (dp + s < n))
        def _():
            left(s, dp + s).start()

        if s == 0:
            from_aside(dp).wait_recv()
            process(dp, True)
        else:

            @pl.when(dp >= s)
            def _():
                aside(dp - s).start()

            @pl.when(dp + s < n)
            def _():
                aside(dp + s).start()

            below = jnp.where(dp >= s, 1, 0)
            above = jnp.where(dp + s < n, 1, 0)

            @pl.loop(0, below + above)
            def _(j):
                b = jnp.where(j < below, dp - s, dp + s)
                from_aside(b).wait_recv()
                process(b, False)

    for s in range(n):

        @pl.when((dp < n - 1) & (dp >= s))
        def _():
            right(s, dp - s).wait_send()

        @pl.when((dp > 0) & (dp + s < n))
        def _():
            left(s, dp + s).wait_send()

        aside(s).wait_send()


def gather_sems(n_dp):
    return [pltpu.SemaphoreType.DMA((n_dp,))] * 6


def line_sum(n, dp, me, make, val, o_ref, buf, send, recv, sync, between=None):
    def move(way, d):
        to = jnp.where(way == 1, dp + 1, dp - 1)
        return remote(buf.at[way, d], buf.at[way, d], send.at[way, d], recv.at[way, d], (to, me))

    def steps(body):
        for j in range(1, n):

            @pl.loop(0, 2)
            def _(phase):
                way = jnp.where(2 * dp < n, 1 - phase, phase)
                d = jnp.where(way == 1, n - j, j - 1)
                first = jnp.where(way == 1, 0, n - 1)
                ahead = jnp.where(way == 1, d - dp, dp - d)

                @pl.when(ahead > 0)
                def _():
                    body(way, d, dp == first)

    def begin(way, d, starts):
        make(d, val.at[d])

        @pl.when(starts)
        def _():
            def put(part):
                buf[way, d, part, :] = val[d, part, :].astype(BF)

            tiles(val.shape[1], 32, put)
            move(way, d).start()

    def follow(way, d, starts):
        @pl.when(jnp.logical_not(starts))
        def _():
            move(way, d).wait_recv()

            def add(part):
                buf[way, d, part, :] = (val[d, part, :] + buf[way, d, part, :].astype(F32)).astype(BF)

            tiles(val.shape[1], 32, add)
            move(way, d).start()

    steps(begin)
    make(dp, o_ref)
    steps(follow)
    if between is not None:
        between()
    for way, first in ((1, 0), (0, n - 1)):

        @pl.when(dp != first)
        def _():
            move(way, dp).wait_recv()

            def add(part):
                o_ref[part, :] += buf[way, dp, part, :].astype(F32)

            tiles(val.shape[1], 32, add)

    sync()
    steps(lambda way, d, starts: move(way, d).wait_send())


def line_scratch(n_dp, length, width):
    return [
        pltpu.VMEM((n_dp, length, width), F32),
        pltpu.VMEM((2, n_dp, length, width), BF),
        pltpu.SemaphoreType.DMA((2, n_dp)),
        pltpu.SemaphoreType.DMA((2, n_dp)),
    ]


def part_of_pair(dp, me, a_ref, w_ref, length, sa, ra, s1, r1):
    parity = me % 2
    partner = me + 1 - 2 * parity

    def make(d, out):
        def rows(side):
            return pl.ds(pl.multiple_of((2 * d + side) * length, length), length)

        def give(part):
            sa[d, :, part] = dot_t(a_ref[rows(1 - parity), :], w_ref[part, :]).astype(BF)

        tiles(out.shape[1], 512, give)
        copy = remote(sa.at[d], ra.at[d], s1.at[d], r1.at[d], (dp, partner))
        copy.start()

        def keep(part):
            out[:, part] = dot_t(a_ref[rows(parity), :], w_ref[part, :])

        tiles(out.shape[1], 512, keep)
        copy.wait_recv()

        def add(part):
            out[part, :] += ra[d, part, :].astype(F32)

        tiles(length, 32, add)

    def done(n):
        for d in range(n):
            remote(sa.at[d], ra.at[d], s1.at[d], r1.at[d], (dp, partner)).wait_send()

    return make, done


def pair_scratch(n_dp, length, width):
    return [pltpu.VMEM((n_dp, length, width), BF)] * 2 + [pltpu.SemaphoreType.DMA((n_dp,))] * 2


def greet_group(n_dp, dp, me):
    partner = me + 1 - 2 * (me % 2)
    greet([(dp, partner)] + [((dp + k) % n_dp, me) for k in range(1, n_dp)])


def ff_forward_kernel(
    n_dp, n, h_ref, up_ref, gain_ref, gu_hbm, d_hbm, wo_hbm,
    res_ref, dm_ref, gp_ref, all_out, pre_out, hid_out, d_out, wo_out,
    all_ref, pre_ref, hid_ref, d_ref, gu_ref, acc, sem_gu, sem_d, sem_out, sd, rd, so, ro, fo, go, *rest,
):
    gather, pair_refs, line_refs = rest[:6], rest[6:10], rest[10:]
    dp, me = lax.axis_index("dp"), lax.axis_index("ctx")
    length, width = h_ref.shape
    fh = hid_ref.shape[1]
    half, parity, pair, partner, ahead, behind = pairs_of(n, me)
    loads_gu = load_rows(gu_hbm, gu_ref, sem_gu)
    mine = pl.ds(pl.multiple_of((2 * dp + me % 2) * length, length), length)
    all_ref[mine, :] = h_ref[...].astype(BF)
    greet(
        [(dp, partner)]
        + [((dp + k) % n_dp, me) for k in range(1, n_dp)]
        + [(dp, a) for a in ahead]
    )
    tall = d_hbm.shape[1]

    def down(d, p):
        return d_ref.at[pl.ds(pl.multiple_of((d * half + p) * tall, tall), tall), :]

    loads_d = [pltpu.make_async_copy(d_hbm.at[d], down(d, pair), sem_d.at[d]) for d in range(n_dp)]
    spreads = [
        remote(d_hbm.at[d], down(d, pair), sd.at[k, d], rd.at[k, d], (dp, a))
        for k, a in enumerate(ahead)
        for d in range(n_dp)
    ]
    for copy in spreads + loads_d:
        copy.start()

    def process(b, own):
        rows = pl.ds(pl.multiple_of(2 * b * length, 2 * length), 2 * length)
        if own:
            for copy in loads_gu:
                copy.wait()

        def hidden(part):
            second = pl.ds(pl.multiple_of(fh + part.start, part.size), part.size)
            gate = dot(all_ref[rows, :], gu_ref[:, part])
            upper = dot(all_ref[rows, :], gu_ref[:, second])
            pre_ref[rows, part] = gate
            pre_ref[rows, second] = upper
            hid_ref[rows, part] = (gate * jax.nn.sigmoid(gate) * upper).astype(BF)

        tiles(fh, 256, hidden)

    gather_group(n_dp, dp, me, all_ref, length, *gather, process)
    for copy in loads_d:
        copy.wait()
    for k, b in enumerate(behind):
        for d in range(n_dp):
            remote(d_hbm.at[d], down(d, b // 2), sd.at[k, d], rd.at[k, d], (dp, b)).wait_recv()

    outs = [
        pltpu.make_async_copy(ref, out, sem_out.at[i])
        for i, (ref, out) in enumerate(
            ((all_ref, all_out), (pre_ref, pre_out), (hid_ref, hid_out), (d_ref, d_out))
        )
    ]
    outs.append(pltpu.make_async_copy(wo_hbm, wo_out.at[me], sem_out.at[4]))
    spreads_wo = [
        remote(wo_hbm, wo_out.at[me], so.at[k], ro.at[k], (dp, a)) for k, a in enumerate(ahead + [partner])
    ]
    for copy in outs + spreads_wo:
        copy.start()
    make, done = part_of_pair(dp, me, hid_ref, d_ref, length, *pair_refs)

    gp_ref[...] = jnp.zeros_like(gp_ref)

    def finish(rows):
        out, up, gain = acc[rows, :], up_ref[rows, :].astype(F32), gain_ref[...]
        scale = rms_scale(out)
        res_ref[rows, :] = (h_ref[rows, :] + out * scale * gain).astype(BF)
        gp_ref[...] += jnp.sum(up * out * scale, axis=0, keepdims=True)
        dm_ref[rows, :] = norm_back(up * gain, out, scale).astype(BF)

    forwards = []

    def last():
        for k, b in enumerate(behind):
            remote(wo_hbm, wo_out.at[b], so.at[k], ro.at[k], (dp, b)).wait_recv()
            forward = remote(wo_out.at[b], wo_out.at[b], fo.at[k], go.at[k], (dp, partner))
            forward.start()
            forwards.append(forward)
        tiles(length, 16, finish)

    line_sum(n_dp, dp, me, make, line_refs[0], acc, *line_refs[1:], last)
    done(n_dp)
    spreads_wo[-1].wait_recv()
    for copy in forwards:
        copy.wait_recv()
    for copy in spreads + spreads_wo + forwards:
        copy.wait_send()
    for copy in outs:
        copy.wait()


def ff_forward(h1, up, gain, w_gu, w_d, w_o, number):
    n_dp, n = lax.axis_size("dp"), lax.axis_size("ctx")
    (length, width), fh = h1.shape, w_d.shape[2]
    tokens = 2 * n_dp * length
    half = n // 2
    low = jax.ShapeDtypeStruct((length, width), BF)
    return pl.pallas_call(
        functools.partial(ff_forward_kernel, n_dp, n),
        out_shape=(
            low,
            low,
            jax.ShapeDtypeStruct((1, width), F32),
            jax.ShapeDtypeStruct((tokens, width), BF),
            jax.ShapeDtypeStruct((tokens, 2 * fh), F32),
            jax.ShapeDtypeStruct((tokens, fh), BF),
            jax.ShapeDtypeStruct((width, fh), BF),
            jax.ShapeDtypeStruct((n,) + w_o.shape, BF),
        ),
        in_specs=[VMEM] * 3 + [ANY] * 3,
        out_specs=(VMEM,) * 3 + (ANY,) * 5,
        scratch_shapes=[
            pltpu.VMEM((tokens, width), BF),
            pltpu.VMEM((tokens, 2 * fh), F32),
            pltpu.VMEM((tokens, fh), BF),
            pltpu.VMEM((width, fh), BF),
            pltpu.VMEM((width, 2 * fh), BF),
            pltpu.VMEM((length, width), F32),
            pltpu.SemaphoreType.DMA((half * n_dp,)),
            pltpu.SemaphoreType.DMA((n_dp,)),
            pltpu.SemaphoreType.DMA((5,)),
            pltpu.SemaphoreType.DMA((half - 1, n_dp)),
            pltpu.SemaphoreType.DMA((half - 1, n_dp)),
            pltpu.SemaphoreType.DMA((half,)),
            pltpu.SemaphoreType.DMA((half,)),
            pltpu.SemaphoreType.DMA((half - 1,)),
            pltpu.SemaphoreType.DMA((half - 1,)),
        ]
        + gather_sems(n_dp)
        + pair_scratch(n_dp, length, width)
        + line_scratch(n_dp, length, width),
        compiler_params=params_of(number, 58),
        cost_estimate=cost(90),
        name="ff_forward",
    )(h1, up, gain, w_gu, w_d, w_o)


def store_rows(n_dp, value_of, out):
    half, _, rows, _ = out.shape

    @pl.loop(0, n_dp * half)
    def _(r):
        out[r % half, r // half] = value_of(pl.ds(pl.multiple_of(r * rows, rows), rows)).astype(BF)


def ff_back_kernel(
    n_dp, dm_ref, hid_ref, d_hbm, pre_hbm, dgu_ref, gd_ref,
    all_ref, d_ref, pre_ref, acc, sem_d, sem_p, *gather,
):
    dp, me = lax.axis_index("dp"), lax.axis_index("ctx")
    length, width = dm_ref.shape
    fh = d_ref.shape[1]
    load = pltpu.make_async_copy(d_hbm, d_ref, sem_d)
    load.start()

    def rows_of(b):
        return pl.ds(pl.multiple_of(2 * b * length, 2 * length), 2 * length)

    def load_pre(b):
        return pltpu.make_async_copy(pre_hbm.at[rows_of(b), :], pre_ref.at[rows_of(b), :], sem_p.at[b])

    for k in range(n_dp):
        load_pre((dp + k) % n_dp).start()
    mine = pl.ds(pl.multiple_of((2 * dp + me % 2) * length, length), length)
    all_ref[mine, :] = dm_ref[...]
    greet_group(n_dp, dp, me)

    def process(b, own):
        rows = rows_of(b)
        if own:
            load.wait()
        load_pre(b).wait()

        def hidden(part):
            second = pl.ds(pl.multiple_of(fh + part.start, part.size), part.size)
            back = dot(all_ref[rows, :], d_ref[:, part])
            gate, upper = pre_ref[rows, part], pre_ref[rows, second]
            sig = jax.nn.sigmoid(gate)
            dgu_ref[rows, part] = (back * upper * sig * (1.0 + gate * (1.0 - sig))).astype(BF)
            dgu_ref[rows, second] = (back * gate * sig).astype(BF)

        tiles(fh, 256, hidden)

        def product(part):
            value = t_dot(all_ref[rows, part], hid_ref[rows, :])
            acc[part, :] = value if own else acc[part, :] + value

        tiles(width, 256, product)

    gather_group(n_dp, dp, me, all_ref, length, *gather, process)
    store_rows(n_dp, lambda part: acc[part, :], gd_ref)


def ff_back(dm, hid, w_d, pre, rows, number):
    n_dp, half = lax.axis_size("dp"), lax.axis_size("ctx") // 2
    (length, width), fh = dm.shape, w_d.shape[1]
    tokens = 2 * n_dp * length
    return pl.pallas_call(
        functools.partial(ff_back_kernel, n_dp),
        out_shape=(
            jax.ShapeDtypeStruct((tokens, 2 * fh), BF),
            jax.ShapeDtypeStruct((half, n_dp, 2 * rows, fh), BF),
        ),
        in_specs=[VMEM, VMEM, ANY, ANY],
        out_specs=(VMEM,) * 2,
        scratch_shapes=[
            pltpu.VMEM((tokens, width), BF),
            pltpu.VMEM((width, fh), BF),
            pltpu.VMEM((tokens, 2 * fh), F32),
            pltpu.VMEM((width, fh), F32),
            pltpu.SemaphoreType.DMA,
            pltpu.SemaphoreType.DMA((n_dp,)),
        ]
        + gather_sems(n_dp),
        compiler_params=params_of(number, 58),
        cost_estimate=cost(45),
        name="ff_back",
    )(dm, hid, w_d, pre)


def ff_scatter_kernel(
    n_dp, n, dgu_ref, gu_hbm, all_hbm, wo_hbm, up_ref, branch_ref, gain_ref, dh_ref, dc_ref, do_ref, gp_ref, gg_out, gv_out,
    gg_ref, gv_ref, gu_ref, all_ref, wo_ref, give_ref, db_ref, mix_ref, acc, sem_gu, sem_all, sem_out, ss, rs, sc, rc, *rest,
):
    dp, me = lax.axis_index("dp"), lax.axis_index("ctx")
    length, width = dh_ref.shape
    pair_refs, line_refs = rest[:4], rest[4:]
    half, parity, pair, partner, ahead, behind = pairs_of(n, me)
    _, _, rows, fh = gg_ref.shape
    loads = load_rows(gu_hbm, gu_ref, sem_gu)
    load = pltpu.make_async_copy(all_hbm, all_ref, sem_all)
    load.start()
    load_wo = pltpu.make_async_copy(wo_hbm, wo_ref, sem_out.at[2])
    load_wo.start()
    greet(
        [(dp, (me + k) % n) for k in range(1, n)] + [((dp + k) % n_dp, me) for k in range(1, n_dp)]
    )
    for copy in loads:
        copy.wait()

    make, done = part_of_pair(dp, me, dgu_ref, gu_ref, length, *pair_refs)
    gp_ref[...] = jnp.zeros_like(gp_ref)

    def finish(rows):
        grad, branch = dh_ref[rows, :] + up_ref[rows, :].astype(F32), branch_ref[rows, :]
        scale = rms_scale(branch)
        dh_ref[rows, :] = grad
        gp_ref[...] += jnp.sum(grad * branch * scale, axis=0, keepdims=True)
        db_ref[rows, :] = norm_back(grad * gain_ref[...], branch, scale).astype(BF)

    load.wait()
    tall = acc.shape[0]

    def grads():
        @pl.loop(0, width // tall)
        def _(j):
            acc[...] = t_dot(all_ref[:, pl.ds(pl.multiple_of(j * tall, tall), tall)], dgu_ref[...])
            for s in range(tall // rows):
                r = j * (tall // rows) + s
                part = slice(s * rows, (s + 1) * rows)
                gg_ref[r % half, r // half] = acc[part, :fh].astype(BF)
                gv_ref[r % half, r // half] = acc[part, fh:].astype(BF)

    val, *line = line_refs
    line_sum(n_dp, dp, me, make, val, dh_ref, *line, lambda: tiles(length, 16, finish), grads)
    done(n_dp)
    outs = [
        pltpu.make_async_copy(ref, out, sem_out.at[i])
        for i, (ref, out) in enumerate(((gg_ref, gg_out), (gv_ref, gv_out)))
    ]
    for copy in outs:
        copy.start()
    load_wo.wait()

    def mine(c):
        return pl.ds(pl.multiple_of(c * length, length), length)

    def send(k):
        to = (me + k) % n
        return remote(give_ref.at[to], do_ref.at[mine(me), :], ss.at[k - 1], rs.at[k - 1], (dp, to))

    def receive(k):
        source = (me + n - k) % n
        return remote(give_ref.at[me], do_ref.at[mine(source), :], ss.at[k - 1], rs.at[k - 1], (dp, source))

    own = rows // 2
    share = n_dp * own
    for c in range(n):
        for d in range(n_dp):
            start, source = c * share + d * own, (d * n + c) * own
            mix_ref[:, start : start + own] = db_ref[:, source : source + own]

    def share_of(c):
        return mix_ref.at[:, pl.ds(pl.multiple_of(c * share, share), share)]

    def send_share(k):
        to = (me + k) % n
        return remote(share_of(to), dc_ref.at[mine(me), :], sc.at[k - 1], rc.at[k - 1], (dp, to))

    def receive_share(k):
        source = (me + n - k) % n
        return remote(share_of(me), dc_ref.at[mine(source), :], sc.at[k - 1], rc.at[k - 1], (dp, source))

    stay = pltpu.make_async_copy(share_of(me), dc_ref.at[mine(me), :], sem_out.at[3])
    stay.start()

    @pl.loop(1, n)
    def _(k):
        to = (me + k) % n
        send_share(k).start()
        give_ref[to] = dot(db_ref[...], wo_ref[to]).astype(BF)
        send(k).start()

    do_ref[mine(me), :] = dot(db_ref[...], wo_ref[me]).astype(BF)
    for k in range(1, n):
        receive(k).wait_recv()
        receive_share(k).wait_recv()
    for k in range(1, n):
        send(k).wait_send()
        send_share(k).wait_send()
    stay.wait()
    for copy in outs:
        copy.wait()


def ff_scatter(dgu, w_gu, h1_all, wo_all, up, branch, gain, number):
    n_dp, n = lax.axis_size("dp"), lax.axis_size("ctx")
    length, width = up.shape
    hc = wo_all.shape[2]
    grad = jax.ShapeDtypeStruct(w_gu.shape[:3] + (w_gu.shape[3] // 2,), BF)
    return pl.pallas_call(
        functools.partial(ff_scatter_kernel, n_dp, n),
        out_shape=(
            jax.ShapeDtypeStruct((length, width), F32),
            jax.ShapeDtypeStruct((n * length, width // n), BF),
            jax.ShapeDtypeStruct((n * length, hc), BF),
            jax.ShapeDtypeStruct((1, width), F32),
            grad,
            grad,
        ),
        in_specs=[VMEM, ANY, ANY, ANY] + [VMEM] * 3,
        out_specs=(VMEM,) * 4 + (ANY,) * 2,
        scratch_shapes=[
            pltpu.VMEM(grad.shape, BF),
            pltpu.VMEM(grad.shape, BF),
            pltpu.VMEM((width, w_gu.shape[3]), BF),
            pltpu.VMEM(h1_all.shape, BF),
            pltpu.VMEM(wo_all.shape, BF),
            pltpu.VMEM((n, length, hc), BF),
            pltpu.VMEM((length, width), BF),
            pltpu.VMEM((length, width), BF),
            pltpu.VMEM((256, w_gu.shape[3]), F32),
            pltpu.SemaphoreType.DMA((w_gu.shape[0] * n_dp,)),
            pltpu.SemaphoreType.DMA,
            pltpu.SemaphoreType.DMA((4,)),
            pltpu.SemaphoreType.DMA((n - 1,)),
            pltpu.SemaphoreType.DMA((n - 1,)),
            pltpu.SemaphoreType.DMA((n - 1,)),
            pltpu.SemaphoreType.DMA((n - 1,)),
        ]
        + pair_scratch(n_dp, length, width)
        + line_scratch(n_dp, length, width),
        compiler_params=params_of(number, 60),
        cost_estimate=cost(50),
        name="ff_scatter",
    )(dgu, w_gu, h1_all, wo_all, up, branch, gain)


def start_kernel(
    n_dp, n, p_hbm, x_ref, h_ref, o_ref, p_ref, y_ref, d_ref,
    p_all, g_ref, w_ref, v_ref, local, sg, rg, sa, ra, sv, rv, ss, rs, fs, fr,
):
    dp, me = lax.axis_index("dp"), lax.axis_index("ctx")
    half, parity, pair, partner, ahead, behind = pairs_of(n, me)
    count, mine, place = group_of(n_dp, n, dp, me)
    columns = p_all.shape[2]
    fh, hc = d_ref.shape[2], v_ref.shape[2]
    loads = [
        pltpu.make_async_copy(
            p_hbm.at[:, pl.ds(part * columns, columns)], p_all.at[part], local.at[part]
        )
        for part in range(4)
    ]
    for part in (1, 2, 0, 3):
        loads[part].start()
    greet_all(n_dp, n, dp, me)
    gathers = [
        remote(x_ref, y_ref.at[me], ss.at[k], rs.at[k], (dp, a))
        for k, a in enumerate(ahead + [partner])
    ]
    own_x = pltpu.make_async_copy(x_ref, y_ref.at[me], local.at[4])
    for copy in gathers + [own_x]:
        copy.start()
    for part in (1, 2):
        loads[part].wait()
        for j in range(count):
            g_ref[j, :, (part - 1) * fh : part * fh] = p_all[part, :, j * fh : (j + 1) * fh].astype(BF)
    sends, receives = swap(g_ref, h_ref, sg, rg, count, mine, place)
    loads[0].wait()
    for c in range(n):
        for matrix in range(4):
            start = (matrix * n + c) * hc
            value = p_all[0, :, start : start + hc].astype(BF)
            if matrix < 3:
                w_ref[c, :, matrix * hc : (matrix + 1) * hc] = value
            else:
                v_ref[c] = value
    for src, dst, send, recv in ((w_ref, o_ref, sa, ra), (v_ref, p_ref, sv, rv)):
        more, waits = swap(src, dst, send, recv, n, me, lambda c: (dp, c))
        sends += more
        receives += waits
    owns = [
        pltpu.make_async_copy(g_ref.at[mine], h_ref.at[mine], local.at[5]),
        pltpu.make_async_copy(w_ref.at[me], o_ref.at[me], local.at[6]),
        pltpu.make_async_copy(v_ref.at[me], p_ref.at[me], local.at[7]),
    ]
    for copy in owns:
        copy.start()
    loads[3].wait()
    for j in range(count):
        d_ref[j] = p_all[3, :, j * fh : (j + 1) * fh].astype(BF)
    forwards = []
    for k, b in enumerate(behind):
        remote(x_ref, y_ref.at[b], ss.at[k], rs.at[k], (dp, b)).wait_recv()
        forward = remote(y_ref.at[b], y_ref.at[b], fs.at[k], fr.at[k], (dp, partner))
        forward.start()
        forwards.append(forward)
    gathers[-1].wait_recv()
    for copy in receives:
        copy.wait_recv()
    for forward in forwards:
        forward.wait()
    for copy in sends + gathers:
        copy.wait_send()
    for copy in owns + [own_x]:
        copy.wait()


def start(params, x, number):
    n_dp, n = lax.axis_size("dp"), lax.axis_size("ctx")
    half, count = n // 2, 2 * n_dp
    (rows, columns), width = params.shape, x.shape[1]
    fh, hc = columns // 4 // count, width // n
    dma = pltpu.SemaphoreType.DMA
    g, w, v = (count, rows, 2 * fh), (n, rows, 3 * hc), (n, rows, hc)
    g_out, w_out, v_out, x_all, d_out = pl.pallas_call(
        functools.partial(start_kernel, n_dp, n),
        out_shape=(
            jax.ShapeDtypeStruct(g, BF),
            jax.ShapeDtypeStruct(w, BF),
            jax.ShapeDtypeStruct(v, BF),
            jax.ShapeDtypeStruct((n,) + x.shape, x.dtype),
            jax.ShapeDtypeStruct((count, rows, fh), BF),
        ),
        in_specs=[ANY] * 2,
        out_specs=(ANY,) * 4 + (VMEM,),
        scratch_shapes=[
            pltpu.VMEM((4, rows, columns // 4), F32),
            pltpu.VMEM(g, BF),
            pltpu.VMEM(w, BF),
            pltpu.VMEM(v, BF),
            dma((8,)),
        ]
        + [dma((count - 1,))] * 2
        + [dma((n - 1,))] * 4
        + [dma((half,))] * 2
        + [dma((half - 1,))] * 2,
        compiler_params=params_of(number),
        cost_estimate=cost(45),
        name="start",
    )(params, x)
    return g_out, w_out, v_out, x_all.reshape(-1, width), d_out


def collect_kernel(
    n_dp, n, g_ref, h_ref, a_ref, w_ref, o_ref, h_out, y_ref,
    acc, pa, qa, pb, qb, local, s1, r1, s2, r2, sh, rh, *line_refs,
):
    dp, me = lax.axis_index("dp"), lax.axis_index("ctx")
    tall = acc.shape[0]
    count, index, place = group_of(n_dp, n, dp, me)
    greet_all(n_dp, n, dp, me)

    def make(d, out):
        def put(part):
            rows = pl.ds(pl.multiple_of(d * tall + part.start, part.size), part.size)
            out[part, :] = g_ref[rows, :].astype(F32)

        tiles(tall, 64, put)

    cols = slice(0, a_ref.shape[1])
    stay = pltpu.make_async_copy(h_ref.at[index], h_out.at[index], local)
    stay.start()
    later = []

    def between():
        later.extend(swap(h_ref, h_out, sh, rh, count, index, place))
        later.append(reduce_ctx(n, dp, me, a_ref, w_ref, cols, y_ref, pa, qa, pb, qb, s1, r1, s2, r2))

    def last():
        def put(part):
            o_ref[part, :] = acc[part, :].astype(BF)

        tiles(tall, 64, put)

    val, *line = line_refs
    line_sum(n_dp, dp, me, make, val, acc, *line, last, between)
    swaps, receives, sums = later
    for copy in receives:
        copy.wait_recv()
    stay.wait()
    for copy in swaps + sums:
        copy.wait_send()


def collect(g, h, a, w, number):
    n_dp, n = lax.axis_size("dp"), lax.axis_size("ctx")
    tall, width = g.shape[0] // n_dp, g.shape[1]
    half, length, features = n // 2, a.shape[0] // n, w.shape[0]
    dma = pltpu.SemaphoreType.DMA
    return pl.pallas_call(
        functools.partial(collect_kernel, n_dp, n),
        out_shape=(
            jax.ShapeDtypeStruct((tall, width), BF),
            jax.ShapeDtypeStruct(h.shape, BF),
            jax.ShapeDtypeStruct((length, features), F32),
        ),
        in_specs=[VMEM, ANY, VMEM, VMEM],
        out_specs=(VMEM, ANY, VMEM),
        scratch_shapes=[
            pltpu.VMEM((tall, width), F32),
            pltpu.VMEM((half, length, features), BF),
            pltpu.VMEM((half, length, features), BF),
            pltpu.VMEM((half - 1, length, features), BF),
            pltpu.VMEM((half - 1, length, features), BF),
            dma,
            dma((half,)),
            dma((half,)),
            dma((half - 1,)),
            dma((half - 1,)),
            dma((2 * n_dp - 1,)),
            dma((2 * n_dp - 1,)),
        ]
        + line_scratch(n_dp, tall, width),
        compiler_params=params_of(number),
        cost_estimate=cost(70),
        name="collect",
    )(g, h, a, w)


def total_kernel(
    n_dp, n, qk_ref, wv_ref, wo_ref, u_ref, gg_ref, gd_ref, qk_gain, attn_gain, ff_gain, ga_ref, gu_ref, o_ref,
    sb, mine, buf, part, all_parts, local, sx, rx, sh, rh, ss, rs, st, rt,
):
    dp, me = lax.axis_index("dp"), lax.axis_index("ctx")
    hc = wv_ref.shape[2]
    count, index, place = group_of(n_dp, n, dp, me)
    greet_all(n_dp, n, dp, me)
    swaps, receives = swap(u_ref, gu_ref, sh, rh, count, index, place)
    stay = pltpu.make_async_copy(u_ref.at[index], gu_ref.at[index], local)
    stay.start()
    sb[:, :, : 2 * hc] = qk_ref[...]
    sb[:, :, 2 * hc : 3 * hc] = wv_ref[...]
    more, waits = swap(sb, ga_ref, sx, rx, n, me, lambda c: (dp, c))
    ga_ref[me] = sb[me]

    def squares(ref):
        acc = jnp.zeros((ref.shape[1], ref.shape[2]), F32)
        for i in range(ref.shape[0]):
            block = ref[i].astype(F32)
            acc += block * block
        return jnp.sum(jnp.sum(acc, axis=0, keepdims=True), axis=1, keepdims=True)

    total = squares(gg_ref) + squares(gd_ref) + squares(wo_ref)
    for copy in waits:
        copy.wait_recv()
    total += squares(ga_ref)
    for copy in receives:
        copy.wait_recv()
    stay.wait()
    total += squares(gu_ref)
    mine[...] = jnp.zeros_like(mine)
    mine[0:2, pl.ds(pl.multiple_of(me * hc, hc), hc)] = qk_gain[...]
    mine[2:3, :] = attn_gain[...]
    mine[3:4, :] = ff_gain[...]
    mine[4:5, :] = jnp.broadcast_to(total, (1, mine.shape[1]))
    copies = swaps + more
    for k in range(1, n):
        copy = remote(mine, buf.at[me], ss.at[k - 1], rs.at[k - 1], (dp, (me + k) % n))
        copy.start()
        copies.append(copy)
    buf[me] = mine[...]
    for k in range(1, n):
        source = (me + n - k) % n
        remote(mine, buf.at[source], ss.at[k - 1], rs.at[k - 1], (dp, source)).wait_recv()
    acc = buf[0]
    for j in range(1, n):
        acc = acc + buf[j]
    part[...] = acc
    all_parts[dp] = acc
    for k in range(1, n_dp):
        copy = remote(part, all_parts.at[dp], st.at[k - 1], rt.at[k - 1], ((dp + k) % n_dp, me))
        copy.start()
        copies.append(copy)
    for k in range(1, n_dp):
        source = (dp + n_dp - k) % n_dp
        remote(part, all_parts.at[source], st.at[k - 1], rt.at[k - 1], (source, me)).wait_recv()
    acc = all_parts[0]
    for j in range(1, n_dp):
        acc = acc + all_parts[j]
    o_ref[...] = acc
    for copy in copies:
        copy.wait_send()


def total_over(qk, wv, wo, u, gg, gd, qk_gain, attn_gain, ff_gain, number):
    n_dp, n = lax.axis_size("dp"), lax.axis_size("ctx")
    rows, hc = qk.shape[0] // n, wv.shape[1]
    shape = (8, attn_gain.shape[1])
    dma = pltpu.SemaphoreType.DMA
    return pl.pallas_call(
        functools.partial(total_kernel, n_dp, n),
        out_shape=(
            jax.ShapeDtypeStruct((n, rows, 3 * hc), BF),
            jax.ShapeDtypeStruct(u.shape, BF),
            jax.ShapeDtypeStruct(shape, F32),
        ),
        in_specs=[VMEM] * 3 + [ANY] + [VMEM] * 5,
        out_specs=(VMEM,) * 3,
        scratch_shapes=[
            pltpu.VMEM((n, rows, 3 * hc), BF),
            pltpu.VMEM(shape, F32),
            pltpu.VMEM((n,) + shape, F32),
            pltpu.VMEM(shape, F32),
            pltpu.VMEM((n_dp,) + shape, F32),
            dma,
            dma((n - 1,)),
            dma((n - 1,)),
            dma((2 * n_dp - 1,)),
            dma((2 * n_dp - 1,)),
            dma((n - 1,)),
            dma((n - 1,)),
            dma((n_dp - 1,)),
            dma((n_dp - 1,)),
        ],
        compiler_params=params_of(number),
        cost_estimate=cost(35),
        name="total",
    )(
        qk.reshape(n, rows, 2 * hc),
        wv.reshape(n, rows, hc),
        wo[None],
        u,
        gg,
        gd,
        qk_gain,
        attn_gain,
        ff_gain,
    )


def adam_kernel(
    sum_ref, gp_ref, gm_ref, gv_ref, p_ref, m_ref, v_ref, ga_ref, go_ref, gg_ref, gu_ref, gd_ref,
    norm_ref, gp_out, gm_out, gv_out, po_ref, mo_ref, vo_ref, g_ref, factor_ref,
):
    part = pl.program_id(0)

    @pl.when((part == 0) & (pl.program_id(1) == 0))
    def _():
        gain = sum_ref[0:4, :]
        squares = jnp.sum(jnp.sum(gain * gain, axis=0, keepdims=True), axis=1, keepdims=True)
        norm = jnp.sqrt(sum_ref[4:5, 0:1] + squares)
        norm_ref[...] = norm
        factor = CLIP / (norm + 1e-06)
        factor_ref[...] = jnp.broadcast_to(factor, factor_ref.shape)
        new = adam_update(gp_ref[...], gm_ref[...], gv_ref[...], gain * factor, GAIN_RATE, 0.0)
        gp_out[...], gm_out[...], gv_out[...] = new

    n, _, three = ga_ref.shape
    hc = three // 3
    fs = gd_ref.shape[2]

    @pl.when(part == 0)
    def _():
        g_ref[:, 3 * n * hc :] = go_ref[...].astype(F32)
        for matrix in range(3):
            for c in range(n):
                start = (matrix * n + c) * hc
                g_ref[:, start : start + hc] = ga_ref[c, :, matrix * hc : (matrix + 1) * hc].astype(F32)

    for index, ref in ((1, gg_ref), (2, gu_ref), (3, gd_ref)):

        @pl.when(part == index)
        def _():
            for d in range(ref.shape[0]):
                g_ref[:, d * fs : (d + 1) * fs] = ref[d].astype(F32)

    clipped = g_ref[...] * factor_ref[0:1, 0:1]
    new_m = BETA1 * m_ref[...] + (1.0 - BETA1) * clipped
    new_v = BETA2 * v_ref[...] + (1.0 - BETA2) * (clipped * clipped)
    root = jnp.sqrt(new_v * (1.0 / (1.0 - BETA2**STEP))) + ADAM_EPS
    po_ref[...] = p_ref[...] * (1.0 - RATE * DECAY) - (new_m * (RATE / (1.0 - BETA1**STEP))) / root
    mo_ref[...] = new_m
    vo_ref[...] = new_v


def adam(sums, gains, gains_first, gains_second, params, first, second, ga, go, gg, gu, gd):
    rows, columns = params.shape
    n, n_dp, fs = ga.shape[0], gd.shape[0], gd.shape[2]
    block = min(rows, 16)
    steps = rows // block
    wide = pl.BlockSpec((block, columns // 4), lambda i, r: (r, i))
    small = pl.BlockSpec(gains.shape, lambda i, r: (0, 0))
    return pl.pallas_call(
        adam_kernel,
        grid=(4, steps),
        out_shape=(jax.ShapeDtypeStruct((1, 1), F32),)
        + (jax.ShapeDtypeStruct(gains.shape, F32),) * 3
        + (jax.ShapeDtypeStruct(params.shape, F32),) * 3,
        in_specs=[
            pl.BlockSpec(sums.shape, lambda i, r: (0, 0)),
            small,
            small,
            small,
            wide,
            wide,
            wide,
            pl.BlockSpec((n, block, ga.shape[2]), lambda i, r: (0, jnp.where(i == 0, r, steps - 1), 0)),
            pl.BlockSpec((block, go.shape[1]), lambda i, r: (jnp.where(i == 0, r, steps - 1), 0)),
            *[
                pl.BlockSpec(
                    (n_dp, block, fs),
                    lambda i, r, part=part: (
                        0,
                        jnp.where(i < part, 0, jnp.where(i == part, r, steps - 1)),
                        0,
                    ),
                )
                for part in (1, 2, 3)
            ],
        ],
        out_specs=(pl.BlockSpec((1, 1), lambda i, r: (0, 0)),) + (small,) * 3 + (wide,) * 3,
        scratch_shapes=[pltpu.VMEM((block, columns // 4), F32), pltpu.VMEM((8, 128), F32)],
        compiler_params=pltpu.CompilerParams(vmem_limit_bytes=48 * 1024 * 1024),
        name="adam",
    )(sums, gains, gains_first, gains_second, params, first, second, ga, go, gg, gu, gd)


def row_sums(value, row):
    pick = lax.broadcasted_iota(jnp.int32, (8, value.shape[1]), 0) == row
    return lax.dot_general(
        pick.astype(F32),
        value,
        (((1,), (1,)), ((), ())),
        preferred_element_type=F32,
        precision=lax.Precision.HIGHEST,
    )


def exchange(n, dp, me, buf, ss, rs):
    copies = []
    for k in range(1, n):
        copy = remote(buf.at[me], buf.at[me], ss.at[k - 1], rs.at[k - 1], (dp, (me + k) % n))
        copy.start()
        copies.append(copy)
    for k in range(1, n):
        source = (me + n - k) % n
        remote(buf.at[me], buf.at[source], ss.at[k - 1], rs.at[k - 1], (dp, source)).wait_recv()
    total = buf[0]
    for j in range(1, n):
        total = total + buf[j]
    for copy in copies:
        copy.wait_send()
    return total


def turn(value, cos, sine):
    return value * cos + pltpu.roll(value, HD // 2, 1) * sine


def mask_of(rows, info_col, info_row):
    pos_i, doc_i = info_col[rows, 0:1], info_col[rows, 1:2]
    return (info_row[1:2, :] == doc_i) & (info_row[0:1, :] <= pos_i)


def attend_kernel(
    n_dp, n, x_ref, w_ref, wo_ref, d_ref, t_ref, norm_ref, gain_ref, cos_ref, sin_ref, col_ref, row_ref,
    y_ref, h_ref, q_ref, k_ref, v_ref, o_ref, pre_ref, scale_ref, lse_ref, wo_all, d_out,
    buf, pa, qa, pb, qb, ss, rs, s1, r1, s2, r2, sw, rw, sd, rd, local,
):
    dp, me = lax.axis_index("dp"), lax.axis_index("ctx")
    seq, width = x_ref.shape
    hc = o_ref.shape[1]
    block = min(seq, 256)
    count, mine, place = group_of(n_dp, n, dp, me)
    greet_all(n_dp, n, dp, me)
    piece = wo_ref.shape[0]

    def part_of(d):
        return wo_all.at[pl.ds(pl.multiple_of(d * piece, piece), piece), :]

    owns = [
        pltpu.make_async_copy(wo_ref, part_of(dp), local.at[0]),
        pltpu.make_async_copy(d_ref.at[mine], d_out.at[mine], local.at[1]),
    ]
    behind_wo = [
        remote(wo_ref, part_of(dp), sw.at[k - 1], rw.at[k - 1], (across(dp, k, n_dp)[0], me))
        for k in range(1, n_dp)
    ]
    for copy in behind_wo + owns:
        copy.start()
    behind_d, receives = swap(d_ref, d_out, sd, rd, count, mine, place)

    @pl.loop(0, seq // block)
    def _(i):
        rows = pl.ds(pl.multiple_of(i * block, block), block)
        value = dot(x_ref[rows, :], w_ref[...])
        pre_ref[rows, :] = value[:, : 2 * hc]
        v_ref[rows, :] = value[:, 2 * hc :].astype(BF)
        squares = value[:, : 2 * hc] * value[:, : 2 * hc]
        buf[me, :, rows] = row_sums(squares[:, :hc], 0) + row_sums(squares[:, hc:], 1)

    scale_ref[...] = jnp.transpose(lax.rsqrt(exchange(n, dp, me, buf, ss, rs) / width + EPS))

    @pl.loop(0, seq // block)
    def _(i):
        rows = pl.ds(pl.multiple_of(i * block, block), block)
        cos, sine = cos_ref[rows, :], sin_ref[rows, :]
        for which, ref, factor in ((0, q_ref, HD ** (-0.5)), (1, k_ref, 1.0)):
            scale = scale_ref[rows, which : which + 1]
            for start in range(0, hc, HD):
                part = slice(start, start + HD)
                value = pre_ref[rows, which * hc + start : which * hc + start + HD] * scale
                ref[rows, part] = (
                    turn(value * gain_ref[which : which + 1, part], cos, sine) * factor
                ).astype(BF)

    def attention(pair, first):
        size = 2 * (seq // n)
        rows = pl.ds(pl.multiple_of(pair * size, size), size)
        visible = mask_of(rows, col_ref, row_ref)
        for head in range(hc // HD):
            part = slice(head * HD, (head + 1) * HD)
            scores = jnp.where(visible, dot_t(q_ref[rows, part], k_ref[:, part]), -jnp.inf)
            top = jnp.max(scores, axis=1, keepdims=True)
            weights = jnp.exp(scores - top)
            total = jnp.sum(weights, axis=1, keepdims=True)
            o_ref[rows, part] = (dot(weights.astype(BF), v_ref[:, part]) / total).astype(BF)
            lse_ref[rows, head : head + 1] = top + jnp.log(total)
        if first:
            owns[0].wait()
            for k in range(1, n_dp):
                _, source = across(dp, k, n_dp)
                remote(wo_ref, part_of(source), sw.at[k - 1], rw.at[k - 1], (source, me)).wait_recv()

    cols = slice(0, hc)
    sums = reduce_ctx(
        n, dp, me, o_ref, wo_all, cols, y_ref, pa, qa, pb, qb, s1, r1, s2, r2, before=attention
    )

    def finish(rows):
        branch = y_ref[rows, :]
        h_ref[rows, :] = t_ref[rows, :].astype(F32) + branch * rms_scale(branch) * norm_ref[...]

    tiles(y_ref.shape[0], 16, finish)
    for copy in receives:
        copy.wait_recv()
    for copy in sums + behind_wo + behind_d:
        copy.wait_send()
    owns[1].wait()


def attend(x_all, w, wo, d, tokens, norm, gain, cos, sine, info_col, info_row, number):
    n_dp, n = lax.axis_size("dp"), lax.axis_size("ctx")
    seq, width = x_all.shape
    half, length, hc = n // 2, seq // n, w.shape[1] // 3
    dma = pltpu.SemaphoreType.DMA
    low = jax.ShapeDtypeStruct((seq, hc), BF)
    return pl.pallas_call(
        functools.partial(attend_kernel, n_dp, n),
        out_shape=(
            jax.ShapeDtypeStruct((length, width), F32),
            jax.ShapeDtypeStruct((length, width), F32),
            low,
            low,
            low,
            low,
            jax.ShapeDtypeStruct((seq, 2 * hc), F32),
            jax.ShapeDtypeStruct((seq, 8), F32),
            jax.ShapeDtypeStruct((seq, 8), F32),
            jax.ShapeDtypeStruct((width, hc), BF),
            jax.ShapeDtypeStruct(d.shape, BF),
        ),
        in_specs=[VMEM] * 2 + [ANY] * 2 + [VMEM] * 7,
        out_specs=(VMEM,) * 10 + (ANY,),
        scratch_shapes=[
            pltpu.VMEM((n, 8, seq), F32),
            pltpu.VMEM((half, length, width), BF),
            pltpu.VMEM((half, length, width), BF),
            pltpu.VMEM((half - 1, length, width), BF),
            pltpu.VMEM((half - 1, length, width), BF),
            dma((n - 1,)),
            dma((n - 1,)),
            dma((half,)),
            dma((half,)),
            dma((half - 1,)),
            dma((half - 1,)),
            dma((n_dp - 1,)),
            dma((n_dp - 1,)),
            dma((2 * n_dp - 1,)),
            dma((2 * n_dp - 1,)),
            dma((2,)),
        ],
        compiler_params=params_of(number),
        cost_estimate=cost(60),
        name="attend",
    )(x_all, w, wo, d, tokens, norm, gain, cos, sine, info_col, info_row)


def slab_give(n_dp, dp, me, g_ref, co_ref, sw, rw):
    tall = co_ref.shape[1]
    gives = []
    for k in range(1, n_dp):
        to, _ = across(dp, k, n_dp)
        part = pl.ds(pl.multiple_of(to * tall, tall), tall)
        copy = remote(g_ref.at[part, :], co_ref.at[k - 1], sw.at[k - 1], rw.at[k - 1], (to, me))
        copy.start()
        gives.append(copy)
    return gives


def slab_sum(dp, gives, g_ref, co_ref, out_ref):
    tall = co_ref.shape[1]
    total = g_ref[pl.ds(pl.multiple_of(dp * tall, tall), tall), :].astype(F32)
    for k, copy in enumerate(gives):
        copy.wait_recv()
        total = total + co_ref[k].astype(F32)
    out_ref[...] = total.astype(BF)


def greet_wide_group(n_dp, dp, me):
    partner = me + 1 - 2 * (me % 2)
    others = [(dp + k) % n_dp for k in range(1, n_dp)]
    greet([(dp, partner)] + [(d, c) for d in others for c in (me, partner)])


def attend_back_kernel(
    n_dp, n, e_ref, do_ref, h_ref, o_hbm, col_ref, row_ref, q_ref, k_ref, v_ref, lse_ref,
    x_ref, gain_ref, cos_ref, sin_ref, pre_ref, scale_ref,
    d_ref, gain_out, g_ref, wv_ref, wo_ref, h_out,
    o_ref, dq_ref, dk_ref, dv_ref, mean_ref, buf, go_ref, co_ref, gv_ref, cv_ref,
    sh, rh, local, sw, rw, sv, rv, ss, rs,
):
    dp, me = lax.axis_index("dp"), lax.axis_index("ctx")
    seq, hc = q_ref.shape
    load = pltpu.make_async_copy(o_hbm, o_ref, local.at[1])
    load.start()
    width = x_ref.shape[1]
    block = min(seq, 256)
    count, index, place = group_of(n_dp, n, dp, me)
    greet_all(n_dp, n, dp, me)
    swaps, receives = swap(h_ref, h_out, sh, rh, count, index, place)
    stay = pltpu.make_async_copy(h_ref.at[index], h_out.at[index], local.at[0])
    stay.start()

    load.wait()

    @pl.loop(0, n)
    def _(c):
        go_ref[:, pl.ds(pl.multiple_of(c * hc, hc), hc)] = t_dot(e_ref[...], o_ref[c]).astype(BF)

    gives = slab_give(n_dp, dp, me, go_ref, co_ref, sw, rw)
    dk_ref[...] = jnp.zeros_like(dk_ref)
    dv_ref[...] = jnp.zeros_like(dv_ref)

    def attention(i):
        rows = pl.ds(pl.multiple_of(i * block, block), block)
        visible = mask_of(rows, col_ref, row_ref)
        for head in range(hc // HD):
            part = slice(head * HD, (head + 1) * HD)
            query, key, value, back = q_ref[rows, part], k_ref[:, part], v_ref[:, part], do_ref[rows, part]
            scores = jnp.where(visible, dot_t(query, key), -jnp.inf)
            probs = jnp.exp(scores - lse_ref[rows, head : head + 1])
            d_probs = dot_t(back, value)
            delta = jnp.sum(probs * d_probs, axis=1, keepdims=True)
            d_scores = (probs * (d_probs - delta)).astype(BF)
            dq_ref[rows, part] = dot(d_scores, key)
            dk_ref[:, part] += t_dot(d_scores, query)
            dv_ref[:, part] += t_dot(probs.astype(BF), back)

    pl.loop(0, seq // block)(attention)

    d_ref[:, 2 * hc :] = dv_ref[...].astype(BF)

    def values(part):
        gv_ref[part, :] = t_dot(x_ref[:, part], d_ref[:, 2 * hc :]).astype(BF)

    tiles(width, 256, values)
    gives_v = slab_give(n_dp, dp, me, gv_ref, cv_ref, sv, rv)
    gain_out[...] = jnp.zeros_like(gain_out)

    @pl.loop(0, seq // block)
    def _(i):
        rows = pl.ds(pl.multiple_of(i * block, block), block)
        cos, sine = cos_ref[rows, :], sin_ref[rows, :]
        sums = jnp.zeros((8, block), F32)
        for which, ref, factor in ((0, dq_ref, HD ** (-0.5)), (1, dk_ref, 1.0)):
            scale = scale_ref[rows, which : which + 1]
            for start in range(0, hc, HD):
                part = slice(start, start + HD)
                pre = pre_ref[rows, which * hc + start : which * hc + start + HD]
                value = turn(ref[rows, part] * factor, cos, -sine)
                gain_out[which : which + 1, part] += jnp.sum(value * pre * scale, axis=0, keepdims=True)
                value = value * gain_ref[which : which + 1, part]
                ref[rows, part] = value
                sums += row_sums(value * pre, which)
        buf[me, :, rows] = sums

    mean_ref[...] = jnp.transpose(exchange(n, dp, me, buf, ss, rs) / width)

    @pl.loop(0, seq // block)
    def _(i):
        rows = pl.ds(pl.multiple_of(i * block, block), block)
        for which, ref in ((0, dq_ref), (1, dk_ref)):
            scale = scale_ref[rows, which : which + 1]
            mean = mean_ref[rows, which : which + 1]
            cols = slice(which * hc, (which + 1) * hc)
            value = scale * (ref[rows, :] - pre_ref[rows, cols] * (scale * scale * mean))
            d_ref[rows, cols] = value.astype(BF)

    def product(part):
        g_ref[part, :] = t_dot(x_ref[:, part], d_ref[:, : 2 * hc]).astype(BF)

    tiles(width, 256, product)
    slab_sum(dp, gives, go_ref, co_ref, wo_ref)
    slab_sum(dp, gives_v, gv_ref, cv_ref, wv_ref)
    for copy in receives:
        copy.wait_recv()
    for copy in swaps + gives + gives_v:
        copy.wait_send()
    stay.wait()


def attend_back(e, do, h, o_all, info_col, info_row, q, k, v, lse, x, gain, cos, sine, pre, scale, number):
    n_dp, n = lax.axis_size("dp"), lax.axis_size("ctx")
    (seq, hc), share, width = q.shape, e.shape[1], x.shape[1]
    dma = pltpu.SemaphoreType.DMA
    return pl.pallas_call(
        functools.partial(attend_back_kernel, n_dp, n),
        out_shape=(
            jax.ShapeDtypeStruct((seq, 3 * hc), BF),
            jax.ShapeDtypeStruct((2, hc), F32),
            jax.ShapeDtypeStruct((width, 2 * hc), BF),
            jax.ShapeDtypeStruct((width // n_dp, hc), BF),
            jax.ShapeDtypeStruct((share // n_dp, n * hc), BF),
            jax.ShapeDtypeStruct(h.shape, BF),
        ),
        in_specs=[VMEM, VMEM, ANY, ANY] + [VMEM] * 12,
        out_specs=(VMEM,) * 5 + (ANY,),
        scratch_shapes=[
            pltpu.VMEM(o_all.shape, BF),
            pltpu.VMEM((seq, hc), F32),
            pltpu.VMEM((seq, hc), F32),
            pltpu.VMEM((seq, hc), F32),
            pltpu.VMEM((seq, 8), F32),
            pltpu.VMEM((n, 8, seq), F32),
            pltpu.VMEM((share, n * hc), BF),
            pltpu.VMEM((n_dp - 1, share // n_dp, n * hc), BF),
            pltpu.VMEM((width, hc), BF),
            pltpu.VMEM((n_dp - 1, width // n_dp, hc), BF),
            dma((2 * n_dp - 1,)),
            dma((2 * n_dp - 1,)),
            dma((2,)),
            dma((n_dp - 1,)),
            dma((n_dp - 1,)),
            dma((n_dp - 1,)),
            dma((n_dp - 1,)),
            dma((n - 1,)),
            dma((n - 1,)),
        ],
        compiler_params=params_of(number),
        cost_estimate=cost(75),
        name="attend_back",
    )(e, do, h, o_all, info_col, info_row, q, k, v, lse, x, gain, cos, sine, pre, scale)


def shards(
    inputs,
    cotangent,
    documents,
    block_place,
    params,
    first_moment,
    second_moment,
    gains,
    gains_first,
    gains_second,
):
    tokens = inputs[0]
    upstream = cotangent[0]
    length, width = tokens.shape
    n_ctx = lax.axis_size("ctx")
    n_dp = lax.axis_size("dp")
    me_ctx = lax.axis_index("ctx")
    seq = length * n_ctx
    rows = params.shape[0]
    ff = (params.shape[1] - 4 * width) // 3
    hc = width // n_ctx
    half, group = n_ctx // 2, 2 * n_dp
    fh = ff // group
    parities = [[2 * p + side for p in range(half)] for side in range(2)]

    def gather_pairs(w):
        w = lax.all_gather(
            w.reshape(group * rows, w.shape[2]), "ctx", axis=0, tiled=True, axis_index_groups=parities
        )
        return w.reshape(half, n_dp, 2 * rows, w.shape[1])

    def scatter_pairs(g):
        g = lax.psum_scatter(
            g.reshape(width, g.shape[3]),
            "ctx",
            scatter_dimension=0,
            tiled=True,
            axis_index_groups=parities,
        )
        return g.reshape(group, rows, g.shape[1])

    w_gu, w_qkv, w_o, x_all, w_d = start(params, tokens, 1)
    w_gu = gather_pairs(w_gu)
    w_qkv = gather_dp(w_qkv.reshape(n_ctx * rows, 3 * hc), 2)

    indices = jnp.arange(seq, dtype=jnp.int32)
    owners = indices // length
    placed = jnp.sum(
        jnp.where(
            owners[:, None] == jnp.arange(n_ctx, dtype=jnp.int32)[None, :], block_place[None, :], 0
        ),
        axis=1,
    )
    pos = placed * length + indices % length
    docs = documents[0]
    info_row = jnp.concatenate([pos[None], docs[None], jnp.zeros((6, seq), jnp.int32)])
    info_col = info_row.T
    cos_tab, sine_tab = rope_tables(pos, HD)
    cos_tab = jnp.concatenate([cos_tab, cos_tab], axis=1)
    sine_tab = jnp.concatenate([-sine_tab, sine_tab], axis=1)
    my_gains = lax.dynamic_slice_in_dim(gains[:2], me_ctx * hc, hc, axis=1)
    tables = (my_gains, cos_tab, sine_tab, info_col, info_row)

    branch, hidden1, queries, keys, values, attn_low, qk_pre, scales, lse, w_o, w_d = attend(
        x_all, w_qkv, w_o.reshape(n_ctx * rows, hc), w_d, tokens, gains[2:3], *tables, 3
    )

    result, d_mlp, g_ff_part, h1_all, gate_up, inner, w_d, w_o = ff_forward(
        hidden1, upstream, gains[3:4], w_gu, w_d.reshape(n_dp, 2 * rows, fh), w_o, 4
    )
    attn_low, d_mlp = lax.optimization_barrier((attn_low, d_mlp))
    attn_all = lax.all_gather(attn_low, "ctx", axis=0)
    d_gu, d_grad = ff_back(d_mlp, inner, w_d, gate_up, rows, 5)
    d_grad = scatter_pairs(d_grad)
    d_h1, d_branch, d_attn, g_attn_part, g_grad, u_grad = ff_scatter(
        d_gu, w_gu, h1_all, w_o, upstream, branch, gains[2:3], 6
    )
    g_grad, u_grad = scatter_pairs(g_grad), scatter_pairs(u_grad)

    d_qkv, d_gain, qk_grad, wv_grad, wo_grad, d_grad = attend_back(
        d_branch, d_attn, d_grad, attn_all, info_col, info_row, queries, keys, values, lse,
        x_all, my_gains, cos_tab, sine_tab, qk_pre, scales, 8,
    )
    qk_grad, g_grad, d_x = collect(qk_grad, g_grad, d_qkv, w_qkv, 9)
    d_input = d_h1 + d_x

    attn_grad, u_grad, sums = total_over(
        qk_grad, wv_grad, wo_grad, u_grad, g_grad, d_grad, d_gain, g_attn_part, g_ff_part, 11
    )
    grad_norm, new_gains, new_gains_first, new_gains_second, new_params, new_first, new_second = adam(
        sums, gains, gains_first, gains_second, params, first_moment, second_moment,
        attn_grad, wo_grad, g_grad, u_grad, d_grad,
    )
    return (
        result[None],
        d_input.astype(BF)[None],
        grad_norm.reshape(()),
        new_params,
        new_first,
        new_second,
        new_gains,
        new_gains_first,
        new_gains_second,
    )


def solution(mesh):
    split, whole = P("dp", "ctx", None), P(("dp", "ctx"), None)
    return jax.shard_map(
        shards,
        mesh=mesh,
        in_specs=(split, split, P("dp", None), P(), whole, whole, whole, P(), P(), P()),
        out_specs=(split, split, P(), whole, whole, whole, P(), P(), P()),
        check_vma=False,
    )
```

```python
import functools

import jax
import jax.numpy as jnp
from jax import lax
from jax.experimental import pallas as pl
from jax.experimental.pallas import tpu as pltpu
from jax.sharding import PartitionSpec as P

HD = 128
STEP = 10
EPS = 1e-06
THETA = 500000.0
CLIP = 1.0
BETA1 = 0.9
BETA2 = 0.95
RATE = 0.03
GAIN_RATE = 0.8
DECAY = 0.1
ADAM_EPS = 1e-08
BF = jnp.bfloat16
F32 = jnp.float32
MESH = pl.DeviceIdType.MESH
ANY = pl.BlockSpec(memory_space=pl.ANY)
VMEM = pl.BlockSpec(memory_space=pltpu.VMEM)
HBM = pl.BlockSpec(memory_space=pltpu.HBM)


def rms_scale(values):
    return lax.rsqrt(jnp.mean(values * values, axis=-1, keepdims=True) + EPS)


def norm_back(upstream, source, scale):
    return scale * (
        upstream - source * scale * scale * jnp.mean(upstream * source, axis=-1, keepdims=True)
    )


def rope_tables(positions, head_size):
    half_size = head_size // 2
    freqs = THETA ** (-jnp.arange(half_size, dtype=jnp.float32) * 2.0 / head_size)
    angles = positions.astype(jnp.float32)[:, None] * freqs[None, :]
    return (jnp.cos(angles), jnp.sin(angles))


def adam_update(weight, first_in, second_in, clipped, rate, decay):
    new_first = BETA1 * first_in + (1.0 - BETA1) * clipped
    new_second = BETA2 * second_in + (1.0 - BETA2) * clipped * clipped
    first_hat = new_first / (1.0 - BETA1**STEP)
    second_hat = new_second / (1.0 - BETA2**STEP)
    new_weight = weight - rate * (first_hat / (jnp.sqrt(second_hat) + ADAM_EPS) + decay * weight)
    return (new_weight, new_first, new_second)


def dot(a, b):
    return jnp.dot(a, b, preferred_element_type=F32)


def dot_t(a, b):
    return lax.dot_general(a, b, (((1,), (1,)), ((), ())), preferred_element_type=F32)


def t_dot(a, b):
    return lax.dot_general(a, b, (((0,), (0,)), ((), ())), preferred_element_type=F32)


def greet(peers):
    barrier = pltpu.get_barrier_semaphore()
    for peer in peers:
        pl.semaphore_signal(barrier, inc=1, device_id=peer, device_id_type=MESH)
    pl.semaphore_wait(barrier, len(peers))


def remote(src, dst, send, recv, peer):
    return pltpu.make_async_remote_copy(
        src_ref=src, dst_ref=dst, send_sem=send, recv_sem=recv, device_id=peer, device_id_type=MESH
    )


def cost(us):
    return pl.CostEstimate(flops=0, bytes_accessed=us * 3_600_000, transcendentals=0)


def params_of(number, vmem=48):
    return pltpu.CompilerParams(
        collective_id=number, has_side_effects=True, vmem_limit_bytes=vmem * 1024 * 1024
    )


def line_steps(n, me, make_right, make_left):
    for s in range(n - 1):

        @pl.when((me < n - 1) & (me >= s))
        def _():
            make_right(s).start()

        @pl.when((me > 0) & (me + s < n))
        def _():
            make_left(s).start()

        @pl.when(me - 1 - s >= 0)
        def _():
            make_right(s, me - 1 - s).wait_recv()

        @pl.when(me + 1 + s < n)
        def _():
            make_left(s, me + 1 + s).wait_recv()

    for s in range(n - 1):

        @pl.when((me < n - 1) & (me >= s))
        def _():
            make_right(s).wait_send()

        @pl.when((me > 0) & (me + s < n))
        def _():
            make_left(s).wait_send()


def pairs_of(n, me):
    half = n // 2
    parity, pair = me % 2, me // 2
    partner = me + 1 - 2 * parity
    ahead = [2 * ((pair + k) % half) + parity for k in range(1, half)]
    behind = [2 * ((pair + half - k) % half) + parity for k in range(1, half)]
    return half, parity, pair, partner, ahead, behind


def gather_dp_kernel(n, x_ref, o_ref, local, sr, rr, sl, rl):
    me, ctx = lax.axis_index("dp"), lax.axis_index("ctx")

    def here(d):
        return (d, ctx)

    greet([here((me + 1) % n), here((me + n - 1) % n)])
    own = pltpu.make_async_copy(x_ref, o_ref.at[me], local)
    own.start()

    def right(s, block=None):
        b = me - s if block is None else block
        return remote(x_ref if s == 0 else o_ref.at[b], o_ref.at[b], sr.at[s], rr.at[s], here(me + 1))

    def left(s, block=None):
        b = me + s if block is None else block
        return remote(x_ref if s == 0 else o_ref.at[b], o_ref.at[b], sl.at[s], rl.at[s], here(me - 1))

    line_steps(n, me, right, left)
    own.wait()


def gather_dp(x, number):
    n = lax.axis_size("dp")
    out = pl.pallas_call(
        functools.partial(gather_dp_kernel, n),
        out_shape=jax.ShapeDtypeStruct((n,) + x.shape, x.dtype),
        in_specs=[ANY],
        out_specs=ANY,
        scratch_shapes=[pltpu.SemaphoreType.DMA] + [pltpu.SemaphoreType.DMA((n - 1,))] * 4,
        compiler_params=params_of(number),
        cost_estimate=cost(60),
        name="gather_dp",
    )(x)
    return out.reshape((n * x.shape[0],) + x.shape[1:])


def group_of(n_dp, n, dp, me):
    pair, parity = me // 2, me % 2
    return 2 * n_dp, 2 * dp + parity, lambda j: (j // 2, 2 * pair + j % 2)


def greet_all(n_dp, n, dp, me):
    partner = me + 1 - 2 * (me % 2)
    others = [(dp + k) % n_dp for k in range(1, n_dp)]
    greet([(dp, (me + k) % n) for k in range(1, n)] + [(d, c) for d in others for c in (me, partner)])


def across(mine, k, count):
    if count & (count - 1):
        return (mine + k) % count, (mine + count - k) % count
    bit, other = 1, mine
    while bit < count:
        if k & bit:
            other = other + bit - 2 * bit * ((other // bit) % 2)
        bit *= 2
    return other, other


def swap(src, dst, send, recv, count, mine, place):
    sends, receives = [], []
    for k in range(1, count):
        to, source = across(mine, k, count)
        sends.append(remote(src.at[to], dst.at[mine], send.at[k - 1], recv.at[k - 1], place(to)))
        receives.append(
            remote(src.at[mine], dst.at[source], send.at[k - 1], recv.at[k - 1], place(source))
        )
    for copy in sends:
        copy.start()
    return sends, receives


def tiles(total, tile, body):
    tile = min(total, tile)

    @pl.loop(0, total // tile)
    def _(j):
        body(pl.ds(pl.multiple_of(j * tile, tile), tile))


def reduce_ctx(n, dp, me, a_ref, w_ref, cols, o_ref, sa, ra, sb, rb, s1, r1, s2, r2, before=None):
    half, parity, pair, partner, ahead, behind = pairs_of(n, me)
    length, width = o_ref.shape

    def rows(block):
        return pl.ds(pl.multiple_of(block * length, length), length)

    first, second = [], []
    for k in range(half):
        target = (pair + k + 1) % half
        if before is not None:
            before(target, k == 0)

        def give(part):
            value = dot_t(a_ref[rows(2 * target + 1 - parity), :], w_ref[part, cols])
            sa[k, :, part] = value.astype(BF)

        tiles(width, 512, give)
        copy = remote(sa.at[k], ra.at[k], s1.at[k], r1.at[k], (dp, partner))
        copy.start()
        first.append(copy)
        copy.wait_recv()

        def keep(part):
            value = dot_t(a_ref[rows(2 * target + parity), :], w_ref[part, cols])
            value = value + ra[k, :, part].astype(F32)
            if k < half - 1:
                sb[k, :, part] = value.astype(BF)
            else:
                o_ref[:, part] = value

        tiles(width, 512, keep)
        if k < half - 1:
            copy = remote(sb.at[k], rb.at[k], s2.at[k], r2.at[k], (dp, 2 * target + parity))
            copy.start()
            second.append(copy)
    for k in range(half - 1):
        second[k].wait_recv()
        o_ref[...] += rb[k].astype(F32)
    return first + second


def load_rows(hbm, vmem, sems):
    half, n_dp, rows, _ = hbm.shape
    copies = []
    for d in range(n_dp):
        for p in range(half):
            part = pl.ds((d * half + p) * rows, rows)
            copies.append(pltpu.make_async_copy(hbm.at[p, d], vmem.at[part, :], sems.at[d * half + p]))
    for copy in copies:
        copy.start()
    return copies


def gather_group(n, dp, me, all_ref, length, sr, rr, sl, rl, sf, rf, process):
    parity = me % 2
    partner = me + 1 - 2 * parity

    def block(b, side):
        start = (2 * b + side) * length
        return all_ref.at[pl.ds(pl.multiple_of(start, length), length), :]

    def right(s, b):
        return remote(block(b, parity), block(b, parity), sr.at[s], rr.at[s], (dp + 1, me))

    def left(s, b):
        return remote(block(b, parity), block(b, parity), sl.at[s], rl.at[s], (dp - 1, me))

    def aside(b):
        return remote(block(b, parity), block(b, parity), sf.at[b], rf.at[b], (dp, partner))

    def from_aside(b):
        return remote(block(b, 1 - parity), block(b, 1 - parity), sf.at[b], rf.at[b], (dp, partner))

    for s in range(n):
        if s == 0:
            aside(dp).start()
        else:

            @pl.when(dp >= s)
            def _():
                right(s - 1, dp - s).wait_recv()

            @pl.when(dp + s < n)
            def _():
                left(s - 1, dp + s).wait_recv()

        @pl.when((dp < n - 1) & (dp >= s))
        def _():
            right(s, dp - s).start()

        @pl.when((dp > 0) & (dp + s < n))
        def _():
            left(s, dp + s).start()

        if s == 0:
            from_aside(dp).wait_recv()
            process(dp, True)
        else:

            @pl.when(dp >= s)
            def _():
                aside(dp - s).start()

            @pl.when(dp + s < n)
            def _():
                aside(dp + s).start()

            below = jnp.where(dp >= s, 1, 0)
            above = jnp.where(dp + s < n, 1, 0)

            @pl.loop(0, below + above)
            def _(j):
                b = jnp.where(j < below, dp - s, dp + s)
                from_aside(b).wait_recv()
                process(b, False)

    for s in range(n):

        @pl.when((dp < n - 1) & (dp >= s))
        def _():
            right(s, dp - s).wait_send()

        @pl.when((dp > 0) & (dp + s < n))
        def _():
            left(s, dp + s).wait_send()

        aside(s).wait_send()


def gather_sems(n_dp):
    return [pltpu.SemaphoreType.DMA((n_dp,))] * 6


def line_sum(n, dp, me, make, val, o_ref, buf, send, recv, sync, between=None):
    def move(way, d):
        to = jnp.where(way == 1, dp + 1, dp - 1)
        return remote(buf.at[way, d], buf.at[way, d], send.at[way, d], recv.at[way, d], (to, me))

    def steps(body):
        for j in range(1, n):

            @pl.loop(0, 2)
            def _(phase):
                way = jnp.where(2 * dp < n, 1 - phase, phase)
                d = jnp.where(way == 1, n - j, j - 1)
                first = jnp.where(way == 1, 0, n - 1)
                ahead = jnp.where(way == 1, d - dp, dp - d)

                @pl.when(ahead > 0)
                def _():
                    body(way, d, dp == first)

    def begin(way, d, starts):
        make(d, val.at[d])

        @pl.when(starts)
        def _():
            def put(part):
                buf[way, d, part, :] = val[d, part, :].astype(BF)

            tiles(val.shape[1], 32, put)
            move(way, d).start()

    def follow(way, d, starts):
        @pl.when(jnp.logical_not(starts))
        def _():
            move(way, d).wait_recv()

            def add(part):
                buf[way, d, part, :] = (val[d, part, :] + buf[way, d, part, :].astype(F32)).astype(BF)

            tiles(val.shape[1], 32, add)
            move(way, d).start()

    steps(begin)
    make(dp, o_ref)
    steps(follow)
    if between is not None:
        between()
    for way, first in ((1, 0), (0, n - 1)):

        @pl.when(dp != first)
        def _():
            move(way, dp).wait_recv()

            def add(part):
                o_ref[part, :] += buf[way, dp, part, :].astype(F32)

            tiles(val.shape[1], 32, add)

    sync()
    steps(lambda way, d, starts: move(way, d).wait_send())


def line_scratch(n_dp, length, width):
    return [
        pltpu.VMEM((n_dp, length, width), F32),
        pltpu.VMEM((2, n_dp, length, width), BF),
        pltpu.SemaphoreType.DMA((2, n_dp)),
        pltpu.SemaphoreType.DMA((2, n_dp)),
    ]


def part_of_pair(dp, me, a_ref, w_ref, length, sa, ra, s1, r1):
    parity = me % 2
    partner = me + 1 - 2 * parity

    def make(d, out):
        def rows(side):
            return pl.ds(pl.multiple_of((2 * d + side) * length, length), length)

        def give(part):
            sa[d, :, part] = dot_t(a_ref[rows(1 - parity), :], w_ref[part, :]).astype(BF)

        tiles(out.shape[1], 512, give)
        copy = remote(sa.at[d], ra.at[d], s1.at[d], r1.at[d], (dp, partner))
        copy.start()

        def keep(part):
            out[:, part] = dot_t(a_ref[rows(parity), :], w_ref[part, :])

        tiles(out.shape[1], 512, keep)
        copy.wait_recv()

        def add(part):
            out[part, :] += ra[d, part, :].astype(F32)

        tiles(length, 32, add)

    def done(n):
        for d in range(n):
            remote(sa.at[d], ra.at[d], s1.at[d], r1.at[d], (dp, partner)).wait_send()

    return make, done


def pair_scratch(n_dp, length, width):
    return [pltpu.VMEM((n_dp, length, width), BF)] * 2 + [pltpu.SemaphoreType.DMA((n_dp,))] * 2


def greet_group(n_dp, dp, me):
    partner = me + 1 - 2 * (me % 2)
    greet([(dp, partner)] + [((dp + k) % n_dp, me) for k in range(1, n_dp)])


def ff_forward_kernel(
    n_dp, n, h_ref, up_ref, gain_ref, gu_hbm, d_hbm, wo_hbm,
    res_ref, dm_ref, gp_ref, all_out, pre_out, hid_out, d_out, wo_out,
    all_ref, pre_ref, hid_ref, d_ref, gu_ref, acc, sem_gu, sem_d, sem_out, sd, rd, so, ro, fo, go, *rest,
):
    gather, pair_refs, line_refs = rest[:6], rest[6:10], rest[10:]
    dp, me = lax.axis_index("dp"), lax.axis_index("ctx")
    length, width = h_ref.shape
    fh = hid_ref.shape[1]
    half, parity, pair, partner, ahead, behind = pairs_of(n, me)
    loads_gu = load_rows(gu_hbm, gu_ref, sem_gu)
    mine = pl.ds(pl.multiple_of((2 * dp + me % 2) * length, length), length)
    all_ref[mine, :] = h_ref[...].astype(BF)
    greet(
        [(dp, partner)]
        + [((dp + k) % n_dp, me) for k in range(1, n_dp)]
        + [(dp, a) for a in ahead]
    )
    tall = d_hbm.shape[1]

    def down(d, p):
        return d_ref.at[pl.ds(pl.multiple_of((d * half + p) * tall, tall), tall), :]

    loads_d = [pltpu.make_async_copy(d_hbm.at[d], down(d, pair), sem_d.at[d]) for d in range(n_dp)]
    spreads = [
        remote(d_hbm.at[d], down(d, pair), sd.at[k, d], rd.at[k, d], (dp, a))
        for k, a in enumerate(ahead)
        for d in range(n_dp)
    ]
    for copy in spreads + loads_d:
        copy.start()

    def process(b, own):
        rows = pl.ds(pl.multiple_of(2 * b * length, 2 * length), 2 * length)
        if own:
            for copy in loads_gu:
                copy.wait()

        def hidden(part):
            second = pl.ds(pl.multiple_of(fh + part.start, part.size), part.size)
            gate = dot(all_ref[rows, :], gu_ref[:, part])
            upper = dot(all_ref[rows, :], gu_ref[:, second])
            pre_ref[rows, part] = gate
            pre_ref[rows, second] = upper
            hid_ref[rows, part] = (gate * jax.nn.sigmoid(gate) * upper).astype(BF)

        tiles(fh, 256, hidden)

    gather_group(n_dp, dp, me, all_ref, length, *gather, process)
    for copy in loads_d:
        copy.wait()
    for k, b in enumerate(behind):
        for d in range(n_dp):
            remote(d_hbm.at[d], down(d, b // 2), sd.at[k, d], rd.at[k, d], (dp, b)).wait_recv()

    outs = [
        pltpu.make_async_copy(ref, out, sem_out.at[i])
        for i, (ref, out) in enumerate(
            ((all_ref, all_out), (pre_ref, pre_out), (hid_ref, hid_out), (d_ref, d_out))
        )
    ]
    outs.append(pltpu.make_async_copy(wo_hbm, wo_out.at[me], sem_out.at[4]))
    spreads_wo = [
        remote(wo_hbm, wo_out.at[me], so.at[k], ro.at[k], (dp, a)) for k, a in enumerate(ahead + [partner])
    ]
    for copy in outs + spreads_wo:
        copy.start()
    make, done = part_of_pair(dp, me, hid_ref, d_ref, length, *pair_refs)

    gp_ref[...] = jnp.zeros_like(gp_ref)

    def finish(rows):
        out, up, gain = acc[rows, :], up_ref[rows, :].astype(F32), gain_ref[...]
        scale = rms_scale(out)
        res_ref[rows, :] = (h_ref[rows, :] + out * scale * gain).astype(BF)
        gp_ref[...] += jnp.sum(up * out * scale, axis=0, keepdims=True)
        dm_ref[rows, :] = norm_back(up * gain, out, scale).astype(BF)

    forwards = []

    def last():
        for k, b in enumerate(behind):
            remote(wo_hbm, wo_out.at[b], so.at[k], ro.at[k], (dp, b)).wait_recv()
            forward = remote(wo_out.at[b], wo_out.at[b], fo.at[k], go.at[k], (dp, partner))
            forward.start()
            forwards.append(forward)
        tiles(length, 16, finish)

    line_sum(n_dp, dp, me, make, line_refs[0], acc, *line_refs[1:], last)
    done(n_dp)
    spreads_wo[-1].wait_recv()
    for copy in forwards:
        copy.wait_recv()
    for copy in spreads + spreads_wo + forwards:
        copy.wait_send()
    for copy in outs:
        copy.wait()


def ff_forward(h1, up, gain, w_gu, w_d, w_o, number):
    n_dp, n = lax.axis_size("dp"), lax.axis_size("ctx")
    (length, width), fh = h1.shape, w_d.shape[2]
    tokens = 2 * n_dp * length
    half = n // 2
    low = jax.ShapeDtypeStruct((length, width), BF)
    return pl.pallas_call(
        functools.partial(ff_forward_kernel, n_dp, n),
        out_shape=(
            low,
            low,
            jax.ShapeDtypeStruct((1, width), F32),
            jax.ShapeDtypeStruct((tokens, width), BF),
            jax.ShapeDtypeStruct((tokens, 2 * fh), F32),
            jax.ShapeDtypeStruct((tokens, fh), BF),
            jax.ShapeDtypeStruct((width, fh), BF),
            jax.ShapeDtypeStruct((n,) + w_o.shape, BF),
        ),
        in_specs=[VMEM] * 3 + [ANY] * 3,
        out_specs=(VMEM,) * 3 + (ANY,) * 5,
        scratch_shapes=[
            pltpu.VMEM((tokens, width), BF),
            pltpu.VMEM((tokens, 2 * fh), F32),
            pltpu.VMEM((tokens, fh), BF),
            pltpu.VMEM((width, fh), BF),
            pltpu.VMEM((width, 2 * fh), BF),
            pltpu.VMEM((length, width), F32),
            pltpu.SemaphoreType.DMA((half * n_dp,)),
            pltpu.SemaphoreType.DMA((n_dp,)),
            pltpu.SemaphoreType.DMA((5,)),
            pltpu.SemaphoreType.DMA((half - 1, n_dp)),
            pltpu.SemaphoreType.DMA((half - 1, n_dp)),
            pltpu.SemaphoreType.DMA((half,)),
            pltpu.SemaphoreType.DMA((half,)),
            pltpu.SemaphoreType.DMA((half - 1,)),
            pltpu.SemaphoreType.DMA((half - 1,)),
        ]
        + gather_sems(n_dp)
        + pair_scratch(n_dp, length, width)
        + line_scratch(n_dp, length, width),
        compiler_params=params_of(number, 58),
        cost_estimate=cost(90),
        name="ff_forward",
    )(h1, up, gain, w_gu, w_d, w_o)


def store_rows(n_dp, value_of, out):
    half, _, rows, _ = out.shape

    @pl.loop(0, n_dp * half)
    def _(r):
        out[r % half, r // half] = value_of(pl.ds(pl.multiple_of(r * rows, rows), rows)).astype(BF)


def ff_back_kernel(
    n_dp, dm_ref, hid_ref, d_hbm, pre_hbm, dgu_ref, gd_ref,
    all_ref, d_ref, pre_ref, acc, sem_d, sem_p, *gather,
):
    dp, me = lax.axis_index("dp"), lax.axis_index("ctx")
    length, width = dm_ref.shape
    fh = d_ref.shape[1]
    load = pltpu.make_async_copy(d_hbm, d_ref, sem_d)
    load.start()

    def rows_of(b):
        return pl.ds(pl.multiple_of(2 * b * length, 2 * length), 2 * length)

    def load_pre(b):
        return pltpu.make_async_copy(pre_hbm.at[rows_of(b), :], pre_ref.at[rows_of(b), :], sem_p.at[b])

    for k in range(n_dp):
        load_pre((dp + k) % n_dp).start()
    mine = pl.ds(pl.multiple_of((2 * dp + me % 2) * length, length), length)
    all_ref[mine, :] = dm_ref[...]
    greet_group(n_dp, dp, me)

    def process(b, own):
        rows = rows_of(b)
        if own:
            load.wait()
        load_pre(b).wait()

        def hidden(part):
            second = pl.ds(pl.multiple_of(fh + part.start, part.size), part.size)
            back = dot(all_ref[rows, :], d_ref[:, part])
            gate, upper = pre_ref[rows, part], pre_ref[rows, second]
            sig = jax.nn.sigmoid(gate)
            dgu_ref[rows, part] = (back * upper * sig * (1.0 + gate * (1.0 - sig))).astype(BF)
            dgu_ref[rows, second] = (back * gate * sig).astype(BF)

        tiles(fh, 256, hidden)

        def product(part):
            value = t_dot(all_ref[rows, part], hid_ref[rows, :])
            acc[part, :] = value if own else acc[part, :] + value

        tiles(width, 256, product)

    gather_group(n_dp, dp, me, all_ref, length, *gather, process)
    store_rows(n_dp, lambda part: acc[part, :], gd_ref)


def ff_back(dm, hid, w_d, pre, rows, number):
    n_dp, half = lax.axis_size("dp"), lax.axis_size("ctx") // 2
    (length, width), fh = dm.shape, w_d.shape[1]
    tokens = 2 * n_dp * length
    return pl.pallas_call(
        functools.partial(ff_back_kernel, n_dp),
        out_shape=(
            jax.ShapeDtypeStruct((tokens, 2 * fh), BF),
            jax.ShapeDtypeStruct((half, n_dp, 2 * rows, fh), BF),
        ),
        in_specs=[VMEM, VMEM, ANY, ANY],
        out_specs=(VMEM,) * 2,
        scratch_shapes=[
            pltpu.VMEM((tokens, width), BF),
            pltpu.VMEM((width, fh), BF),
            pltpu.VMEM((tokens, 2 * fh), F32),
            pltpu.VMEM((width, fh), F32),
            pltpu.SemaphoreType.DMA,
            pltpu.SemaphoreType.DMA((n_dp,)),
        ]
        + gather_sems(n_dp),
        compiler_params=params_of(number, 58),
        cost_estimate=cost(45),
        name="ff_back",
    )(dm, hid, w_d, pre)


def ff_scatter_kernel(
    n_dp, n, dgu_ref, gu_hbm, all_hbm, dh_ref, gg_out, gv_out,
    gg_ref, gv_ref, gu_ref, all_ref, acc, sem_gu, sem_all, sem_out, *rest,
):
    dp, me = lax.axis_index("dp"), lax.axis_index("ctx")
    length, width = dh_ref.shape
    pair_refs, line_refs = rest[:4], rest[4:]
    half, parity, pair, partner, ahead, behind = pairs_of(n, me)
    _, _, rows, fh = gg_ref.shape
    loads = load_rows(gu_hbm, gu_ref, sem_gu)
    load = pltpu.make_async_copy(all_hbm, all_ref, sem_all)
    load.start()
    greet_group(n_dp, dp, me)
    for copy in loads:
        copy.wait()

    make, done = part_of_pair(dp, me, dgu_ref, gu_ref, length, *pair_refs)
    load.wait()
    tall = acc.shape[0]

    def grads():
        @pl.loop(0, width // tall)
        def _(j):
            acc[...] = t_dot(all_ref[:, pl.ds(pl.multiple_of(j * tall, tall), tall)], dgu_ref[...])
            for s in range(tall // rows):
                r = j * (tall // rows) + s
                part = slice(s * rows, (s + 1) * rows)
                gg_ref[r % half, r // half] = acc[part, :fh].astype(BF)
                gv_ref[r % half, r // half] = acc[part, fh:].astype(BF)

    val, *line = line_refs
    line_sum(n_dp, dp, me, make, val, dh_ref, *line, lambda: None, grads)
    done(n_dp)
    outs = [
        pltpu.make_async_copy(ref, out, sem_out.at[i])
        for i, (ref, out) in enumerate(((gg_ref, gg_out), (gv_ref, gv_out)))
    ]
    for copy in outs:
        copy.start()
    for copy in outs:
        copy.wait()


def ff_scatter(dgu, w_gu, h1_all, length, number):
    n_dp, n = lax.axis_size("dp"), lax.axis_size("ctx")
    width = h1_all.shape[1]
    grad = jax.ShapeDtypeStruct(w_gu.shape[:3] + (w_gu.shape[3] // 2,), BF)
    return pl.pallas_call(
        functools.partial(ff_scatter_kernel, n_dp, n),
        out_shape=(
            jax.ShapeDtypeStruct((length, width), F32),
            grad,
            grad,
        ),
        in_specs=[VMEM, ANY, ANY],
        out_specs=(VMEM,) + (ANY,) * 2,
        scratch_shapes=[
            pltpu.VMEM(grad.shape, BF),
            pltpu.VMEM(grad.shape, BF),
            pltpu.VMEM((width, w_gu.shape[3]), BF),
            pltpu.VMEM(h1_all.shape, BF),
            pltpu.VMEM((256, w_gu.shape[3]), F32),
            pltpu.SemaphoreType.DMA((w_gu.shape[0] * n_dp,)),
            pltpu.SemaphoreType.DMA,
            pltpu.SemaphoreType.DMA((2,)),
        ]
        + pair_scratch(n_dp, length, width)
        + line_scratch(n_dp, length, width),
        compiler_params=params_of(number, 60),
        cost_estimate=cost(50),
        name="ff_scatter",
    )(dgu, w_gu, h1_all)


def start_kernel(
    n_dp, n, p_hbm, x_ref, h_ref, o_ref, p_ref, y_ref, d_ref,
    p_all, g_ref, w_ref, v_ref, local, sg, rg, sa, ra, sv, rv, ss, rs, fs, fr,
):
    dp, me = lax.axis_index("dp"), lax.axis_index("ctx")
    half, parity, pair, partner, ahead, behind = pairs_of(n, me)
    count, mine, place = group_of(n_dp, n, dp, me)
    columns = p_all.shape[2]
    fh, hc = d_ref.shape[2], v_ref.shape[2]
    loads = [
        pltpu.make_async_copy(
            p_hbm.at[:, pl.ds(part * columns, columns)], p_all.at[part], local.at[part]
        )
        for part in range(4)
    ]
    for part in (1, 2, 0, 3):
        loads[part].start()
    greet_all(n_dp, n, dp, me)
    gathers = [
        remote(x_ref, y_ref.at[me], ss.at[k], rs.at[k], (dp, a))
        for k, a in enumerate(ahead + [partner])
    ]
    own_x = pltpu.make_async_copy(x_ref, y_ref.at[me], local.at[4])
    for copy in gathers + [own_x]:
        copy.start()
    for part in (1, 2):
        loads[part].wait()
        for j in range(count):
            g_ref[j, :, (part - 1) * fh : part * fh] = p_all[part, :, j * fh : (j + 1) * fh].astype(BF)
    sends, receives = swap(g_ref, h_ref, sg, rg, count, mine, place)
    loads[0].wait()
    for c in range(n):
        for matrix in range(4):
            start = (matrix * n + c) * hc
            value = p_all[0, :, start : start + hc].astype(BF)
            if matrix < 3:
                w_ref[c, :, matrix * hc : (matrix + 1) * hc] = value
            else:
                v_ref[c] = value
    for src, dst, send, recv in ((w_ref, o_ref, sa, ra), (v_ref, p_ref, sv, rv)):
        more, waits = swap(src, dst, send, recv, n, me, lambda c: (dp, c))
        sends += more
        receives += waits
    owns = [
        pltpu.make_async_copy(g_ref.at[mine], h_ref.at[mine], local.at[5]),
        pltpu.make_async_copy(w_ref.at[me], o_ref.at[me], local.at[6]),
        pltpu.make_async_copy(v_ref.at[me], p_ref.at[me], local.at[7]),
    ]
    for copy in owns:
        copy.start()
    loads[3].wait()
    for j in range(count):
        d_ref[j] = p_all[3, :, j * fh : (j + 1) * fh].astype(BF)
    forwards = []
    for k, b in enumerate(behind):
        remote(x_ref, y_ref.at[b], ss.at[k], rs.at[k], (dp, b)).wait_recv()
        forward = remote(y_ref.at[b], y_ref.at[b], fs.at[k], fr.at[k], (dp, partner))
        forward.start()
        forwards.append(forward)
    gathers[-1].wait_recv()
    for copy in receives:
        copy.wait_recv()
    for forward in forwards:
        forward.wait()
    for copy in sends + gathers:
        copy.wait_send()
    for copy in owns + [own_x]:
        copy.wait()


def start(params, x, number):
    n_dp, n = lax.axis_size("dp"), lax.axis_size("ctx")
    half, count = n // 2, 2 * n_dp
    (rows, columns), width = params.shape, x.shape[1]
    fh, hc = columns // 4 // count, width // n
    dma = pltpu.SemaphoreType.DMA
    g, w, v = (count, rows, 2 * fh), (n, rows, 3 * hc), (n, rows, hc)
    g_out, w_out, v_out, x_all, d_out = pl.pallas_call(
        functools.partial(start_kernel, n_dp, n),
        out_shape=(
            jax.ShapeDtypeStruct(g, BF),
            jax.ShapeDtypeStruct(w, BF),
            jax.ShapeDtypeStruct(v, BF),
            jax.ShapeDtypeStruct((n,) + x.shape, x.dtype),
            jax.ShapeDtypeStruct((count, rows, fh), BF),
        ),
        in_specs=[ANY] * 2,
        out_specs=(ANY,) * 4 + (VMEM,),
        scratch_shapes=[
            pltpu.VMEM((4, rows, columns // 4), F32),
            pltpu.VMEM(g, BF),
            pltpu.VMEM(w, BF),
            pltpu.VMEM(v, BF),
            dma((8,)),
        ]
        + [dma((count - 1,))] * 2
        + [dma((n - 1,))] * 4
        + [dma((half,))] * 2
        + [dma((half - 1,))] * 2,
        compiler_params=params_of(number),
        cost_estimate=cost(45),
        name="start",
    )(params, x)
    return g_out, w_out, v_out, x_all.reshape(-1, width), d_out


def collect_kernel(
    n_dp, n, g_ref, h_ref, a_ref, w_ref, b_ref, o_ref, h_out, y_ref,
    sum_ref, acc, pa, qa, pb, qb, local, s1, r1, s2, r2, sh, rh, *line_refs,
):
    dp, me = lax.axis_index("dp"), lax.axis_index("ctx")
    tall = acc.shape[0]
    count, index, place = group_of(n_dp, n, dp, me)
    greet_all(n_dp, n, dp, me)

    def make(d, out):
        def put(part):
            rows = pl.ds(pl.multiple_of(d * tall + part.start, part.size), part.size)
            out[part, :] = g_ref[rows, :].astype(F32)

        tiles(tall, 64, put)

    cols = slice(0, a_ref.shape[1])
    stay = pltpu.make_async_copy(h_ref.at[index], h_out.at[index], local)
    stay.start()
    later = []

    def between():
        later.extend(swap(h_ref, h_out, sh, rh, count, index, place))
        later.append(reduce_ctx(n, dp, me, a_ref, w_ref, cols, sum_ref, pa, qa, pb, qb, s1, r1, s2, r2))

    def last():
        def put(part):
            o_ref[part, :] = acc[part, :].astype(BF)

        tiles(tall, 64, put)

    def join(part):
        y_ref[part, :] = (sum_ref[part, :] + b_ref[part, :]).astype(BF)

    val, *line = line_refs
    line_sum(n_dp, dp, me, make, val, acc, *line, last, between)
    swaps, receives, sums = later
    tiles(y_ref.shape[0], 32, join)
    for copy in receives:
        copy.wait_recv()
    stay.wait()
    for copy in swaps + sums:
        copy.wait_send()


def collect(g, h, a, w, b, number):
    n_dp, n = lax.axis_size("dp"), lax.axis_size("ctx")
    tall, width = g.shape[0] // n_dp, g.shape[1]
    half, length, features = n // 2, a.shape[0] // n, w.shape[0]
    dma = pltpu.SemaphoreType.DMA
    return pl.pallas_call(
        functools.partial(collect_kernel, n_dp, n),
        out_shape=(
            jax.ShapeDtypeStruct((tall, width), BF),
            jax.ShapeDtypeStruct(h.shape, BF),
            jax.ShapeDtypeStruct((length, features), BF),
        ),
        in_specs=[VMEM, ANY, VMEM, VMEM, VMEM],
        out_specs=(VMEM, ANY, VMEM),
        scratch_shapes=[
            pltpu.VMEM((length, features), F32),
            pltpu.VMEM((tall, width), F32),
            pltpu.VMEM((half, length, features), BF),
            pltpu.VMEM((half, length, features), BF),
            pltpu.VMEM((half - 1, length, features), BF),
            pltpu.VMEM((half - 1, length, features), BF),
            dma,
            dma((half,)),
            dma((half,)),
            dma((half - 1,)),
            dma((half - 1,)),
            dma((2 * n_dp - 1,)),
            dma((2 * n_dp - 1,)),
        ]
        + line_scratch(n_dp, tall, width),
        compiler_params=params_of(number),
        cost_estimate=cost(70),
        name="collect",
    )(g, h, a, w, b)


def total_kernel(
    n_dp, n, qk_ref, wv_ref, wo_ref, u_ref, gg_ref, gd_ref, qk_gain, attn_gain, ff_gain, p_hbm, m_hbm, v_hbm,
    ga_ref, gu_ref, o_ref, p_out, m_out, v_out,
    sb, mine, buf, part, all_parts, square, buf_s, part_s, all_s, local, sx, rx, sh, rh,
    ss, rs, st, rt, s1, r1, s2, r2, sem_copy,
):
    dp, me = lax.axis_index("dp"), lax.axis_index("ctx")
    hc = wv_ref.shape[2]
    count, index, place = group_of(n_dp, n, dp, me)
    greet_all(n_dp, n, dp, me)
    swaps, receives = swap(u_ref, gu_ref, sh, rh, count, index, place)
    stay = pltpu.make_async_copy(u_ref.at[index], gu_ref.at[index], local)
    stay.start()
    moves = [
        pltpu.make_async_copy(source, target, sem_copy.at[i])
        for i, (source, target) in enumerate(((p_hbm, p_out), (m_hbm, m_out), (v_hbm, v_out)))
    ]
    for copy in moves:
        copy.start()
    sb[:, :, : 2 * hc] = qk_ref[...]
    sb[:, :, 2 * hc : 3 * hc] = wv_ref[...]
    more, waits = swap(sb, ga_ref, sx, rx, n, me, lambda c: (dp, c))
    ga_ref[me] = sb[me]

    def squares(ref):
        acc = jnp.zeros((ref.shape[1], ref.shape[2]), F32)
        for i in range(ref.shape[0]):
            block = ref[i].astype(F32)
            acc += block * block
        return jnp.sum(jnp.sum(acc, axis=0, keepdims=True), axis=1, keepdims=True)

    copies = swaps + more

    def sum_all(value, rows, along, columns, send, recv, send_dp, recv_dp):
        for k in range(1, n):
            copy = remote(value, rows.at[me], send.at[k - 1], recv.at[k - 1], (dp, (me + k) % n))
            copy.start()
            copies.append(copy)
        rows[me] = value[...]
        for k in range(1, n):
            source = (me + n - k) % n
            remote(value, rows.at[source], send.at[k - 1], recv.at[k - 1], (dp, source)).wait_recv()
        acc = rows[0]
        for j in range(1, n):
            acc = acc + rows[j]
        along[...] = acc
        columns[dp] = acc
        for k in range(1, n_dp):
            to = (dp + k) % n_dp
            copy = remote(along, columns.at[dp], send_dp.at[k - 1], recv_dp.at[k - 1], (to, me))
            copy.start()
            copies.append(copy)
        for k in range(1, n_dp):
            source = (dp + n_dp - k) % n_dp
            remote(along, columns.at[source], send_dp.at[k - 1], recv_dp.at[k - 1], (source, me)).wait_recv()
        acc = columns[0]
        for j in range(1, n_dp):
            acc = acc + columns[j]
        return acc

    mine[...] = jnp.zeros_like(mine)
    mine[0:2, pl.ds(pl.multiple_of(me * hc, hc), hc)] = qk_gain[...]
    mine[2:3, :] = attn_gain[...]
    mine[3:4, :] = ff_gain[...]
    o_ref[...] = sum_all(mine, buf, part, all_parts, ss, rs, st, rt)
    total = squares(gg_ref) + squares(gd_ref) + squares(wo_ref)
    for copy in waits:
        copy.wait_recv()
    total += squares(ga_ref)
    for copy in receives:
        copy.wait_recv()
    stay.wait()
    total += squares(gu_ref)
    square[...] = jnp.broadcast_to(total, square.shape)
    total = sum_all(square, buf_s, part_s, all_s, s1, r1, s2, r2)
    o_ref[4:5, :] = jnp.broadcast_to(total[0:1, 0:1], (1, o_ref.shape[1]))
    for copy in copies:
        copy.wait_send()
    for copy in moves:
        copy.wait()


def total_over(qk, wv, wo, u, gg, gd, qk_gain, attn_gain, ff_gain, masters, number):
    n_dp, n = lax.axis_size("dp"), lax.axis_size("ctx")
    rows, hc = qk.shape[0] // n, wv.shape[1]
    shape = (8, attn_gain.shape[1])
    dma = pltpu.SemaphoreType.DMA
    return pl.pallas_call(
        functools.partial(total_kernel, n_dp, n),
        out_shape=(
            jax.ShapeDtypeStruct((n, rows, 3 * hc), BF),
            jax.ShapeDtypeStruct(u.shape, BF),
            jax.ShapeDtypeStruct(shape, F32),
            *[jax.ShapeDtypeStruct(a.shape, F32) for a in masters],
        ),
        in_specs=[VMEM] * 3 + [ANY] + [VMEM] * 5 + [HBM] * 3,
        out_specs=(VMEM,) * 3 + (ANY,) * 3,
        scratch_shapes=[
            pltpu.VMEM((n, rows, 3 * hc), BF),
            pltpu.VMEM(shape, F32),
            pltpu.VMEM((n,) + shape, F32),
            pltpu.VMEM(shape, F32),
            pltpu.VMEM((n_dp,) + shape, F32),
            pltpu.VMEM((8, 128), F32),
            pltpu.VMEM((n, 8, 128), F32),
            pltpu.VMEM((8, 128), F32),
            pltpu.VMEM((n_dp, 8, 128), F32),
            dma,
            dma((n - 1,)),
            dma((n - 1,)),
            dma((2 * n_dp - 1,)),
            dma((2 * n_dp - 1,)),
            dma((n - 1,)),
            dma((n - 1,)),
            dma((n_dp - 1,)),
            dma((n_dp - 1,)),
            dma((n - 1,)),
            dma((n - 1,)),
            dma((n_dp - 1,)),
            dma((n_dp - 1,)),
            dma((3,)),
        ],
        compiler_params=params_of(number, 14),
        cost_estimate=cost(35),
        name="total",
    )(
        qk.reshape(n, rows, 2 * hc),
        wv.reshape(n, rows, hc),
        wo[None],
        u,
        gg,
        gd,
        qk_gain,
        attn_gain,
        ff_gain,
        *masters,
    )


def adam_kernel(
    sum_ref, gp_ref, gm_ref, gv_ref, p_ref, m_ref, v_ref, ga_ref, go_ref, gg_ref, gu_ref, gd_ref,
    norm_ref, gp_out, gm_out, gv_out, po_ref, mo_ref, vo_ref, g_ref, factor_ref,
):
    part = pl.program_id(0)

    @pl.when((part == 0) & (pl.program_id(1) == 0))
    def _():
        gain = sum_ref[0:4, :]
        squares = jnp.sum(jnp.sum(gain * gain, axis=0, keepdims=True), axis=1, keepdims=True)
        norm = jnp.sqrt(sum_ref[4:5, 0:1] + squares)
        norm_ref[...] = norm
        factor = CLIP / (norm + 1e-06)
        factor_ref[...] = jnp.broadcast_to(factor, factor_ref.shape)
        new = adam_update(gp_ref[...], gm_ref[...], gv_ref[...], gain * factor, GAIN_RATE, 0.0)
        gp_out[...], gm_out[...], gv_out[...] = new

    n, _, three = ga_ref.shape
    hc = three // 3
    fs = gd_ref.shape[2]

    @pl.when(part == 0)
    def _():
        g_ref[:, 3 * n * hc :] = go_ref[...].astype(F32)
        for matrix in range(3):
            for c in range(n):
                start = (matrix * n + c) * hc
                g_ref[:, start : start + hc] = ga_ref[c, :, matrix * hc : (matrix + 1) * hc].astype(F32)

    for index, ref in ((1, gg_ref), (2, gu_ref), (3, gd_ref)):

        @pl.when(part == index)
        def _():
            for d in range(ref.shape[0]):
                g_ref[:, d * fs : (d + 1) * fs] = ref[d].astype(F32)

    clipped = g_ref[...] * factor_ref[0:1, 0:1]
    new_m = BETA1 * m_ref[...] + (1.0 - BETA1) * clipped
    new_v = BETA2 * v_ref[...] + (1.0 - BETA2) * (clipped * clipped)
    hat = new_v * (1.0 / (1.0 - BETA2**STEP))
    root = hat * lax.rsqrt(jnp.maximum(hat, 1e-36)) + ADAM_EPS
    change = (new_m * (RATE / (1.0 - BETA1**STEP))) * pl.reciprocal(root, approx=True)
    po_ref[...] = p_ref[...] * (1.0 - RATE * DECAY) - change
    mo_ref[...] = new_m
    vo_ref[...] = new_v


def adam(sums, gains, gains_first, gains_second, params, first, second, ga, go, gg, gu, gd):
    rows, columns = params.shape
    n, n_dp, fs = ga.shape[0], gd.shape[0], gd.shape[2]
    block = min(rows, 32)
    steps = rows // block
    wide = pl.BlockSpec((block, columns // 4), lambda i, r: (r, i))
    small = pl.BlockSpec(gains.shape, lambda i, r: (0, 0))
    return pl.pallas_call(
        adam_kernel,
        grid=(4, steps),
        out_shape=(jax.ShapeDtypeStruct((1, 1), F32),)
        + (jax.ShapeDtypeStruct(gains.shape, F32),) * 3
        + (jax.ShapeDtypeStruct(params.shape, F32),) * 3,
        in_specs=[
            pl.BlockSpec(sums.shape, lambda i, r: (0, 0)),
            small,
            small,
            small,
            wide,
            wide,
            wide,
            pl.BlockSpec((n, block, ga.shape[2]), lambda i, r: (0, jnp.where(i == 0, r, steps - 1), 0)),
            pl.BlockSpec((block, go.shape[1]), lambda i, r: (jnp.where(i == 0, r, steps - 1), 0)),
            *[
                pl.BlockSpec(
                    (n_dp, block, fs),
                    lambda i, r, part=part: (
                        0,
                        jnp.where(i < part, 0, jnp.where(i == part, r, steps - 1)),
                        0,
                    ),
                )
                for part in (1, 2, 3)
            ],
        ],
        out_specs=(pl.BlockSpec((1, 1), lambda i, r: (0, 0)),) + (small,) * 3 + (wide,) * 3,
        scratch_shapes=[pltpu.VMEM((block, columns // 4), F32), pltpu.VMEM((8, 128), F32)],
        compiler_params=pltpu.CompilerParams(vmem_limit_bytes=22 * 1024 * 1024),
        name="adam",
    )(sums, gains, gains_first, gains_second, params, first, second, ga, go, gg, gu, gd)


def row_sums(value, row):
    pick = lax.broadcasted_iota(jnp.int32, (8, value.shape[1]), 0) == row
    return lax.dot_general(
        pick.astype(F32),
        value,
        (((1,), (1,)), ((), ())),
        preferred_element_type=F32,
        precision=lax.Precision.HIGHEST,
    )


def exchange(n, dp, me, buf, ss, rs):
    copies = []
    for k in range(1, n):
        copy = remote(buf.at[me], buf.at[me], ss.at[k - 1], rs.at[k - 1], (dp, (me + k) % n))
        copy.start()
        copies.append(copy)
    for k in range(1, n):
        source = (me + n - k) % n
        remote(buf.at[me], buf.at[source], ss.at[k - 1], rs.at[k - 1], (dp, source)).wait_recv()
    total = buf[0]
    for j in range(1, n):
        total = total + buf[j]
    for copy in copies:
        copy.wait_send()
    return total


def turn(value, cos, sine):
    return value * cos + pltpu.roll(value, HD // 2, 1) * sine


def mask_of(rows, info_col, info_row):
    pos_i, doc_i = info_col[rows, 0:1], info_col[rows, 1:2]
    return (info_row[1:2, :] == doc_i) & (info_row[0:1, :] <= pos_i)


def attend_kernel(
    n_dp, n, x_ref, w_ref, wo_ref, d_ref, t_ref, norm_ref, gain_ref, cos_ref, sin_ref, col_ref, row_ref,
    y_ref, h_ref, q_ref, k_ref, v_ref, o_ref, pre_ref, scale_ref, lse_ref, wo_all, d_out,
    buf, pa, qa, pb, qb, ss, rs, s1, r1, s2, r2, sw, rw, sd, rd, local,
):
    dp, me = lax.axis_index("dp"), lax.axis_index("ctx")
    seq, width = x_ref.shape
    hc = o_ref.shape[1]
    block = min(seq, 256)
    count, mine, place = group_of(n_dp, n, dp, me)
    greet_all(n_dp, n, dp, me)
    piece = wo_ref.shape[0]

    def part_of(d):
        return wo_all.at[pl.ds(pl.multiple_of(d * piece, piece), piece), :]

    owns = [
        pltpu.make_async_copy(wo_ref, part_of(dp), local.at[0]),
        pltpu.make_async_copy(d_ref.at[mine], d_out.at[mine], local.at[1]),
    ]
    behind_wo = [
        remote(wo_ref, part_of(dp), sw.at[k - 1], rw.at[k - 1], (across(dp, k, n_dp)[0], me))
        for k in range(1, n_dp)
    ]
    for copy in behind_wo + owns:
        copy.start()
    behind_d, receives = swap(d_ref, d_out, sd, rd, count, mine, place)

    @pl.loop(0, seq // block)
    def _(i):
        rows = pl.ds(pl.multiple_of(i * block, block), block)
        value = dot(x_ref[rows, :], w_ref[...])
        pre_ref[rows, :] = value[:, : 2 * hc]
        v_ref[rows, :] = value[:, 2 * hc :].astype(BF)
        squares = value[:, : 2 * hc] * value[:, : 2 * hc]
        buf[me, :, rows] = row_sums(squares[:, :hc], 0) + row_sums(squares[:, hc:], 1)

    scale_ref[...] = jnp.transpose(lax.rsqrt(exchange(n, dp, me, buf, ss, rs) / width + EPS))

    @pl.loop(0, seq // block)
    def _(i):
        rows = pl.ds(pl.multiple_of(i * block, block), block)
        cos, sine = cos_ref[rows, :], sin_ref[rows, :]
        for which, ref, factor in ((0, q_ref, HD ** (-0.5)), (1, k_ref, 1.0)):
            scale = scale_ref[rows, which : which + 1]
            for start in range(0, hc, HD):
                part = slice(start, start + HD)
                value = pre_ref[rows, which * hc + start : which * hc + start + HD] * scale
                ref[rows, part] = (
                    turn(value * gain_ref[which : which + 1, part], cos, sine) * factor
                ).astype(BF)

    def attention(pair, first):
        size = 2 * (seq // n)
        rows = pl.ds(pl.multiple_of(pair * size, size), size)
        visible = mask_of(rows, col_ref, row_ref)
        for head in range(hc // HD):
            part = slice(head * HD, (head + 1) * HD)
            scores = jnp.where(visible, dot_t(q_ref[rows, part], k_ref[:, part]), -jnp.inf)
            top = jnp.max(scores, axis=1, keepdims=True)
            weights = jnp.exp(scores - top)
            total = jnp.sum(weights, axis=1, keepdims=True)
            o_ref[rows, part] = (dot(weights.astype(BF), v_ref[:, part]) / total).astype(BF)
            lse_ref[rows, head : head + 1] = top + jnp.log(total)
        if first:
            owns[0].wait()
            for k in range(1, n_dp):
                _, source = across(dp, k, n_dp)
                remote(wo_ref, part_of(source), sw.at[k - 1], rw.at[k - 1], (source, me)).wait_recv()

    cols = slice(0, hc)
    sums = reduce_ctx(
        n, dp, me, o_ref, wo_all, cols, y_ref, pa, qa, pb, qb, s1, r1, s2, r2, before=attention
    )

    def finish(rows):
        branch = y_ref[rows, :]
        h_ref[rows, :] = t_ref[rows, :].astype(F32) + branch * rms_scale(branch) * norm_ref[...]

    tiles(y_ref.shape[0], 16, finish)
    for copy in receives:
        copy.wait_recv()
    for copy in sums + behind_wo + behind_d:
        copy.wait_send()
    owns[1].wait()


def attend(x_all, w, wo, d, tokens, norm, gain, cos, sine, info_col, info_row, number):
    n_dp, n = lax.axis_size("dp"), lax.axis_size("ctx")
    seq, width = x_all.shape
    half, length, hc = n // 2, seq // n, w.shape[1] // 3
    dma = pltpu.SemaphoreType.DMA
    low = jax.ShapeDtypeStruct((seq, hc), BF)
    return pl.pallas_call(
        functools.partial(attend_kernel, n_dp, n),
        out_shape=(
            jax.ShapeDtypeStruct((length, width), F32),
            jax.ShapeDtypeStruct((length, width), F32),
            low,
            low,
            low,
            low,
            jax.ShapeDtypeStruct((seq, 2 * hc), F32),
            jax.ShapeDtypeStruct((seq, 8), F32),
            jax.ShapeDtypeStruct((seq, 8), F32),
            jax.ShapeDtypeStruct((width, hc), BF),
            jax.ShapeDtypeStruct(d.shape, BF),
        ),
        in_specs=[VMEM] * 2 + [ANY] * 2 + [VMEM] * 7,
        out_specs=(VMEM,) * 10 + (ANY,),
        scratch_shapes=[
            pltpu.VMEM((n, 8, seq), F32),
            pltpu.VMEM((half, length, width), BF),
            pltpu.VMEM((half, length, width), BF),
            pltpu.VMEM((half - 1, length, width), BF),
            pltpu.VMEM((half - 1, length, width), BF),
            dma((n - 1,)),
            dma((n - 1,)),
            dma((half,)),
            dma((half,)),
            dma((half - 1,)),
            dma((half - 1,)),
            dma((n_dp - 1,)),
            dma((n_dp - 1,)),
            dma((2 * n_dp - 1,)),
            dma((2 * n_dp - 1,)),
            dma((2,)),
        ],
        compiler_params=params_of(number),
        cost_estimate=cost(60),
        name="attend",
    )(x_all, w, wo, d, tokens, norm, gain, cos, sine, info_col, info_row)


def slab_give(n_dp, dp, me, g_ref, co_ref, sw, rw):
    tall = co_ref.shape[1]
    gives = []
    for k in range(1, n_dp):
        to, _ = across(dp, k, n_dp)
        part = pl.ds(pl.multiple_of(to * tall, tall), tall)
        copy = remote(g_ref.at[part, :], co_ref.at[k - 1], sw.at[k - 1], rw.at[k - 1], (to, me))
        copy.start()
        gives.append(copy)
    return gives


def slab_sum(dp, gives, g_ref, co_ref, out_ref):
    tall = co_ref.shape[1]
    total = g_ref[pl.ds(pl.multiple_of(dp * tall, tall), tall), :].astype(F32)
    for k, copy in enumerate(gives):
        copy.wait_recv()
        total = total + co_ref[k].astype(F32)
    out_ref[...] = total.astype(BF)


def greet_wide_group(n_dp, dp, me):
    partner = me + 1 - 2 * (me % 2)
    others = [(dp + k) % n_dp for k in range(1, n_dp)]
    greet([(dp, partner)] + [(d, c) for d in others for c in (me, partner)])


def attend_back_kernel(
    n_dp, n, sum_ref, up_ref, branch_ref, norm_ref, wo_hbm, h_ref, o_hbm, col_ref, row_ref, q_ref, k_ref, v_ref, lse_ref,
    x_hbm, gain_ref, cos_ref, sin_ref, pre_hbm, scale_ref,
    dh_ref, gp_ref, d_ref, gain_out, g_ref, wv_ref, wo_ref, h_out,
    x_ref, pre_ref, wall_ref, db_ref, mix_ref, give_ref, e_ref, do_ref, o_ref, dq_ref, dk_ref, dv_ref, mean_ref, buf, go_ref, co_ref, gv_ref, cv_ref,
    sh, rh, local, sw, rw, sv, rv, ss, rs, sc, rc, sx, rx,
):
    dp, me = lax.axis_index("dp"), lax.axis_index("ctx")
    seq, hc = q_ref.shape
    load_wo = pltpu.make_async_copy(wo_hbm, wall_ref, local.at[2])
    load_wo.start()
    later = [
        pltpu.make_async_copy(src, dst, local.at[i])
        for i, (src, dst) in enumerate(((x_hbm, x_ref), (pre_hbm, pre_ref)), 4)
    ]
    load = pltpu.make_async_copy(o_hbm, o_ref, local.at[1])
    load.start()
    length, width = dh_ref.shape
    block = min(seq, 256)
    count, index, place = group_of(n_dp, n, dp, me)
    greet_all(n_dp, n, dp, me)
    swaps, receives = swap(h_ref, h_out, sh, rh, count, index, place)
    stay = pltpu.make_async_copy(h_ref.at[index], h_out.at[index], local.at[0])
    stay.start()

    gp_ref[...] = jnp.zeros_like(gp_ref)

    def finish(rows):
        grad, branch = sum_ref[rows, :] + up_ref[rows, :].astype(F32), branch_ref[rows, :]
        scale = rms_scale(branch)
        dh_ref[rows, :] = grad
        gp_ref[...] += jnp.sum(grad * branch * scale, axis=0, keepdims=True)
        db_ref[rows, :] = norm_back(grad * norm_ref[...], branch, scale).astype(BF)

    tiles(length, 16, finish)
    load_wo.wait()

    def mine(c):
        return pl.ds(pl.multiple_of(c * length, length), length)

    def send(k):
        to = (me + k) % n
        return remote(give_ref.at[to], do_ref.at[mine(me), :], sx.at[k - 1], rx.at[k - 1], (dp, to))

    def receive(k):
        source = (me + n - k) % n
        return remote(give_ref.at[me], do_ref.at[mine(source), :], sx.at[k - 1], rx.at[k - 1], (dp, source))

    share = width // n
    own = share // n_dp
    for c in range(n):
        for d in range(n_dp):
            start, source = c * share + d * own, (d * n + c) * own
            mix_ref[:, start : start + own] = db_ref[:, source : source + own]

    def share_of(c):
        return mix_ref.at[:, pl.ds(pl.multiple_of(c * share, share), share)]

    def send_share(k):
        to = (me + k) % n
        return remote(share_of(to), e_ref.at[mine(me), :], sc.at[k - 1], rc.at[k - 1], (dp, to))

    def receive_share(k):
        source = (me + n - k) % n
        return remote(share_of(me), e_ref.at[mine(source), :], sc.at[k - 1], rc.at[k - 1], (dp, source))

    stay_share = pltpu.make_async_copy(share_of(me), e_ref.at[mine(me), :], local.at[3])
    stay_share.start()

    @pl.loop(1, n)
    def _(k):
        to = (me + k) % n
        send_share(k).start()
        give_ref[to] = dot(db_ref[...], wall_ref[to]).astype(BF)
        send(k).start()

    do_ref[mine(me), :] = dot(db_ref[...], wall_ref[me]).astype(BF)
    for k in range(1, n):
        receive(k).wait_recv()
        receive_share(k).wait_recv()
    for k in range(1, n):
        send(k).wait_send()
        send_share(k).wait_send()
    stay_share.wait()
    load.wait()
    for copy in later:
        copy.start()

    @pl.loop(0, n)
    def _(c):
        go_ref[:, pl.ds(pl.multiple_of(c * hc, hc), hc)] = t_dot(e_ref[...], o_ref[c]).astype(BF)

    gives = slab_give(n_dp, dp, me, go_ref, co_ref, sw, rw)
    dk_ref[...] = jnp.zeros_like(dk_ref)
    dv_ref[...] = jnp.zeros_like(dv_ref)

    def attention(i):
        rows = pl.ds(pl.multiple_of(i * block, block), block)
        visible = mask_of(rows, col_ref, row_ref)
        for head in range(hc // HD):
            part = slice(head * HD, (head + 1) * HD)
            query, key, value, back = q_ref[rows, part], k_ref[:, part], v_ref[:, part], do_ref[rows, part]
            scores = jnp.where(visible, dot_t(query, key), -jnp.inf)
            probs = jnp.exp(scores - lse_ref[rows, head : head + 1])
            d_probs = dot_t(back, value)
            delta = jnp.sum(probs * d_probs, axis=1, keepdims=True)
            d_scores = (probs * (d_probs - delta)).astype(BF)
            dq_ref[rows, part] = dot(d_scores, key)
            dk_ref[:, part] += t_dot(d_scores, query)
            dv_ref[:, part] += t_dot(probs.astype(BF), back)

    pl.loop(0, seq // block)(attention)

    for copy in later:
        copy.wait()
    d_ref[:, 2 * hc :] = dv_ref[...].astype(BF)

    def values(part):
        gv_ref[part, :] = t_dot(x_ref[:, part], d_ref[:, 2 * hc :]).astype(BF)

    tiles(width, 256, values)
    gives_v = slab_give(n_dp, dp, me, gv_ref, cv_ref, sv, rv)
    gain_out[...] = jnp.zeros_like(gain_out)

    @pl.loop(0, seq // block)
    def _(i):
        rows = pl.ds(pl.multiple_of(i * block, block), block)
        cos, sine = cos_ref[rows, :], sin_ref[rows, :]
        sums = jnp.zeros((8, block), F32)
        for which, ref, factor in ((0, dq_ref, HD ** (-0.5)), (1, dk_ref, 1.0)):
            scale = scale_ref[rows, which : which + 1]
            for start in range(0, hc, HD):
                part = slice(start, start + HD)
                pre = pre_ref[rows, which * hc + start : which * hc + start + HD]
                value = turn(ref[rows, part] * factor, cos, -sine)
                gain_out[which : which + 1, part] += jnp.sum(value * pre * scale, axis=0, keepdims=True)
                value = value * gain_ref[which : which + 1, part]
                ref[rows, part] = value
                sums += row_sums(value * pre, which)
        buf[me, :, rows] = sums

    mean_ref[...] = jnp.transpose(exchange(n, dp, me, buf, ss, rs) / width)

    @pl.loop(0, seq // block)
    def _(i):
        rows = pl.ds(pl.multiple_of(i * block, block), block)
        for which, ref in ((0, dq_ref), (1, dk_ref)):
            scale = scale_ref[rows, which : which + 1]
            mean = mean_ref[rows, which : which + 1]
            cols = slice(which * hc, (which + 1) * hc)
            value = scale * (ref[rows, :] - pre_ref[rows, cols] * (scale * scale * mean))
            d_ref[rows, cols] = value.astype(BF)

    def product(part):
        g_ref[part, :] = t_dot(x_ref[:, part], d_ref[:, : 2 * hc]).astype(BF)

    tiles(width, 256, product)
    slab_sum(dp, gives, go_ref, co_ref, wo_ref)
    slab_sum(dp, gives_v, gv_ref, cv_ref, wv_ref)
    for copy in receives:
        copy.wait_recv()
    for copy in swaps + gives + gives_v:
        copy.wait_send()
    stay.wait()


def attend_back(sums, up, branch, norm, wo_all, h, o_all, info_col, info_row, q, k, v, lse, x, gain, cos, sine, pre, scale, number):
    n_dp, n = lax.axis_size("dp"), lax.axis_size("ctx")
    (seq, hc), (length, width) = q.shape, branch.shape
    share = width // n
    dma = pltpu.SemaphoreType.DMA
    return pl.pallas_call(
        functools.partial(attend_back_kernel, n_dp, n),
        out_shape=(
            jax.ShapeDtypeStruct((length, width), F32),
            jax.ShapeDtypeStruct((1, width), F32),
            jax.ShapeDtypeStruct((seq, 3 * hc), BF),
            jax.ShapeDtypeStruct((2, hc), F32),
            jax.ShapeDtypeStruct((width, 2 * hc), BF),
            jax.ShapeDtypeStruct((width // n_dp, hc), BF),
            jax.ShapeDtypeStruct((share // n_dp, n * hc), BF),
            jax.ShapeDtypeStruct(h.shape, BF),
        ),
        in_specs=[VMEM] * 4 + [ANY] * 3 + [VMEM] * 6 + [ANY] + [VMEM] * 3 + [ANY, VMEM],
        out_specs=(VMEM,) * 7 + (ANY,),
        scratch_shapes=[
            pltpu.VMEM(x.shape, BF),
            pltpu.VMEM(pre.shape, F32),
            pltpu.VMEM(wo_all.shape, BF),
            pltpu.VMEM((length, width), BF),
            pltpu.VMEM((length, width), BF),
            pltpu.VMEM((n, length, hc), BF),
            pltpu.VMEM((seq, share), BF),
            pltpu.VMEM((seq, hc), BF),
            pltpu.VMEM(o_all.shape, BF),
            pltpu.VMEM((seq, hc), F32),
            pltpu.VMEM((seq, hc), F32),
            pltpu.VMEM((seq, hc), F32),
            pltpu.VMEM((seq, 8), F32),
            pltpu.VMEM((n, 8, seq), F32),
            pltpu.VMEM((share, n * hc), BF),
            pltpu.VMEM((n_dp - 1, share // n_dp, n * hc), BF),
            pltpu.VMEM((width, hc), BF),
            pltpu.VMEM((n_dp - 1, width // n_dp, hc), BF),
            dma((2 * n_dp - 1,)),
            dma((2 * n_dp - 1,)),
            dma((6,)),
            dma((n_dp - 1,)),
            dma((n_dp - 1,)),
            dma((n_dp - 1,)),
            dma((n_dp - 1,)),
            dma((n - 1,)),
            dma((n - 1,)),
            dma((n - 1,)),
            dma((n - 1,)),
            dma((n - 1,)),
            dma((n - 1,)),
        ],
        compiler_params=params_of(number, 56),
        cost_estimate=cost(75),
        name="attend_back",
    )(sums, up, branch, norm, wo_all, h, o_all, info_col, info_row, q, k, v, lse, x, gain, cos, sine, pre, scale)


def shards(
    inputs,
    cotangent,
    documents,
    block_place,
    params,
    first_moment,
    second_moment,
    gains,
    gains_first,
    gains_second,
):
    tokens = inputs[0]
    upstream = cotangent[0]
    length, width = tokens.shape
    n_ctx = lax.axis_size("ctx")
    n_dp = lax.axis_size("dp")
    me_ctx = lax.axis_index("ctx")
    seq = length * n_ctx
    rows = params.shape[0]
    ff = (params.shape[1] - 4 * width) // 3
    hc = width // n_ctx
    half, group = n_ctx // 2, 2 * n_dp
    fh = ff // group
    parities = [[2 * p + side for p in range(half)] for side in range(2)]

    def gather_pairs(w):
        w = lax.all_gather(
            w.reshape(group * rows, w.shape[2]), "ctx", axis=0, tiled=True, axis_index_groups=parities
        )
        return w.reshape(half, n_dp, 2 * rows, w.shape[1])

    def scatter_pairs(g):
        g = lax.psum_scatter(
            g.reshape(width, g.shape[3]),
            "ctx",
            scatter_dimension=0,
            tiled=True,
            axis_index_groups=parities,
        )
        return g.reshape(group, rows, g.shape[1])

    w_gu, w_qkv, w_o, x_all, w_d = start(params, tokens, 1)
    w_gu = gather_pairs(w_gu)
    w_qkv = gather_dp(w_qkv.reshape(n_ctx * rows, 3 * hc), 2)

    indices = jnp.arange(seq, dtype=jnp.int32)
    owners = indices // length
    placed = jnp.sum(
        jnp.where(
            owners[:, None] == jnp.arange(n_ctx, dtype=jnp.int32)[None, :], block_place[None, :], 0
        ),
        axis=1,
    )
    pos = placed * length + indices % length
    docs = documents[0]
    info_row = jnp.concatenate([pos[None], docs[None], jnp.zeros((6, seq), jnp.int32)])
    info_col = info_row.T
    cos_tab, sine_tab = rope_tables(pos, HD)
    cos_tab = jnp.concatenate([cos_tab, cos_tab], axis=1)
    sine_tab = jnp.concatenate([-sine_tab, sine_tab], axis=1)
    my_gains = lax.dynamic_slice_in_dim(gains[:2], me_ctx * hc, hc, axis=1)
    tables = (my_gains, cos_tab, sine_tab, info_col, info_row)

    branch, hidden1, queries, keys, values, attn_low, qk_pre, scales, lse, w_o, w_d = attend(
        x_all, w_qkv, w_o.reshape(n_ctx * rows, hc), w_d, tokens, gains[2:3], *tables, 3
    )

    result, d_mlp, g_ff_part, h1_all, gate_up, inner, w_d, w_o = ff_forward(
        hidden1, upstream, gains[3:4], w_gu, w_d.reshape(n_dp, 2 * rows, fh), w_o, 4
    )
    attn_low, d_mlp = lax.optimization_barrier((attn_low, d_mlp))
    attn_all = lax.all_gather(attn_low, "ctx", axis=0)
    d_gu, d_grad = ff_back(d_mlp, inner, w_d, gate_up, rows, 5)
    d_grad = scatter_pairs(d_grad)
    d_sums, g_grad, u_grad = ff_scatter(d_gu, w_gu, h1_all, length, 6)
    g_grad, u_grad = scatter_pairs(g_grad), scatter_pairs(u_grad)

    d_h1, g_attn_part, d_qkv, d_gain, qk_grad, wv_grad, wo_grad, d_grad = attend_back(
        d_sums, upstream, branch, gains[2:3], w_o, d_grad, attn_all, info_col, info_row, queries, keys, values, lse,
        x_all, my_gains, cos_tab, sine_tab, qk_pre, scales, 8,
    )
    qk_grad, g_grad, d_input = collect(qk_grad, g_grad, d_qkv, w_qkv, d_h1, 9)

    attn_grad, u_grad, sums, *masters = total_over(
        qk_grad, wv_grad, wo_grad, u_grad, g_grad, d_grad, d_gain, g_attn_part, g_ff_part,
        (params, first_moment, second_moment), 11,
    )
    grad_norm, new_gains, new_gains_first, new_gains_second, new_params, new_first, new_second = adam(
        sums, gains, gains_first, gains_second, *masters,
        attn_grad, wo_grad, g_grad, u_grad, d_grad,
    )
    return (
        result[None],
        d_input[None],
        grad_norm.reshape(()),
        new_params,
        new_first,
        new_second,
        new_gains,
        new_gains_first,
        new_gains_second,
    )


def solution(mesh):
    split, whole = P("dp", "ctx", None), P(("dp", "ctx"), None)
    return jax.shard_map(
        shards,
        mesh=mesh,
        in_specs=(split, split, P("dp", None), P(), whole, whole, whole, P(), P(), P()),
        out_specs=(split, split, P(), whole, whole, whole, P(), P(), P()),
        check_vma=False,
    )
```

```python
import functools

import jax
import jax.numpy as jnp
import numpy as np
from jax import lax
from jax.experimental import pallas as pl
from jax.experimental.pallas import tpu as pltpu
from jax.sharding import PartitionSpec as P

HD = 128
STEP = 10
EPS = 1e-06
THETA = 500000.0
CLIP = 1.0
BETA1 = 0.9
BETA2 = 0.95
RATE = 0.03
GAIN_RATE = 0.8
DECAY = 0.1
ADAM_EPS = 1e-08
BF = jnp.bfloat16
F32 = jnp.float32
MESH = pl.DeviceIdType.MESH
ANY = pl.BlockSpec(memory_space=pl.ANY)
VMEM = pl.BlockSpec(memory_space=pltpu.VMEM)
HBM = pl.BlockSpec(memory_space=pltpu.HBM)


def rms_scale(values):
    return lax.rsqrt(jnp.mean(values * values, axis=-1, keepdims=True) + EPS)


def norm_back(upstream, source, scale):
    return scale * (
        upstream - source * scale * scale * jnp.mean(upstream * source, axis=-1, keepdims=True)
    )


def adam_update(weight, first_in, second_in, clipped, rate, decay):
    new_first = BETA1 * first_in + (1.0 - BETA1) * clipped
    new_second = BETA2 * second_in + (1.0 - BETA2) * clipped * clipped
    first_hat = new_first / (1.0 - BETA1**STEP)
    second_hat = new_second / (1.0 - BETA2**STEP)
    new_weight = weight - rate * (first_hat / (jnp.sqrt(second_hat) + ADAM_EPS) + decay * weight)
    return (new_weight, new_first, new_second)


def dot(a, b):
    return jnp.dot(a, b, preferred_element_type=F32)


def dot_t(a, b):
    return lax.dot_general(a, b, (((1,), (1,)), ((), ())), preferred_element_type=F32)


def t_dot(a, b):
    return lax.dot_general(a, b, (((0,), (0,)), ((), ())), preferred_element_type=F32)


def loads_of(pairs, sems, first=0):
    copies = [pltpu.make_async_copy(a, b, sems.at[first + i]) for i, (a, b) in enumerate(pairs)]
    for copy in copies:
        copy.start()
    return copies


def greet(peers):
    barrier = pltpu.get_barrier_semaphore()
    for peer in peers:
        pl.semaphore_signal(barrier, inc=1, device_id=peer, device_id_type=MESH)
    pl.semaphore_wait(barrier, len(peers))


def remote(src, dst, send, recv, peer):
    return pltpu.make_async_remote_copy(
        src_ref=src, dst_ref=dst, send_sem=send, recv_sem=recv, device_id=peer, device_id_type=MESH
    )


def cost(us):
    return pl.CostEstimate(flops=0, bytes_accessed=us * 3_600_000, transcendentals=0)


def params_of(number, vmem=62):
    return pltpu.CompilerParams(
        collective_id=number, has_side_effects=True, vmem_limit_bytes=vmem * 1024 * 1024
    )


def line_steps(n, me, make_right, make_left, meanwhile):
    for s in range(n - 1):

        @pl.when((me < n - 1) & (me >= s))
        def _():
            make_right(s).start()

        @pl.when((me > 0) & (me + s < n))
        def _():
            make_left(s).start()

        if s == 0:
            meanwhile()

        @pl.when(me - 1 - s >= 0)
        def _():
            make_right(s, me - 1 - s).wait_recv()

        @pl.when(me + 1 + s < n)
        def _():
            make_left(s, me + 1 + s).wait_recv()

    for s in range(n - 1):

        @pl.when((me < n - 1) & (me >= s))
        def _():
            make_right(s).wait_send()

        @pl.when((me > 0) & (me + s < n))
        def _():
            make_left(s).wait_send()


def pairs_of(n, me):
    half = n // 2
    parity, pair = me % 2, me // 2
    partner = me + 1 - 2 * parity
    ahead = [2 * ((pair + k) % half) + parity for k in range(1, half)]
    behind = [2 * ((pair + half - k) % half) + parity for k in range(1, half)]
    return half, parity, pair, partner, ahead, behind


def gather_dp_kernel(
    n, n_ctx, place_ref, doc_ref, freq_ref, x_ref, cos_ref, sin_ref, row_ref, col_ref, o_ref,
    local, sr, rr, sl, rl,
):
    me, ctx = lax.axis_index("dp"), lax.axis_index("ctx")

    def here(d):
        return (d, ctx)

    greet([here((me + 1) % n), here((me + n - 1) % n)])
    own = pltpu.make_async_copy(x_ref, o_ref.at[me], local)
    own.start()

    def right(s, block=None):
        b = me - s if block is None else block
        return remote(x_ref if s == 0 else o_ref.at[b], o_ref.at[b], sr.at[s], rr.at[s], here(me + 1))

    def left(s, block=None):
        b = me + s if block is None else block
        return remote(x_ref if s == 0 else o_ref.at[b], o_ref.at[b], sl.at[s], rl.at[s], here(me - 1))

    def tables():
        length = cos_ref.shape[0] // n_ctx
        head = cos_ref.shape[1]
        sign = jnp.where(lax.broadcasted_iota(jnp.int32, (length, head), 1) < head // 2, -1.0, 1.0)
        row_ref[...] = jnp.zeros_like(row_ref)
        row_ref[1:2, :] = doc_ref[...].astype(F32)
        for c in range(n_ctx):
            rows = slice(c * length, (c + 1) * length)
            base = place_ref[c] * length
            angles = (base + lax.broadcasted_iota(jnp.int32, (length, head), 0)).astype(F32) * freq_ref[...]
            cos_ref[rows, :] = jnp.cos(angles)
            sin_ref[rows, :] = jnp.sin(angles) * sign
            row_ref[0:1, rows] = (base + lax.broadcasted_iota(jnp.int32, (1, length), 1)).astype(F32)
        col_ref[...] = jnp.transpose(row_ref[...])

    line_steps(n, me, right, left, tables)
    own.wait()


def gather_dp(x, places, docs, number):
    n, n_ctx = lax.axis_size("dp"), lax.axis_size("ctx")
    seq = docs.shape[1]
    half = np.arange(HD // 2, dtype=np.float64) * 2.0 / HD
    freqs = np.tile(THETA**-half, 2)[None].astype(np.float32)
    *tables, out = pl.pallas_call(
        functools.partial(gather_dp_kernel, n, n_ctx),
        out_shape=(
            jax.ShapeDtypeStruct((seq, HD), F32),
            jax.ShapeDtypeStruct((seq, HD), F32),
            jax.ShapeDtypeStruct((8, seq), F32),
            jax.ShapeDtypeStruct((seq, 8), F32),
            jax.ShapeDtypeStruct((n,) + x.shape, x.dtype),
        ),
        in_specs=[pl.BlockSpec(memory_space=pltpu.SMEM), VMEM, VMEM, ANY],
        out_specs=(VMEM,) * 4 + (ANY,),
        scratch_shapes=[pltpu.SemaphoreType.DMA] + [pltpu.SemaphoreType.DMA((n - 1,))] * 4,
        compiler_params=params_of(number),
        cost_estimate=cost(60),
        name="gather_dp",
    )(places, docs, jnp.asarray(freqs), x)
    return out.reshape((n * x.shape[0],) + x.shape[1:]), tables


def group_of(n_dp, n, dp, me):
    pair, parity = me // 2, me % 2
    return 2 * n_dp, 2 * dp + parity, lambda j: (j // 2, 2 * pair + j % 2)


def greet_all(n_dp, n, dp, me):
    partner = me + 1 - 2 * (me % 2)
    others = [(dp + k) % n_dp for k in range(1, n_dp)]
    greet([(dp, (me + k) % n) for k in range(1, n)] + [(d, c) for d in others for c in (me, partner)])


def across(mine, k, count):
    if count & (count - 1):
        return (mine + k) % count, (mine + count - k) % count
    bit, other = 1, mine
    while bit < count:
        if k & bit:
            other = other + bit - 2 * bit * ((other // bit) % 2)
        bit *= 2
    return other, other


def swap(src, dst, send, recv, count, mine, place):
    sends, receives = [], []
    for k in range(1, count):
        to, source = across(mine, k, count)
        sends.append(remote(src.at[to], dst.at[mine], send.at[k - 1], recv.at[k - 1], place(to)))
        receives.append(
            remote(src.at[mine], dst.at[source], send.at[k - 1], recv.at[k - 1], place(source))
        )
    for copy in sends:
        copy.start()
    return sends, receives


def tiles(total, tile, body):
    tile = min(total, tile)

    @pl.loop(0, total // tile)
    def _(j):
        body(pl.ds(pl.multiple_of(j * tile, tile), tile))


def reduce_ctx(n, dp, me, a_ref, w_ref, cols, o_ref, sa, ra, sb, rb, s1, r1, s2, r2, before=None):
    half, parity, pair, partner, ahead, behind = pairs_of(n, me)
    length, width = o_ref.shape

    def rows(block):
        return pl.ds(pl.multiple_of(block * length, length), length)

    first, second = [], []
    for k in range(half):
        target = (pair + k + 1) % half
        if before is not None:
            before(target, k == 0)

        def give(part):
            value = dot_t(a_ref[rows(2 * target + 1 - parity), :], w_ref[part, cols])
            sa[k, :, part] = value.astype(BF)

        tiles(width, 512, give)
        copy = remote(sa.at[k], ra.at[k], s1.at[k], r1.at[k], (dp, partner))
        copy.start()
        first.append(copy)
        copy.wait_recv()

        def keep(part):
            value = dot_t(a_ref[rows(2 * target + parity), :], w_ref[part, cols])
            value = value + ra[k, :, part].astype(F32)
            if k < half - 1:
                sb[k, :, part] = value.astype(BF)
            else:
                o_ref[:, part] = value

        tiles(width, 512, keep)
        if k < half - 1:
            copy = remote(sb.at[k], rb.at[k], s2.at[k], r2.at[k], (dp, 2 * target + parity))
            copy.start()
            second.append(copy)
    for k in range(half - 1):
        second[k].wait_recv()
        o_ref[...] += rb[k].astype(F32)
    return first + second


def load_rows(hbm, vmem, sems):
    half, n_dp, rows, _ = hbm.shape
    copies = []
    for d in range(n_dp):
        for p in range(half):
            part = pl.ds((d * half + p) * rows, rows)
            copies.append(pltpu.make_async_copy(hbm.at[p, d], vmem.at[part, :], sems.at[d * half + p]))
    for copy in copies:
        copy.start()
    return copies


def gather_group(n, dp, me, all_ref, length, sr, rr, sl, rl, sf, rf, process):
    parity = me % 2
    partner = me + 1 - 2 * parity

    def block(b, side):
        start = (2 * b + side) * length
        return all_ref.at[pl.ds(pl.multiple_of(start, length), length), :]

    def right(s, b):
        return remote(block(b, parity), block(b, parity), sr.at[s], rr.at[s], (dp + 1, me))

    def left(s, b):
        return remote(block(b, parity), block(b, parity), sl.at[s], rl.at[s], (dp - 1, me))

    def aside(b):
        return remote(block(b, parity), block(b, parity), sf.at[b], rf.at[b], (dp, partner))

    def from_aside(b):
        return remote(block(b, 1 - parity), block(b, 1 - parity), sf.at[b], rf.at[b], (dp, partner))

    for s in range(n):
        if s == 0:
            aside(dp).start()
        else:

            @pl.when(dp >= s)
            def _():
                right(s - 1, dp - s).wait_recv()

            @pl.when(dp + s < n)
            def _():
                left(s - 1, dp + s).wait_recv()

        @pl.when((dp < n - 1) & (dp >= s))
        def _():
            right(s, dp - s).start()

        @pl.when((dp > 0) & (dp + s < n))
        def _():
            left(s, dp + s).start()

        if s == 0:
            from_aside(dp).wait_recv()
            process(dp, True)
        else:

            @pl.when(dp >= s)
            def _():
                aside(dp - s).start()

            @pl.when(dp + s < n)
            def _():
                aside(dp + s).start()

            below = jnp.where(dp >= s, 1, 0)
            above = jnp.where(dp + s < n, 1, 0)

            @pl.loop(0, below + above)
            def _(j):
                b = jnp.where(j < below, dp - s, dp + s)
                from_aside(b).wait_recv()
                process(b, False)

    for s in range(n):

        @pl.when((dp < n - 1) & (dp >= s))
        def _():
            right(s, dp - s).wait_send()

        @pl.when((dp > 0) & (dp + s < n))
        def _():
            left(s, dp + s).wait_send()

        aside(s).wait_send()


def gather_sems(n_dp):
    return [pltpu.SemaphoreType.DMA((n_dp,))] * 6


def line_sum(n, dp, me, make, val, o_ref, buf, send, recv, sync, between=None):
    def move(way, d):
        to = jnp.where(way == 1, dp + 1, dp - 1)
        return remote(buf.at[way, d], buf.at[way, d], send.at[way, d], recv.at[way, d], (to, me))

    def steps(body):
        for j in range(1, n):

            @pl.loop(0, 2)
            def _(phase):
                way = jnp.where(2 * dp < n, 1 - phase, phase)
                d = jnp.where(way == 1, n - j, j - 1)
                first = jnp.where(way == 1, 0, n - 1)
                ahead = jnp.where(way == 1, d - dp, dp - d)

                @pl.when(ahead > 0)
                def _():
                    body(way, d, dp == first)

    def begin(way, d, starts):
        make(d, val.at[d])

        @pl.when(starts)
        def _():
            def put(part):
                buf[way, d, part, :] = val[d, part, :].astype(BF)

            tiles(val.shape[1], 32, put)
            move(way, d).start()

    def follow(way, d, starts):
        @pl.when(jnp.logical_not(starts))
        def _():
            move(way, d).wait_recv()

            def add(part):
                buf[way, d, part, :] = (val[d, part, :] + buf[way, d, part, :].astype(F32)).astype(BF)

            tiles(val.shape[1], 32, add)
            move(way, d).start()

    steps(begin)
    make(dp, o_ref)
    steps(follow)
    if between is not None:
        between()
    for way, first in ((1, 0), (0, n - 1)):

        @pl.when(dp != first)
        def _():
            move(way, dp).wait_recv()

            def add(part):
                o_ref[part, :] += buf[way, dp, part, :].astype(F32)

            tiles(val.shape[1], 32, add)

    sync()
    steps(lambda way, d, starts: move(way, d).wait_send())


def line_scratch(n_dp, length, width):
    return [
        pltpu.VMEM((n_dp, length, width), F32),
        pltpu.VMEM((2, n_dp, length, width), BF),
        pltpu.SemaphoreType.DMA((2, n_dp)),
        pltpu.SemaphoreType.DMA((2, n_dp)),
    ]


def part_of_pair(dp, me, a_ref, w_ref, length, sa, ra, s1, r1):
    parity = me % 2
    partner = me + 1 - 2 * parity

    def make(d, out):
        def rows(side):
            return pl.ds(pl.multiple_of((2 * d + side) * length, length), length)

        def give(part):
            sa[d, :, part] = dot_t(a_ref[rows(1 - parity), :], w_ref[part, :]).astype(BF)

        tiles(out.shape[1], 512, give)
        copy = remote(sa.at[d], ra.at[d], s1.at[d], r1.at[d], (dp, partner))
        copy.start()

        def keep(part):
            out[:, part] = dot_t(a_ref[rows(parity), :], w_ref[part, :])

        tiles(out.shape[1], 512, keep)
        copy.wait_recv()

        def add(part):
            out[part, :] += ra[d, part, :].astype(F32)

        tiles(length, 32, add)

    def done(n):
        for d in range(n):
            remote(sa.at[d], ra.at[d], s1.at[d], r1.at[d], (dp, partner)).wait_send()

    return make, done


def pair_scratch(n_dp, length, width):
    return [pltpu.VMEM((n_dp, length, width), BF)] * 2 + [pltpu.SemaphoreType.DMA((n_dp,))] * 2


def greet_group(n_dp, dp, me):
    partner = me + 1 - 2 * (me % 2)
    greet([(dp, partner)] + [((dp + k) % n_dp, me) for k in range(1, n_dp)])


def ff_forward_kernel(
    n_dp, n, h_ref, up_ref, gain_ref, gu_hbm, d_hbm, wo_hbm,
    res_ref, dm_ref, gp_ref, all_out, pre_out, hid_out, d_out, wo_out,
    all_ref, pre_ref, hid_ref, d_ref, gu_ref, acc, sem_gu, sem_d, sem_out, sd, rd, so, ro, fo, go, *rest,
):
    gather, pair_refs, line_refs = rest[:6], rest[6:10], rest[10:]
    dp, me = lax.axis_index("dp"), lax.axis_index("ctx")
    length, width = h_ref.shape
    fh = hid_ref.shape[1]
    half, parity, pair, partner, ahead, behind = pairs_of(n, me)
    loads_gu = load_rows(gu_hbm, gu_ref, sem_gu)
    mine = pl.ds(pl.multiple_of((2 * dp + me % 2) * length, length), length)
    all_ref[mine, :] = h_ref[...].astype(BF)
    greet(
        [(dp, partner)]
        + [((dp + k) % n_dp, me) for k in range(1, n_dp)]
        + [(dp, a) for a in ahead]
    )
    tall = d_hbm.shape[1]

    def down(d, p):
        return d_ref.at[pl.ds(pl.multiple_of((d * half + p) * tall, tall), tall), :]

    loads_d = [pltpu.make_async_copy(d_hbm.at[d], down(d, pair), sem_d.at[d]) for d in range(n_dp)]
    spreads = [
        remote(d_hbm.at[d], down(d, pair), sd.at[k, d], rd.at[k, d], (dp, a))
        for k, a in enumerate(ahead)
        for d in range(n_dp)
    ]
    for copy in spreads + loads_d:
        copy.start()

    def process(b, own):
        rows = pl.ds(pl.multiple_of(2 * b * length, 2 * length), 2 * length)
        if own:
            for copy in loads_gu:
                copy.wait()

        def hidden(part):
            second = pl.ds(pl.multiple_of(fh + part.start, part.size), part.size)
            gate = dot(all_ref[rows, :], gu_ref[:, part])
            upper = dot(all_ref[rows, :], gu_ref[:, second])
            pre_ref[rows, part] = gate
            pre_ref[rows, second] = upper
            hid_ref[rows, part] = (gate * jax.nn.sigmoid(gate) * upper).astype(BF)

        tiles(fh, 256, hidden)

    gather_group(n_dp, dp, me, all_ref, length, *gather, process)
    for copy in loads_d:
        copy.wait()
    for k, b in enumerate(behind):
        for d in range(n_dp):
            remote(d_hbm.at[d], down(d, b // 2), sd.at[k, d], rd.at[k, d], (dp, b)).wait_recv()

    outs = [
        pltpu.make_async_copy(ref, out, sem_out.at[i])
        for i, (ref, out) in enumerate(
            ((all_ref, all_out), (pre_ref, pre_out), (hid_ref, hid_out), (d_ref, d_out))
        )
    ]
    outs.append(pltpu.make_async_copy(wo_hbm, wo_out.at[me], sem_out.at[4]))
    spreads_wo = [
        remote(wo_hbm, wo_out.at[me], so.at[k], ro.at[k], (dp, a)) for k, a in enumerate(ahead + [partner])
    ]
    for copy in outs + spreads_wo:
        copy.start()
    make, done = part_of_pair(dp, me, hid_ref, d_ref, length, *pair_refs)

    gp_ref[...] = jnp.zeros_like(gp_ref)

    def finish(rows):
        out, up, gain = acc[rows, :], up_ref[rows, :].astype(F32), gain_ref[...]
        scale = rms_scale(out)
        res_ref[rows, :] = (h_ref[rows, :] + out * scale * gain).astype(BF)
        gp_ref[...] += jnp.sum(up * out * scale, axis=0, keepdims=True)
        dm_ref[rows, :] = norm_back(up * gain, out, scale).astype(BF)

    forwards = []

    def last():
        for k, b in enumerate(behind):
            remote(wo_hbm, wo_out.at[b], so.at[k], ro.at[k], (dp, b)).wait_recv()
            forward = remote(wo_out.at[b], wo_out.at[b], fo.at[k], go.at[k], (dp, partner))
            forward.start()
            forwards.append(forward)
        tiles(length, 16, finish)

    line_sum(n_dp, dp, me, make, line_refs[0], acc, *line_refs[1:], last)
    done(n_dp)
    spreads_wo[-1].wait_recv()
    for copy in forwards:
        copy.wait_recv()
    for copy in spreads + spreads_wo + forwards:
        copy.wait_send()
    for copy in outs:
        copy.wait()


def ff_forward(h1, up, gain, w_gu, w_d, w_o, number):
    n_dp, n = lax.axis_size("dp"), lax.axis_size("ctx")
    (length, width), fh = h1.shape, w_d.shape[2]
    tokens = 2 * n_dp * length
    half = n // 2
    low = jax.ShapeDtypeStruct((length, width), BF)
    return pl.pallas_call(
        functools.partial(ff_forward_kernel, n_dp, n),
        out_shape=(
            low,
            low,
            jax.ShapeDtypeStruct((1, width), F32),
            jax.ShapeDtypeStruct((tokens, width), BF),
            jax.ShapeDtypeStruct((tokens, 2 * fh), F32),
            jax.ShapeDtypeStruct((tokens, fh), BF),
            jax.ShapeDtypeStruct((width, fh), BF),
            jax.ShapeDtypeStruct((n,) + w_o.shape, BF),
        ),
        in_specs=[VMEM] * 3 + [ANY] * 3,
        out_specs=(VMEM,) * 3 + (ANY,) * 5,
        scratch_shapes=[
            pltpu.VMEM((tokens, width), BF),
            pltpu.VMEM((tokens, 2 * fh), F32),
            pltpu.VMEM((tokens, fh), BF),
            pltpu.VMEM((width, fh), BF),
            pltpu.VMEM((width, 2 * fh), BF),
            pltpu.VMEM((length, width), F32),
            pltpu.SemaphoreType.DMA((half * n_dp,)),
            pltpu.SemaphoreType.DMA((n_dp,)),
            pltpu.SemaphoreType.DMA((5,)),
            pltpu.SemaphoreType.DMA((half - 1, n_dp)),
            pltpu.SemaphoreType.DMA((half - 1, n_dp)),
            pltpu.SemaphoreType.DMA((half,)),
            pltpu.SemaphoreType.DMA((half,)),
            pltpu.SemaphoreType.DMA((half - 1,)),
            pltpu.SemaphoreType.DMA((half - 1,)),
        ]
        + gather_sems(n_dp)
        + pair_scratch(n_dp, length, width)
        + line_scratch(n_dp, length, width),
        compiler_params=params_of(number),
        cost_estimate=cost(90),
        name="ff_forward",
    )(h1, up, gain, w_gu, w_d, w_o)


def store_rows(n_dp, value_of, out):
    half, _, rows, _ = out.shape

    @pl.loop(0, n_dp * half)
    def _(r):
        out[r % half, r // half] = value_of(pl.ds(pl.multiple_of(r * rows, rows), rows)).astype(BF)


def ff_back_kernel(
    n_dp, dm_ref, hid_ref, d_hbm, pre_hbm, dgu_out, gd_out,
    dgu_ref, gd_ref, sem_out, all_ref, d_ref, pre_ref, acc, sem_d, sem_p, *gather,
):
    dp, me = lax.axis_index("dp"), lax.axis_index("ctx")
    length, width = dm_ref.shape
    fh = d_ref.shape[1]
    load = pltpu.make_async_copy(d_hbm, d_ref, sem_d)
    load.start()

    def rows_of(b):
        return pl.ds(pl.multiple_of(2 * b * length, 2 * length), 2 * length)

    def load_pre(b):
        return pltpu.make_async_copy(pre_hbm.at[rows_of(b), :], pre_ref.at[rows_of(b), :], sem_p.at[b])

    for k in range(n_dp):
        load_pre((dp + k) % n_dp).start()
    mine = pl.ds(pl.multiple_of((2 * dp + me % 2) * length, length), length)
    all_ref[mine, :] = dm_ref[...]
    greet_group(n_dp, dp, me)

    def process(b, own):
        rows = rows_of(b)
        if own:
            load.wait()
        load_pre(b).wait()

        def hidden(part):
            second = pl.ds(pl.multiple_of(fh + part.start, part.size), part.size)
            back = dot(all_ref[rows, :], d_ref[:, part])
            gate, upper = pre_ref[rows, part], pre_ref[rows, second]
            sig = jax.nn.sigmoid(gate)
            dgu_ref[rows, part] = (back * upper * sig * (1.0 + gate * (1.0 - sig))).astype(BF)
            dgu_ref[rows, second] = (back * gate * sig).astype(BF)

        tiles(fh, 256, hidden)

        def product(part):
            value = t_dot(all_ref[rows, part], hid_ref[rows, :])
            acc[part, :] = value if own else acc[part, :] + value

        tiles(width, 256, product)

    gather_group(n_dp, dp, me, all_ref, length, *gather, process)
    outs = loads_of(((dgu_ref, dgu_out),), sem_out)
    store_rows(n_dp, lambda part: acc[part, :], gd_ref)
    for copy in outs + loads_of(((gd_ref, gd_out),), sem_out, 1):
        copy.wait()


def ff_back(dm, hid, w_d, pre, rows, number):
    n_dp, half = lax.axis_size("dp"), lax.axis_size("ctx") // 2
    (length, width), fh = dm.shape, w_d.shape[1]
    tokens = 2 * n_dp * length
    return pl.pallas_call(
        functools.partial(ff_back_kernel, n_dp),
        out_shape=(
            jax.ShapeDtypeStruct((tokens, 2 * fh), BF),
            jax.ShapeDtypeStruct((half, n_dp, 2 * rows, fh), BF),
        ),
        in_specs=[VMEM, VMEM, ANY, ANY],
        out_specs=(ANY,) * 2,
        scratch_shapes=[
            pltpu.VMEM((tokens, 2 * fh), BF),
            pltpu.VMEM((half, n_dp, 2 * rows, fh), BF),
            pltpu.SemaphoreType.DMA((2,)),
            pltpu.VMEM((tokens, width), BF),
            pltpu.VMEM((width, fh), BF),
            pltpu.VMEM((tokens, 2 * fh), F32),
            pltpu.VMEM((width, fh), F32),
            pltpu.SemaphoreType.DMA,
            pltpu.SemaphoreType.DMA((n_dp,)),
        ]
        + gather_sems(n_dp),
        compiler_params=params_of(number),
        cost_estimate=cost(45),
        name="ff_back",
    )(dm, hid, w_d, pre)


def ff_scatter_kernel(
    n_dp, n, dgu_hbm, gu_hbm, all_hbm, dh_ref, gg_out, gv_out,
    gg_ref, gv_ref, dgu_ref, gu_ref, all_ref, acc, sem_gu, sem_all, sem_out, *rest,
):
    dp, me = lax.axis_index("dp"), lax.axis_index("ctx")
    length, width = dh_ref.shape
    pair_refs, line_refs = rest[:4], rest[4:]
    half, parity, pair, partner, ahead, behind = pairs_of(n, me)
    _, _, rows, fh = gg_ref.shape
    loads = load_rows(gu_hbm, gu_ref, sem_gu) + loads_of(((dgu_hbm, dgu_ref),), sem_out, 2)
    load = pltpu.make_async_copy(all_hbm, all_ref, sem_all)
    load.start()
    greet_group(n_dp, dp, me)
    for copy in loads:
        copy.wait()

    make, done = part_of_pair(dp, me, dgu_ref, gu_ref, length, *pair_refs)
    load.wait()
    tall = acc.shape[0]

    def grads():
        @pl.loop(0, width // tall)
        def _(j):
            acc[...] = t_dot(all_ref[:, pl.ds(pl.multiple_of(j * tall, tall), tall)], dgu_ref[...])
            for s in range(tall // rows):
                r = j * (tall // rows) + s
                part = slice(s * rows, (s + 1) * rows)
                gg_ref[r % half, r // half] = acc[part, :fh].astype(BF)
                gv_ref[r % half, r // half] = acc[part, fh:].astype(BF)

    val, *line = line_refs
    line_sum(n_dp, dp, me, make, val, dh_ref, *line, lambda: None, grads)
    done(n_dp)
    outs = [
        pltpu.make_async_copy(ref, out, sem_out.at[i])
        for i, (ref, out) in enumerate(((gg_ref, gg_out), (gv_ref, gv_out)))
    ]
    for copy in outs:
        copy.start()
    for copy in outs:
        copy.wait()


def ff_scatter(dgu, w_gu, h1_all, length, number):
    n_dp, n = lax.axis_size("dp"), lax.axis_size("ctx")
    width = h1_all.shape[1]
    grad = jax.ShapeDtypeStruct(w_gu.shape[:3] + (w_gu.shape[3] // 2,), BF)
    return pl.pallas_call(
        functools.partial(ff_scatter_kernel, n_dp, n),
        out_shape=(
            jax.ShapeDtypeStruct((length, width), F32),
            grad,
            grad,
        ),
        in_specs=[ANY] * 3,
        out_specs=(VMEM,) + (ANY,) * 2,
        scratch_shapes=[
            pltpu.VMEM(grad.shape, BF),
            pltpu.VMEM(grad.shape, BF),
            pltpu.VMEM(dgu.shape, BF),
            pltpu.VMEM((width, w_gu.shape[3]), BF),
            pltpu.VMEM(h1_all.shape, BF),
            pltpu.VMEM((256, w_gu.shape[3]), F32),
            pltpu.SemaphoreType.DMA((w_gu.shape[0] * n_dp,)),
            pltpu.SemaphoreType.DMA,
            pltpu.SemaphoreType.DMA((3,)),
        ]
        + pair_scratch(n_dp, length, width)
        + line_scratch(n_dp, length, width),
        compiler_params=params_of(number),
        cost_estimate=cost(50),
        name="ff_scatter",
    )(dgu, w_gu, h1_all)


def start_kernel(
    n_dp, n, p_hbm, x_ref, h_ref, o_ref, p_ref, y_ref, d_ref,
    p_all, g_ref, w_ref, v_ref, local, sg, rg, sa, ra, sv, rv, ss, rs, fs, fr,
):
    dp, me = lax.axis_index("dp"), lax.axis_index("ctx")
    half, parity, pair, partner, ahead, behind = pairs_of(n, me)
    count, mine, place = group_of(n_dp, n, dp, me)
    columns = p_all.shape[2]
    fh, hc = d_ref.shape[2], v_ref.shape[2]
    loads = [
        pltpu.make_async_copy(
            p_hbm.at[:, pl.ds(part * columns, columns)], p_all.at[part], local.at[part]
        )
        for part in range(4)
    ]
    for part in (1, 2, 0, 3):
        loads[part].start()
    greet_all(n_dp, n, dp, me)
    gathers = [
        remote(x_ref, y_ref.at[me], ss.at[k], rs.at[k], (dp, a))
        for k, a in enumerate(ahead + [partner])
    ]
    own_x = pltpu.make_async_copy(x_ref, y_ref.at[me], local.at[4])
    for copy in gathers + [own_x]:
        copy.start()
    for part in (1, 2):
        loads[part].wait()
        for j in range(count):
            g_ref[j, :, (part - 1) * fh : part * fh] = p_all[part, :, j * fh : (j + 1) * fh].astype(BF)
    sends, receives = swap(g_ref, h_ref, sg, rg, count, mine, place)
    loads[0].wait()
    for c in range(n):
        for matrix in range(4):
            start = (matrix * n + c) * hc
            value = p_all[0, :, start : start + hc].astype(BF)
            if matrix < 3:
                w_ref[c, :, matrix * hc : (matrix + 1) * hc] = value
            else:
                v_ref[c] = value
    for src, dst, send, recv in ((w_ref, o_ref, sa, ra), (v_ref, p_ref, sv, rv)):
        more, waits = swap(src, dst, send, recv, n, me, lambda c: (dp, c))
        sends += more
        receives += waits
    owns = [
        pltpu.make_async_copy(g_ref.at[mine], h_ref.at[mine], local.at[5]),
        pltpu.make_async_copy(w_ref.at[me], o_ref.at[me], local.at[6]),
        pltpu.make_async_copy(v_ref.at[me], p_ref.at[me], local.at[7]),
    ]
    for copy in owns:
        copy.start()
    loads[3].wait()
    for j in range(count):
        d_ref[j] = p_all[3, :, j * fh : (j + 1) * fh].astype(BF)
    forwards = []
    for k, b in enumerate(behind):
        remote(x_ref, y_ref.at[b], ss.at[k], rs.at[k], (dp, b)).wait_recv()
        forward = remote(y_ref.at[b], y_ref.at[b], fs.at[k], fr.at[k], (dp, partner))
        forward.start()
        forwards.append(forward)
    gathers[-1].wait_recv()
    for copy in receives:
        copy.wait_recv()
    for forward in forwards:
        forward.wait()
    for copy in sends + gathers:
        copy.wait_send()
    for copy in owns + [own_x]:
        copy.wait()


def start(params, x, number):
    n_dp, n = lax.axis_size("dp"), lax.axis_size("ctx")
    half, count = n // 2, 2 * n_dp
    (rows, columns), width = params.shape, x.shape[1]
    fh, hc = columns // 4 // count, width // n
    dma = pltpu.SemaphoreType.DMA
    g, w, v = (count, rows, 2 * fh), (n, rows, 3 * hc), (n, rows, hc)
    g_out, w_out, v_out, x_all, d_out = pl.pallas_call(
        functools.partial(start_kernel, n_dp, n),
        out_shape=(
            jax.ShapeDtypeStruct(g, BF),
            jax.ShapeDtypeStruct(w, BF),
            jax.ShapeDtypeStruct(v, BF),
            jax.ShapeDtypeStruct((n,) + x.shape, x.dtype),
            jax.ShapeDtypeStruct((count, rows, fh), BF),
        ),
        in_specs=[ANY] * 2,
        out_specs=(ANY,) * 4 + (VMEM,),
        scratch_shapes=[
            pltpu.VMEM((4, rows, columns // 4), F32),
            pltpu.VMEM(g, BF),
            pltpu.VMEM(w, BF),
            pltpu.VMEM(v, BF),
            dma((8,)),
        ]
        + [dma((count - 1,))] * 2
        + [dma((n - 1,))] * 4
        + [dma((half,))] * 2
        + [dma((half - 1,))] * 2,
        compiler_params=params_of(number),
        cost_estimate=cost(45),
        name="start",
    )(params, x)
    return g_out, w_out, v_out, x_all.reshape(-1, width), d_out


def collect_kernel(
    n_dp, n, g_ref, h_ref, a_hbm, w_hbm, b_hbm, o_ref, h_out, y_ref,
    a_ref, w_ref, b_ref, sem_in, sum_ref, acc, pa, qa, pb, qb, local, s1, r1, s2, r2, sh, rh, *line_refs,
):
    dp, me = lax.axis_index("dp"), lax.axis_index("ctx")
    loads = loads_of(((a_hbm, a_ref), (w_hbm, w_ref), (b_hbm, b_ref)), sem_in)
    tall = acc.shape[0]
    count, index, place = group_of(n_dp, n, dp, me)
    greet_all(n_dp, n, dp, me)

    def make(d, out):
        def put(part):
            rows = pl.ds(pl.multiple_of(d * tall + part.start, part.size), part.size)
            out[part, :] = g_ref[rows, :].astype(F32)

        tiles(tall, 64, put)

    cols = slice(0, a_ref.shape[1])
    stay = pltpu.make_async_copy(h_ref.at[index], h_out.at[index], local)
    stay.start()
    later = []

    def between():
        later.extend(swap(h_ref, h_out, sh, rh, count, index, place))
        for copy in loads:
            copy.wait()
        later.append(reduce_ctx(n, dp, me, a_ref, w_ref, cols, sum_ref, pa, qa, pb, qb, s1, r1, s2, r2))

    def last():
        def put(part):
            o_ref[part, :] = acc[part, :].astype(BF)

        tiles(tall, 64, put)

    def join(part):
        y_ref[part, :] = (sum_ref[part, :] + b_ref[part, :]).astype(BF)

    val, *line = line_refs
    line_sum(n_dp, dp, me, make, val, acc, *line, last, between)
    swaps, receives, sums = later
    tiles(y_ref.shape[0], 32, join)
    for copy in receives:
        copy.wait_recv()
    stay.wait()
    for copy in swaps + sums:
        copy.wait_send()


def collect(g, h, a, w, b, number):
    n_dp, n = lax.axis_size("dp"), lax.axis_size("ctx")
    tall, width = g.shape[0] // n_dp, g.shape[1]
    half, length, features = n // 2, a.shape[0] // n, w.shape[0]
    dma = pltpu.SemaphoreType.DMA
    return pl.pallas_call(
        functools.partial(collect_kernel, n_dp, n),
        out_shape=(
            jax.ShapeDtypeStruct((tall, width), BF),
            jax.ShapeDtypeStruct(h.shape, BF),
            jax.ShapeDtypeStruct((length, features), BF),
        ),
        in_specs=[VMEM] + [ANY] * 4,
        out_specs=(VMEM, ANY, VMEM),
        scratch_shapes=[
            pltpu.VMEM(a.shape, BF),
            pltpu.VMEM(w.shape, BF),
            pltpu.VMEM(b.shape, F32),
            dma((3,)),
            pltpu.VMEM((length, features), F32),
            pltpu.VMEM((tall, width), F32),
            pltpu.VMEM((half, length, features), BF),
            pltpu.VMEM((half, length, features), BF),
            pltpu.VMEM((half - 1, length, features), BF),
            pltpu.VMEM((half - 1, length, features), BF),
            dma,
            dma((half,)),
            dma((half,)),
            dma((half - 1,)),
            dma((half - 1,)),
            dma((2 * n_dp - 1,)),
            dma((2 * n_dp - 1,)),
        ]
        + line_scratch(n_dp, tall, width),
        compiler_params=params_of(number),
        cost_estimate=cost(70),
        name="collect",
    )(g, h, a, w, b)


def total_kernel(
    n_dp, n, qk_ref, wv_ref, wo_ref, u_ref, gg_ref, gd_ref, qk_gain, attn_gain, ff_gain, p_hbm, m_hbm, v_hbm,
    ga_ref, gu_ref, o_ref, p_out, m_out, v_out,
    sb, mine, buf, part, all_parts, square, buf_s, part_s, all_s, local, sx, rx, sh, rh,
    ss, rs, st, rt, s1, r1, s2, r2, sem_copy,
):
    dp, me = lax.axis_index("dp"), lax.axis_index("ctx")
    hc = wv_ref.shape[2]
    count, index, place = group_of(n_dp, n, dp, me)
    greet_all(n_dp, n, dp, me)
    swaps, receives = swap(u_ref, gu_ref, sh, rh, count, index, place)
    stay = pltpu.make_async_copy(u_ref.at[index], gu_ref.at[index], local)
    stay.start()
    moves = [
        pltpu.make_async_copy(source, target, sem_copy.at[i])
        for i, (source, target) in enumerate(((p_hbm, p_out), (m_hbm, m_out), (v_hbm, v_out)))
    ]
    for copy in moves:
        copy.start()
    sb[:, :, : 2 * hc] = qk_ref[...]
    sb[:, :, 2 * hc : 3 * hc] = wv_ref[...]
    more, waits = swap(sb, ga_ref, sx, rx, n, me, lambda c: (dp, c))
    ga_ref[me] = sb[me]

    def squares(ref):
        acc = jnp.zeros((ref.shape[1], ref.shape[2]), F32)
        for i in range(ref.shape[0]):
            block = ref[i].astype(F32)
            acc += block * block
        return jnp.sum(jnp.sum(acc, axis=0, keepdims=True), axis=1, keepdims=True)

    copies = swaps + more

    def sum_all(value, rows, along, columns, send, recv, send_dp, recv_dp):
        for k in range(1, n):
            copy = remote(value, rows.at[me], send.at[k - 1], recv.at[k - 1], (dp, (me + k) % n))
            copy.start()
            copies.append(copy)
        rows[me] = value[...]
        for k in range(1, n):
            source = (me + n - k) % n
            remote(value, rows.at[source], send.at[k - 1], recv.at[k - 1], (dp, source)).wait_recv()
        acc = rows[0]
        for j in range(1, n):
            acc = acc + rows[j]
        along[...] = acc
        columns[dp] = acc
        for k in range(1, n_dp):
            to = (dp + k) % n_dp
            copy = remote(along, columns.at[dp], send_dp.at[k - 1], recv_dp.at[k - 1], (to, me))
            copy.start()
            copies.append(copy)
        for k in range(1, n_dp):
            source = (dp + n_dp - k) % n_dp
            remote(along, columns.at[source], send_dp.at[k - 1], recv_dp.at[k - 1], (source, me)).wait_recv()
        acc = columns[0]
        for j in range(1, n_dp):
            acc = acc + columns[j]
        return acc

    mine[...] = jnp.zeros_like(mine)
    mine[0:2, pl.ds(pl.multiple_of(me * hc, hc), hc)] = qk_gain[...]
    mine[2:3, :] = attn_gain[...]
    mine[3:4, :] = ff_gain[...]
    o_ref[...] = sum_all(mine, buf, part, all_parts, ss, rs, st, rt)
    total = squares(gg_ref) + squares(gd_ref) + squares(wo_ref)
    for copy in waits:
        copy.wait_recv()
    total += squares(ga_ref)
    for copy in receives:
        copy.wait_recv()
    stay.wait()
    total += squares(gu_ref)
    square[...] = jnp.broadcast_to(total, square.shape)
    total = sum_all(square, buf_s, part_s, all_s, s1, r1, s2, r2)
    o_ref[4:5, :] = jnp.broadcast_to(total[0:1, 0:1], (1, o_ref.shape[1]))
    for copy in copies:
        copy.wait_send()
    for copy in moves:
        copy.wait()


def total_over(qk, wv, wo, u, gg, gd, qk_gain, attn_gain, ff_gain, masters, number):
    n_dp, n = lax.axis_size("dp"), lax.axis_size("ctx")
    rows, hc = qk.shape[0] // n, wv.shape[1]
    shape = (8, attn_gain.shape[1])
    dma = pltpu.SemaphoreType.DMA
    return pl.pallas_call(
        functools.partial(total_kernel, n_dp, n),
        out_shape=(
            jax.ShapeDtypeStruct((n, rows, 3 * hc), BF),
            jax.ShapeDtypeStruct(u.shape, BF),
            jax.ShapeDtypeStruct(shape, F32),
            *[jax.ShapeDtypeStruct(a.shape, F32) for a in masters],
        ),
        in_specs=[VMEM] * 3 + [ANY] + [VMEM] * 5 + [HBM] * 3,
        out_specs=(VMEM,) * 3 + (ANY,) * 3,
        scratch_shapes=[
            pltpu.VMEM((n, rows, 3 * hc), BF),
            pltpu.VMEM(shape, F32),
            pltpu.VMEM((n,) + shape, F32),
            pltpu.VMEM(shape, F32),
            pltpu.VMEM((n_dp,) + shape, F32),
            pltpu.VMEM((8, 128), F32),
            pltpu.VMEM((n, 8, 128), F32),
            pltpu.VMEM((8, 128), F32),
            pltpu.VMEM((n_dp, 8, 128), F32),
            dma,
            dma((n - 1,)),
            dma((n - 1,)),
            dma((2 * n_dp - 1,)),
            dma((2 * n_dp - 1,)),
            dma((n - 1,)),
            dma((n - 1,)),
            dma((n_dp - 1,)),
            dma((n_dp - 1,)),
            dma((n - 1,)),
            dma((n - 1,)),
            dma((n_dp - 1,)),
            dma((n_dp - 1,)),
            dma((3,)),
        ],
        compiler_params=params_of(number, 19),
        cost_estimate=cost(35),
        name="total",
    )(
        qk.reshape(n, rows, 2 * hc),
        wv.reshape(n, rows, hc),
        wo[None],
        u,
        gg,
        gd,
        qk_gain,
        attn_gain,
        ff_gain,
        *masters,
    )


def adam_kernel(
    sum_ref, gp_ref, gm_ref, gv_ref, p_ref, m_ref, v_ref, ga_ref, go_ref, gg_ref, gu_ref, gd_ref,
    norm_ref, gp_out, gm_out, gv_out, po_ref, mo_ref, vo_ref, g_ref, factor_ref,
):
    part = pl.program_id(0)

    @pl.when((part == 0) & (pl.program_id(1) == 0))
    def _():
        gain = sum_ref[0:4, :]
        squares = jnp.sum(jnp.sum(gain * gain, axis=0, keepdims=True), axis=1, keepdims=True)
        norm = jnp.sqrt(sum_ref[4:5, 0:1] + squares)
        norm_ref[...] = norm
        factor = CLIP / (norm + 1e-06)
        factor_ref[...] = jnp.broadcast_to(factor, factor_ref.shape)
        new = adam_update(gp_ref[...], gm_ref[...], gv_ref[...], gain * factor, GAIN_RATE, 0.0)
        gp_out[...], gm_out[...], gv_out[...] = new

    n, _, three = ga_ref.shape
    hc = three // 3
    fs = gd_ref.shape[2]

    @pl.when(part == 0)
    def _():
        g_ref[:, 3 * n * hc :] = go_ref[...].astype(F32)
        for matrix in range(3):
            for c in range(n):
                start = (matrix * n + c) * hc
                g_ref[:, start : start + hc] = ga_ref[c, :, matrix * hc : (matrix + 1) * hc].astype(F32)

    for index, ref in ((1, gg_ref), (2, gu_ref), (3, gd_ref)):

        @pl.when(part == index)
        def _():
            for d in range(ref.shape[0]):
                g_ref[:, d * fs : (d + 1) * fs] = ref[d].astype(F32)

    clipped = g_ref[...] * factor_ref[0:1, 0:1]
    new_m = BETA1 * m_ref[...] + (1.0 - BETA1) * clipped
    new_v = BETA2 * v_ref[...] + (1.0 - BETA2) * (clipped * clipped)
    hat = new_v * (1.0 / (1.0 - BETA2**STEP))
    root = hat * lax.rsqrt(jnp.maximum(hat, 1e-36)) + ADAM_EPS
    change = (new_m * (RATE / (1.0 - BETA1**STEP))) * pl.reciprocal(root, approx=True)
    po_ref[...] = p_ref[...] * (1.0 - RATE * DECAY) - change
    mo_ref[...] = new_m
    vo_ref[...] = new_v


def adam(sums, gains, gains_first, gains_second, params, first, second, ga, go, gg, gu, gd):
    rows, columns = params.shape
    n, n_dp, fs = ga.shape[0], gd.shape[0], gd.shape[2]
    block = min(rows, 32)
    steps = rows // block
    wide = pl.BlockSpec((block, columns // 4), lambda i, r: (r, i))
    small = pl.BlockSpec(gains.shape, lambda i, r: (0, 0))
    return pl.pallas_call(
        adam_kernel,
        grid=(4, steps),
        out_shape=(jax.ShapeDtypeStruct((1, 1), F32),)
        + (jax.ShapeDtypeStruct(gains.shape, F32),) * 3
        + (jax.ShapeDtypeStruct(params.shape, F32),) * 3,
        in_specs=[
            pl.BlockSpec(sums.shape, lambda i, r: (0, 0)),
            small,
            small,
            small,
            wide,
            wide,
            wide,
            pl.BlockSpec((n, block, ga.shape[2]), lambda i, r: (0, jnp.where(i == 0, r, steps - 1), 0)),
            pl.BlockSpec((block, go.shape[1]), lambda i, r: (jnp.where(i == 0, r, steps - 1), 0)),
            *[
                pl.BlockSpec(
                    (n_dp, block, fs),
                    lambda i, r, part=part: (
                        0,
                        jnp.where(i < part, 0, jnp.where(i == part, r, steps - 1)),
                        0,
                    ),
                )
                for part in (1, 2, 3)
            ],
        ],
        out_specs=(pl.BlockSpec((1, 1), lambda i, r: (0, 0)),) + (small,) * 3 + (wide,) * 3,
        scratch_shapes=[pltpu.VMEM((block, columns // 4), F32), pltpu.VMEM((8, 128), F32)],
        compiler_params=pltpu.CompilerParams(vmem_limit_bytes=22 * 1024 * 1024),
        name="adam",
    )(sums, gains, gains_first, gains_second, params, first, second, ga, go, gg, gu, gd)


def row_sums(value, row):
    pick = lax.broadcasted_iota(jnp.int32, (8, value.shape[1]), 0) == row
    return lax.dot_general(
        pick.astype(F32),
        value,
        (((1,), (1,)), ((), ())),
        preferred_element_type=F32,
        precision=lax.Precision.HIGHEST,
    )


def exchange(n, dp, me, buf, ss, rs):
    copies = []
    for k in range(1, n):
        copy = remote(buf.at[me], buf.at[me], ss.at[k - 1], rs.at[k - 1], (dp, (me + k) % n))
        copy.start()
        copies.append(copy)
    for k in range(1, n):
        source = (me + n - k) % n
        remote(buf.at[me], buf.at[source], ss.at[k - 1], rs.at[k - 1], (dp, source)).wait_recv()
    total = buf[0]
    for j in range(1, n):
        total = total + buf[j]
    for copy in copies:
        copy.wait_send()
    return total


def turn(value, cos, sine):
    return value * cos + pltpu.roll(value, HD // 2, 1) * sine


def mask_of(rows, info_col, info_row):
    pos_i, doc_i = info_col[rows, 0:1], info_col[rows, 1:2]
    return (info_row[1:2, :] == doc_i) & (info_row[0:1, :] <= pos_i)


def attend_kernel(
    n_dp, n, x_hbm, w_hbm, wo_ref, d_ref, t_ref, norm_ref, gain_ref, cos_ref, sin_ref, col_ref, row_ref,
    y_ref, h_ref, q_out, k_out, v_out, o_ref, pre_out, scale_ref, lse_ref, wo_all, d_out,
    buf, pa, qa, pb, qb, ss, rs, s1, r1, s2, r2, sw, rw, sd, rd, local,
    x_ref, w_ref, q_ref, k_ref, v_ref, pre_ref, sem_in, sem_out,
):
    dp, me = lax.axis_index("dp"), lax.axis_index("ctx")
    loads = loads_of(((x_hbm, x_ref), (w_hbm, w_ref)), sem_in)
    seq, width = x_ref.shape
    hc = o_ref.shape[1]
    block = min(seq, 256)
    count, mine, place = group_of(n_dp, n, dp, me)
    greet_all(n_dp, n, dp, me)
    piece = wo_ref.shape[0]

    def part_of(d):
        return wo_all.at[pl.ds(pl.multiple_of(d * piece, piece), piece), :]

    owns = [
        pltpu.make_async_copy(wo_ref, part_of(dp), local.at[0]),
        pltpu.make_async_copy(d_ref.at[mine], d_out.at[mine], local.at[1]),
    ]
    behind_wo = [
        remote(wo_ref, part_of(dp), sw.at[k - 1], rw.at[k - 1], (across(dp, k, n_dp)[0], me))
        for k in range(1, n_dp)
    ]
    for copy in behind_wo + owns:
        copy.start()
    behind_d, receives = swap(d_ref, d_out, sd, rd, count, mine, place)

    for copy in loads:
        copy.wait()

    @pl.loop(0, seq // block)
    def _(i):
        rows = pl.ds(pl.multiple_of(i * block, block), block)
        value = dot(x_ref[rows, :], w_ref[...])
        pre_ref[rows, :] = value[:, : 2 * hc]
        v_ref[rows, :] = value[:, 2 * hc :].astype(BF)
        squares = value[:, : 2 * hc] * value[:, : 2 * hc]
        buf[me, :, rows] = row_sums(squares[:, :hc], 0) + row_sums(squares[:, hc:], 1)

    scale_ref[...] = jnp.transpose(lax.rsqrt(exchange(n, dp, me, buf, ss, rs) / width + EPS))

    @pl.loop(0, seq // block)
    def _(i):
        rows = pl.ds(pl.multiple_of(i * block, block), block)
        cos, sine = cos_ref[rows, :], sin_ref[rows, :]
        for which, ref, factor in ((0, q_ref, HD ** (-0.5)), (1, k_ref, 1.0)):
            scale = scale_ref[rows, which : which + 1]
            for start in range(0, hc, HD):
                part = slice(start, start + HD)
                value = pre_ref[rows, which * hc + start : which * hc + start + HD] * scale
                ref[rows, part] = (
                    turn(value * gain_ref[which : which + 1, part], cos, sine) * factor
                ).astype(BF)

    def attention(pair, first):
        size = 2 * (seq // n)
        rows = pl.ds(pl.multiple_of(pair * size, size), size)
        visible = mask_of(rows, col_ref, row_ref)
        for head in range(hc // HD):
            part = slice(head * HD, (head + 1) * HD)
            scores = jnp.where(visible, dot_t(q_ref[rows, part], k_ref[:, part]), -jnp.inf)
            top = jnp.max(scores, axis=1, keepdims=True)
            weights = jnp.exp(scores - top)
            total = jnp.sum(weights, axis=1, keepdims=True)
            o_ref[rows, part] = (dot(weights.astype(BF), v_ref[:, part]) / total).astype(BF)
            lse_ref[rows, head : head + 1] = top + jnp.log(total)
        if first:
            owns[0].wait()
            for k in range(1, n_dp):
                _, source = across(dp, k, n_dp)
                remote(wo_ref, part_of(source), sw.at[k - 1], rw.at[k - 1], (source, me)).wait_recv()

    outs = loads_of(((pre_ref, pre_out), (q_ref, q_out), (k_ref, k_out), (v_ref, v_out)), sem_out)
    cols = slice(0, hc)
    sums = reduce_ctx(
        n, dp, me, o_ref, wo_all, cols, y_ref, pa, qa, pb, qb, s1, r1, s2, r2, before=attention
    )

    def finish(rows):
        branch = y_ref[rows, :]
        h_ref[rows, :] = t_ref[rows, :].astype(F32) + branch * rms_scale(branch) * norm_ref[...]

    tiles(y_ref.shape[0], 16, finish)
    for copy in receives:
        copy.wait_recv()
    for copy in sums + behind_wo + behind_d:
        copy.wait_send()
    for copy in outs + owns[1:]:
        copy.wait()


def attend(x_all, w, wo, d, tokens, norm, gain, cos, sine, info_col, info_row, number):
    n_dp, n = lax.axis_size("dp"), lax.axis_size("ctx")
    seq, width = x_all.shape
    half, length, hc = n // 2, seq // n, w.shape[1] // 3
    dma = pltpu.SemaphoreType.DMA
    low = jax.ShapeDtypeStruct((seq, hc), BF)
    return pl.pallas_call(
        functools.partial(attend_kernel, n_dp, n),
        out_shape=(
            jax.ShapeDtypeStruct((length, width), F32),
            jax.ShapeDtypeStruct((length, width), F32),
            low,
            low,
            low,
            low,
            jax.ShapeDtypeStruct((seq, 2 * hc), F32),
            jax.ShapeDtypeStruct((seq, 8), F32),
            jax.ShapeDtypeStruct((seq, 8), F32),
            jax.ShapeDtypeStruct((width, hc), BF),
            jax.ShapeDtypeStruct(d.shape, BF),
        ),
        in_specs=[ANY] * 4 + [VMEM] * 7,
        out_specs=(VMEM,) * 2 + (ANY,) * 3 + (VMEM, ANY) + (VMEM,) * 3 + (ANY,),
        scratch_shapes=[
            pltpu.VMEM((n, 8, seq), F32),
            pltpu.VMEM((half, length, width), BF),
            pltpu.VMEM((half, length, width), BF),
            pltpu.VMEM((half - 1, length, width), BF),
            pltpu.VMEM((half - 1, length, width), BF),
            dma((n - 1,)),
            dma((n - 1,)),
            dma((half,)),
            dma((half,)),
            dma((half - 1,)),
            dma((half - 1,)),
            dma((n_dp - 1,)),
            dma((n_dp - 1,)),
            dma((2 * n_dp - 1,)),
            dma((2 * n_dp - 1,)),
            dma((2,)),
            pltpu.VMEM(x_all.shape, BF),
            pltpu.VMEM(w.shape, BF),
            *[pltpu.VMEM((seq, hc), BF)] * 3,
            pltpu.VMEM((seq, 2 * hc), F32),
            dma((2,)),
            dma((4,)),
        ],
        compiler_params=params_of(number),
        cost_estimate=cost(60),
        name="attend",
    )(x_all, w, wo, d, tokens, norm, gain, cos, sine, info_col, info_row)


def slab_give(n_dp, dp, me, g_ref, co_ref, sw, rw):
    tall = co_ref.shape[1]
    gives = []
    for k in range(1, n_dp):
        to, _ = across(dp, k, n_dp)
        part = pl.ds(pl.multiple_of(to * tall, tall), tall)
        copy = remote(g_ref.at[part, :], co_ref.at[k - 1], sw.at[k - 1], rw.at[k - 1], (to, me))
        copy.start()
        gives.append(copy)
    return gives


def slab_sum(dp, gives, g_ref, co_ref, out_ref):
    tall = co_ref.shape[1]
    total = g_ref[pl.ds(pl.multiple_of(dp * tall, tall), tall), :].astype(F32)
    for k, copy in enumerate(gives):
        copy.wait_recv()
        total = total + co_ref[k].astype(F32)
    out_ref[...] = total.astype(BF)


def greet_wide_group(n_dp, dp, me):
    partner = me + 1 - 2 * (me % 2)
    others = [(dp + k) % n_dp for k in range(1, n_dp)]
    greet([(dp, partner)] + [(d, c) for d in others for c in (me, partner)])


def attend_back_kernel(
    n_dp, n, sum_ref, up_ref, branch_ref, norm_ref, wo_hbm, h_ref, o_hbm, col_ref, row_ref, q_hbm, k_hbm, v_hbm, lse_ref,
    x_hbm, gain_ref, cos_hbm, sin_hbm, pre_hbm, scale_ref,
    dh_ref, gp_ref, d_ref, gain_out, g_ref, wv_ref, wo_ref, h_out,
    q_ref, k_ref, v_ref, cos_ref, sin_ref, x_ref, pre_ref, wall_ref, db_ref, mix_ref, give_ref, e_ref, do_ref, o_ref, dq_ref, dk_ref, dv_ref, mean_ref, buf, go_ref, co_ref, gv_ref, cv_ref,
    sh, rh, local, sw, rw, sv, rv, ss, rs, sc, rc, sx, rx,
):
    dp, me = lax.axis_index("dp"), lax.axis_index("ctx")
    seq, hc = q_ref.shape
    load_wo = pltpu.make_async_copy(wo_hbm, wall_ref, local.at[2])
    load_wo.start()
    later = [
        pltpu.make_async_copy(src, dst, local.at[i])
        for i, (src, dst) in enumerate(((x_hbm, x_ref), (pre_hbm, pre_ref)), 4)
    ]
    load = pltpu.make_async_copy(o_hbm, o_ref, local.at[1])
    load.start()
    tables = ((q_hbm, q_ref), (k_hbm, k_ref), (v_hbm, v_ref), (cos_hbm, cos_ref), (sin_hbm, sin_ref))
    loads = loads_of(tables, local, 6)
    length, width = dh_ref.shape
    block = min(seq, 256)
    count, index, place = group_of(n_dp, n, dp, me)
    greet_all(n_dp, n, dp, me)
    swaps, receives = swap(h_ref, h_out, sh, rh, count, index, place)
    stay = pltpu.make_async_copy(h_ref.at[index], h_out.at[index], local.at[0])
    stay.start()

    gp_ref[...] = jnp.zeros_like(gp_ref)

    def finish(rows):
        grad, branch = sum_ref[rows, :] + up_ref[rows, :].astype(F32), branch_ref[rows, :]
        scale = rms_scale(branch)
        dh_ref[rows, :] = grad
        gp_ref[...] += jnp.sum(grad * branch * scale, axis=0, keepdims=True)
        db_ref[rows, :] = norm_back(grad * norm_ref[...], branch, scale).astype(BF)

    tiles(length, 16, finish)
    load_wo.wait()

    def mine(c):
        return pl.ds(pl.multiple_of(c * length, length), length)

    def send(k):
        to = (me + k) % n
        return remote(give_ref.at[to], do_ref.at[mine(me), :], sx.at[k - 1], rx.at[k - 1], (dp, to))

    def receive(k):
        source = (me + n - k) % n
        return remote(give_ref.at[me], do_ref.at[mine(source), :], sx.at[k - 1], rx.at[k - 1], (dp, source))

    share = width // n
    own = share // n_dp
    for c in range(n):
        for d in range(n_dp):
            start, source = c * share + d * own, (d * n + c) * own
            mix_ref[:, start : start + own] = db_ref[:, source : source + own]

    def share_of(c):
        return mix_ref.at[:, pl.ds(pl.multiple_of(c * share, share), share)]

    def send_share(k):
        to = (me + k) % n
        return remote(share_of(to), e_ref.at[mine(me), :], sc.at[k - 1], rc.at[k - 1], (dp, to))

    def receive_share(k):
        source = (me + n - k) % n
        return remote(share_of(me), e_ref.at[mine(source), :], sc.at[k - 1], rc.at[k - 1], (dp, source))

    stay_share = pltpu.make_async_copy(share_of(me), e_ref.at[mine(me), :], local.at[3])
    stay_share.start()

    @pl.loop(1, n)
    def _(k):
        to = (me + k) % n
        send_share(k).start()
        give_ref[to] = dot(db_ref[...], wall_ref[to]).astype(BF)
        send(k).start()

    do_ref[mine(me), :] = dot(db_ref[...], wall_ref[me]).astype(BF)
    for k in range(1, n):
        receive(k).wait_recv()
        receive_share(k).wait_recv()
    for k in range(1, n):
        send(k).wait_send()
        send_share(k).wait_send()
    stay_share.wait()
    load.wait()
    for copy in later:
        copy.start()

    @pl.loop(0, n)
    def _(c):
        go_ref[:, pl.ds(pl.multiple_of(c * hc, hc), hc)] = t_dot(e_ref[...], o_ref[c]).astype(BF)

    gives = slab_give(n_dp, dp, me, go_ref, co_ref, sw, rw)
    dk_ref[...] = jnp.zeros_like(dk_ref)
    dv_ref[...] = jnp.zeros_like(dv_ref)

    def attention(i):
        rows = pl.ds(pl.multiple_of(i * block, block), block)
        visible = mask_of(rows, col_ref, row_ref)
        for head in range(hc // HD):
            part = slice(head * HD, (head + 1) * HD)
            query, key, value, back = q_ref[rows, part], k_ref[:, part], v_ref[:, part], do_ref[rows, part]
            scores = jnp.where(visible, dot_t(query, key), -jnp.inf)
            probs = jnp.exp(scores - lse_ref[rows, head : head + 1])
            d_probs = dot_t(back, value)
            delta = jnp.sum(probs * d_probs, axis=1, keepdims=True)
            d_scores = (probs * (d_probs - delta)).astype(BF)
            dq_ref[rows, part] = dot(d_scores, key)
            dk_ref[:, part] += t_dot(d_scores, query)
            dv_ref[:, part] += t_dot(probs.astype(BF), back)

    for copy in loads:
        copy.wait()
    pl.loop(0, seq // block)(attention)

    for copy in later:
        copy.wait()
    d_ref[:, 2 * hc :] = dv_ref[...].astype(BF)

    def values(part):
        gv_ref[part, :] = t_dot(x_ref[:, part], d_ref[:, 2 * hc :]).astype(BF)

    tiles(width, 256, values)
    gives_v = slab_give(n_dp, dp, me, gv_ref, cv_ref, sv, rv)
    gain_out[...] = jnp.zeros_like(gain_out)

    @pl.loop(0, seq // block)
    def _(i):
        rows = pl.ds(pl.multiple_of(i * block, block), block)
        cos, sine = cos_ref[rows, :], sin_ref[rows, :]
        sums = jnp.zeros((8, block), F32)
        for which, ref, factor in ((0, dq_ref, HD ** (-0.5)), (1, dk_ref, 1.0)):
            scale = scale_ref[rows, which : which + 1]
            for start in range(0, hc, HD):
                part = slice(start, start + HD)
                pre = pre_ref[rows, which * hc + start : which * hc + start + HD]
                value = turn(ref[rows, part] * factor, cos, -sine)
                gain_out[which : which + 1, part] += jnp.sum(value * pre * scale, axis=0, keepdims=True)
                value = value * gain_ref[which : which + 1, part]
                ref[rows, part] = value
                sums += row_sums(value * pre, which)
        buf[me, :, rows] = sums

    mean_ref[...] = jnp.transpose(exchange(n, dp, me, buf, ss, rs) / width)

    @pl.loop(0, seq // block)
    def _(i):
        rows = pl.ds(pl.multiple_of(i * block, block), block)
        for which, ref in ((0, dq_ref), (1, dk_ref)):
            scale = scale_ref[rows, which : which + 1]
            mean = mean_ref[rows, which : which + 1]
            cols = slice(which * hc, (which + 1) * hc)
            value = scale * (ref[rows, :] - pre_ref[rows, cols] * (scale * scale * mean))
            d_ref[rows, cols] = value.astype(BF)

    def product(part):
        g_ref[part, :] = t_dot(x_ref[:, part], d_ref[:, : 2 * hc]).astype(BF)

    tiles(width, 256, product)
    slab_sum(dp, gives, go_ref, co_ref, wo_ref)
    slab_sum(dp, gives_v, gv_ref, cv_ref, wv_ref)
    for copy in receives:
        copy.wait_recv()
    for copy in swaps + gives + gives_v:
        copy.wait_send()
    stay.wait()


def attend_back(sums, up, branch, norm, wo_all, h, o_all, info_col, info_row, q, k, v, lse, x, gain, cos, sine, pre, scale, number):
    n_dp, n = lax.axis_size("dp"), lax.axis_size("ctx")
    (seq, hc), (length, width) = q.shape, branch.shape
    share = width // n
    dma = pltpu.SemaphoreType.DMA
    return pl.pallas_call(
        functools.partial(attend_back_kernel, n_dp, n),
        out_shape=(
            jax.ShapeDtypeStruct((length, width), F32),
            jax.ShapeDtypeStruct((1, width), F32),
            jax.ShapeDtypeStruct((seq, 3 * hc), BF),
            jax.ShapeDtypeStruct((2, hc), F32),
            jax.ShapeDtypeStruct((width, 2 * hc), BF),
            jax.ShapeDtypeStruct((width // n_dp, hc), BF),
            jax.ShapeDtypeStruct((share // n_dp, n * hc), BF),
            jax.ShapeDtypeStruct(h.shape, BF),
        ),
        in_specs=[VMEM] * 4 + [ANY] * 3 + [VMEM] * 2 + [ANY] * 3 + [VMEM, ANY, VMEM] + [ANY] * 3 + [VMEM],
        out_specs=(VMEM,) * 7 + (ANY,),
        scratch_shapes=[
            *[pltpu.VMEM((seq, hc), BF)] * 3,
            *[pltpu.VMEM(cos.shape, F32)] * 2,
            pltpu.VMEM(x.shape, BF),
            pltpu.VMEM(pre.shape, F32),
            pltpu.VMEM(wo_all.shape, BF),
            pltpu.VMEM((length, width), BF),
            pltpu.VMEM((length, width), BF),
            pltpu.VMEM((n, length, hc), BF),
            pltpu.VMEM((seq, share), BF),
            pltpu.VMEM((seq, hc), BF),
            pltpu.VMEM(o_all.shape, BF),
            pltpu.VMEM((seq, hc), F32),
            pltpu.VMEM((seq, hc), F32),
            pltpu.VMEM((seq, hc), F32),
            pltpu.VMEM((seq, 8), F32),
            pltpu.VMEM((n, 8, seq), F32),
            pltpu.VMEM((share, n * hc), BF),
            pltpu.VMEM((n_dp - 1, share // n_dp, n * hc), BF),
            pltpu.VMEM((width, hc), BF),
            pltpu.VMEM((n_dp - 1, width // n_dp, hc), BF),
            dma((2 * n_dp - 1,)),
            dma((2 * n_dp - 1,)),
            dma((11,)),
            dma((n_dp - 1,)),
            dma((n_dp - 1,)),
            dma((n_dp - 1,)),
            dma((n_dp - 1,)),
            dma((n - 1,)),
            dma((n - 1,)),
            dma((n - 1,)),
            dma((n - 1,)),
            dma((n - 1,)),
            dma((n - 1,)),
        ],
        compiler_params=params_of(number),
        cost_estimate=cost(75),
        name="attend_back",
    )(sums, up, branch, norm, wo_all, h, o_all, info_col, info_row, q, k, v, lse, x, gain, cos, sine, pre, scale)


def shards(
    inputs,
    cotangent,
    documents,
    block_place,
    params,
    first_moment,
    second_moment,
    gains,
    gains_first,
    gains_second,
):
    tokens = inputs[0]
    upstream = cotangent[0]
    length, width = tokens.shape
    n_ctx = lax.axis_size("ctx")
    n_dp = lax.axis_size("dp")
    me_ctx = lax.axis_index("ctx")
    seq = length * n_ctx
    rows = params.shape[0]
    ff = (params.shape[1] - 4 * width) // 3
    hc = width // n_ctx
    half, group = n_ctx // 2, 2 * n_dp
    fh = ff // group
    parities = [[2 * p + side for p in range(half)] for side in range(2)]

    def gather_pairs(w):
        w = lax.all_gather(
            w.reshape(group * rows, w.shape[2]), "ctx", axis=0, tiled=True, axis_index_groups=parities
        )
        return w.reshape(half, n_dp, 2 * rows, w.shape[1])

    def scatter_pairs(g):
        g = lax.psum_scatter(
            g.reshape(width, g.shape[3]),
            "ctx",
            scatter_dimension=0,
            tiled=True,
            axis_index_groups=parities,
        )
        return g.reshape(group, rows, g.shape[1])

    w_gu, w_qkv, w_o, x_all, w_d = start(params, tokens, 1)
    w_gu = gather_pairs(w_gu)
    w_qkv, (cos_tab, sine_tab, info_row, info_col) = gather_dp(
        w_qkv.reshape(n_ctx * rows, 3 * hc), block_place, documents, 2
    )
    my_gains = lax.dynamic_slice_in_dim(gains[:2], me_ctx * hc, hc, axis=1)
    tables = (my_gains, cos_tab, sine_tab, info_col, info_row)

    branch, hidden1, queries, keys, values, attn_low, qk_pre, scales, lse, w_o, w_d = attend(
        x_all, w_qkv, w_o.reshape(n_ctx * rows, hc), w_d, tokens, gains[2:3], *tables, 3
    )

    result, d_mlp, g_ff_part, h1_all, gate_up, inner, w_d, w_o = ff_forward(
        hidden1, upstream, gains[3:4], w_gu, w_d.reshape(n_dp, 2 * rows, fh), w_o, 4
    )
    attn_low, d_mlp = lax.optimization_barrier((attn_low, d_mlp))
    attn_all = lax.all_gather(attn_low, "ctx", axis=0)
    d_gu, d_grad = ff_back(d_mlp, inner, w_d, gate_up, rows, 5)
    d_grad = scatter_pairs(d_grad)
    d_sums, g_grad, u_grad = ff_scatter(d_gu, w_gu, h1_all, length, 6)
    g_grad, u_grad = scatter_pairs(g_grad), scatter_pairs(u_grad)

    d_h1, g_attn_part, d_qkv, d_gain, qk_grad, wv_grad, wo_grad, d_grad = attend_back(
        d_sums, upstream, branch, gains[2:3], w_o, d_grad, attn_all, info_col, info_row, queries, keys, values, lse,
        x_all, my_gains, cos_tab, sine_tab, qk_pre, scales, 8,
    )
    qk_grad, g_grad, d_input = collect(qk_grad, g_grad, d_qkv, w_qkv, d_h1, 9)

    attn_grad, u_grad, sums, *masters = total_over(
        qk_grad, wv_grad, wo_grad, u_grad, g_grad, d_grad, d_gain, g_attn_part, g_ff_part,
        (params, first_moment, second_moment), 11,
    )
    grad_norm, new_gains, new_gains_first, new_gains_second, new_params, new_first, new_second = adam(
        sums, gains, gains_first, gains_second, *masters,
        attn_grad, wo_grad, g_grad, u_grad, d_grad,
    )
    return (
        result[None],
        d_input[None],
        grad_norm.reshape(()),
        new_params,
        new_first,
        new_second,
        new_gains,
        new_gains_first,
        new_gains_second,
    )


def solution(mesh):
    split, whole = P("dp", "ctx", None), P(("dp", "ctx"), None)
    return jax.shard_map(
        shards,
        mesh=mesh,
        in_specs=(split, split, P("dp", None), P(), whole, whole, whole, P(), P(), P()),
        out_specs=(split, split, P(), whole, whole, whole, P(), P(), P()),
        check_vma=False,
    )
```

```python
import functools

import jax
import jax.numpy as jnp
import numpy as np
from jax import lax
from jax.experimental import pallas as pl
from jax.experimental.pallas import tpu as pltpu
from jax.sharding import PartitionSpec as P

HD = 128
STEP = 10
EPS = 1e-06
THETA = 500000.0
CLIP = 1.0
BETA1 = 0.9
BETA2 = 0.95
RATE = 0.03
GAIN_RATE = 0.8
DECAY = 0.1
ADAM_EPS = 1e-08
BF = jnp.bfloat16
F32 = jnp.float32
MESH = pl.DeviceIdType.MESH
ANY = pl.BlockSpec(memory_space=pl.ANY)
VMEM = pl.BlockSpec(memory_space=pltpu.VMEM)
HBM = pl.BlockSpec(memory_space=pltpu.HBM)


def rms_scale(values):
    return lax.rsqrt(jnp.mean(values * values, axis=-1, keepdims=True) + EPS)


def norm_back(upstream, source, scale):
    return scale * (
        upstream - source * scale * scale * jnp.mean(upstream * source, axis=-1, keepdims=True)
    )


def adam_update(weight, first_in, second_in, clipped, rate, decay):
    new_first = BETA1 * first_in + (1.0 - BETA1) * clipped
    new_second = BETA2 * second_in + (1.0 - BETA2) * clipped * clipped
    first_hat = new_first / (1.0 - BETA1**STEP)
    second_hat = new_second / (1.0 - BETA2**STEP)
    new_weight = weight - rate * (first_hat / (jnp.sqrt(second_hat) + ADAM_EPS) + decay * weight)
    return (new_weight, new_first, new_second)


def dot(a, b):
    return jnp.dot(a, b, preferred_element_type=F32)


def dot_t(a, b):
    return lax.dot_general(a, b, (((1,), (1,)), ((), ())), preferred_element_type=F32)


def t_dot(a, b):
    return lax.dot_general(a, b, (((0,), (0,)), ((), ())), preferred_element_type=F32)


def loads_of(pairs, sems, first=0):
    copies = [pltpu.make_async_copy(a, b, sems.at[first + i]) for i, (a, b) in enumerate(pairs)]
    for copy in copies:
        copy.start()
    return copies


def greet(peers):
    barrier = pltpu.get_barrier_semaphore()
    for peer in peers:
        pl.semaphore_signal(barrier, inc=1, device_id=peer, device_id_type=MESH)
    pl.semaphore_wait(barrier, len(peers))


def remote(src, dst, send, recv, peer):
    return pltpu.make_async_remote_copy(
        src_ref=src, dst_ref=dst, send_sem=send, recv_sem=recv, device_id=peer, device_id_type=MESH
    )


def cost(us):
    return pl.CostEstimate(flops=0, bytes_accessed=us * 3_600_000, transcendentals=0)


def params_of(number, vmem=62):
    return pltpu.CompilerParams(
        collective_id=number, has_side_effects=True, vmem_limit_bytes=vmem * 1024 * 1024
    )


def line_steps(n, me, make_right, make_left, meanwhile):
    for s in range(n - 1):

        @pl.when((me < n - 1) & (me >= s))
        def _():
            make_right(s).start()

        @pl.when((me > 0) & (me + s < n))
        def _():
            make_left(s).start()

        if s == 0:
            meanwhile()

        @pl.when(me - 1 - s >= 0)
        def _():
            make_right(s, me - 1 - s).wait_recv()

        @pl.when(me + 1 + s < n)
        def _():
            make_left(s, me + 1 + s).wait_recv()

    for s in range(n - 1):

        @pl.when((me < n - 1) & (me >= s))
        def _():
            make_right(s).wait_send()

        @pl.when((me > 0) & (me + s < n))
        def _():
            make_left(s).wait_send()


def pairs_of(n, me):
    half = n // 2
    parity, pair = me % 2, me // 2
    partner = me + 1 - 2 * parity
    ahead = [2 * ((pair + k) % half) + parity for k in range(1, half)]
    behind = [2 * ((pair + half - k) % half) + parity for k in range(1, half)]
    return half, parity, pair, partner, ahead, behind


def gather_dp_kernel(
    n, n_ctx, place_ref, doc_ref, freq_ref, x_ref, cos_out, sin_out, row_ref, col_ref, o_ref,
    cos_ref, sin_ref, sem_out, local, sr, rr, sl, rl,
):
    me, ctx = lax.axis_index("dp"), lax.axis_index("ctx")

    def here(d):
        return (d, ctx)

    greet([here((me + 1) % n), here((me + n - 1) % n)])
    own = pltpu.make_async_copy(x_ref, o_ref.at[me], local)
    own.start()

    def right(s, block=None):
        b = me - s if block is None else block
        return remote(x_ref if s == 0 else o_ref.at[b], o_ref.at[b], sr.at[s], rr.at[s], here(me + 1))

    def left(s, block=None):
        b = me + s if block is None else block
        return remote(x_ref if s == 0 else o_ref.at[b], o_ref.at[b], sl.at[s], rl.at[s], here(me - 1))

    outs = []

    def tables():
        length = cos_ref.shape[0] // n_ctx
        head = cos_ref.shape[1]
        sign = jnp.where(lax.broadcasted_iota(jnp.int32, (length, head), 1) < head // 2, -1.0, 1.0)
        row_ref[...] = jnp.zeros_like(row_ref)
        row_ref[1:2, :] = doc_ref[...].astype(F32)
        for c in range(n_ctx):
            rows = slice(c * length, (c + 1) * length)
            base = place_ref[c] * length
            angles = (base + lax.broadcasted_iota(jnp.int32, (length, head), 0)).astype(F32) * freq_ref[...]
            cos_ref[rows, :] = jnp.cos(angles)
            sin_ref[rows, :] = jnp.sin(angles) * sign
            row_ref[0:1, rows] = (base + lax.broadcasted_iota(jnp.int32, (1, length), 1)).astype(F32)
        col_ref[...] = jnp.transpose(row_ref[...])
        outs.extend(loads_of(((cos_ref, cos_out), (sin_ref, sin_out)), sem_out))

    line_steps(n, me, right, left, tables)
    for copy in outs + [own]:
        copy.wait()


def gather_dp(x, places, docs, number):
    n, n_ctx = lax.axis_size("dp"), lax.axis_size("ctx")
    seq = docs.shape[1]
    half = np.arange(HD // 2, dtype=np.float64) * 2.0 / HD
    freqs = np.tile(THETA**-half, 2)[None].astype(np.float32)
    *tables, out = pl.pallas_call(
        functools.partial(gather_dp_kernel, n, n_ctx),
        out_shape=(
            jax.ShapeDtypeStruct((seq, HD), F32),
            jax.ShapeDtypeStruct((seq, HD), F32),
            jax.ShapeDtypeStruct((8, seq), F32),
            jax.ShapeDtypeStruct((seq, 8), F32),
            jax.ShapeDtypeStruct((n,) + x.shape, x.dtype),
        ),
        in_specs=[pl.BlockSpec(memory_space=pltpu.SMEM), VMEM, VMEM, ANY],
        out_specs=(ANY,) * 2 + (VMEM,) * 2 + (ANY,),
        scratch_shapes=[pltpu.VMEM((seq, HD), F32)] * 2
        + [pltpu.SemaphoreType.DMA((2,))]
        + [pltpu.SemaphoreType.DMA] + [pltpu.SemaphoreType.DMA((n - 1,))] * 4,
        compiler_params=params_of(number),
        cost_estimate=cost(60),
        name="gather_dp",
    )(places, docs, jnp.asarray(freqs), x)
    return out.reshape((n * x.shape[0],) + x.shape[1:]), tables


def group_of(n_dp, n, dp, me):
    pair, parity = me // 2, me % 2
    return 2 * n_dp, 2 * dp + parity, lambda j: (j // 2, 2 * pair + j % 2)


def greet_all(n_dp, n, dp, me):
    partner = me + 1 - 2 * (me % 2)
    others = [(dp + k) % n_dp for k in range(1, n_dp)]
    greet([(dp, (me + k) % n) for k in range(1, n)] + [(d, c) for d in others for c in (me, partner)])


def across(mine, k, count):
    if count & (count - 1):
        return (mine + k) % count, (mine + count - k) % count
    bit, other = 1, mine
    while bit < count:
        if k & bit:
            other = other + bit - 2 * bit * ((other // bit) % 2)
        bit *= 2
    return other, other


def swap(src, dst, send, recv, count, mine, place):
    sends, receives = [], []
    for k in range(1, count):
        to, source = across(mine, k, count)
        sends.append(remote(src.at[to], dst.at[mine], send.at[k - 1], recv.at[k - 1], place(to)))
        receives.append(
            remote(src.at[mine], dst.at[source], send.at[k - 1], recv.at[k - 1], place(source))
        )
    for copy in sends:
        copy.start()
    return sends, receives


def tiles(total, tile, body):
    tile = min(total, tile)

    @pl.loop(0, total // tile)
    def _(j):
        body(pl.ds(pl.multiple_of(j * tile, tile), tile))


def reduce_ctx(n, dp, me, a_ref, w_ref, cols, o_ref, sa, ra, sb, rb, s1, r1, s2, r2, before=None):
    half, parity, pair, partner, ahead, behind = pairs_of(n, me)
    length, width = o_ref.shape

    def rows(block):
        return pl.ds(pl.multiple_of(block * length, length), length)

    first, second = [], []
    for k in range(half):
        target = (pair + k + 1) % half
        if before is not None:
            before(target, k == 0)

        def give(part):
            value = dot_t(a_ref[rows(2 * target + 1 - parity), :], w_ref[part, cols])
            sa[k, :, part] = value.astype(BF)

        tiles(width, 512, give)
        copy = remote(sa.at[k], ra.at[k], s1.at[k], r1.at[k], (dp, partner))
        copy.start()
        first.append(copy)
        copy.wait_recv()

        def keep(part):
            value = dot_t(a_ref[rows(2 * target + parity), :], w_ref[part, cols])
            value = value + ra[k, :, part].astype(F32)
            if k < half - 1:
                sb[k, :, part] = value.astype(BF)
            else:
                o_ref[:, part] = value

        tiles(width, 512, keep)
        if k < half - 1:
            copy = remote(sb.at[k], rb.at[k], s2.at[k], r2.at[k], (dp, 2 * target + parity))
            copy.start()
            second.append(copy)
    for k in range(half - 1):
        second[k].wait_recv()
        o_ref[...] += rb[k].astype(F32)
    return first + second


def load_rows(hbm, vmem, sems):
    half, n_dp, rows, _ = hbm.shape
    copies = []
    for d in range(n_dp):
        for p in range(half):
            part = pl.ds((d * half + p) * rows, rows)
            copies.append(pltpu.make_async_copy(hbm.at[p, d], vmem.at[part, :], sems.at[d * half + p]))
    for copy in copies:
        copy.start()
    return copies


def gather_group(n, dp, me, all_ref, length, sr, rr, sl, rl, sf, rf, process):
    parity = me % 2
    partner = me + 1 - 2 * parity

    def block(b, side):
        start = (2 * b + side) * length
        return all_ref.at[pl.ds(pl.multiple_of(start, length), length), :]

    def right(s, b):
        return remote(block(b, parity), block(b, parity), sr.at[s], rr.at[s], (dp + 1, me))

    def left(s, b):
        return remote(block(b, parity), block(b, parity), sl.at[s], rl.at[s], (dp - 1, me))

    def aside(b):
        return remote(block(b, parity), block(b, parity), sf.at[b], rf.at[b], (dp, partner))

    def from_aside(b):
        return remote(block(b, 1 - parity), block(b, 1 - parity), sf.at[b], rf.at[b], (dp, partner))

    for s in range(n):
        if s == 0:
            aside(dp).start()
        else:

            @pl.when(dp >= s)
            def _():
                right(s - 1, dp - s).wait_recv()

            @pl.when(dp + s < n)
            def _():
                left(s - 1, dp + s).wait_recv()

        @pl.when((dp < n - 1) & (dp >= s))
        def _():
            right(s, dp - s).start()

        @pl.when((dp > 0) & (dp + s < n))
        def _():
            left(s, dp + s).start()

        if s == 0:
            from_aside(dp).wait_recv()
            process(dp, True)
        else:

            @pl.when(dp >= s)
            def _():
                aside(dp - s).start()

            @pl.when(dp + s < n)
            def _():
                aside(dp + s).start()

            below = jnp.where(dp >= s, 1, 0)
            above = jnp.where(dp + s < n, 1, 0)

            @pl.loop(0, below + above)
            def _(j):
                b = jnp.where(j < below, dp - s, dp + s)
                from_aside(b).wait_recv()
                process(b, False)

    for s in range(n):

        @pl.when((dp < n - 1) & (dp >= s))
        def _():
            right(s, dp - s).wait_send()

        @pl.when((dp > 0) & (dp + s < n))
        def _():
            left(s, dp + s).wait_send()

        aside(s).wait_send()


def gather_sems(n_dp):
    return [pltpu.SemaphoreType.DMA((n_dp,))] * 6


def line_sum(n, dp, me, make, val, o_ref, buf, send, recv, sync, between=None):
    def move(way, d):
        to = jnp.where(way == 1, dp + 1, dp - 1)
        return remote(buf.at[way, d], buf.at[way, d], send.at[way, d], recv.at[way, d], (to, me))

    def steps(body):
        for j in range(1, n):

            @pl.loop(0, 2)
            def _(phase):
                way = jnp.where(2 * dp < n, 1 - phase, phase)
                d = jnp.where(way == 1, n - j, j - 1)
                first = jnp.where(way == 1, 0, n - 1)
                ahead = jnp.where(way == 1, d - dp, dp - d)

                @pl.when(ahead > 0)
                def _():
                    body(way, d, dp == first)

    def begin(way, d, starts):
        make(d, val.at[d])

        @pl.when(starts)
        def _():
            def put(part):
                buf[way, d, part, :] = val[d, part, :].astype(BF)

            tiles(val.shape[1], 32, put)
            move(way, d).start()

    def follow(way, d, starts):
        @pl.when(jnp.logical_not(starts))
        def _():
            move(way, d).wait_recv()

            def add(part):
                buf[way, d, part, :] = (val[d, part, :] + buf[way, d, part, :].astype(F32)).astype(BF)

            tiles(val.shape[1], 32, add)
            move(way, d).start()

    steps(begin)
    make(dp, o_ref)
    steps(follow)
    if between is not None:
        between()
    for way, first in ((1, 0), (0, n - 1)):

        @pl.when(dp != first)
        def _():
            move(way, dp).wait_recv()

            def add(part):
                o_ref[part, :] += buf[way, dp, part, :].astype(F32)

            tiles(val.shape[1], 32, add)

    sync()
    steps(lambda way, d, starts: move(way, d).wait_send())


def line_scratch(n_dp, length, width):
    return [
        pltpu.VMEM((n_dp, length, width), F32),
        pltpu.VMEM((2, n_dp, length, width), BF),
        pltpu.SemaphoreType.DMA((2, n_dp)),
        pltpu.SemaphoreType.DMA((2, n_dp)),
    ]


def part_of_pair(dp, me, a_ref, w_ref, length, sa, ra, s1, r1):
    parity = me % 2
    partner = me + 1 - 2 * parity

    def make(d, out):
        def rows(side):
            return pl.ds(pl.multiple_of((2 * d + side) * length, length), length)

        def give(part):
            sa[d, :, part] = dot_t(a_ref[rows(1 - parity), :], w_ref[part, :]).astype(BF)

        tiles(out.shape[1], 512, give)
        copy = remote(sa.at[d], ra.at[d], s1.at[d], r1.at[d], (dp, partner))
        copy.start()

        def keep(part):
            out[:, part] = dot_t(a_ref[rows(parity), :], w_ref[part, :])

        tiles(out.shape[1], 512, keep)
        copy.wait_recv()

        def add(part):
            out[part, :] += ra[d, part, :].astype(F32)

        tiles(length, 32, add)

    def done(n):
        for d in range(n):
            remote(sa.at[d], ra.at[d], s1.at[d], r1.at[d], (dp, partner)).wait_send()

    return make, done


def pair_scratch(n_dp, length, width):
    return [pltpu.VMEM((n_dp, length, width), BF)] * 2 + [pltpu.SemaphoreType.DMA((n_dp,))] * 2


def greet_group(n_dp, dp, me):
    partner = me + 1 - 2 * (me % 2)
    greet([(dp, partner)] + [((dp + k) % n_dp, me) for k in range(1, n_dp)])


def ff_forward_kernel(
    n_dp, n, h_ref, up_ref, gain_ref, gu_hbm, d_hbm, wo_hbm,
    res_ref, dm_ref, gp_ref, all_out, pre_out, hid_out, d_out, wo_out,
    all_ref, pre_ref, hid_ref, d_ref, gu_ref, acc, sem_gu, sem_d, sem_out, sd, rd, so, ro, fo, go, *rest,
):
    gather, pair_refs, line_refs = rest[:6], rest[6:10], rest[10:]
    dp, me = lax.axis_index("dp"), lax.axis_index("ctx")
    length, width = h_ref.shape
    fh = hid_ref.shape[1]
    half, parity, pair, partner, ahead, behind = pairs_of(n, me)
    loads_gu = load_rows(gu_hbm, gu_ref, sem_gu)
    mine = pl.ds(pl.multiple_of((2 * dp + me % 2) * length, length), length)
    all_ref[mine, :] = h_ref[...].astype(BF)
    greet(
        [(dp, partner)]
        + [((dp + k) % n_dp, me) for k in range(1, n_dp)]
        + [(dp, a) for a in ahead]
    )
    tall = d_hbm.shape[1]

    def down(d, p):
        return d_ref.at[pl.ds(pl.multiple_of((d * half + p) * tall, tall), tall), :]

    loads_d = [pltpu.make_async_copy(d_hbm.at[d], down(d, pair), sem_d.at[d]) for d in range(n_dp)]
    spreads = [
        remote(d_hbm.at[d], down(d, pair), sd.at[k, d], rd.at[k, d], (dp, a))
        for k, a in enumerate(ahead)
        for d in range(n_dp)
    ]
    for copy in spreads + loads_d:
        copy.start()

    def process(b, own):
        rows = pl.ds(pl.multiple_of(2 * b * length, 2 * length), 2 * length)
        if own:
            for copy in loads_gu:
                copy.wait()

        def hidden(part):
            second = pl.ds(pl.multiple_of(fh + part.start, part.size), part.size)
            gate = dot(all_ref[rows, :], gu_ref[:, part])
            upper = dot(all_ref[rows, :], gu_ref[:, second])
            pre_ref[rows, part] = gate
            pre_ref[rows, second] = upper
            hid_ref[rows, part] = (gate * jax.nn.sigmoid(gate) * upper).astype(BF)

        tiles(fh, 256, hidden)

    gather_group(n_dp, dp, me, all_ref, length, *gather, process)
    for copy in loads_d:
        copy.wait()
    for k, b in enumerate(behind):
        for d in range(n_dp):
            remote(d_hbm.at[d], down(d, b // 2), sd.at[k, d], rd.at[k, d], (dp, b)).wait_recv()

    outs = [
        pltpu.make_async_copy(ref, out, sem_out.at[i])
        for i, (ref, out) in enumerate(
            ((all_ref, all_out), (pre_ref, pre_out), (hid_ref, hid_out), (d_ref, d_out))
        )
    ]
    outs.append(pltpu.make_async_copy(wo_hbm, wo_out.at[me], sem_out.at[4]))
    spreads_wo = [
        remote(wo_hbm, wo_out.at[me], so.at[k], ro.at[k], (dp, a)) for k, a in enumerate(ahead + [partner])
    ]
    for copy in outs + spreads_wo:
        copy.start()
    make, done = part_of_pair(dp, me, hid_ref, d_ref, length, *pair_refs)

    gp_ref[...] = jnp.zeros_like(gp_ref)

    def finish(rows):
        out, up, gain = acc[rows, :], up_ref[rows, :].astype(F32), gain_ref[...]
        scale = rms_scale(out)
        res_ref[rows, :] = (h_ref[rows, :] + out * scale * gain).astype(BF)
        gp_ref[...] += jnp.sum(up * out * scale, axis=0, keepdims=True)
        dm_ref[rows, :] = norm_back(up * gain, out, scale).astype(BF)

    forwards = []

    def last():
        for k, b in enumerate(behind):
            remote(wo_hbm, wo_out.at[b], so.at[k], ro.at[k], (dp, b)).wait_recv()
            forward = remote(wo_out.at[b], wo_out.at[b], fo.at[k], go.at[k], (dp, partner))
            forward.start()
            forwards.append(forward)
        tiles(length, 16, finish)

    line_sum(n_dp, dp, me, make, line_refs[0], acc, *line_refs[1:], last)
    done(n_dp)
    spreads_wo[-1].wait_recv()
    for copy in forwards:
        copy.wait_recv()
    for copy in spreads + spreads_wo + forwards:
        copy.wait_send()
    for copy in outs:
        copy.wait()


def ff_forward(h1, up, gain, w_gu, w_d, w_o, number):
    n_dp, n = lax.axis_size("dp"), lax.axis_size("ctx")
    (length, width), fh = h1.shape, w_d.shape[2]
    tokens = 2 * n_dp * length
    half = n // 2
    low = jax.ShapeDtypeStruct((length, width), BF)
    return pl.pallas_call(
        functools.partial(ff_forward_kernel, n_dp, n),
        out_shape=(
            low,
            low,
            jax.ShapeDtypeStruct((1, width), F32),
            jax.ShapeDtypeStruct((tokens, width), BF),
            jax.ShapeDtypeStruct((tokens, 2 * fh), F32),
            jax.ShapeDtypeStruct((tokens, fh), BF),
            jax.ShapeDtypeStruct((width, fh), BF),
            jax.ShapeDtypeStruct((n,) + w_o.shape, BF),
        ),
        in_specs=[VMEM] * 3 + [ANY] * 3,
        out_specs=(VMEM,) * 3 + (ANY,) * 5,
        scratch_shapes=[
            pltpu.VMEM((tokens, width), BF),
            pltpu.VMEM((tokens, 2 * fh), F32),
            pltpu.VMEM((tokens, fh), BF),
            pltpu.VMEM((width, fh), BF),
            pltpu.VMEM((width, 2 * fh), BF),
            pltpu.VMEM((length, width), F32),
            pltpu.SemaphoreType.DMA((half * n_dp,)),
            pltpu.SemaphoreType.DMA((n_dp,)),
            pltpu.SemaphoreType.DMA((5,)),
            pltpu.SemaphoreType.DMA((half - 1, n_dp)),
            pltpu.SemaphoreType.DMA((half - 1, n_dp)),
            pltpu.SemaphoreType.DMA((half,)),
            pltpu.SemaphoreType.DMA((half,)),
            pltpu.SemaphoreType.DMA((half - 1,)),
            pltpu.SemaphoreType.DMA((half - 1,)),
        ]
        + gather_sems(n_dp)
        + pair_scratch(n_dp, length, width)
        + line_scratch(n_dp, length, width),
        compiler_params=params_of(number),
        cost_estimate=cost(90),
        name="ff_forward",
    )(h1, up, gain, w_gu, w_d, w_o)


def store_rows(n_dp, value_of, out):
    half, _, rows, _ = out.shape

    @pl.loop(0, n_dp * half)
    def _(r):
        out[r % half, r // half] = value_of(pl.ds(pl.multiple_of(r * rows, rows), rows)).astype(BF)


def ff_back_kernel(
    n_dp, dm_ref, hid_ref, d_hbm, pre_hbm, dgu_out, gd_out,
    dgu_ref, gd_ref, sem_out, all_ref, d_ref, pre_ref, acc, sem_d, sem_p, *gather,
):
    dp, me = lax.axis_index("dp"), lax.axis_index("ctx")
    length, width = dm_ref.shape
    fh = d_ref.shape[1]
    load = pltpu.make_async_copy(d_hbm, d_ref, sem_d)
    load.start()

    def rows_of(b):
        return pl.ds(pl.multiple_of(2 * b * length, 2 * length), 2 * length)

    def load_pre(b):
        return pltpu.make_async_copy(pre_hbm.at[rows_of(b), :], pre_ref.at[rows_of(b), :], sem_p.at[b])

    for k in range(n_dp):
        load_pre((dp + k) % n_dp).start()
    mine = pl.ds(pl.multiple_of((2 * dp + me % 2) * length, length), length)
    all_ref[mine, :] = dm_ref[...]
    greet_group(n_dp, dp, me)

    def process(b, own):
        rows = rows_of(b)
        if own:
            load.wait()
        load_pre(b).wait()

        def hidden(part):
            second = pl.ds(pl.multiple_of(fh + part.start, part.size), part.size)
            back = dot(all_ref[rows, :], d_ref[:, part])
            gate, upper = pre_ref[rows, part], pre_ref[rows, second]
            sig = jax.nn.sigmoid(gate)
            dgu_ref[rows, part] = (back * upper * sig * (1.0 + gate * (1.0 - sig))).astype(BF)
            dgu_ref[rows, second] = (back * gate * sig).astype(BF)

        tiles(fh, 256, hidden)

        def product(part):
            value = t_dot(all_ref[rows, part], hid_ref[rows, :])
            acc[part, :] = value if own else acc[part, :] + value

        tiles(width, 256, product)

    gather_group(n_dp, dp, me, all_ref, length, *gather, process)
    outs = loads_of(((dgu_ref, dgu_out),), sem_out)
    store_rows(n_dp, lambda part: acc[part, :], gd_ref)
    for copy in outs + loads_of(((gd_ref, gd_out),), sem_out, 1):
        copy.wait()


def ff_back(dm, hid, w_d, pre, rows, number):
    n_dp, half = lax.axis_size("dp"), lax.axis_size("ctx") // 2
    (length, width), fh = dm.shape, w_d.shape[1]
    tokens = 2 * n_dp * length
    return pl.pallas_call(
        functools.partial(ff_back_kernel, n_dp),
        out_shape=(
            jax.ShapeDtypeStruct((tokens, 2 * fh), BF),
            jax.ShapeDtypeStruct((half, n_dp, 2 * rows, fh), BF),
        ),
        in_specs=[VMEM, VMEM, ANY, ANY],
        out_specs=(ANY,) * 2,
        scratch_shapes=[
            pltpu.VMEM((tokens, 2 * fh), BF),
            pltpu.VMEM((half, n_dp, 2 * rows, fh), BF),
            pltpu.SemaphoreType.DMA((2,)),
            pltpu.VMEM((tokens, width), BF),
            pltpu.VMEM((width, fh), BF),
            pltpu.VMEM((tokens, 2 * fh), F32),
            pltpu.VMEM((width, fh), F32),
            pltpu.SemaphoreType.DMA,
            pltpu.SemaphoreType.DMA((n_dp,)),
        ]
        + gather_sems(n_dp),
        compiler_params=params_of(number),
        cost_estimate=cost(45),
        name="ff_back",
    )(dm, hid, w_d, pre)


def ff_scatter_kernel(
    n_dp, n, dgu_hbm, gu_hbm, all_hbm, dh_ref, gg_out, gv_out,
    gg_ref, gv_ref, dgu_ref, gu_ref, all_ref, acc, sem_gu, sem_all, sem_out, *rest,
):
    dp, me = lax.axis_index("dp"), lax.axis_index("ctx")
    length, width = dh_ref.shape
    pair_refs, line_refs = rest[:4], rest[4:]
    half, parity, pair, partner, ahead, behind = pairs_of(n, me)
    _, _, rows, fh = gg_ref.shape
    loads = load_rows(gu_hbm, gu_ref, sem_gu) + loads_of(((dgu_hbm, dgu_ref),), sem_out, 2)
    load = pltpu.make_async_copy(all_hbm, all_ref, sem_all)
    load.start()
    greet_group(n_dp, dp, me)
    for copy in loads:
        copy.wait()

    make, done = part_of_pair(dp, me, dgu_ref, gu_ref, length, *pair_refs)
    load.wait()
    tall = acc.shape[0]

    def grads():
        @pl.loop(0, width // tall)
        def _(j):
            acc[...] = t_dot(all_ref[:, pl.ds(pl.multiple_of(j * tall, tall), tall)], dgu_ref[...])
            for s in range(tall // rows):
                r = j * (tall // rows) + s
                part = slice(s * rows, (s + 1) * rows)
                gg_ref[r % half, r // half] = acc[part, :fh].astype(BF)
                gv_ref[r % half, r // half] = acc[part, fh:].astype(BF)

    val, *line = line_refs
    line_sum(n_dp, dp, me, make, val, dh_ref, *line, lambda: None, grads)
    done(n_dp)
    outs = [
        pltpu.make_async_copy(ref, out, sem_out.at[i])
        for i, (ref, out) in enumerate(((gg_ref, gg_out), (gv_ref, gv_out)))
    ]
    for copy in outs:
        copy.start()
    for copy in outs:
        copy.wait()


def ff_scatter(dgu, w_gu, h1_all, length, number):
    n_dp, n = lax.axis_size("dp"), lax.axis_size("ctx")
    width = h1_all.shape[1]
    grad = jax.ShapeDtypeStruct(w_gu.shape[:3] + (w_gu.shape[3] // 2,), BF)
    return pl.pallas_call(
        functools.partial(ff_scatter_kernel, n_dp, n),
        out_shape=(
            jax.ShapeDtypeStruct((length, width), F32),
            grad,
            grad,
        ),
        in_specs=[ANY] * 3,
        out_specs=(VMEM,) + (ANY,) * 2,
        scratch_shapes=[
            pltpu.VMEM(grad.shape, BF),
            pltpu.VMEM(grad.shape, BF),
            pltpu.VMEM(dgu.shape, BF),
            pltpu.VMEM((width, w_gu.shape[3]), BF),
            pltpu.VMEM(h1_all.shape, BF),
            pltpu.VMEM((256, w_gu.shape[3]), F32),
            pltpu.SemaphoreType.DMA((w_gu.shape[0] * n_dp,)),
            pltpu.SemaphoreType.DMA,
            pltpu.SemaphoreType.DMA((3,)),
        ]
        + pair_scratch(n_dp, length, width)
        + line_scratch(n_dp, length, width),
        compiler_params=params_of(number),
        cost_estimate=cost(50),
        name="ff_scatter",
    )(dgu, w_gu, h1_all)


def start_kernel(
    n_dp, n, p_hbm, x_ref, h_ref, o_ref, p_ref, y_ref, d_ref,
    p_all, g_ref, w_ref, v_ref, local, sg, rg, sa, ra, sv, rv, ss, rs, fs, fr,
):
    dp, me = lax.axis_index("dp"), lax.axis_index("ctx")
    half, parity, pair, partner, ahead, behind = pairs_of(n, me)
    count, mine, place = group_of(n_dp, n, dp, me)
    columns = p_all.shape[2]
    fh, hc = d_ref.shape[2], v_ref.shape[2]
    loads = [
        pltpu.make_async_copy(
            p_hbm.at[:, pl.ds(part * columns, columns)], p_all.at[part], local.at[part]
        )
        for part in range(4)
    ]
    for part in (1, 2, 0, 3):
        loads[part].start()
    greet_all(n_dp, n, dp, me)
    gathers = [
        remote(x_ref, y_ref.at[me], ss.at[k], rs.at[k], (dp, a))
        for k, a in enumerate(ahead + [partner])
    ]
    own_x = pltpu.make_async_copy(x_ref, y_ref.at[me], local.at[4])
    for copy in gathers + [own_x]:
        copy.start()
    for part in (1, 2):
        loads[part].wait()
        for j in range(count):
            g_ref[j, :, (part - 1) * fh : part * fh] = p_all[part, :, j * fh : (j + 1) * fh].astype(BF)
    sends, receives = swap(g_ref, h_ref, sg, rg, count, mine, place)
    loads[0].wait()
    for c in range(n):
        for matrix in range(4):
            start = (matrix * n + c) * hc
            value = p_all[0, :, start : start + hc].astype(BF)
            if matrix < 3:
                w_ref[c, :, matrix * hc : (matrix + 1) * hc] = value
            else:
                v_ref[c] = value
    for src, dst, send, recv in ((w_ref, o_ref, sa, ra), (v_ref, p_ref, sv, rv)):
        more, waits = swap(src, dst, send, recv, n, me, lambda c: (dp, c))
        sends += more
        receives += waits
    owns = [
        pltpu.make_async_copy(g_ref.at[mine], h_ref.at[mine], local.at[5]),
        pltpu.make_async_copy(w_ref.at[me], o_ref.at[me], local.at[6]),
        pltpu.make_async_copy(v_ref.at[me], p_ref.at[me], local.at[7]),
    ]
    for copy in owns:
        copy.start()
    loads[3].wait()
    for j in range(count):
        d_ref[j] = p_all[3, :, j * fh : (j + 1) * fh].astype(BF)
    forwards = []
    for k, b in enumerate(behind):
        remote(x_ref, y_ref.at[b], ss.at[k], rs.at[k], (dp, b)).wait_recv()
        forward = remote(y_ref.at[b], y_ref.at[b], fs.at[k], fr.at[k], (dp, partner))
        forward.start()
        forwards.append(forward)
    gathers[-1].wait_recv()
    for copy in receives:
        copy.wait_recv()
    for forward in forwards:
        forward.wait()
    for copy in sends + gathers:
        copy.wait_send()
    for copy in owns + [own_x]:
        copy.wait()


def start(params, x, number):
    n_dp, n = lax.axis_size("dp"), lax.axis_size("ctx")
    half, count = n // 2, 2 * n_dp
    (rows, columns), width = params.shape, x.shape[1]
    fh, hc = columns // 4 // count, width // n
    dma = pltpu.SemaphoreType.DMA
    g, w, v = (count, rows, 2 * fh), (n, rows, 3 * hc), (n, rows, hc)
    g_out, w_out, v_out, x_all, d_out = pl.pallas_call(
        functools.partial(start_kernel, n_dp, n),
        out_shape=(
            jax.ShapeDtypeStruct(g, BF),
            jax.ShapeDtypeStruct(w, BF),
            jax.ShapeDtypeStruct(v, BF),
            jax.ShapeDtypeStruct((n,) + x.shape, x.dtype),
            jax.ShapeDtypeStruct((count, rows, fh), BF),
        ),
        in_specs=[ANY] * 2,
        out_specs=(ANY,) * 4 + (VMEM,),
        scratch_shapes=[
            pltpu.VMEM((4, rows, columns // 4), F32),
            pltpu.VMEM(g, BF),
            pltpu.VMEM(w, BF),
            pltpu.VMEM(v, BF),
            dma((8,)),
        ]
        + [dma((count - 1,))] * 2
        + [dma((n - 1,))] * 4
        + [dma((half,))] * 2
        + [dma((half - 1,))] * 2,
        compiler_params=params_of(number),
        cost_estimate=cost(45),
        name="start",
    )(params, x)
    return g_out, w_out, v_out, x_all.reshape(-1, width), d_out


def collect_kernel(
    n_dp, n, g_ref, h_ref, a_ref, w_ref, b_ref, o_ref, h_out, y_ref,
    sum_ref, acc, pa, qa, pb, qb, local, s1, r1, s2, r2, sh, rh, *line_refs,
):
    dp, me = lax.axis_index("dp"), lax.axis_index("ctx")
    tall = acc.shape[0]
    count, index, place = group_of(n_dp, n, dp, me)
    greet_all(n_dp, n, dp, me)

    def make(d, out):
        def put(part):
            rows = pl.ds(pl.multiple_of(d * tall + part.start, part.size), part.size)
            out[part, :] = g_ref[rows, :].astype(F32)

        tiles(tall, 64, put)

    cols = slice(0, a_ref.shape[1])
    stay = pltpu.make_async_copy(h_ref.at[index], h_out.at[index], local)
    stay.start()
    later = []

    def between():
        later.extend(swap(h_ref, h_out, sh, rh, count, index, place))
        later.append(reduce_ctx(n, dp, me, a_ref, w_ref, cols, sum_ref, pa, qa, pb, qb, s1, r1, s2, r2))

    def last():
        def put(part):
            o_ref[part, :] = acc[part, :].astype(BF)

        tiles(tall, 64, put)

    def join(part):
        y_ref[part, :] = (sum_ref[part, :] + b_ref[part, :]).astype(BF)

    val, *line = line_refs
    line_sum(n_dp, dp, me, make, val, acc, *line, last, between)
    swaps, receives, sums = later
    tiles(y_ref.shape[0], 32, join)
    for copy in receives:
        copy.wait_recv()
    stay.wait()
    for copy in swaps + sums:
        copy.wait_send()


def collect(g, h, a, w, b, number):
    n_dp, n = lax.axis_size("dp"), lax.axis_size("ctx")
    tall, width = g.shape[0] // n_dp, g.shape[1]
    half, length, features = n // 2, a.shape[0] // n, w.shape[0]
    dma = pltpu.SemaphoreType.DMA
    return pl.pallas_call(
        functools.partial(collect_kernel, n_dp, n),
        out_shape=(
            jax.ShapeDtypeStruct((tall, width), BF),
            jax.ShapeDtypeStruct(h.shape, BF),
            jax.ShapeDtypeStruct((length, features), BF),
        ),
        in_specs=[VMEM, ANY, VMEM, VMEM, VMEM],
        out_specs=(VMEM, ANY, VMEM),
        scratch_shapes=[
            pltpu.VMEM((length, features), F32),
            pltpu.VMEM((tall, width), F32),
            pltpu.VMEM((half, length, features), BF),
            pltpu.VMEM((half, length, features), BF),
            pltpu.VMEM((half - 1, length, features), BF),
            pltpu.VMEM((half - 1, length, features), BF),
            dma,
            dma((half,)),
            dma((half,)),
            dma((half - 1,)),
            dma((half - 1,)),
            dma((2 * n_dp - 1,)),
            dma((2 * n_dp - 1,)),
        ]
        + line_scratch(n_dp, tall, width),
        compiler_params=params_of(number),
        cost_estimate=cost(70),
        name="collect",
    )(g, h, a, w, b)


def total_kernel(
    n_dp, n, qk_ref, wv_ref, wo_ref, u_ref, gg_ref, gd_ref, qk_gain, attn_gain, ff_gain, p_hbm, m_hbm, v_hbm,
    ga_ref, gu_ref, o_ref, p_out, m_out, v_out,
    sb, mine, buf, part, all_parts, square, buf_s, part_s, all_s, local, sx, rx, sh, rh,
    ss, rs, st, rt, s1, r1, s2, r2, sem_copy,
):
    dp, me = lax.axis_index("dp"), lax.axis_index("ctx")
    hc = wv_ref.shape[2]
    count, index, place = group_of(n_dp, n, dp, me)
    greet_all(n_dp, n, dp, me)
    swaps, receives = swap(u_ref, gu_ref, sh, rh, count, index, place)
    stay = pltpu.make_async_copy(u_ref.at[index], gu_ref.at[index], local)
    stay.start()
    moves = [
        pltpu.make_async_copy(source, target, sem_copy.at[i])
        for i, (source, target) in enumerate(((p_hbm, p_out), (m_hbm, m_out), (v_hbm, v_out)))
    ]
    for copy in moves:
        copy.start()
    sb[:, :, : 2 * hc] = qk_ref[...]
    sb[:, :, 2 * hc : 3 * hc] = wv_ref[...]
    more, waits = swap(sb, ga_ref, sx, rx, n, me, lambda c: (dp, c))
    ga_ref[me] = sb[me]

    def squares(ref):
        acc = jnp.zeros((ref.shape[1], ref.shape[2]), F32)
        for i in range(ref.shape[0]):
            block = ref[i].astype(F32)
            acc += block * block
        return jnp.sum(jnp.sum(acc, axis=0, keepdims=True), axis=1, keepdims=True)

    copies = swaps + more

    def sum_all(value, rows, along, columns, send, recv, send_dp, recv_dp):
        for k in range(1, n):
            copy = remote(value, rows.at[me], send.at[k - 1], recv.at[k - 1], (dp, (me + k) % n))
            copy.start()
            copies.append(copy)
        rows[me] = value[...]
        for k in range(1, n):
            source = (me + n - k) % n
            remote(value, rows.at[source], send.at[k - 1], recv.at[k - 1], (dp, source)).wait_recv()
        acc = rows[0]
        for j in range(1, n):
            acc = acc + rows[j]
        along[...] = acc
        columns[dp] = acc
        for k in range(1, n_dp):
            to = (dp + k) % n_dp
            copy = remote(along, columns.at[dp], send_dp.at[k - 1], recv_dp.at[k - 1], (to, me))
            copy.start()
            copies.append(copy)
        for k in range(1, n_dp):
            source = (dp + n_dp - k) % n_dp
            remote(along, columns.at[source], send_dp.at[k - 1], recv_dp.at[k - 1], (source, me)).wait_recv()
        acc = columns[0]
        for j in range(1, n_dp):
            acc = acc + columns[j]
        return acc

    mine[...] = jnp.zeros_like(mine)
    mine[0:2, pl.ds(pl.multiple_of(me * hc, hc), hc)] = qk_gain[...]
    mine[2:3, :] = attn_gain[...]
    mine[3:4, :] = ff_gain[...]
    o_ref[...] = sum_all(mine, buf, part, all_parts, ss, rs, st, rt)
    total = squares(gg_ref) + squares(gd_ref) + squares(wo_ref)
    for copy in waits:
        copy.wait_recv()
    total += squares(ga_ref)
    for copy in receives:
        copy.wait_recv()
    stay.wait()
    total += squares(gu_ref)
    square[...] = jnp.broadcast_to(total, square.shape)
    total = sum_all(square, buf_s, part_s, all_s, s1, r1, s2, r2)
    o_ref[4:5, :] = jnp.broadcast_to(total[0:1, 0:1], (1, o_ref.shape[1]))
    for copy in copies:
        copy.wait_send()
    for copy in moves:
        copy.wait()


def total_over(qk, wv, wo, u, gg, gd, qk_gain, attn_gain, ff_gain, masters, number):
    n_dp, n = lax.axis_size("dp"), lax.axis_size("ctx")
    rows, hc = qk.shape[0] // n, wv.shape[1]
    shape = (8, attn_gain.shape[1])
    dma = pltpu.SemaphoreType.DMA
    return pl.pallas_call(
        functools.partial(total_kernel, n_dp, n),
        out_shape=(
            jax.ShapeDtypeStruct((n, rows, 3 * hc), BF),
            jax.ShapeDtypeStruct(u.shape, BF),
            jax.ShapeDtypeStruct(shape, F32),
            *[jax.ShapeDtypeStruct(a.shape, F32) for a in masters],
        ),
        in_specs=[VMEM] * 3 + [ANY] + [VMEM] * 5 + [HBM] * 3,
        out_specs=(VMEM,) * 3 + (ANY,) * 3,
        scratch_shapes=[
            pltpu.VMEM((n, rows, 3 * hc), BF),
            pltpu.VMEM(shape, F32),
            pltpu.VMEM((n,) + shape, F32),
            pltpu.VMEM(shape, F32),
            pltpu.VMEM((n_dp,) + shape, F32),
            pltpu.VMEM((8, 128), F32),
            pltpu.VMEM((n, 8, 128), F32),
            pltpu.VMEM((8, 128), F32),
            pltpu.VMEM((n_dp, 8, 128), F32),
            dma,
            dma((n - 1,)),
            dma((n - 1,)),
            dma((2 * n_dp - 1,)),
            dma((2 * n_dp - 1,)),
            dma((n - 1,)),
            dma((n - 1,)),
            dma((n_dp - 1,)),
            dma((n_dp - 1,)),
            dma((n - 1,)),
            dma((n - 1,)),
            dma((n_dp - 1,)),
            dma((n_dp - 1,)),
            dma((3,)),
        ],
        compiler_params=params_of(number, 19),
        cost_estimate=cost(35),
        name="total",
    )(
        qk.reshape(n, rows, 2 * hc),
        wv.reshape(n, rows, hc),
        wo[None],
        u,
        gg,
        gd,
        qk_gain,
        attn_gain,
        ff_gain,
        *masters,
    )


def adam_kernel(
    sum_ref, gp_ref, gm_ref, gv_ref, p_ref, m_ref, v_ref, ga_ref, go_ref, gg_ref, gu_ref, gd_ref,
    norm_ref, gp_out, gm_out, gv_out, po_ref, mo_ref, vo_ref, g_ref, factor_ref,
):
    part = pl.program_id(0)

    @pl.when((part == 0) & (pl.program_id(1) == 0))
    def _():
        gain = sum_ref[0:4, :]
        squares = jnp.sum(jnp.sum(gain * gain, axis=0, keepdims=True), axis=1, keepdims=True)
        norm = jnp.sqrt(sum_ref[4:5, 0:1] + squares)
        norm_ref[...] = norm
        factor = CLIP / (norm + 1e-06)
        factor_ref[...] = jnp.broadcast_to(factor, factor_ref.shape)
        new = adam_update(gp_ref[...], gm_ref[...], gv_ref[...], gain * factor, GAIN_RATE, 0.0)
        gp_out[...], gm_out[...], gv_out[...] = new

    n, _, three = ga_ref.shape
    hc = three // 3
    fs = gd_ref.shape[2]

    @pl.when(part == 0)
    def _():
        g_ref[:, 3 * n * hc :] = go_ref[...].astype(F32)
        for matrix in range(3):
            for c in range(n):
                start = (matrix * n + c) * hc
                g_ref[:, start : start + hc] = ga_ref[c, :, matrix * hc : (matrix + 1) * hc].astype(F32)

    for index, ref in ((1, gg_ref), (2, gu_ref), (3, gd_ref)):

        @pl.when(part == index)
        def _():
            for d in range(ref.shape[0]):
                g_ref[:, d * fs : (d + 1) * fs] = ref[d].astype(F32)

    clipped = g_ref[...] * factor_ref[0:1, 0:1]
    new_m = BETA1 * m_ref[...] + (1.0 - BETA1) * clipped
    new_v = BETA2 * v_ref[...] + (1.0 - BETA2) * (clipped * clipped)
    hat = new_v * (1.0 / (1.0 - BETA2**STEP))
    root = hat * lax.rsqrt(jnp.maximum(hat, 1e-36)) + ADAM_EPS
    change = (new_m * (RATE / (1.0 - BETA1**STEP))) * pl.reciprocal(root, approx=True)
    po_ref[...] = p_ref[...] * (1.0 - RATE * DECAY) - change
    mo_ref[...] = new_m
    vo_ref[...] = new_v


def adam(sums, gains, gains_first, gains_second, params, first, second, ga, go, gg, gu, gd):
    rows, columns = params.shape
    n, n_dp, fs = ga.shape[0], gd.shape[0], gd.shape[2]
    block = min(rows, 32)
    steps = rows // block
    wide = pl.BlockSpec((block, columns // 4), lambda i, r: (r, i))
    small = pl.BlockSpec(gains.shape, lambda i, r: (0, 0))
    return pl.pallas_call(
        adam_kernel,
        grid=(4, steps),
        out_shape=(jax.ShapeDtypeStruct((1, 1), F32),)
        + (jax.ShapeDtypeStruct(gains.shape, F32),) * 3
        + (jax.ShapeDtypeStruct(params.shape, F32),) * 3,
        in_specs=[
            pl.BlockSpec(sums.shape, lambda i, r: (0, 0)),
            small,
            small,
            small,
            wide,
            wide,
            wide,
            pl.BlockSpec((n, block, ga.shape[2]), lambda i, r: (0, jnp.where(i == 0, r, steps - 1), 0)),
            pl.BlockSpec((block, go.shape[1]), lambda i, r: (jnp.where(i == 0, r, steps - 1), 0)),
            *[
                pl.BlockSpec(
                    (n_dp, block, fs),
                    lambda i, r, part=part: (
                        0,
                        jnp.where(i < part, 0, jnp.where(i == part, r, steps - 1)),
                        0,
                    ),
                )
                for part in (1, 2, 3)
            ],
        ],
        out_specs=(pl.BlockSpec((1, 1), lambda i, r: (0, 0)),) + (small,) * 3 + (wide,) * 3,
        scratch_shapes=[pltpu.VMEM((block, columns // 4), F32), pltpu.VMEM((8, 128), F32)],
        compiler_params=pltpu.CompilerParams(vmem_limit_bytes=22 * 1024 * 1024),
        name="adam",
    )(sums, gains, gains_first, gains_second, params, first, second, ga, go, gg, gu, gd)


def row_sums(value, row):
    pick = lax.broadcasted_iota(jnp.int32, (8, value.shape[1]), 0) == row
    return lax.dot_general(
        pick.astype(F32),
        value,
        (((1,), (1,)), ((), ())),
        preferred_element_type=F32,
        precision=lax.Precision.HIGHEST,
    )


def exchange(n, dp, me, buf, ss, rs):
    copies = []
    for k in range(1, n):
        copy = remote(buf.at[me], buf.at[me], ss.at[k - 1], rs.at[k - 1], (dp, (me + k) % n))
        copy.start()
        copies.append(copy)
    for k in range(1, n):
        source = (me + n - k) % n
        remote(buf.at[me], buf.at[source], ss.at[k - 1], rs.at[k - 1], (dp, source)).wait_recv()
    total = buf[0]
    for j in range(1, n):
        total = total + buf[j]
    for copy in copies:
        copy.wait_send()
    return total


def turn(value, cos, sine):
    return value * cos + pltpu.roll(value, HD // 2, 1) * sine


def mask_of(rows, info_col, info_row):
    pos_i, doc_i = info_col[rows, 0:1], info_col[rows, 1:2]
    return (info_row[1:2, :] == doc_i) & (info_row[0:1, :] <= pos_i)


def attend_kernel(
    n_dp, n, x_hbm, w_hbm, wo_ref, d_ref, t_ref, norm_ref, gain_ref, cos_ref, sin_ref, col_ref, row_ref,
    y_ref, h_ref, q_out, k_out, v_out, o_ref, pre_out, scale_ref, lse_ref, wo_all, d_out,
    buf, pa, qa, pb, qb, ss, rs, s1, r1, s2, r2, sw, rw, sd, rd, local,
    x_ref, w_ref, q_ref, k_ref, v_ref, pre_ref, sem_in, sem_out,
):
    dp, me = lax.axis_index("dp"), lax.axis_index("ctx")
    loads = loads_of(((x_hbm, x_ref), (w_hbm, w_ref)), sem_in)
    seq, width = x_ref.shape
    hc = o_ref.shape[1]
    block = min(seq, 256)
    count, mine, place = group_of(n_dp, n, dp, me)
    greet_all(n_dp, n, dp, me)
    piece = wo_ref.shape[0]

    def part_of(d):
        return wo_all.at[pl.ds(pl.multiple_of(d * piece, piece), piece), :]

    owns = [
        pltpu.make_async_copy(wo_ref, part_of(dp), local.at[0]),
        pltpu.make_async_copy(d_ref.at[mine], d_out.at[mine], local.at[1]),
    ]
    behind_wo = [
        remote(wo_ref, part_of(dp), sw.at[k - 1], rw.at[k - 1], (across(dp, k, n_dp)[0], me))
        for k in range(1, n_dp)
    ]
    for copy in behind_wo + owns:
        copy.start()
    behind_d, receives = swap(d_ref, d_out, sd, rd, count, mine, place)

    for copy in loads:
        copy.wait()

    @pl.loop(0, seq // block)
    def _(i):
        rows = pl.ds(pl.multiple_of(i * block, block), block)
        value = dot(x_ref[rows, :], w_ref[...])
        pre_ref[rows, :] = value[:, : 2 * hc]
        v_ref[rows, :] = value[:, 2 * hc :].astype(BF)
        squares = value[:, : 2 * hc] * value[:, : 2 * hc]
        buf[me, :, rows] = row_sums(squares[:, :hc], 0) + row_sums(squares[:, hc:], 1)

    scale_ref[...] = jnp.transpose(lax.rsqrt(exchange(n, dp, me, buf, ss, rs) / width + EPS))

    @pl.loop(0, seq // block)
    def _(i):
        rows = pl.ds(pl.multiple_of(i * block, block), block)
        cos, sine = cos_ref[rows, :], sin_ref[rows, :]
        for which, ref, factor in ((0, q_ref, HD ** (-0.5)), (1, k_ref, 1.0)):
            scale = scale_ref[rows, which : which + 1]
            for start in range(0, hc, HD):
                part = slice(start, start + HD)
                value = pre_ref[rows, which * hc + start : which * hc + start + HD] * scale
                ref[rows, part] = (
                    turn(value * gain_ref[which : which + 1, part], cos, sine) * factor
                ).astype(BF)

    def attention(pair, first):
        size = 2 * (seq // n)
        rows = pl.ds(pl.multiple_of(pair * size, size), size)
        visible = mask_of(rows, col_ref, row_ref)
        for head in range(hc // HD):
            part = slice(head * HD, (head + 1) * HD)
            scores = jnp.where(visible, dot_t(q_ref[rows, part], k_ref[:, part]), -jnp.inf)
            top = jnp.max(scores, axis=1, keepdims=True)
            weights = jnp.exp(scores - top)
            total = jnp.sum(weights, axis=1, keepdims=True)
            o_ref[rows, part] = (dot(weights.astype(BF), v_ref[:, part]) / total).astype(BF)
            lse_ref[rows, head : head + 1] = top + jnp.log(total)
        if first:
            owns[0].wait()
            for k in range(1, n_dp):
                _, source = across(dp, k, n_dp)
                remote(wo_ref, part_of(source), sw.at[k - 1], rw.at[k - 1], (source, me)).wait_recv()

    outs = loads_of(((pre_ref, pre_out), (q_ref, q_out), (k_ref, k_out), (v_ref, v_out)), sem_out)
    cols = slice(0, hc)
    sums = reduce_ctx(
        n, dp, me, o_ref, wo_all, cols, y_ref, pa, qa, pb, qb, s1, r1, s2, r2, before=attention
    )

    def finish(rows):
        branch = y_ref[rows, :]
        h_ref[rows, :] = t_ref[rows, :].astype(F32) + branch * rms_scale(branch) * norm_ref[...]

    tiles(y_ref.shape[0], 16, finish)
    for copy in receives:
        copy.wait_recv()
    for copy in sums + behind_wo + behind_d:
        copy.wait_send()
    for copy in outs + owns[1:]:
        copy.wait()


def attend(x_all, w, wo, d, tokens, norm, gain, cos, sine, info_col, info_row, number):
    n_dp, n = lax.axis_size("dp"), lax.axis_size("ctx")
    seq, width = x_all.shape
    half, length, hc = n // 2, seq // n, w.shape[1] // 3
    dma = pltpu.SemaphoreType.DMA
    low = jax.ShapeDtypeStruct((seq, hc), BF)
    return pl.pallas_call(
        functools.partial(attend_kernel, n_dp, n),
        out_shape=(
            jax.ShapeDtypeStruct((length, width), F32),
            jax.ShapeDtypeStruct((length, width), F32),
            low,
            low,
            low,
            low,
            jax.ShapeDtypeStruct((seq, 2 * hc), F32),
            jax.ShapeDtypeStruct((seq, 8), F32),
            jax.ShapeDtypeStruct((seq, 8), F32),
            jax.ShapeDtypeStruct((width, hc), BF),
            jax.ShapeDtypeStruct(d.shape, BF),
        ),
        in_specs=[ANY] * 4 + [VMEM] * 7,
        out_specs=(VMEM,) * 2 + (ANY,) * 3 + (VMEM, ANY) + (VMEM,) * 3 + (ANY,),
        scratch_shapes=[
            pltpu.VMEM((n, 8, seq), F32),
            pltpu.VMEM((half, length, width), BF),
            pltpu.VMEM((half, length, width), BF),
            pltpu.VMEM((half - 1, length, width), BF),
            pltpu.VMEM((half - 1, length, width), BF),
            dma((n - 1,)),
            dma((n - 1,)),
            dma((half,)),
            dma((half,)),
            dma((half - 1,)),
            dma((half - 1,)),
            dma((n_dp - 1,)),
            dma((n_dp - 1,)),
            dma((2 * n_dp - 1,)),
            dma((2 * n_dp - 1,)),
            dma((2,)),
            pltpu.VMEM(x_all.shape, BF),
            pltpu.VMEM(w.shape, BF),
            *[pltpu.VMEM((seq, hc), BF)] * 3,
            pltpu.VMEM((seq, 2 * hc), F32),
            dma((2,)),
            dma((4,)),
        ],
        compiler_params=params_of(number),
        cost_estimate=cost(60),
        name="attend",
    )(x_all, w, wo, d, tokens, norm, gain, cos, sine, info_col, info_row)


def slab_give(n_dp, dp, me, g_ref, co_ref, sw, rw):
    tall = co_ref.shape[1]
    gives = []
    for k in range(1, n_dp):
        to, _ = across(dp, k, n_dp)
        part = pl.ds(pl.multiple_of(to * tall, tall), tall)
        copy = remote(g_ref.at[part, :], co_ref.at[k - 1], sw.at[k - 1], rw.at[k - 1], (to, me))
        copy.start()
        gives.append(copy)
    return gives


def slab_sum(dp, gives, g_ref, co_ref, out_ref):
    tall = co_ref.shape[1]
    total = g_ref[pl.ds(pl.multiple_of(dp * tall, tall), tall), :].astype(F32)
    for k, copy in enumerate(gives):
        copy.wait_recv()
        total = total + co_ref[k].astype(F32)
    out_ref[...] = total.astype(BF)


def greet_wide_group(n_dp, dp, me):
    partner = me + 1 - 2 * (me % 2)
    others = [(dp + k) % n_dp for k in range(1, n_dp)]
    greet([(dp, partner)] + [(d, c) for d in others for c in (me, partner)])


def attend_back_kernel(
    n_dp, n, sum_ref, up_ref, branch_ref, norm_ref, wo_hbm, h_ref, o_hbm, col_ref, row_ref, q_hbm, k_hbm, v_hbm, lse_ref,
    x_hbm, gain_ref, cos_hbm, sin_hbm, pre_hbm, scale_ref,
    dh_ref, gp_ref, d_ref, gain_out, g_ref, wv_ref, wo_ref, h_out,
    q_ref, k_ref, v_ref, cos_ref, sin_ref, x_ref, pre_ref, wall_ref, db_ref, mix_ref, give_ref, e_ref, do_ref, o_ref, dq_ref, dk_ref, dv_ref, mean_ref, buf, go_ref, co_ref, gv_ref, cv_ref,
    sh, rh, local, sw, rw, sv, rv, ss, rs, sc, rc, sx, rx,
):
    dp, me = lax.axis_index("dp"), lax.axis_index("ctx")
    seq, hc = q_ref.shape
    load_wo = pltpu.make_async_copy(wo_hbm, wall_ref, local.at[2])
    load_wo.start()
    later = [
        pltpu.make_async_copy(src, dst, local.at[i])
        for i, (src, dst) in enumerate(((x_hbm, x_ref), (pre_hbm, pre_ref)), 4)
    ]
    load = pltpu.make_async_copy(o_hbm, o_ref, local.at[1])
    load.start()
    tables = ((q_hbm, q_ref), (k_hbm, k_ref), (v_hbm, v_ref), (cos_hbm, cos_ref), (sin_hbm, sin_ref))
    loads = loads_of(tables, local, 6)
    length, width = dh_ref.shape
    block = min(seq, 256)
    count, index, place = group_of(n_dp, n, dp, me)
    greet_all(n_dp, n, dp, me)
    swaps, receives = swap(h_ref, h_out, sh, rh, count, index, place)
    stay = pltpu.make_async_copy(h_ref.at[index], h_out.at[index], local.at[0])
    stay.start()

    gp_ref[...] = jnp.zeros_like(gp_ref)

    def finish(rows):
        grad, branch = sum_ref[rows, :] + up_ref[rows, :].astype(F32), branch_ref[rows, :]
        scale = rms_scale(branch)
        dh_ref[rows, :] = grad
        gp_ref[...] += jnp.sum(grad * branch * scale, axis=0, keepdims=True)
        db_ref[rows, :] = norm_back(grad * norm_ref[...], branch, scale).astype(BF)

    tiles(length, 16, finish)
    load_wo.wait()

    def mine(c):
        return pl.ds(pl.multiple_of(c * length, length), length)

    def send(k):
        to = (me + k) % n
        return remote(give_ref.at[to], do_ref.at[mine(me), :], sx.at[k - 1], rx.at[k - 1], (dp, to))

    def receive(k):
        source = (me + n - k) % n
        return remote(give_ref.at[me], do_ref.at[mine(source), :], sx.at[k - 1], rx.at[k - 1], (dp, source))

    share = width // n
    own = share // n_dp
    for c in range(n):
        for d in range(n_dp):
            start, source = c * share + d * own, (d * n + c) * own
            mix_ref[:, start : start + own] = db_ref[:, source : source + own]

    def share_of(c):
        return mix_ref.at[:, pl.ds(pl.multiple_of(c * share, share), share)]

    def send_share(k):
        to = (me + k) % n
        return remote(share_of(to), e_ref.at[mine(me), :], sc.at[k - 1], rc.at[k - 1], (dp, to))

    def receive_share(k):
        source = (me + n - k) % n
        return remote(share_of(me), e_ref.at[mine(source), :], sc.at[k - 1], rc.at[k - 1], (dp, source))

    stay_share = pltpu.make_async_copy(share_of(me), e_ref.at[mine(me), :], local.at[3])
    stay_share.start()

    @pl.loop(1, n)
    def _(k):
        to = (me + k) % n
        send_share(k).start()
        give_ref[to] = dot(db_ref[...], wall_ref[to]).astype(BF)
        send(k).start()

    do_ref[mine(me), :] = dot(db_ref[...], wall_ref[me]).astype(BF)
    for k in range(1, n):
        receive(k).wait_recv()
        receive_share(k).wait_recv()
    for k in range(1, n):
        send(k).wait_send()
        send_share(k).wait_send()
    stay_share.wait()
    load.wait()
    for copy in later:
        copy.start()

    @pl.loop(0, n)
    def _(c):
        go_ref[:, pl.ds(pl.multiple_of(c * hc, hc), hc)] = t_dot(e_ref[...], o_ref[c]).astype(BF)

    gives = slab_give(n_dp, dp, me, go_ref, co_ref, sw, rw)
    dk_ref[...] = jnp.zeros_like(dk_ref)
    dv_ref[...] = jnp.zeros_like(dv_ref)

    def attention(i):
        rows = pl.ds(pl.multiple_of(i * block, block), block)
        visible = mask_of(rows, col_ref, row_ref)
        for head in range(hc // HD):
            part = slice(head * HD, (head + 1) * HD)
            query, key, value, back = q_ref[rows, part], k_ref[:, part], v_ref[:, part], do_ref[rows, part]
            scores = jnp.where(visible, dot_t(query, key), -jnp.inf)
            probs = jnp.exp(scores - lse_ref[rows, head : head + 1])
            d_probs = dot_t(back, value)
            delta = jnp.sum(probs * d_probs, axis=1, keepdims=True)
            d_scores = (probs * (d_probs - delta)).astype(BF)
            dq_ref[rows, part] = dot(d_scores, key)
            dk_ref[:, part] += t_dot(d_scores, query)
            dv_ref[:, part] += t_dot(probs.astype(BF), back)

    for copy in loads:
        copy.wait()
    pl.loop(0, seq // block)(attention)

    for copy in later:
        copy.wait()
    d_ref[:, 2 * hc :] = dv_ref[...].astype(BF)

    def values(part):
        gv_ref[part, :] = t_dot(x_ref[:, part], d_ref[:, 2 * hc :]).astype(BF)

    tiles(width, 256, values)
    gives_v = slab_give(n_dp, dp, me, gv_ref, cv_ref, sv, rv)
    gain_out[...] = jnp.zeros_like(gain_out)

    @pl.loop(0, seq // block)
    def _(i):
        rows = pl.ds(pl.multiple_of(i * block, block), block)
        cos, sine = cos_ref[rows, :], sin_ref[rows, :]
        sums = jnp.zeros((8, block), F32)
        for which, ref, factor in ((0, dq_ref, HD ** (-0.5)), (1, dk_ref, 1.0)):
            scale = scale_ref[rows, which : which + 1]
            for start in range(0, hc, HD):
                part = slice(start, start + HD)
                pre = pre_ref[rows, which * hc + start : which * hc + start + HD]
                value = turn(ref[rows, part] * factor, cos, -sine)
                gain_out[which : which + 1, part] += jnp.sum(value * pre * scale, axis=0, keepdims=True)
                value = value * gain_ref[which : which + 1, part]
                ref[rows, part] = value
                sums += row_sums(value * pre, which)
        buf[me, :, rows] = sums

    mean_ref[...] = jnp.transpose(exchange(n, dp, me, buf, ss, rs) / width)

    @pl.loop(0, seq // block)
    def _(i):
        rows = pl.ds(pl.multiple_of(i * block, block), block)
        for which, ref in ((0, dq_ref), (1, dk_ref)):
            scale = scale_ref[rows, which : which + 1]
            mean = mean_ref[rows, which : which + 1]
            cols = slice(which * hc, (which + 1) * hc)
            value = scale * (ref[rows, :] - pre_ref[rows, cols] * (scale * scale * mean))
            d_ref[rows, cols] = value.astype(BF)

    def product(part):
        g_ref[part, :] = t_dot(x_ref[:, part], d_ref[:, : 2 * hc]).astype(BF)

    tiles(width, 256, product)
    slab_sum(dp, gives, go_ref, co_ref, wo_ref)
    slab_sum(dp, gives_v, gv_ref, cv_ref, wv_ref)
    for copy in receives:
        copy.wait_recv()
    for copy in swaps + gives + gives_v:
        copy.wait_send()
    stay.wait()


def attend_back(sums, up, branch, norm, wo_all, h, o_all, info_col, info_row, q, k, v, lse, x, gain, cos, sine, pre, scale, number):
    n_dp, n = lax.axis_size("dp"), lax.axis_size("ctx")
    (seq, hc), (length, width) = q.shape, branch.shape
    share = width // n
    dma = pltpu.SemaphoreType.DMA
    return pl.pallas_call(
        functools.partial(attend_back_kernel, n_dp, n),
        out_shape=(
            jax.ShapeDtypeStruct((length, width), F32),
            jax.ShapeDtypeStruct((1, width), F32),
            jax.ShapeDtypeStruct((seq, 3 * hc), BF),
            jax.ShapeDtypeStruct((2, hc), F32),
            jax.ShapeDtypeStruct((width, 2 * hc), BF),
            jax.ShapeDtypeStruct((width // n_dp, hc), BF),
            jax.ShapeDtypeStruct((share // n_dp, n * hc), BF),
            jax.ShapeDtypeStruct(h.shape, BF),
        ),
        in_specs=[VMEM] * 4 + [ANY] * 3 + [VMEM] * 2 + [ANY] * 3 + [VMEM, ANY, VMEM] + [ANY] * 3 + [VMEM],
        out_specs=(VMEM,) * 7 + (ANY,),
        scratch_shapes=[
            *[pltpu.VMEM((seq, hc), BF)] * 3,
            *[pltpu.VMEM(cos.shape, F32)] * 2,
            pltpu.VMEM(x.shape, BF),
            pltpu.VMEM(pre.shape, F32),
            pltpu.VMEM(wo_all.shape, BF),
            pltpu.VMEM((length, width), BF),
            pltpu.VMEM((length, width), BF),
            pltpu.VMEM((n, length, hc), BF),
            pltpu.VMEM((seq, share), BF),
            pltpu.VMEM((seq, hc), BF),
            pltpu.VMEM(o_all.shape, BF),
            pltpu.VMEM((seq, hc), F32),
            pltpu.VMEM((seq, hc), F32),
            pltpu.VMEM((seq, hc), F32),
            pltpu.VMEM((seq, 8), F32),
            pltpu.VMEM((n, 8, seq), F32),
            pltpu.VMEM((share, n * hc), BF),
            pltpu.VMEM((n_dp - 1, share // n_dp, n * hc), BF),
            pltpu.VMEM((width, hc), BF),
            pltpu.VMEM((n_dp - 1, width // n_dp, hc), BF),
            dma((2 * n_dp - 1,)),
            dma((2 * n_dp - 1,)),
            dma((11,)),
            dma((n_dp - 1,)),
            dma((n_dp - 1,)),
            dma((n_dp - 1,)),
            dma((n_dp - 1,)),
            dma((n - 1,)),
            dma((n - 1,)),
            dma((n - 1,)),
            dma((n - 1,)),
            dma((n - 1,)),
            dma((n - 1,)),
        ],
        compiler_params=params_of(number),
        cost_estimate=cost(75),
        name="attend_back",
    )(sums, up, branch, norm, wo_all, h, o_all, info_col, info_row, q, k, v, lse, x, gain, cos, sine, pre, scale)


def shards(
    inputs,
    cotangent,
    documents,
    block_place,
    params,
    first_moment,
    second_moment,
    gains,
    gains_first,
    gains_second,
):
    tokens = inputs[0]
    upstream = cotangent[0]
    length, width = tokens.shape
    n_ctx = lax.axis_size("ctx")
    n_dp = lax.axis_size("dp")
    me_ctx = lax.axis_index("ctx")
    seq = length * n_ctx
    rows = params.shape[0]
    ff = (params.shape[1] - 4 * width) // 3
    hc = width // n_ctx
    half, group = n_ctx // 2, 2 * n_dp
    fh = ff // group
    parities = [[2 * p + side for p in range(half)] for side in range(2)]

    def gather_pairs(w):
        w = lax.all_gather(
            w.reshape(group * rows, w.shape[2]), "ctx", axis=0, tiled=True, axis_index_groups=parities
        )
        return w.reshape(half, n_dp, 2 * rows, w.shape[1])

    def scatter_pairs(g):
        g = lax.psum_scatter(
            g.reshape(width, g.shape[3]),
            "ctx",
            scatter_dimension=0,
            tiled=True,
            axis_index_groups=parities,
        )
        return g.reshape(group, rows, g.shape[1])

    w_gu, w_qkv, w_o, x_all, w_d = start(params, tokens, 1)
    w_gu = gather_pairs(w_gu)
    w_qkv, (cos_tab, sine_tab, info_row, info_col) = gather_dp(
        w_qkv.reshape(n_ctx * rows, 3 * hc), block_place, documents, 2
    )
    my_gains = lax.dynamic_slice_in_dim(gains[:2], me_ctx * hc, hc, axis=1)
    tables = (my_gains, cos_tab, sine_tab, info_col, info_row)

    branch, hidden1, queries, keys, values, attn_low, qk_pre, scales, lse, w_o, w_d = attend(
        x_all, w_qkv, w_o.reshape(n_ctx * rows, hc), w_d, tokens, gains[2:3], *tables, 3
    )

    result, d_mlp, g_ff_part, h1_all, gate_up, inner, w_d, w_o = ff_forward(
        hidden1, upstream, gains[3:4], w_gu, w_d.reshape(n_dp, 2 * rows, fh), w_o, 4
    )
    attn_low, d_mlp = lax.optimization_barrier((attn_low, d_mlp))
    attn_all = lax.all_gather(attn_low, "ctx", axis=0)
    d_gu, d_grad = ff_back(d_mlp, inner, w_d, gate_up, rows, 5)
    d_grad = scatter_pairs(d_grad)
    d_sums, g_grad, u_grad = ff_scatter(d_gu, w_gu, h1_all, length, 6)
    g_grad, u_grad = scatter_pairs(g_grad), scatter_pairs(u_grad)

    d_h1, g_attn_part, d_qkv, d_gain, qk_grad, wv_grad, wo_grad, d_grad = attend_back(
        d_sums, upstream, branch, gains[2:3], w_o, d_grad, attn_all, info_col, info_row, queries, keys, values, lse,
        x_all, my_gains, cos_tab, sine_tab, qk_pre, scales, 8,
    )
    qk_grad, g_grad, d_input = collect(qk_grad, g_grad, d_qkv, w_qkv, d_h1, 9)

    attn_grad, u_grad, sums, *masters = total_over(
        qk_grad, wv_grad, wo_grad, u_grad, g_grad, d_grad, d_gain, g_attn_part, g_ff_part,
        (params, first_moment, second_moment), 11,
    )
    grad_norm, new_gains, new_gains_first, new_gains_second, new_params, new_first, new_second = adam(
        sums, gains, gains_first, gains_second, *masters,
        attn_grad, wo_grad, g_grad, u_grad, d_grad,
    )
    return (
        result[None],
        d_input[None],
        grad_norm.reshape(()),
        new_params,
        new_first,
        new_second,
        new_gains,
        new_gains_first,
        new_gains_second,
    )


def solution(mesh):
    split, whole = P("dp", "ctx", None), P(("dp", "ctx"), None)
    return jax.shard_map(
        shards,
        mesh=mesh,
        in_specs=(split, split, P("dp", None), P(), whole, whole, whole, P(), P(), P()),
        out_specs=(split, split, P(), whole, whole, whole, P(), P(), P()),
        check_vma=False,
    )
```

```python
import functools

import jax
import jax.numpy as jnp
import numpy as np
from jax import lax
from jax.experimental import pallas as pl
from jax.experimental.pallas import tpu as pltpu
from jax.sharding import PartitionSpec as P

HD = 128
STEP = 10
EPS = 1e-06
THETA = 500000.0
CLIP = 1.0
BETA1 = 0.9
BETA2 = 0.95
RATE = 0.03
GAIN_RATE = 0.8
DECAY = 0.1
ADAM_EPS = 1e-08
BF = jnp.bfloat16
F32 = jnp.float32
MESH = pl.DeviceIdType.MESH
ANY = pl.BlockSpec(memory_space=pl.ANY)
VMEM = pl.BlockSpec(memory_space=pltpu.VMEM)
HBM = pl.BlockSpec(memory_space=pltpu.HBM)


def rms_scale(values):
    return lax.rsqrt(jnp.mean(values * values, axis=-1, keepdims=True) + EPS)


def norm_back(upstream, source, scale):
    return scale * (
        upstream - source * scale * scale * jnp.mean(upstream * source, axis=-1, keepdims=True)
    )


def adam_update(weight, first_in, second_in, clipped, rate, decay):
    new_first = BETA1 * first_in + (1.0 - BETA1) * clipped
    new_second = BETA2 * second_in + (1.0 - BETA2) * clipped * clipped
    first_hat = new_first / (1.0 - BETA1**STEP)
    second_hat = new_second / (1.0 - BETA2**STEP)
    new_weight = weight - rate * (first_hat / (jnp.sqrt(second_hat) + ADAM_EPS) + decay * weight)
    return (new_weight, new_first, new_second)


def dot(a, b):
    return jnp.dot(a, b, preferred_element_type=F32)


def dot_t(a, b):
    return lax.dot_general(a, b, (((1,), (1,)), ((), ())), preferred_element_type=F32)


def t_dot(a, b):
    return lax.dot_general(a, b, (((0,), (0,)), ((), ())), preferred_element_type=F32)


def loads_of(pairs, sems, first=0):
    copies = [pltpu.make_async_copy(a, b, sems.at[first + i]) for i, (a, b) in enumerate(pairs)]
    for copy in copies:
        copy.start()
    return copies


def greet(peers):
    barrier = pltpu.get_barrier_semaphore()
    for peer in peers:
        pl.semaphore_signal(barrier, inc=1, device_id=peer, device_id_type=MESH)
    pl.semaphore_wait(barrier, len(peers))


def remote(src, dst, send, recv, peer):
    return pltpu.make_async_remote_copy(
        src_ref=src, dst_ref=dst, send_sem=send, recv_sem=recv, device_id=peer, device_id_type=MESH
    )


def cost(us):
    return pl.CostEstimate(flops=0, bytes_accessed=us * 3_600_000, transcendentals=0)


def params_of(number, vmem=62):
    return pltpu.CompilerParams(
        collective_id=number, has_side_effects=True, vmem_limit_bytes=vmem * 1024 * 1024
    )


def line_steps(n, me, make_right, make_left, meanwhile):
    for s in range(n - 1):

        @pl.when((me < n - 1) & (me >= s))
        def _():
            make_right(s).start()

        @pl.when((me > 0) & (me + s < n))
        def _():
            make_left(s).start()

        if s == 0:
            meanwhile()

        @pl.when(me - 1 - s >= 0)
        def _():
            make_right(s, me - 1 - s).wait_recv()

        @pl.when(me + 1 + s < n)
        def _():
            make_left(s, me + 1 + s).wait_recv()

    for s in range(n - 1):

        @pl.when((me < n - 1) & (me >= s))
        def _():
            make_right(s).wait_send()

        @pl.when((me > 0) & (me + s < n))
        def _():
            make_left(s).wait_send()


def pairs_of(n, me):
    half = n // 2
    parity, pair = me % 2, me // 2
    partner = me + 1 - 2 * parity
    ahead = [2 * ((pair + k) % half) + parity for k in range(1, half)]
    behind = [2 * ((pair + half - k) % half) + parity for k in range(1, half)]
    return half, parity, pair, partner, ahead, behind


def gather_dp_kernel(
    n, n_ctx, place_ref, doc_ref, freq_ref, x_ref, cos_out, sin_out, row_ref, col_ref, o_ref,
    cos_ref, sin_ref, sem_out, local, sr, rr, sl, rl,
):
    me, ctx = lax.axis_index("dp"), lax.axis_index("ctx")

    def here(d):
        return (d, ctx)

    greet([here((me + 1) % n), here((me + n - 1) % n)])
    own = pltpu.make_async_copy(x_ref, o_ref.at[me], local)
    own.start()

    def right(s, block=None):
        b = me - s if block is None else block
        return remote(x_ref if s == 0 else o_ref.at[b], o_ref.at[b], sr.at[s], rr.at[s], here(me + 1))

    def left(s, block=None):
        b = me + s if block is None else block
        return remote(x_ref if s == 0 else o_ref.at[b], o_ref.at[b], sl.at[s], rl.at[s], here(me - 1))

    outs = []

    def tables():
        length = cos_ref.shape[0] // n_ctx
        head = cos_ref.shape[1]
        sign = jnp.where(lax.broadcasted_iota(jnp.int32, (length, head), 1) < head // 2, -1.0, 1.0)
        row_ref[...] = jnp.zeros_like(row_ref)
        row_ref[1:2, :] = doc_ref[...].astype(F32)
        for c in range(n_ctx):
            rows = slice(c * length, (c + 1) * length)
            base = place_ref[c] * length
            angles = (base + lax.broadcasted_iota(jnp.int32, (length, head), 0)).astype(F32) * freq_ref[...]
            cos_ref[rows, :] = jnp.cos(angles)
            sin_ref[rows, :] = jnp.sin(angles) * sign
            row_ref[0:1, rows] = (base + lax.broadcasted_iota(jnp.int32, (1, length), 1)).astype(F32)
        col_ref[...] = jnp.transpose(row_ref[...])
        outs.extend(loads_of(((cos_ref, cos_out), (sin_ref, sin_out)), sem_out))

    line_steps(n, me, right, left, tables)
    for copy in outs + [own]:
        copy.wait()


def gather_dp(x, places, docs, number):
    n, n_ctx = lax.axis_size("dp"), lax.axis_size("ctx")
    seq = docs.shape[1]
    half = np.arange(HD // 2, dtype=np.float64) * 2.0 / HD
    freqs = np.tile(THETA**-half, 2)[None].astype(np.float32)
    *tables, out = pl.pallas_call(
        functools.partial(gather_dp_kernel, n, n_ctx),
        out_shape=(
            jax.ShapeDtypeStruct((seq, HD), F32),
            jax.ShapeDtypeStruct((seq, HD), F32),
            jax.ShapeDtypeStruct((8, seq), F32),
            jax.ShapeDtypeStruct((seq, 8), F32),
            jax.ShapeDtypeStruct((n,) + x.shape, x.dtype),
        ),
        in_specs=[pl.BlockSpec(memory_space=pltpu.SMEM), VMEM, VMEM, ANY],
        out_specs=(ANY,) * 2 + (VMEM,) * 2 + (ANY,),
        scratch_shapes=[pltpu.VMEM((seq, HD), F32)] * 2
        + [pltpu.SemaphoreType.DMA((2,))]
        + [pltpu.SemaphoreType.DMA] + [pltpu.SemaphoreType.DMA((n - 1,))] * 4,
        compiler_params=params_of(number),
        cost_estimate=cost(60),
        name="gather_dp",
    )(places, docs, jnp.asarray(freqs), x)
    return out.reshape((n * x.shape[0],) + x.shape[1:]), tables


def group_of(n_dp, n, dp, me):
    pair, parity = me // 2, me % 2
    return 2 * n_dp, 2 * dp + parity, lambda j: (j // 2, 2 * pair + j % 2)


def greet_all(n_dp, n, dp, me):
    partner = me + 1 - 2 * (me % 2)
    others = [(dp + k) % n_dp for k in range(1, n_dp)]
    greet([(dp, (me + k) % n) for k in range(1, n)] + [(d, c) for d in others for c in (me, partner)])


def across(mine, k, count):
    if count & (count - 1):
        return (mine + k) % count, (mine + count - k) % count
    bit, other = 1, mine
    while bit < count:
        if k & bit:
            other = other + bit - 2 * bit * ((other // bit) % 2)
        bit *= 2
    return other, other


def swap(src, dst, send, recv, count, mine, place):
    sends, receives = [], []
    for k in range(1, count):
        to, source = across(mine, k, count)
        sends.append(remote(src.at[to], dst.at[mine], send.at[k - 1], recv.at[k - 1], place(to)))
        receives.append(
            remote(src.at[mine], dst.at[source], send.at[k - 1], recv.at[k - 1], place(source))
        )
    for copy in sends:
        copy.start()
    return sends, receives


def tiles(total, tile, body):
    tile = min(total, tile)

    @pl.loop(0, total // tile)
    def _(j):
        body(pl.ds(pl.multiple_of(j * tile, tile), tile))


def reduce_ctx(n, dp, me, a_ref, w_ref, cols, o_ref, sa, ra, sb, rb, s1, r1, s2, r2, before=None):
    half, parity, pair, partner, ahead, behind = pairs_of(n, me)
    length, width = o_ref.shape

    def rows(block):
        return pl.ds(pl.multiple_of(block * length, length), length)

    first, second = [], []
    for k in range(half):
        target = (pair + k + 1) % half
        if before is not None:
            before(target, k == 0)

        def give(part):
            value = dot_t(a_ref[rows(2 * target + 1 - parity), :], w_ref[part, cols])
            sa[k, :, part] = value.astype(BF)

        tiles(width, 512, give)
        copy = remote(sa.at[k], ra.at[k], s1.at[k], r1.at[k], (dp, partner))
        copy.start()
        first.append(copy)
        copy.wait_recv()

        def keep(part):
            value = dot_t(a_ref[rows(2 * target + parity), :], w_ref[part, cols])
            value = value + ra[k, :, part].astype(F32)
            if k < half - 1:
                sb[k, :, part] = value.astype(BF)
            else:
                o_ref[:, part] = value

        tiles(width, 512, keep)
        if k < half - 1:
            copy = remote(sb.at[k], rb.at[k], s2.at[k], r2.at[k], (dp, 2 * target + parity))
            copy.start()
            second.append(copy)
    for k in range(half - 1):
        second[k].wait_recv()
        o_ref[...] += rb[k].astype(F32)
    return first + second


def load_rows(hbm, vmem, sems):
    half, n_dp, rows, _ = hbm.shape
    copies = []
    for d in range(n_dp):
        for p in range(half):
            part = pl.ds((d * half + p) * rows, rows)
            copies.append(pltpu.make_async_copy(hbm.at[p, d], vmem.at[part, :], sems.at[d * half + p]))
    for copy in copies:
        copy.start()
    return copies


def gather_group(n, dp, me, all_ref, length, sr, rr, sl, rl, sf, rf, process):
    parity = me % 2
    partner = me + 1 - 2 * parity

    def block(b, side):
        start = (2 * b + side) * length
        return all_ref.at[pl.ds(pl.multiple_of(start, length), length), :]

    def right(s, b):
        return remote(block(b, parity), block(b, parity), sr.at[s], rr.at[s], (dp + 1, me))

    def left(s, b):
        return remote(block(b, parity), block(b, parity), sl.at[s], rl.at[s], (dp - 1, me))

    def aside(b):
        return remote(block(b, parity), block(b, parity), sf.at[b], rf.at[b], (dp, partner))

    def from_aside(b):
        return remote(block(b, 1 - parity), block(b, 1 - parity), sf.at[b], rf.at[b], (dp, partner))

    for s in range(n):
        if s == 0:
            aside(dp).start()
        else:

            @pl.when(dp >= s)
            def _():
                right(s - 1, dp - s).wait_recv()

            @pl.when(dp + s < n)
            def _():
                left(s - 1, dp + s).wait_recv()

        @pl.when((dp < n - 1) & (dp >= s))
        def _():
            right(s, dp - s).start()

        @pl.when((dp > 0) & (dp + s < n))
        def _():
            left(s, dp + s).start()

        if s == 0:
            from_aside(dp).wait_recv()
            process(dp, True)
        else:

            @pl.when(dp >= s)
            def _():
                aside(dp - s).start()

            @pl.when(dp + s < n)
            def _():
                aside(dp + s).start()

            below = jnp.where(dp >= s, 1, 0)
            above = jnp.where(dp + s < n, 1, 0)

            @pl.loop(0, below + above)
            def _(j):
                b = jnp.where(j < below, dp - s, dp + s)
                from_aside(b).wait_recv()
                process(b, False)

    for s in range(n):

        @pl.when((dp < n - 1) & (dp >= s))
        def _():
            right(s, dp - s).wait_send()

        @pl.when((dp > 0) & (dp + s < n))
        def _():
            left(s, dp + s).wait_send()

        aside(s).wait_send()


def gather_sems(n_dp):
    return [pltpu.SemaphoreType.DMA((n_dp,))] * 6


def line_sum(n, dp, me, make, val, o_ref, buf, send, recv, sync, between=None):
    def move(way, d):
        to = jnp.where(way == 1, dp + 1, dp - 1)
        return remote(buf.at[way, d], buf.at[way, d], send.at[way, d], recv.at[way, d], (to, me))

    def steps(body):
        for j in range(1, n):

            @pl.loop(0, 2)
            def _(phase):
                way = jnp.where(2 * dp < n, 1 - phase, phase)
                d = jnp.where(way == 1, n - j, j - 1)
                first = jnp.where(way == 1, 0, n - 1)
                ahead = jnp.where(way == 1, d - dp, dp - d)

                @pl.when(ahead > 0)
                def _():
                    body(way, d, dp == first)

    def begin(way, d, starts):
        make(d, val.at[d])

        @pl.when(starts)
        def _():
            def put(part):
                buf[way, d, part, :] = val[d, part, :].astype(BF)

            tiles(val.shape[1], 32, put)
            move(way, d).start()

    def follow(way, d, starts):
        @pl.when(jnp.logical_not(starts))
        def _():
            move(way, d).wait_recv()

            def add(part):
                buf[way, d, part, :] = (val[d, part, :] + buf[way, d, part, :].astype(F32)).astype(BF)

            tiles(val.shape[1], 32, add)
            move(way, d).start()

    steps(begin)
    make(dp, o_ref)
    steps(follow)
    if between is not None:
        between()
    for way, first in ((1, 0), (0, n - 1)):

        @pl.when(dp != first)
        def _():
            move(way, dp).wait_recv()

            def add(part):
                o_ref[part, :] += buf[way, dp, part, :].astype(F32)

            tiles(val.shape[1], 32, add)

    sync()
    steps(lambda way, d, starts: move(way, d).wait_send())


def line_scratch(n_dp, length, width):
    return [
        pltpu.VMEM((n_dp, length, width), F32),
        pltpu.VMEM((2, n_dp, length, width), BF),
        pltpu.SemaphoreType.DMA((2, n_dp)),
        pltpu.SemaphoreType.DMA((2, n_dp)),
    ]


def part_of_pair(dp, me, a_ref, w_ref, length, sa, ra, s1, r1):
    parity = me % 2
    partner = me + 1 - 2 * parity

    def make(d, out):
        def rows(side):
            return pl.ds(pl.multiple_of((2 * d + side) * length, length), length)

        def give(part):
            sa[d, :, part] = dot_t(a_ref[rows(1 - parity), :], w_ref[part, :]).astype(BF)

        tiles(out.shape[1], 2048, give)
        copy = remote(sa.at[d], ra.at[d], s1.at[d], r1.at[d], (dp, partner))
        copy.start()

        def keep(part):
            out[:, part] = dot_t(a_ref[rows(parity), :], w_ref[part, :])

        tiles(out.shape[1], 2048, keep)
        copy.wait_recv()

        def add(part):
            out[part, :] += ra[d, part, :].astype(F32)

        tiles(length, 32, add)

    def done(n):
        for d in range(n):
            remote(sa.at[d], ra.at[d], s1.at[d], r1.at[d], (dp, partner)).wait_send()

    return make, done


def pair_scratch(n_dp, length, width):
    return [pltpu.VMEM((n_dp, length, width), BF)] * 2 + [pltpu.SemaphoreType.DMA((n_dp,))] * 2


def greet_group(n_dp, dp, me):
    partner = me + 1 - 2 * (me % 2)
    greet([(dp, partner)] + [((dp + k) % n_dp, me) for k in range(1, n_dp)])


def ff_forward_kernel(
    n_dp, n, h_ref, up_ref, gain_ref, gu_hbm, d_hbm, wo_hbm,
    res_ref, dm_ref, gp_ref, all_out, pre_out, hid_out, d_out, wo_out,
    all_ref, pre_ref, hid_ref, d_ref, gu_ref, acc, sem_gu, sem_d, sem_out, sd, rd, so, ro, fo, go, *rest,
):
    gather, pair_refs, line_refs = rest[:6], rest[6:10], rest[10:]
    dp, me = lax.axis_index("dp"), lax.axis_index("ctx")
    length, width = h_ref.shape
    fh = hid_ref.shape[1]
    half, parity, pair, partner, ahead, behind = pairs_of(n, me)
    loads_gu = load_rows(gu_hbm, gu_ref, sem_gu)
    mine = pl.ds(pl.multiple_of((2 * dp + me % 2) * length, length), length)
    all_ref[mine, :] = h_ref[...].astype(BF)
    greet(
        [(dp, partner)]
        + [((dp + k) % n_dp, me) for k in range(1, n_dp)]
        + [(dp, a) for a in ahead]
    )
    tall = d_hbm.shape[1]

    def down(d, p):
        return d_ref.at[pl.ds(pl.multiple_of((d * half + p) * tall, tall), tall), :]

    loads_d = [pltpu.make_async_copy(d_hbm.at[d], down(d, pair), sem_d.at[d]) for d in range(n_dp)]
    spreads = [
        remote(d_hbm.at[d], down(d, pair), sd.at[k, d], rd.at[k, d], (dp, a))
        for k, a in enumerate(ahead)
        for d in range(n_dp)
    ]
    for copy in spreads + loads_d:
        copy.start()

    def process(b, own):
        rows = pl.ds(pl.multiple_of(2 * b * length, 2 * length), 2 * length)
        if own:
            for copy in loads_gu:
                copy.wait()

        def hidden(part):
            second = pl.ds(pl.multiple_of(fh + part.start, part.size), part.size)
            gate = dot(all_ref[rows, :], gu_ref[:, part])
            upper = dot(all_ref[rows, :], gu_ref[:, second])
            pre_ref[rows, part] = gate
            pre_ref[rows, second] = upper
            hid_ref[rows, part] = (gate * jax.nn.sigmoid(gate) * upper).astype(BF)

        tiles(fh, 256, hidden)

    gather_group(n_dp, dp, me, all_ref, length, *gather, process)
    for copy in loads_d:
        copy.wait()
    for k, b in enumerate(behind):
        for d in range(n_dp):
            remote(d_hbm.at[d], down(d, b // 2), sd.at[k, d], rd.at[k, d], (dp, b)).wait_recv()

    outs = [
        pltpu.make_async_copy(ref, out, sem_out.at[i])
        for i, (ref, out) in enumerate(
            ((all_ref, all_out), (pre_ref, pre_out), (hid_ref, hid_out), (d_ref, d_out))
        )
    ]
    outs.append(pltpu.make_async_copy(wo_hbm, wo_out.at[me], sem_out.at[4]))
    spreads_wo = [
        remote(wo_hbm, wo_out.at[me], so.at[k], ro.at[k], (dp, a)) for k, a in enumerate(ahead + [partner])
    ]
    for copy in outs + spreads_wo:
        copy.start()
    make, done = part_of_pair(dp, me, hid_ref, d_ref, length, *pair_refs)

    gp_ref[...] = jnp.zeros_like(gp_ref)

    def finish(rows):
        out, up, gain = acc[rows, :], up_ref[rows, :].astype(F32), gain_ref[...]
        scale = rms_scale(out)
        res_ref[rows, :] = (h_ref[rows, :] + out * scale * gain).astype(BF)
        gp_ref[...] += jnp.sum(up * out * scale, axis=0, keepdims=True)
        dm_ref[rows, :] = norm_back(up * gain, out, scale).astype(BF)

    forwards = []

    def last():
        for k, b in enumerate(behind):
            remote(wo_hbm, wo_out.at[b], so.at[k], ro.at[k], (dp, b)).wait_recv()
            forward = remote(wo_out.at[b], wo_out.at[b], fo.at[k], go.at[k], (dp, partner))
            forward.start()
            forwards.append(forward)
        tiles(length, 16, finish)

    line_sum(n_dp, dp, me, make, line_refs[0], acc, *line_refs[1:], last)
    done(n_dp)
    spreads_wo[-1].wait_recv()
    for copy in forwards:
        copy.wait_recv()
    for copy in spreads + spreads_wo + forwards:
        copy.wait_send()
    for copy in outs:
        copy.wait()


def ff_forward(h1, up, gain, w_gu, w_d, w_o, number):
    n_dp, n = lax.axis_size("dp"), lax.axis_size("ctx")
    (length, width), fh = h1.shape, w_d.shape[2]
    tokens = 2 * n_dp * length
    half = n // 2
    low = jax.ShapeDtypeStruct((length, width), BF)
    return pl.pallas_call(
        functools.partial(ff_forward_kernel, n_dp, n),
        out_shape=(
            low,
            low,
            jax.ShapeDtypeStruct((1, width), F32),
            jax.ShapeDtypeStruct((tokens, width), BF),
            jax.ShapeDtypeStruct((tokens, 2 * fh), F32),
            jax.ShapeDtypeStruct((tokens, fh), BF),
            jax.ShapeDtypeStruct((width, fh), BF),
            jax.ShapeDtypeStruct((n,) + w_o.shape, BF),
        ),
        in_specs=[VMEM] * 3 + [ANY] * 3,
        out_specs=(VMEM,) * 3 + (ANY,) * 5,
        scratch_shapes=[
            pltpu.VMEM((tokens, width), BF),
            pltpu.VMEM((tokens, 2 * fh), F32),
            pltpu.VMEM((tokens, fh), BF),
            pltpu.VMEM((width, fh), BF),
            pltpu.VMEM((width, 2 * fh), BF),
            pltpu.VMEM((length, width), F32),
            pltpu.SemaphoreType.DMA((half * n_dp,)),
            pltpu.SemaphoreType.DMA((n_dp,)),
            pltpu.SemaphoreType.DMA((5,)),
            pltpu.SemaphoreType.DMA((half - 1, n_dp)),
            pltpu.SemaphoreType.DMA((half - 1, n_dp)),
            pltpu.SemaphoreType.DMA((half,)),
            pltpu.SemaphoreType.DMA((half,)),
            pltpu.SemaphoreType.DMA((half - 1,)),
            pltpu.SemaphoreType.DMA((half - 1,)),
        ]
        + gather_sems(n_dp)
        + pair_scratch(n_dp, length, width)
        + line_scratch(n_dp, length, width),
        compiler_params=params_of(number),
        cost_estimate=cost(90),
        name="ff_forward",
    )(h1, up, gain, w_gu, w_d, w_o)


def store_rows(n_dp, value_of, out):
    half, _, rows, _ = out.shape

    @pl.loop(0, n_dp * half)
    def _(r):
        out[r % half, r // half] = value_of(pl.ds(pl.multiple_of(r * rows, rows), rows)).astype(BF)


def ff_back_kernel(
    n_dp, dm_ref, hid_ref, d_hbm, pre_hbm, dgu_out, gd_out,
    dgu_ref, gd_ref, sem_out, all_ref, d_ref, pre_ref, acc, sem_d, sem_p, *gather,
):
    dp, me = lax.axis_index("dp"), lax.axis_index("ctx")
    length, width = dm_ref.shape
    fh = d_ref.shape[1]
    load = pltpu.make_async_copy(d_hbm, d_ref, sem_d)
    load.start()

    def rows_of(b):
        return pl.ds(pl.multiple_of(2 * b * length, 2 * length), 2 * length)

    def load_pre(b):
        return pltpu.make_async_copy(pre_hbm.at[rows_of(b), :], pre_ref.at[rows_of(b), :], sem_p.at[b])

    for k in range(n_dp):
        load_pre((dp + k) % n_dp).start()
    mine = pl.ds(pl.multiple_of((2 * dp + me % 2) * length, length), length)
    all_ref[mine, :] = dm_ref[...]
    greet_group(n_dp, dp, me)

    def process(b, own):
        rows = rows_of(b)
        if own:
            load.wait()
        load_pre(b).wait()

        def hidden(part):
            second = pl.ds(pl.multiple_of(fh + part.start, part.size), part.size)
            back = dot(all_ref[rows, :], d_ref[:, part])
            gate, upper = pre_ref[rows, part], pre_ref[rows, second]
            sig = jax.nn.sigmoid(gate)
            dgu_ref[rows, part] = (back * upper * sig * (1.0 + gate * (1.0 - sig))).astype(BF)
            dgu_ref[rows, second] = (back * gate * sig).astype(BF)

        tiles(fh, 256, hidden)

        def product(part):
            value = t_dot(all_ref[rows, part], hid_ref[rows, :])
            acc[part, :] = value if own else acc[part, :] + value

        tiles(width, 256, product)

    gather_group(n_dp, dp, me, all_ref, length, *gather, process)
    outs = loads_of(((dgu_ref, dgu_out),), sem_out)
    store_rows(n_dp, lambda part: acc[part, :], gd_ref)
    for copy in outs + loads_of(((gd_ref, gd_out),), sem_out, 1):
        copy.wait()


def ff_back(dm, hid, w_d, pre, rows, number):
    n_dp, half = lax.axis_size("dp"), lax.axis_size("ctx") // 2
    (length, width), fh = dm.shape, w_d.shape[1]
    tokens = 2 * n_dp * length
    return pl.pallas_call(
        functools.partial(ff_back_kernel, n_dp),
        out_shape=(
            jax.ShapeDtypeStruct((tokens, 2 * fh), BF),
            jax.ShapeDtypeStruct((half, n_dp, 2 * rows, fh), BF),
        ),
        in_specs=[VMEM, VMEM, ANY, ANY],
        out_specs=(ANY,) * 2,
        scratch_shapes=[
            pltpu.VMEM((tokens, 2 * fh), BF),
            pltpu.VMEM((half, n_dp, 2 * rows, fh), BF),
            pltpu.SemaphoreType.DMA((2,)),
            pltpu.VMEM((tokens, width), BF),
            pltpu.VMEM((width, fh), BF),
            pltpu.VMEM((tokens, 2 * fh), F32),
            pltpu.VMEM((width, fh), F32),
            pltpu.SemaphoreType.DMA,
            pltpu.SemaphoreType.DMA((n_dp,)),
        ]
        + gather_sems(n_dp),
        compiler_params=params_of(number),
        cost_estimate=cost(45),
        name="ff_back",
    )(dm, hid, w_d, pre)


def ff_scatter_kernel(
    n_dp, n, dgu_hbm, gu_hbm, all_hbm, dh_ref, gg_out, gv_out,
    gg_ref, gv_ref, dgu_ref, gu_ref, all_ref, acc, sem_gu, sem_all, sem_out, *rest,
):
    dp, me = lax.axis_index("dp"), lax.axis_index("ctx")
    length, width = dh_ref.shape
    pair_refs, line_refs = rest[:4], rest[4:]
    half, parity, pair, partner, ahead, behind = pairs_of(n, me)
    _, _, rows, fh = gg_ref.shape
    loads = load_rows(gu_hbm, gu_ref, sem_gu) + loads_of(((dgu_hbm, dgu_ref),), sem_out, 2)
    load = pltpu.make_async_copy(all_hbm, all_ref, sem_all)
    load.start()
    greet_group(n_dp, dp, me)
    for copy in loads:
        copy.wait()

    make, done = part_of_pair(dp, me, dgu_ref, gu_ref, length, *pair_refs)
    load.wait()
    tall = acc.shape[0]

    def grads():
        @pl.loop(0, width // tall)
        def _(j):
            acc[...] = t_dot(all_ref[:, pl.ds(pl.multiple_of(j * tall, tall), tall)], dgu_ref[...])
            for s in range(tall // rows):
                r = j * (tall // rows) + s
                part = slice(s * rows, (s + 1) * rows)
                gg_ref[r % half, r // half] = acc[part, :fh].astype(BF)
                gv_ref[r % half, r // half] = acc[part, fh:].astype(BF)

    val, *line = line_refs
    line_sum(n_dp, dp, me, make, val, dh_ref, *line, lambda: None, grads)
    done(n_dp)
    outs = [
        pltpu.make_async_copy(ref, out, sem_out.at[i])
        for i, (ref, out) in enumerate(((gg_ref, gg_out), (gv_ref, gv_out)))
    ]
    for copy in outs:
        copy.start()
    for copy in outs:
        copy.wait()


def ff_scatter(dgu, w_gu, h1_all, length, number):
    n_dp, n = lax.axis_size("dp"), lax.axis_size("ctx")
    width = h1_all.shape[1]
    grad = jax.ShapeDtypeStruct(w_gu.shape[:3] + (w_gu.shape[3] // 2,), BF)
    return pl.pallas_call(
        functools.partial(ff_scatter_kernel, n_dp, n),
        out_shape=(
            jax.ShapeDtypeStruct((length, width), F32),
            grad,
            grad,
        ),
        in_specs=[ANY] * 3,
        out_specs=(VMEM,) + (ANY,) * 2,
        scratch_shapes=[
            pltpu.VMEM(grad.shape, BF),
            pltpu.VMEM(grad.shape, BF),
            pltpu.VMEM(dgu.shape, BF),
            pltpu.VMEM((width, w_gu.shape[3]), BF),
            pltpu.VMEM(h1_all.shape, BF),
            pltpu.VMEM((256, w_gu.shape[3]), F32),
            pltpu.SemaphoreType.DMA((w_gu.shape[0] * n_dp,)),
            pltpu.SemaphoreType.DMA,
            pltpu.SemaphoreType.DMA((3,)),
        ]
        + pair_scratch(n_dp, length, width)
        + line_scratch(n_dp, length, width),
        compiler_params=params_of(number),
        cost_estimate=cost(50),
        name="ff_scatter",
    )(dgu, w_gu, h1_all)


def start_kernel(
    n_dp, n, p_hbm, x_ref, h_ref, o_ref, p_ref, y_ref, d_ref,
    p_all, g_ref, w_ref, v_ref, local, sg, rg, sa, ra, sv, rv, ss, rs, fs, fr,
):
    dp, me = lax.axis_index("dp"), lax.axis_index("ctx")
    half, parity, pair, partner, ahead, behind = pairs_of(n, me)
    count, mine, place = group_of(n_dp, n, dp, me)
    columns = p_all.shape[2]
    fh, hc = d_ref.shape[2], v_ref.shape[2]
    loads = [
        pltpu.make_async_copy(
            p_hbm.at[:, pl.ds(part * columns, columns)], p_all.at[part], local.at[part]
        )
        for part in range(4)
    ]
    for part in (1, 2, 0, 3):
        loads[part].start()
    greet_all(n_dp, n, dp, me)
    gathers = [
        remote(x_ref, y_ref.at[me], ss.at[k], rs.at[k], (dp, a))
        for k, a in enumerate(ahead + [partner])
    ]
    own_x = pltpu.make_async_copy(x_ref, y_ref.at[me], local.at[4])
    for copy in gathers + [own_x]:
        copy.start()
    for part in (1, 2):
        loads[part].wait()
        for j in range(count):
            g_ref[j, :, (part - 1) * fh : part * fh] = p_all[part, :, j * fh : (j + 1) * fh].astype(BF)
    sends, receives = swap(g_ref, h_ref, sg, rg, count, mine, place)
    loads[0].wait()
    for c in range(n):
        for matrix in range(4):
            start = (matrix * n + c) * hc
            value = p_all[0, :, start : start + hc].astype(BF)
            if matrix < 3:
                w_ref[c, :, matrix * hc : (matrix + 1) * hc] = value
            else:
                v_ref[c] = value
    for src, dst, send, recv in ((w_ref, o_ref, sa, ra), (v_ref, p_ref, sv, rv)):
        more, waits = swap(src, dst, send, recv, n, me, lambda c: (dp, c))
        sends += more
        receives += waits
    owns = [
        pltpu.make_async_copy(g_ref.at[mine], h_ref.at[mine], local.at[5]),
        pltpu.make_async_copy(w_ref.at[me], o_ref.at[me], local.at[6]),
        pltpu.make_async_copy(v_ref.at[me], p_ref.at[me], local.at[7]),
    ]
    for copy in owns:
        copy.start()
    loads[3].wait()
    for j in range(count):
        d_ref[j] = p_all[3, :, j * fh : (j + 1) * fh].astype(BF)
    forwards = []
    for k, b in enumerate(behind):
        remote(x_ref, y_ref.at[b], ss.at[k], rs.at[k], (dp, b)).wait_recv()
        forward = remote(y_ref.at[b], y_ref.at[b], fs.at[k], fr.at[k], (dp, partner))
        forward.start()
        forwards.append(forward)
    gathers[-1].wait_recv()
    for copy in receives:
        copy.wait_recv()
    for forward in forwards:
        forward.wait()
    for copy in sends + gathers:
        copy.wait_send()
    for copy in owns + [own_x]:
        copy.wait()


def start(params, x, number):
    n_dp, n = lax.axis_size("dp"), lax.axis_size("ctx")
    half, count = n // 2, 2 * n_dp
    (rows, columns), width = params.shape, x.shape[1]
    fh, hc = columns // 4 // count, width // n
    dma = pltpu.SemaphoreType.DMA
    g, w, v = (count, rows, 2 * fh), (n, rows, 3 * hc), (n, rows, hc)
    g_out, w_out, v_out, x_all, d_out = pl.pallas_call(
        functools.partial(start_kernel, n_dp, n),
        out_shape=(
            jax.ShapeDtypeStruct(g, BF),
            jax.ShapeDtypeStruct(w, BF),
            jax.ShapeDtypeStruct(v, BF),
            jax.ShapeDtypeStruct((n,) + x.shape, x.dtype),
            jax.ShapeDtypeStruct((count, rows, fh), BF),
        ),
        in_specs=[ANY] * 2,
        out_specs=(ANY,) * 4 + (VMEM,),
        scratch_shapes=[
            pltpu.VMEM((4, rows, columns // 4), F32),
            pltpu.VMEM(g, BF),
            pltpu.VMEM(w, BF),
            pltpu.VMEM(v, BF),
            dma((8,)),
        ]
        + [dma((count - 1,))] * 2
        + [dma((n - 1,))] * 4
        + [dma((half,))] * 2
        + [dma((half - 1,))] * 2,
        compiler_params=params_of(number),
        cost_estimate=cost(45),
        name="start",
    )(params, x)
    return g_out, w_out, v_out, x_all.reshape(-1, width), d_out


def collect_kernel(
    n_dp, n, g_ref, h_ref, a_ref, w_ref, b_ref, o_ref, h_out, y_ref,
    sum_ref, acc, pa, qa, pb, qb, local, s1, r1, s2, r2, sh, rh, *line_refs,
):
    dp, me = lax.axis_index("dp"), lax.axis_index("ctx")
    tall = acc.shape[0]
    count, index, place = group_of(n_dp, n, dp, me)
    greet_all(n_dp, n, dp, me)

    def make(d, out):
        def put(part):
            rows = pl.ds(pl.multiple_of(d * tall + part.start, part.size), part.size)
            out[part, :] = g_ref[rows, :].astype(F32)

        tiles(tall, 64, put)

    cols = slice(0, a_ref.shape[1])
    stay = pltpu.make_async_copy(h_ref.at[index], h_out.at[index], local)
    stay.start()
    later = []

    def between():
        later.extend(swap(h_ref, h_out, sh, rh, count, index, place))
        later.append(reduce_ctx(n, dp, me, a_ref, w_ref, cols, sum_ref, pa, qa, pb, qb, s1, r1, s2, r2))

    def last():
        def put(part):
            o_ref[part, :] = acc[part, :].astype(BF)

        tiles(tall, 64, put)

    def join(part):
        y_ref[part, :] = (sum_ref[part, :] + b_ref[part, :]).astype(BF)

    val, *line = line_refs
    line_sum(n_dp, dp, me, make, val, acc, *line, last, between)
    swaps, receives, sums = later
    tiles(y_ref.shape[0], 32, join)
    for copy in receives:
        copy.wait_recv()
    stay.wait()
    for copy in swaps + sums:
        copy.wait_send()


def collect(g, h, a, w, b, number):
    n_dp, n = lax.axis_size("dp"), lax.axis_size("ctx")
    tall, width = g.shape[0] // n_dp, g.shape[1]
    half, length, features = n // 2, a.shape[0] // n, w.shape[0]
    dma = pltpu.SemaphoreType.DMA
    return pl.pallas_call(
        functools.partial(collect_kernel, n_dp, n),
        out_shape=(
            jax.ShapeDtypeStruct((tall, width), BF),
            jax.ShapeDtypeStruct(h.shape, BF),
            jax.ShapeDtypeStruct((length, features), BF),
        ),
        in_specs=[VMEM, ANY, VMEM, VMEM, VMEM],
        out_specs=(VMEM, ANY, VMEM),
        scratch_shapes=[
            pltpu.VMEM((length, features), F32),
            pltpu.VMEM((tall, width), F32),
            pltpu.VMEM((half, length, features), BF),
            pltpu.VMEM((half, length, features), BF),
            pltpu.VMEM((half - 1, length, features), BF),
            pltpu.VMEM((half - 1, length, features), BF),
            dma,
            dma((half,)),
            dma((half,)),
            dma((half - 1,)),
            dma((half - 1,)),
            dma((2 * n_dp - 1,)),
            dma((2 * n_dp - 1,)),
        ]
        + line_scratch(n_dp, tall, width),
        compiler_params=params_of(number),
        cost_estimate=cost(70),
        name="collect",
    )(g, h, a, w, b)


def total_kernel(
    n_dp, n, qk_ref, wv_ref, wo_ref, u_ref, gg_ref, gd_ref, qk_gain, attn_gain, ff_gain, p_hbm, m_hbm, v_hbm,
    ga_ref, gu_ref, o_ref, p_out, m_out, v_out,
    sb, mine, buf, part, all_parts, square, buf_s, part_s, all_s, local, sx, rx, sh, rh,
    ss, rs, st, rt, s1, r1, s2, r2, sem_copy,
):
    dp, me = lax.axis_index("dp"), lax.axis_index("ctx")
    hc = wv_ref.shape[2]
    count, index, place = group_of(n_dp, n, dp, me)
    greet_all(n_dp, n, dp, me)
    swaps, receives = swap(u_ref, gu_ref, sh, rh, count, index, place)
    stay = pltpu.make_async_copy(u_ref.at[index], gu_ref.at[index], local)
    stay.start()
    moves = [
        pltpu.make_async_copy(source, target, sem_copy.at[i])
        for i, (source, target) in enumerate(((p_hbm, p_out), (m_hbm, m_out), (v_hbm, v_out)))
    ]
    for copy in moves:
        copy.start()
    sb[:, :, : 2 * hc] = qk_ref[...]
    sb[:, :, 2 * hc : 3 * hc] = wv_ref[...]
    more, waits = swap(sb, ga_ref, sx, rx, n, me, lambda c: (dp, c))
    ga_ref[me] = sb[me]

    def squares(ref):
        acc = jnp.zeros((ref.shape[1], ref.shape[2]), F32)
        for i in range(ref.shape[0]):
            block = ref[i].astype(F32)
            acc += block * block
        return jnp.sum(jnp.sum(acc, axis=0, keepdims=True), axis=1, keepdims=True)

    copies = swaps + more

    def sum_all(value, rows, along, columns, send, recv, send_dp, recv_dp):
        for k in range(1, n):
            copy = remote(value, rows.at[me], send.at[k - 1], recv.at[k - 1], (dp, (me + k) % n))
            copy.start()
            copies.append(copy)
        rows[me] = value[...]
        for k in range(1, n):
            source = (me + n - k) % n
            remote(value, rows.at[source], send.at[k - 1], recv.at[k - 1], (dp, source)).wait_recv()
        acc = rows[0]
        for j in range(1, n):
            acc = acc + rows[j]
        along[...] = acc
        columns[dp] = acc
        for k in range(1, n_dp):
            to = (dp + k) % n_dp
            copy = remote(along, columns.at[dp], send_dp.at[k - 1], recv_dp.at[k - 1], (to, me))
            copy.start()
            copies.append(copy)
        for k in range(1, n_dp):
            source = (dp + n_dp - k) % n_dp
            remote(along, columns.at[source], send_dp.at[k - 1], recv_dp.at[k - 1], (source, me)).wait_recv()
        acc = columns[0]
        for j in range(1, n_dp):
            acc = acc + columns[j]
        return acc

    mine[...] = jnp.zeros_like(mine)
    mine[0:2, pl.ds(pl.multiple_of(me * hc, hc), hc)] = qk_gain[...]
    mine[2:3, :] = attn_gain[...]
    mine[3:4, :] = ff_gain[...]
    o_ref[...] = sum_all(mine, buf, part, all_parts, ss, rs, st, rt)
    total = squares(gg_ref) + squares(gd_ref) + squares(wo_ref)
    for copy in waits:
        copy.wait_recv()
    total += squares(ga_ref)
    for copy in receives:
        copy.wait_recv()
    stay.wait()
    total += squares(gu_ref)
    square[...] = jnp.broadcast_to(total, square.shape)
    total = sum_all(square, buf_s, part_s, all_s, s1, r1, s2, r2)
    o_ref[4:5, :] = jnp.broadcast_to(total[0:1, 0:1], (1, o_ref.shape[1]))
    for copy in copies:
        copy.wait_send()
    for copy in moves:
        copy.wait()


def total_over(qk, wv, wo, u, gg, gd, qk_gain, attn_gain, ff_gain, masters, number):
    n_dp, n = lax.axis_size("dp"), lax.axis_size("ctx")
    rows, hc = qk.shape[0] // n, wv.shape[1]
    shape = (8, attn_gain.shape[1])
    dma = pltpu.SemaphoreType.DMA
    return pl.pallas_call(
        functools.partial(total_kernel, n_dp, n),
        out_shape=(
            jax.ShapeDtypeStruct((n, rows, 3 * hc), BF),
            jax.ShapeDtypeStruct(u.shape, BF),
            jax.ShapeDtypeStruct(shape, F32),
            *[jax.ShapeDtypeStruct(a.shape, F32) for a in masters],
        ),
        in_specs=[VMEM] * 3 + [ANY] + [VMEM] * 5 + [HBM] * 3,
        out_specs=(VMEM,) * 3 + (ANY,) * 3,
        scratch_shapes=[
            pltpu.VMEM((n, rows, 3 * hc), BF),
            pltpu.VMEM(shape, F32),
            pltpu.VMEM((n,) + shape, F32),
            pltpu.VMEM(shape, F32),
            pltpu.VMEM((n_dp,) + shape, F32),
            pltpu.VMEM((8, 128), F32),
            pltpu.VMEM((n, 8, 128), F32),
            pltpu.VMEM((8, 128), F32),
            pltpu.VMEM((n_dp, 8, 128), F32),
            dma,
            dma((n - 1,)),
            dma((n - 1,)),
            dma((2 * n_dp - 1,)),
            dma((2 * n_dp - 1,)),
            dma((n - 1,)),
            dma((n - 1,)),
            dma((n_dp - 1,)),
            dma((n_dp - 1,)),
            dma((n - 1,)),
            dma((n - 1,)),
            dma((n_dp - 1,)),
            dma((n_dp - 1,)),
            dma((3,)),
        ],
        compiler_params=params_of(number, 19),
        cost_estimate=cost(35),
        name="total",
    )(
        qk.reshape(n, rows, 2 * hc),
        wv.reshape(n, rows, hc),
        wo[None],
        u,
        gg,
        gd,
        qk_gain,
        attn_gain,
        ff_gain,
        *masters,
    )


def adam_kernel(
    sum_ref, gp_ref, gm_ref, gv_ref, p_ref, m_ref, v_ref, ga_ref, go_ref, gg_ref, gu_ref, gd_ref,
    norm_ref, gp_out, gm_out, gv_out, po_ref, mo_ref, vo_ref, g_ref, factor_ref,
):
    part = pl.program_id(0)

    @pl.when((part == 0) & (pl.program_id(1) == 0))
    def _():
        gain = sum_ref[0:4, :]
        squares = jnp.sum(jnp.sum(gain * gain, axis=0, keepdims=True), axis=1, keepdims=True)
        norm = jnp.sqrt(sum_ref[4:5, 0:1] + squares)
        norm_ref[...] = norm
        factor = CLIP / (norm + 1e-06)
        factor_ref[...] = jnp.broadcast_to(factor, factor_ref.shape)
        new = adam_update(gp_ref[...], gm_ref[...], gv_ref[...], gain * factor, GAIN_RATE, 0.0)
        gp_out[...], gm_out[...], gv_out[...] = new

    n, _, three = ga_ref.shape
    hc = three // 3
    fs = gd_ref.shape[2]

    @pl.when(part == 0)
    def _():
        g_ref[:, 3 * n * hc :] = go_ref[...].astype(F32)
        for matrix in range(3):
            for c in range(n):
                start = (matrix * n + c) * hc
                g_ref[:, start : start + hc] = ga_ref[c, :, matrix * hc : (matrix + 1) * hc].astype(F32)

    for index, ref in ((1, gg_ref), (2, gu_ref), (3, gd_ref)):

        @pl.when(part == index)
        def _():
            for d in range(ref.shape[0]):
                g_ref[:, d * fs : (d + 1) * fs] = ref[d].astype(F32)

    clipped = g_ref[...] * factor_ref[0:1, 0:1]
    new_m = BETA1 * m_ref[...] + (1.0 - BETA1) * clipped
    new_v = BETA2 * v_ref[...] + (1.0 - BETA2) * (clipped * clipped)
    hat = new_v * (1.0 / (1.0 - BETA2**STEP))
    root = hat * lax.rsqrt(jnp.maximum(hat, 1e-36)) + ADAM_EPS
    change = (new_m * (RATE / (1.0 - BETA1**STEP))) * pl.reciprocal(root, approx=True)
    po_ref[...] = p_ref[...] * (1.0 - RATE * DECAY) - change
    mo_ref[...] = new_m
    vo_ref[...] = new_v


def adam(sums, gains, gains_first, gains_second, params, first, second, ga, go, gg, gu, gd):
    rows, columns = params.shape
    n, n_dp, fs = ga.shape[0], gd.shape[0], gd.shape[2]
    block = min(rows, 32)
    steps = rows // block
    wide = pl.BlockSpec((block, columns // 4), lambda i, r: (r, i))
    small = pl.BlockSpec(gains.shape, lambda i, r: (0, 0))
    return pl.pallas_call(
        adam_kernel,
        grid=(4, steps),
        out_shape=(jax.ShapeDtypeStruct((1, 1), F32),)
        + (jax.ShapeDtypeStruct(gains.shape, F32),) * 3
        + (jax.ShapeDtypeStruct(params.shape, F32),) * 3,
        in_specs=[
            pl.BlockSpec(sums.shape, lambda i, r: (0, 0)),
            small,
            small,
            small,
            wide,
            wide,
            wide,
            pl.BlockSpec((n, block, ga.shape[2]), lambda i, r: (0, jnp.where(i == 0, r, steps - 1), 0)),
            pl.BlockSpec((block, go.shape[1]), lambda i, r: (jnp.where(i == 0, r, steps - 1), 0)),
            *[
                pl.BlockSpec(
                    (n_dp, block, fs),
                    lambda i, r, part=part: (
                        0,
                        jnp.where(i < part, 0, jnp.where(i == part, r, steps - 1)),
                        0,
                    ),
                )
                for part in (1, 2, 3)
            ],
        ],
        out_specs=(pl.BlockSpec((1, 1), lambda i, r: (0, 0)),) + (small,) * 3 + (wide,) * 3,
        scratch_shapes=[pltpu.VMEM((block, columns // 4), F32), pltpu.VMEM((8, 128), F32)],
        compiler_params=pltpu.CompilerParams(vmem_limit_bytes=22 * 1024 * 1024),
        name="adam",
    )(sums, gains, gains_first, gains_second, params, first, second, ga, go, gg, gu, gd)


def row_sums(value, row):
    pick = lax.broadcasted_iota(jnp.int32, (8, value.shape[1]), 0) == row
    return lax.dot_general(
        pick.astype(F32),
        value,
        (((1,), (1,)), ((), ())),
        preferred_element_type=F32,
        precision=lax.Precision.HIGHEST,
    )


def exchange(n, dp, me, buf, ss, rs):
    copies = []
    for k in range(1, n):
        copy = remote(buf.at[me], buf.at[me], ss.at[k - 1], rs.at[k - 1], (dp, (me + k) % n))
        copy.start()
        copies.append(copy)
    for k in range(1, n):
        source = (me + n - k) % n
        remote(buf.at[me], buf.at[source], ss.at[k - 1], rs.at[k - 1], (dp, source)).wait_recv()
    total = buf[0]
    for j in range(1, n):
        total = total + buf[j]
    for copy in copies:
        copy.wait_send()
    return total


def turn(value, cos, sine):
    return value * cos + pltpu.roll(value, HD // 2, 1) * sine


def mask_of(rows, info_col, info_row):
    pos_i, doc_i = info_col[rows, 0:1], info_col[rows, 1:2]
    return (info_row[1:2, :] == doc_i) & (info_row[0:1, :] <= pos_i)


def attend_kernel(
    n_dp, n, x_hbm, w_hbm, wo_ref, d_ref, t_ref, norm_ref, gain_ref, cos_ref, sin_ref, col_ref, row_ref,
    y_ref, h_ref, q_out, k_out, v_out, o_ref, pre_out, scale_ref, lse_ref, wo_all, d_out,
    buf, pa, qa, pb, qb, ss, rs, s1, r1, s2, r2, sw, rw, sd, rd, local,
    x_ref, w_ref, q_ref, k_ref, v_ref, pre_ref, sem_in, sem_out,
):
    dp, me = lax.axis_index("dp"), lax.axis_index("ctx")
    loads = loads_of(((x_hbm, x_ref), (w_hbm, w_ref)), sem_in)
    seq, width = x_ref.shape
    hc = o_ref.shape[1]
    block = min(seq, 256)
    count, mine, place = group_of(n_dp, n, dp, me)
    greet_all(n_dp, n, dp, me)
    piece = wo_ref.shape[0]

    def part_of(d):
        return wo_all.at[pl.ds(pl.multiple_of(d * piece, piece), piece), :]

    owns = [
        pltpu.make_async_copy(wo_ref, part_of(dp), local.at[0]),
        pltpu.make_async_copy(d_ref.at[mine], d_out.at[mine], local.at[1]),
    ]
    behind_wo = [
        remote(wo_ref, part_of(dp), sw.at[k - 1], rw.at[k - 1], (across(dp, k, n_dp)[0], me))
        for k in range(1, n_dp)
    ]
    for copy in behind_wo + owns:
        copy.start()
    behind_d, receives = swap(d_ref, d_out, sd, rd, count, mine, place)

    for copy in loads:
        copy.wait()

    @pl.loop(0, seq // block)
    def _(i):
        rows = pl.ds(pl.multiple_of(i * block, block), block)
        value = dot(x_ref[rows, :], w_ref[...])
        pre_ref[rows, :] = value[:, : 2 * hc]
        v_ref[rows, :] = value[:, 2 * hc :].astype(BF)
        squares = value[:, : 2 * hc] * value[:, : 2 * hc]
        buf[me, :, rows] = row_sums(squares[:, :hc], 0) + row_sums(squares[:, hc:], 1)

    scale_ref[...] = jnp.transpose(lax.rsqrt(exchange(n, dp, me, buf, ss, rs) / width + EPS))

    @pl.loop(0, seq // block)
    def _(i):
        rows = pl.ds(pl.multiple_of(i * block, block), block)
        cos, sine = cos_ref[rows, :], sin_ref[rows, :]
        for which, ref, factor in ((0, q_ref, HD ** (-0.5)), (1, k_ref, 1.0)):
            scale = scale_ref[rows, which : which + 1]
            for start in range(0, hc, HD):
                part = slice(start, start + HD)
                value = pre_ref[rows, which * hc + start : which * hc + start + HD] * scale
                ref[rows, part] = (
                    turn(value * gain_ref[which : which + 1, part], cos, sine) * factor
                ).astype(BF)

    def attention(pair, first):
        size = 2 * (seq // n)
        rows = pl.ds(pl.multiple_of(pair * size, size), size)
        visible = mask_of(rows, col_ref, row_ref)
        for head in range(hc // HD):
            part = slice(head * HD, (head + 1) * HD)
            scores = jnp.where(visible, dot_t(q_ref[rows, part], k_ref[:, part]), -jnp.inf)
            top = jnp.max(scores, axis=1, keepdims=True)
            weights = jnp.exp(scores - top)
            total = jnp.sum(weights, axis=1, keepdims=True)
            o_ref[rows, part] = (dot(weights.astype(BF), v_ref[:, part]) / total).astype(BF)
            lse_ref[rows, head : head + 1] = top + jnp.log(total)
        if first:
            owns[0].wait()
            for k in range(1, n_dp):
                _, source = across(dp, k, n_dp)
                remote(wo_ref, part_of(source), sw.at[k - 1], rw.at[k - 1], (source, me)).wait_recv()

    outs = loads_of(((pre_ref, pre_out), (q_ref, q_out), (k_ref, k_out), (v_ref, v_out)), sem_out)
    cols = slice(0, hc)
    sums = reduce_ctx(
        n, dp, me, o_ref, wo_all, cols, y_ref, pa, qa, pb, qb, s1, r1, s2, r2, before=attention
    )

    def finish(rows):
        branch = y_ref[rows, :]
        h_ref[rows, :] = t_ref[rows, :].astype(F32) + branch * rms_scale(branch) * norm_ref[...]

    tiles(y_ref.shape[0], 16, finish)
    for copy in receives:
        copy.wait_recv()
    for copy in sums + behind_wo + behind_d:
        copy.wait_send()
    for copy in outs + owns[1:]:
        copy.wait()


def attend(x_all, w, wo, d, tokens, norm, gain, cos, sine, info_col, info_row, number):
    n_dp, n = lax.axis_size("dp"), lax.axis_size("ctx")
    seq, width = x_all.shape
    half, length, hc = n // 2, seq // n, w.shape[1] // 3
    dma = pltpu.SemaphoreType.DMA
    low = jax.ShapeDtypeStruct((seq, hc), BF)
    return pl.pallas_call(
        functools.partial(attend_kernel, n_dp, n),
        out_shape=(
            jax.ShapeDtypeStruct((length, width), F32),
            jax.ShapeDtypeStruct((length, width), F32),
            low,
            low,
            low,
            low,
            jax.ShapeDtypeStruct((seq, 2 * hc), F32),
            jax.ShapeDtypeStruct((seq, 8), F32),
            jax.ShapeDtypeStruct((seq, 8), F32),
            jax.ShapeDtypeStruct((width, hc), BF),
            jax.ShapeDtypeStruct(d.shape, BF),
        ),
        in_specs=[ANY] * 4 + [VMEM] * 7,
        out_specs=(VMEM,) * 2 + (ANY,) * 3 + (VMEM, ANY) + (VMEM,) * 3 + (ANY,),
        scratch_shapes=[
            pltpu.VMEM((n, 8, seq), F32),
            pltpu.VMEM((half, length, width), BF),
            pltpu.VMEM((half, length, width), BF),
            pltpu.VMEM((half - 1, length, width), BF),
            pltpu.VMEM((half - 1, length, width), BF),
            dma((n - 1,)),
            dma((n - 1,)),
            dma((half,)),
            dma((half,)),
            dma((half - 1,)),
            dma((half - 1,)),
            dma((n_dp - 1,)),
            dma((n_dp - 1,)),
            dma((2 * n_dp - 1,)),
            dma((2 * n_dp - 1,)),
            dma((2,)),
            pltpu.VMEM(x_all.shape, BF),
            pltpu.VMEM(w.shape, BF),
            *[pltpu.VMEM((seq, hc), BF)] * 3,
            pltpu.VMEM((seq, 2 * hc), F32),
            dma((2,)),
            dma((4,)),
        ],
        compiler_params=params_of(number),
        cost_estimate=cost(60),
        name="attend",
    )(x_all, w, wo, d, tokens, norm, gain, cos, sine, info_col, info_row)


def slab_give(n_dp, dp, me, g_ref, co_ref, sw, rw):
    tall = co_ref.shape[1]
    gives = []
    for k in range(1, n_dp):
        to, _ = across(dp, k, n_dp)
        part = pl.ds(pl.multiple_of(to * tall, tall), tall)
        copy = remote(g_ref.at[part, :], co_ref.at[k - 1], sw.at[k - 1], rw.at[k - 1], (to, me))
        copy.start()
        gives.append(copy)
    return gives


def slab_sum(dp, gives, g_ref, co_ref, out_ref):
    tall = co_ref.shape[1]
    total = g_ref[pl.ds(pl.multiple_of(dp * tall, tall), tall), :].astype(F32)
    for k, copy in enumerate(gives):
        copy.wait_recv()
        total = total + co_ref[k].astype(F32)
    out_ref[...] = total.astype(BF)


def greet_wide_group(n_dp, dp, me):
    partner = me + 1 - 2 * (me % 2)
    others = [(dp + k) % n_dp for k in range(1, n_dp)]
    greet([(dp, partner)] + [(d, c) for d in others for c in (me, partner)])


def attend_back_kernel(
    n_dp, n, sum_ref, up_ref, branch_ref, norm_ref, wo_hbm, h_ref, o_hbm, col_ref, row_ref, q_hbm, k_hbm, v_hbm, lse_ref,
    x_hbm, gain_ref, cos_hbm, sin_hbm, pre_hbm, scale_ref,
    dh_ref, gp_ref, d_ref, gain_out, g_ref, wv_ref, wo_ref, h_out,
    q_ref, k_ref, v_ref, cos_ref, sin_ref, x_ref, pre_ref, wall_ref, db_ref, mix_ref, give_ref, e_ref, do_ref, o_ref, dq_ref, dk_ref, dv_ref, mean_ref, buf, go_ref, co_ref, gv_ref, cv_ref,
    sh, rh, local, sw, rw, sv, rv, ss, rs, sc, rc, sx, rx,
):
    dp, me = lax.axis_index("dp"), lax.axis_index("ctx")
    seq, hc = q_ref.shape
    load_wo = pltpu.make_async_copy(wo_hbm, wall_ref, local.at[2])
    load_wo.start()
    later = [
        pltpu.make_async_copy(src, dst, local.at[i])
        for i, (src, dst) in enumerate(((x_hbm, x_ref), (pre_hbm, pre_ref)), 4)
    ]
    load = pltpu.make_async_copy(o_hbm, o_ref, local.at[1])
    load.start()
    tables = ((q_hbm, q_ref), (k_hbm, k_ref), (v_hbm, v_ref), (cos_hbm, cos_ref), (sin_hbm, sin_ref))
    loads = loads_of(tables, local, 6)
    length, width = dh_ref.shape
    block = min(seq, 256)
    count, index, place = group_of(n_dp, n, dp, me)
    greet_all(n_dp, n, dp, me)
    swaps, receives = swap(h_ref, h_out, sh, rh, count, index, place)
    stay = pltpu.make_async_copy(h_ref.at[index], h_out.at[index], local.at[0])
    stay.start()

    gp_ref[...] = jnp.zeros_like(gp_ref)

    def finish(rows):
        grad, branch = sum_ref[rows, :] + up_ref[rows, :].astype(F32), branch_ref[rows, :]
        scale = rms_scale(branch)
        dh_ref[rows, :] = grad
        gp_ref[...] += jnp.sum(grad * branch * scale, axis=0, keepdims=True)
        db_ref[rows, :] = norm_back(grad * norm_ref[...], branch, scale).astype(BF)

    tiles(length, 16, finish)
    load_wo.wait()

    def mine(c):
        return pl.ds(pl.multiple_of(c * length, length), length)

    def send(k):
        to = (me + k) % n
        return remote(give_ref.at[to], do_ref.at[mine(me), :], sx.at[k - 1], rx.at[k - 1], (dp, to))

    def receive(k):
        source = (me + n - k) % n
        return remote(give_ref.at[me], do_ref.at[mine(source), :], sx.at[k - 1], rx.at[k - 1], (dp, source))

    share = width // n
    own = share // n_dp
    for c in range(n):
        for d in range(n_dp):
            start, source = c * share + d * own, (d * n + c) * own
            mix_ref[:, start : start + own] = db_ref[:, source : source + own]

    def share_of(c):
        return mix_ref.at[:, pl.ds(pl.multiple_of(c * share, share), share)]

    def send_share(k):
        to = (me + k) % n
        return remote(share_of(to), e_ref.at[mine(me), :], sc.at[k - 1], rc.at[k - 1], (dp, to))

    def receive_share(k):
        source = (me + n - k) % n
        return remote(share_of(me), e_ref.at[mine(source), :], sc.at[k - 1], rc.at[k - 1], (dp, source))

    stay_share = pltpu.make_async_copy(share_of(me), e_ref.at[mine(me), :], local.at[3])
    stay_share.start()

    @pl.loop(1, n)
    def _(k):
        to = (me + k) % n
        send_share(k).start()
        give_ref[to] = dot(db_ref[...], wall_ref[to]).astype(BF)
        send(k).start()

    do_ref[mine(me), :] = dot(db_ref[...], wall_ref[me]).astype(BF)
    for k in range(1, n):
        receive(k).wait_recv()
        receive_share(k).wait_recv()
    for k in range(1, n):
        send(k).wait_send()
        send_share(k).wait_send()
    stay_share.wait()
    load.wait()
    for copy in later:
        copy.start()

    @pl.loop(0, n)
    def _(c):
        go_ref[:, pl.ds(pl.multiple_of(c * hc, hc), hc)] = t_dot(e_ref[...], o_ref[c]).astype(BF)

    gives = slab_give(n_dp, dp, me, go_ref, co_ref, sw, rw)
    dk_ref[...] = jnp.zeros_like(dk_ref)
    dv_ref[...] = jnp.zeros_like(dv_ref)

    def attention(i):
        rows = pl.ds(pl.multiple_of(i * block, block), block)
        visible = mask_of(rows, col_ref, row_ref)
        for head in range(hc // HD):
            part = slice(head * HD, (head + 1) * HD)
            query, key, value, back = q_ref[rows, part], k_ref[:, part], v_ref[:, part], do_ref[rows, part]
            scores = jnp.where(visible, dot_t(query, key), -jnp.inf)
            probs = jnp.exp(scores - lse_ref[rows, head : head + 1])
            d_probs = dot_t(back, value)
            delta = jnp.sum(probs * d_probs, axis=1, keepdims=True)
            d_scores = (probs * (d_probs - delta)).astype(BF)
            dq_ref[rows, part] = dot(d_scores, key)
            dk_ref[:, part] += t_dot(d_scores, query)
            dv_ref[:, part] += t_dot(probs.astype(BF), back)

    for copy in loads:
        copy.wait()
    pl.loop(0, seq // block)(attention)

    for copy in later:
        copy.wait()
    d_ref[:, 2 * hc :] = dv_ref[...].astype(BF)

    def values(part):
        gv_ref[part, :] = t_dot(x_ref[:, part], d_ref[:, 2 * hc :]).astype(BF)

    tiles(width, 256, values)
    gives_v = slab_give(n_dp, dp, me, gv_ref, cv_ref, sv, rv)
    gain_out[...] = jnp.zeros_like(gain_out)

    @pl.loop(0, seq // block)
    def _(i):
        rows = pl.ds(pl.multiple_of(i * block, block), block)
        cos, sine = cos_ref[rows, :], sin_ref[rows, :]
        sums = jnp.zeros((8, block), F32)
        for which, ref, factor in ((0, dq_ref, HD ** (-0.5)), (1, dk_ref, 1.0)):
            scale = scale_ref[rows, which : which + 1]
            for start in range(0, hc, HD):
                part = slice(start, start + HD)
                pre = pre_ref[rows, which * hc + start : which * hc + start + HD]
                value = turn(ref[rows, part] * factor, cos, -sine)
                gain_out[which : which + 1, part] += jnp.sum(value * pre * scale, axis=0, keepdims=True)
                value = value * gain_ref[which : which + 1, part]
                ref[rows, part] = value
                sums += row_sums(value * pre, which)
        buf[me, :, rows] = sums

    mean_ref[...] = jnp.transpose(exchange(n, dp, me, buf, ss, rs) / width)

    @pl.loop(0, seq // block)
    def _(i):
        rows = pl.ds(pl.multiple_of(i * block, block), block)
        for which, ref in ((0, dq_ref), (1, dk_ref)):
            scale = scale_ref[rows, which : which + 1]
            mean = mean_ref[rows, which : which + 1]
            cols = slice(which * hc, (which + 1) * hc)
            value = scale * (ref[rows, :] - pre_ref[rows, cols] * (scale * scale * mean))
            d_ref[rows, cols] = value.astype(BF)

    def product(part):
        g_ref[part, :] = t_dot(x_ref[:, part], d_ref[:, : 2 * hc]).astype(BF)

    tiles(width, 256, product)
    slab_sum(dp, gives, go_ref, co_ref, wo_ref)
    slab_sum(dp, gives_v, gv_ref, cv_ref, wv_ref)
    for copy in receives:
        copy.wait_recv()
    for copy in swaps + gives + gives_v:
        copy.wait_send()
    stay.wait()


def attend_back(sums, up, branch, norm, wo_all, h, o_all, info_col, info_row, q, k, v, lse, x, gain, cos, sine, pre, scale, number):
    n_dp, n = lax.axis_size("dp"), lax.axis_size("ctx")
    (seq, hc), (length, width) = q.shape, branch.shape
    share = width // n
    dma = pltpu.SemaphoreType.DMA
    return pl.pallas_call(
        functools.partial(attend_back_kernel, n_dp, n),
        out_shape=(
            jax.ShapeDtypeStruct((length, width), F32),
            jax.ShapeDtypeStruct((1, width), F32),
            jax.ShapeDtypeStruct((seq, 3 * hc), BF),
            jax.ShapeDtypeStruct((2, hc), F32),
            jax.ShapeDtypeStruct((width, 2 * hc), BF),
            jax.ShapeDtypeStruct((width // n_dp, hc), BF),
            jax.ShapeDtypeStruct((share // n_dp, n * hc), BF),
            jax.ShapeDtypeStruct(h.shape, BF),
        ),
        in_specs=[VMEM] * 4 + [ANY] * 3 + [VMEM] * 2 + [ANY] * 3 + [VMEM, ANY, VMEM] + [ANY] * 3 + [VMEM],
        out_specs=(VMEM,) * 7 + (ANY,),
        scratch_shapes=[
            *[pltpu.VMEM((seq, hc), BF)] * 3,
            *[pltpu.VMEM(cos.shape, F32)] * 2,
            pltpu.VMEM(x.shape, BF),
            pltpu.VMEM(pre.shape, F32),
            pltpu.VMEM(wo_all.shape, BF),
            pltpu.VMEM((length, width), BF),
            pltpu.VMEM((length, width), BF),
            pltpu.VMEM((n, length, hc), BF),
            pltpu.VMEM((seq, share), BF),
            pltpu.VMEM((seq, hc), BF),
            pltpu.VMEM(o_all.shape, BF),
            pltpu.VMEM((seq, hc), F32),
            pltpu.VMEM((seq, hc), F32),
            pltpu.VMEM((seq, hc), F32),
            pltpu.VMEM((seq, 8), F32),
            pltpu.VMEM((n, 8, seq), F32),
            pltpu.VMEM((share, n * hc), BF),
            pltpu.VMEM((n_dp - 1, share // n_dp, n * hc), BF),
            pltpu.VMEM((width, hc), BF),
            pltpu.VMEM((n_dp - 1, width // n_dp, hc), BF),
            dma((2 * n_dp - 1,)),
            dma((2 * n_dp - 1,)),
            dma((11,)),
            dma((n_dp - 1,)),
            dma((n_dp - 1,)),
            dma((n_dp - 1,)),
            dma((n_dp - 1,)),
            dma((n - 1,)),
            dma((n - 1,)),
            dma((n - 1,)),
            dma((n - 1,)),
            dma((n - 1,)),
            dma((n - 1,)),
        ],
        compiler_params=params_of(number),
        cost_estimate=cost(75),
        name="attend_back",
    )(sums, up, branch, norm, wo_all, h, o_all, info_col, info_row, q, k, v, lse, x, gain, cos, sine, pre, scale)


def shards(
    inputs,
    cotangent,
    documents,
    block_place,
    params,
    first_moment,
    second_moment,
    gains,
    gains_first,
    gains_second,
):
    tokens = inputs[0]
    upstream = cotangent[0]
    length, width = tokens.shape
    n_ctx = lax.axis_size("ctx")
    n_dp = lax.axis_size("dp")
    me_ctx = lax.axis_index("ctx")
    seq = length * n_ctx
    rows = params.shape[0]
    ff = (params.shape[1] - 4 * width) // 3
    hc = width // n_ctx
    half, group = n_ctx // 2, 2 * n_dp
    fh = ff // group
    parities = [[2 * p + side for p in range(half)] for side in range(2)]

    def gather_pairs(w):
        w = lax.all_gather(
            w.reshape(group * rows, w.shape[2]), "ctx", axis=0, tiled=True, axis_index_groups=parities
        )
        return w.reshape(half, n_dp, 2 * rows, w.shape[1])

    def scatter_pairs(g):
        g = lax.psum_scatter(
            g.reshape(width, g.shape[3]),
            "ctx",
            scatter_dimension=0,
            tiled=True,
            axis_index_groups=parities,
        )
        return g.reshape(group, rows, g.shape[1])

    w_gu, w_qkv, w_o, x_all, w_d = start(params, tokens, 1)
    w_gu = gather_pairs(w_gu)
    w_qkv, (cos_tab, sine_tab, info_row, info_col) = gather_dp(
        w_qkv.reshape(n_ctx * rows, 3 * hc), block_place, documents, 2
    )
    my_gains = lax.dynamic_slice_in_dim(gains[:2], me_ctx * hc, hc, axis=1)
    tables = (my_gains, cos_tab, sine_tab, info_col, info_row)

    branch, hidden1, queries, keys, values, attn_low, qk_pre, scales, lse, w_o, w_d = attend(
        x_all, w_qkv, w_o.reshape(n_ctx * rows, hc), w_d, tokens, gains[2:3], *tables, 3
    )

    result, d_mlp, g_ff_part, h1_all, gate_up, inner, w_d, w_o = ff_forward(
        hidden1, upstream, gains[3:4], w_gu, w_d.reshape(n_dp, 2 * rows, fh), w_o, 4
    )
    attn_low, d_mlp = lax.optimization_barrier((attn_low, d_mlp))
    attn_all = lax.all_gather(attn_low, "ctx", axis=0)
    d_gu, d_grad = ff_back(d_mlp, inner, w_d, gate_up, rows, 5)
    d_grad = scatter_pairs(d_grad)
    d_sums, g_grad, u_grad = ff_scatter(d_gu, w_gu, h1_all, length, 6)
    g_grad, u_grad = scatter_pairs(g_grad), scatter_pairs(u_grad)

    d_h1, g_attn_part, d_qkv, d_gain, qk_grad, wv_grad, wo_grad, d_grad = attend_back(
        d_sums, upstream, branch, gains[2:3], w_o, d_grad, attn_all, info_col, info_row, queries, keys, values, lse,
        x_all, my_gains, cos_tab, sine_tab, qk_pre, scales, 8,
    )
    qk_grad, g_grad, d_input = collect(qk_grad, g_grad, d_qkv, w_qkv, d_h1, 9)

    attn_grad, u_grad, sums, *masters = total_over(
        qk_grad, wv_grad, wo_grad, u_grad, g_grad, d_grad, d_gain, g_attn_part, g_ff_part,
        (params, first_moment, second_moment), 11,
    )
    grad_norm, new_gains, new_gains_first, new_gains_second, new_params, new_first, new_second = adam(
        sums, gains, gains_first, gains_second, *masters,
        attn_grad, wo_grad, g_grad, u_grad, d_grad,
    )
    return (
        result[None],
        d_input[None],
        grad_norm.reshape(()),
        new_params,
        new_first,
        new_second,
        new_gains,
        new_gains_first,
        new_gains_second,
    )


def solution(mesh):
    split, whole = P("dp", "ctx", None), P(("dp", "ctx"), None)
    return jax.shard_map(
        shards,
        mesh=mesh,
        in_specs=(split, split, P("dp", None), P(), whole, whole, whole, P(), P(), P()),
        out_specs=(split, split, P(), whole, whole, whole, P(), P(), P()),
        check_vma=False,
    )
```
